32 devices in a mesh: seq: 16 (over z, y, core), chan: 2 (over x).
Axes of the slice: x: 2, y: 2, z: 4, core: 2. Of those that a mesh axis runs over, the one named last changes fastest.
Arguments:
- tokens: bfloat16 [2, 4096, 1536], P(None, 'seq'), may hold values from -6 to 6
- gain_mix: float32 [1536], replicated, may hold values from 0.25 to 1.75
- w_in: bfloat16 [3, 1536, 1536], P(None, None, 'chan'), may hold values from -0.15625 to 0.15625
- kernel: float32 [3, 1536], P(None, 'chan'), may hold values from -3 to 3
- w_out: bfloat16 [1536, 1536], P('chan'), may hold values from -0.15625 to 0.15625
- gain_ffn: float32 [1536], replicated, may hold values from 0.25 to 1.75
- w_gate: bfloat16 [1536, 6912], P(None, 'chan'), may hold values from -0.15625 to 0.15625
- w_up: bfloat16 [1536, 6912], P(None, 'chan'), may hold values from -0.15625 to 0.15625
- w_down: bfloat16 [6912, 1536], P('chan'), may hold values from -0.078125 to 0.078125
- cotangent: bfloat16 [2, 4096, 1536], P(None, 'seq'), may hold values from -6 to 6
Outputs:
- block_out: bfloat16 [2, 4096, 1536], P(None, 'seq')
- d_tokens: bfloat16 [2, 4096, 1536], P(None, 'seq')
- g_gain_mix: float32 [1536], P('seq')
- g_w_in: float32 [3, 1536, 1536], P(None, 'seq', 'chan')
- g_kernel: float32 [3, 2, 768], P(None, 'chan', 'seq')
- g_w_out: float32 [1536, 1536], P('chan', 'seq')
- g_gain_ffn: float32 [1536], P('seq')
- g_w_gate: float32 [1536, 6912], P('seq', 'chan')
- g_w_up: float32 [1536, 6912], P('seq', 'chan')
- g_w_down: float32 [6912, 1536], P('chan', 'seq')
The draws below stay inside these ranges and needn't reach their ends.
All inputs are finite; a program needn't handle non-finite values.
Results may differ from the reference program's by a relative error of at most 0.017.
Values may be sent and summed in bfloat16 or wider, within the bound.
A program may use at most 320 MiB of HBM per device.

```python
import jax
import jax.numpy as jnp
from jax import lax

D = 1536
FF = 6912
KW = 3
SEQS = 2
LENGTH = 4096
N_CHAN = 2


def strengthened(drawn, own_key, source, target, blocks, factor):
    owner, partner = [(jnp.arange(drawn.shape[axis_at]) // (drawn.shape[axis_at] // blocks)).reshape([-1 if axis == axis_at else 1 for axis in range(drawn.ndim)]) for axis_at in (source, target)]
    chosen = jax.random.permutation(own_key, blocks)[partner]
    strong = (owner == chosen) | (owner == (partner + blocks // 2) % blocks)
    return jnp.where(strong, factor * drawn, drawn)


def shard_levels(key, extent, cuts, smallest, top_value):
    loudness = 1.0
    for dim, shards_of in cuts:
        draws = jax.random.uniform(jax.random.fold_in(jax.random.fold_in(key, 6), dim), (shards_of,), jnp.float32, smallest / len(cuts), top_value / len(cuts))
        loudness = loudness * jnp.repeat(jnp.exp(draws), extent[dim] // shards_of).reshape((-1,) + (1,) * (len(extent) - 1 - dim))
    return loudness


def normal_values(stream_key, shape, deviation, limit, shards=(), dtype=jnp.bfloat16):
    entries = jax.random.normal(stream_key, shape, jnp.float32) * deviation
    if len(shards) > 0:
        entries = shard_levels(stream_key, shape, shards, -0.22, 0.18) * entries
    return jnp.clip(entries, min=-limit, max=limit).astype(dtype)


def gaussian_with(stream_key, extent, spread, reach, cuts, heavy, kind=jnp.bfloat16):
    values = spread * jax.random.normal(stream_key, extent, jnp.float32)
    if cuts:
        values = values * shard_levels(stream_key, extent, cuts, -0.22, 0.18)
    return jnp.clip(strengthened(values, jax.random.fold_in(stream_key, 3), *heavy), -reach, reach).astype(kind)


def setup_inputs(seed: int = 0) -> dict:
    key_list = jax.random.split(jax.random.key(seed), 11)
    tokens = normal_values(key_list[0], (SEQS, LENGTH, D), 1.0, 6.0, ((1, 16),))
    gain_mix = jnp.clip(1.0 + 0.15 * jax.random.normal(key_list[1], (D,), jnp.float32), 0.25, 1.75)
    w_in = normal_values(key_list[2], (KW, D, D), D ** -0.5, 0.15625, ((2, 2),))
    kernel = normal_values(key_list[3], (KW, D), 0.6, 3.0, ((1, 2),), jnp.float32)
    w_out = normal_values(key_list[4], (D, D), D ** -0.5, 0.15625, ((0, 2),))
    gain_ffn = jnp.clip(1.0 + 0.15 * jax.random.normal(key_list[5], (D,), jnp.float32), 0.25, 1.75)
    w_gate = normal_values(key_list[6], (D, FF), D ** -0.5, 0.15625, ((1, 2),))
    w_up = normal_values(key_list[7], (D, FF), D ** -0.5, 0.15625, ((1, 2),))
    w_down = normal_values(key_list[8], (FF, D), FF ** -0.5, 0.078125, ((0, 2),))
    cotangent = gaussian_with(key_list[9], (SEQS, LENGTH, D), 1.0, 6.0, ((1, 16),), (1, 2, 16, 2.0))
    return {"tokens": tokens, "gain_mix": gain_mix, "w_in": w_in, "kernel": kernel, "w_out": w_out, "gain_ffn": gain_ffn, "w_gate": w_gate, "w_up": w_up, "w_down": w_down, "cotangent": cotangent}


epsilon = 1e-05

@jax.custom_vjp
def low(v):
    return lax.optimization_barrier(v.astype(jnp.bfloat16)).astype(jnp.float32)

@jax.custom_vjp
def low_back(v):
    return v

def low_keep(v):
    return (low(v), None)

def low_pass(kept, grad):
    return (grad,)

def back_keep(v):
    return (v, None)

def back_low(kept, grad):
    return (low(grad),)
low.defvjp(low_keep, low_pass)
low_back.defvjp(back_keep, back_low)

def rms_scale(vector):
    return lax.rsqrt(lax.optimization_barrier(jnp.mean(vector * vector, axis=-1, keepdims=True)) + epsilon)

def matmul(lhs_mat, rhs_mat):
    return jnp.dot(lhs_mat, rhs_mat, precision=lax.Precision.HIGHEST, preferred_element_type=jnp.float32)

def forward(tokens_f, gain_mix, w_in, kernel, w_out, gain_ffn, w_gate, w_up, w_down):
    h_mix = low(tokens_f * rms_scale(tokens_f) * gain_mix)
    proj_b = low_back(matmul(h_mix, w_in[0]))
    proj_c = low_back(matmul(h_mix, w_in[1]))
    proj_x = low_back(matmul(h_mix, w_in[2]))
    conv_in = low_back(low(proj_b * proj_x))
    padded = jnp.pad(conv_in, ((2, 0), (0, 0)))
    conv_out = kernel[0] * padded[:-2] + kernel[1] * padded[1:-1] + kernel[2] * padded[2:]
    gated = low(proj_c * conv_out)
    residual = tokens_f + low_back(matmul(gated, w_out))
    h_ffn = low(residual * rms_scale(residual) * gain_ffn)
    gate_pre = low_back(matmul(h_ffn, w_gate))
    up_value = low_back(matmul(h_ffn, w_up))
    hidden = low(jax.nn.silu(gate_pre) * up_value)
    return residual + matmul(hidden, w_down)

def add_up(running, addend):
    return running + addend

def reference(tokens, gain_mix, w_in, kernel, w_out, gain_ffn, w_gate, w_up, w_down, cotangent):
    params = (gain_mix.astype(jnp.float32), w_in.astype(jnp.float32), kernel.astype(jnp.float32), w_out.astype(jnp.float32), gain_ffn.astype(jnp.float32), w_gate.astype(jnp.float32), w_up.astype(jnp.float32), w_down.astype(jnp.float32))

    def one_sequence(totals, inputs):
        tokens_seq, cot_seq = inputs
        result, pullback = jax.vjp(forward, tokens_seq.astype(jnp.float32), *params)
        grads = pullback(cot_seq.astype(jnp.float32))
        totals = jax.tree.map(add_up, totals, tuple(grads[1:]))
        return (totals, (result.astype(jnp.bfloat16), grads[0].astype(jnp.bfloat16)))
    initial = jax.tree.map(jnp.zeros_like, params)
    totals, (block_out, d_tokens) = lax.scan(one_sequence, initial, (tokens, cotangent))
    return (block_out, d_tokens, totals[0], totals[1], totals[2].reshape(KW, N_CHAN, D // N_CHAN), totals[3], totals[4], totals[5], totals[6], totals[7])
```

```python
import functools

import jax
import jax.numpy as jnp
from jax import lax
from jax.experimental import pallas as pl
from jax.experimental.pallas import tpu as pltpu
from jax.sharding import PartitionSpec as P

epsilon = 1e-05
BF = jnp.bfloat16
F32 = jnp.float32
MESH = pl.DeviceIdType.MESH
LANE = 128
NZ = 4
ROWS_CHUNK = 128
ZF_COLS = 1152


def nn(a, b):
    return jnp.dot(a, b, preferred_element_type=F32)


def tn(a, b):
    return lax.dot_general(a, b, (((0,), (0,)), ((), ())), preferred_element_type=F32)


def nt(a, b):
    return lax.dot_general(a, b, (((1,), (1,)), ((), ())), preferred_element_type=F32)


def inv_rms(v):
    return lax.rsqrt(jnp.mean(v * v, axis=-1, keepdims=True) + epsilon)


class Take:
    def __init__(self, limit):
        self.used, self.limit = 0, limit

    def __call__(self, count=1):
        base = self.used
        self.used += count
        assert self.used <= self.limit
        return base


N_SEND, N_RECV, N_LOCAL = 128, 192, 64


def step_kernel(
    dims,
    tokens, gain_mix, w_in, taps, w_out, gain_ffn, w_gate, w_up, w_down, cot,
    block_out, d_tokens, g_ffn, g_conv, small_out,
    gb0, gb1, gb2, gb3, gb4, yb0, yb1, yb2, yb3, yb4, zb0, zb1, zb2, zb3, zb4,
    cr_dh, cr_dn, xr_dh, xr_dn, xr_d1,
    tok_v, wg_v, wu_v, wd_v, dy_v, h2_v, h1_v, hid, dg, du, pb, pc, px, bx, gated, resid, mix_r,
    ring, rb, ld, outs, halo_s, halo_r, dhalo_s, dhalo_r, tail, pb_tail, px_tail,
    sm, sm_r, ss, rs, ls,
):
    R, T, D, CL, FL, FW = dims
    S = R // T
    CH = CL // 2
    GR = D // NZ
    SR = GR // 2
    DR = SR // 2
    NCH = R // ROWS_CHUNK
    take_s, take_r, take_l = Take(N_SEND), Take(N_RECV), Take(N_LOCAL)

    s = lax.axis_index("seq")
    x = lax.axis_index("chan")
    n_seq = 4 * NZ
    z, y, c = s // 4, (s // 2) % 2, s % 2

    def did(z_, y_, c_):
        return ((z_ * 2 + y_) * 2 + c_, x)

    core_dev = did(z, y, 1 - c)
    y_dev = did(z, 1 - y, c)
    x_dev = (s, 1 - x)
    mid = jnp.logical_and(z > 0, z < NZ - 1)
    end = jnp.logical_not(mid)

    def remote(src, dst, si, ri, dev):
        return pltpu.make_async_remote_copy(
            src_ref=src, dst_ref=dst, send_sem=ss.at[si], recv_sem=rs.at[ri],
            device_id=dev, device_id_type=MESH,
        )

    def wait_recv(dst, ri):
        remote(dst, dst, 0, ri, core_dev).wait_recv()

    def wait_send(src, si):
        remote(src, src, si, 0, core_dev).wait_send()

    def local(src, dst, li):
        return pltpu.make_async_copy(src, dst, ls.at[li])

    l_tok, l_win, l_wout, l_dy = take_l(), take_l(3), take_l(), take_l()
    ld_tok = local(tokens, tok_v, l_tok)
    ld_tok.start()
    win_views = [wg_v.at[:, pl.ds(0, CL)], wg_v.at[:, pl.ds(CL, CL)], wu_v.at[:, pl.ds(0, CL)]]
    wout_view = wd_v.at[pl.ds(0, CL), :]

    def load_w_in():
        return [local(w_in.at[m], win_views[m], l_win + m) for m in range(3)]

    for cp in load_w_in():
        cp.start()
    ld_wout = local(w_out, wout_view, l_wout)
    ld_wout.start()
    ld_dy = local(cot, dy_v.at[0], l_dy)
    ld_dy.start()

    bar = pltpu.get_barrier_semaphore()

    def greet(dev):
        pl.semaphore_signal(bar, inc=1, device_id=dev, device_id_type=MESH)

    greet(core_dev)
    greet(y_dev)
    greet(x_dev)
    for k in range(1, NZ):
        greet(did((z + k) % NZ, y, c))
    has_prev = s > 0
    has_next = s < n_seq - 1
    prev_dev = ((s + n_seq - 1) % n_seq, x)
    next_dev = ((s + 1) % n_seq, x)
    greet(prev_dev)
    greet(next_dev)
    pl.semaphore_wait(bar, 4 + NZ)

    s_dy, r_dy = take_s(), take_r()
    send_dy = remote(cot, dy_v.at[1], s_dy, r_dy, core_dev)
    send_dy.start()

    sm[...] = jnp.zeros_like(sm)
    k_taps = [taps[t : t + 1, :] for t in range(3)]

    ld_tok.wait()

    def norm_rows(k, _):
        rows = pl.ds(pl.multiple_of(k * ROWS_CHUNK, ROWS_CHUNK), ROWS_CHUNK)
        xv = tok_v[rows, :].astype(F32)
        h1_v[0, rows, :] = (xv * inv_rms(xv) * gain_mix[...]).astype(BF)
        return 0

    lax.fori_loop(0, NCH, norm_rows, 0)
    s_h1, r_h1 = take_s(), take_r()
    send_h1 = remote(h1_v.at[0], h1_v.at[1], s_h1, r_h1, core_dev)
    send_h1.start()
    for cp in load_w_in():
        cp.wait()

    NC = CL // 256

    def in_proj(j, _):
        cols = pl.ds(pl.multiple_of(j * 256, 256), 256)
        cols1 = pl.ds(pl.multiple_of(CL + j * 256, 256), 256)
        h = h1_v[0]
        b = nn(h, wg_v[:, cols])
        pb[:, cols] = b.astype(BF)
        xx = nn(h, wu_v[:, cols])
        px[:, cols] = xx.astype(BF)
        bx[:, cols] = (b * xx).astype(BF)
        pc[:, cols] = nn(h, wg_v[:, cols1]).astype(BF)
        return 0

    lax.fori_loop(0, NC, in_proj, 0)
    l_w = take_l(3)
    win_start = pl.multiple_of(c * (FL - FW), LANE)
    ld_wg = local(w_gate.at[:, pl.ds(win_start, FW)], wg_v, l_w)
    ld_wu = local(w_up.at[:, pl.ds(win_start, FW)], wu_v, l_w + 1)
    ld_wd = local(w_down.at[pl.ds(win_start, FW), :], wd_v, l_w + 2)
    ld_wg.start()
    ld_wu.start()

    s_ha, r_ha = take_s(), take_r()
    for q in range(S):
        halo_s[q] = bx[q * T + T - 16 : q * T + T, :]
    send_halo = remote(halo_s, halo_r, s_ha, r_ha, next_dev)

    @pl.when(has_next)
    def _():
        send_halo.start()

    @pl.when(has_prev)
    def _():
        wait_recv(halo_r, r_ha)

    @pl.when(jnp.logical_not(has_prev))
    def _():
        halo_r[...] = jnp.zeros_like(halo_r)

    row_iota = lax.broadcasted_iota(jnp.int32, (T, 256), 0)

    def conv_terms(q, cols):
        now = bx[pl.ds(q * T, T), cols].astype(F32)
        h = halo_r[q, :, cols].astype(F32)
        h14 = jnp.broadcast_to(h[14:15], now.shape)
        h15 = jnp.broadcast_to(h[15:16], now.shape)
        one = jnp.where(row_iota == 0, h15, pltpu.roll(now, 1, 0))
        two = jnp.where(row_iota == 0, h14, jnp.where(row_iota == 1, h15, pltpu.roll(now, 2, 0)))
        return now, one, two

    def tap_cols(cols):
        return [taps[t : t + 1, cols] for t in range(3)]

    ld_wout.wait()
    s_mx, r_mx = take_s(NCH), take_r(NCH)
    CPS = T // ROWS_CHUNK
    for q in range(S):

        def conv_tile(j, _, q=q):
            cols = pl.ds(pl.multiple_of(j * 256, 256), 256)
            now, one, two = conv_terms(q, cols)
            k0, k1, k2 = tap_cols(cols)
            cv = k0 * two + k1 * one + k2 * now
            rows = pl.ds(q * T, T)
            gated[rows, cols] = (pc[rows, cols].astype(F32) * cv).astype(BF)
            return 0

        lax.fori_loop(0, NC, conv_tile, 0)

        def out_tile(j, _, q=q):
            cols = pl.ds(pl.multiple_of(j * 512, 512), 512)
            v = nn(gated[q * T : q * T + T, :], wd_v[0:CL, cols]).astype(BF)
            ring[q * CPS : q * CPS + CPS, :, cols] = v.reshape(CPS, ROWS_CHUNK, 512)
            return 0

        lax.fori_loop(0, D // 512, out_tile, 0)
        for k in range(q * CPS, q * CPS + CPS):
            remote(ring.at[k], mix_r.at[k], s_mx + k, r_mx + k, x_dev).start()
    ld_wd.start()

    s_h2, r_h2 = take_s(NCH), take_r(NCH)
    ld_dy.wait()
    send_dy.wait()
    ld_wg.wait()
    ld_wu.wait()
    ld_wd.wait()
    NF = FW // 256
    overlap = 2 * FW - FL
    col_iota = lax.broadcasted_iota(jnp.int32, (2 * ROWS_CHUNK, 256), 1)

    def residual_chunk(k):
        rows = pl.ds(pl.multiple_of(k * ROWS_CHUNK, ROWS_CHUNK), ROWS_CHUNK)
        wait_recv(mix_r.at[k], r_mx + k)
        res = tok_v[rows, :].astype(F32) + (ring[k].astype(F32) + mix_r[k].astype(F32))
        resid[rows, :] = res
        h2_v[0, rows, :] = (res * inv_rms(res) * gain_ffn[...]).astype(BF)
        remote(h2_v.at[0, rows], h2_v.at[1, rows], s_h2 + k, r_h2 + k, core_dev).start()

    def ffn_chunk(k):
        rows = pl.ds(pl.multiple_of(k * ROWS_CHUNK, ROWS_CHUNK), ROWS_CHUNK)
        wait_recv(h2_v.at[1, rows], r_h2 + k)

        def tile(j, _):
            cols = pl.ds(pl.multiple_of(j * 256, 256), 256)
            h = h2_v[:, rows, :].reshape(2 * ROWS_CHUNK, D)
            e = dy_v[:, rows, :].reshape(2 * ROWS_CHUNK, D)
            g = nn(h, wg_v[:, cols])
            u = nn(h, wu_v[:, cols])
            dh = nt(e, wd_v[cols, :])
            keep = col_iota + j * 256 >= c * overlap
            sg = jax.nn.sigmoid(g)
            si = g * sg
            dh = jnp.where(keep, dh, 0.0)
            shape = (2, ROWS_CHUNK, 256)
            hid[:, rows, cols] = jnp.where(keep, si * u, 0.0).astype(BF).reshape(shape)
            dg[:, rows, cols] = (dh * u * sg * (1.0 + g * (1.0 - sg))).astype(BF).reshape(shape)
            du[:, rows, cols] = (dh * si).astype(BF).reshape(shape)
            return 0

        lax.fori_loop(0, NF, tile, 0)

    residual_chunk(0)

    def chunk_loop(k, _):
        @pl.when(k + 1 < NCH)
        def _():
            residual_chunk(k + 1)

        ffn_chunk(k)
        return 0

    lax.fori_loop(0, NCH, chunk_loop, 0)
    for k in range(NCH):
        wait_send(ring.at[k], s_mx + k)
        wait_send(h2_v.at[0, pl.ds(k * ROWS_CHUNK, ROWS_CHUNK)], s_h2 + k)

    gbs = [gb0, gb1, gb2, gb3, gb4]
    ybs = [yb0, yb1, yb2, yb3, yb4]
    zbs = [zb0, zb1, zb2, zb3, zb4]
    widths = [ZF_COLS, FW - ZF_COLS, FW, FW, 2 * CL]
    s_y = [None] + [take_s(NZ) for _ in range(4)]
    r_y = [None] + [take_r(NZ) for _ in range(4)]
    s_z = [take_s(2 * NZ)] + [take_s(NZ) for _ in range(4)]
    r_z = [take_r(4 * NZ)] + [take_r(2 * NZ) for _ in range(4)]

    def order(e):
        if e == NZ - 1:
            return z
        per_z = {0: (3, 2, 1), 1: (3, 0, 2), 2: (0, 3, 1), 3: (0, 1, 2)}
        v = jnp.int32(per_z[3][e])
        for zz in range(3):
            v = jnp.where(z == zz, per_z[zz][e], v)
        return v

    def order_dyn(u):
        v = order(NZ - 1)
        for e in range(NZ - 1):
            v = jnp.where(u == e, order(e), v)
        return v

    def z_send(j, src, e, zp, h=None):
        to_right = zp > z
        d = jnp.where(to_right, 0, 1)
        dev = did(jnp.clip(jnp.where(to_right, z + 1, z - 1), 0, NZ - 1), y, c)
        if h is None:
            return remote(src, zbs[j].at[d, zp], s_z[j] + e, r_z[j] + d * NZ + zp, dev)
        return remote(
            src, zbs[j].at[d, zp, h], s_z[j] + 2 * e + h, r_z[j] + (d * NZ + zp) * 2 + h, dev
        )

    l_g = take_l(12)

    def g_block(lhs_ref, rhs_ref, zp, pair):
        lhs = lhs_ref[:, :, pl.ds(pl.multiple_of(zp * GR, GR), GR)].reshape(2 * R, GR)
        half = FW // 2
        for n in range(2):
            v = tn(lhs, rhs_ref[:, :, n * half : (n + 1) * half].reshape(2 * R, half)).astype(BF)
            outs[2 * pair, :, n * half : (n + 1) * half] = v[:SR]
            outs[2 * pair + 1, :, n * half : (n + 1) * half] = v[SR:]

    def g_step(u, _):
        zp = order_dyn(u)

        def down_copies():
            return [
                cp
                for h in range(2)
                for cp in (
                    local(outs.at[h, :, pl.ds(0, ZF_COLS)], gb0.at[zp, h], l_g + 2 * h),
                    local(
                        outs.at[h, :, pl.ds(ZF_COLS, FW - ZF_COLS)], gb1.at[zp, h], l_g + 2 * h + 1
                    ),
                )
            ]

        def plain_copies(gb, pair, li):
            return [local(outs.at[2 * pair + h], gb.at[zp, h], li + h) for h in range(2)]

        def y_send(j):
            remote(gbs[j].at[zp, 1 - y], ybs[j].at[zp], s_y[j] + u, r_y[j] + u, y_dev).start()

        g_block(dy_v, hid, zp, 0)
        for cp in down_copies():
            cp.start()
        g_block(h2_v, dg, zp, 1)
        for cp in plain_copies(gb2, 1, l_g + 4):
            cp.start()
        for cp in down_copies():
            cp.wait()
        y_send(1)

        @pl.when(jnp.logical_and(end, u < NZ - 1))
        def _():
            for h in range(2):
                z_send(0, gb0.at[zp, h], u, zp, h).start()

        g_block(h2_v, du, zp, 0)
        for cp in plain_copies(gb3, 0, l_g + 6):
            cp.start()
        for cp in plain_copies(gb2, 1, l_g + 4):
            cp.wait()
        y_send(2)
        for cp in plain_copies(gb3, 0, l_g + 6):
            cp.wait()
        y_send(3)
        return 0

    lax.fori_loop(0, NZ, g_step, 0)

    l_e = take_l(4)
    slot_last = [None] * outs.shape[0]
    slot_next = [0]

    def claim_slot():
        o = slot_next[0]
        slot_next[0] = (o + 1) % outs.shape[0]
        if slot_last[o] is not None:
            slot_last[o]()
            slot_last[o] = None
        return o

    ADD_ROWS = 32

    def add_into(dst, srcs):
        def rows_add(k, _):
            rows = pl.ds(pl.multiple_of(k * ADD_ROWS, ADD_ROWS), ADD_ROWS)
            acc = srcs[0][rows, :].astype(F32)
            for src in srcs[1:]:
                acc = acc + src[rows, :].astype(F32)
            dst[rows, :] = acc.astype(BF)
            return 0

        lax.fori_loop(0, SR // ADD_ROWS, rows_add, 0)

    def add_more(dst, src):
        def rows_add(k, _):
            rows = pl.ds(pl.multiple_of(k * ADD_ROWS, ADD_ROWS), ADD_ROWS)
            dst[rows, :] = (dst[rows, :].astype(F32) + src[rows, :].astype(F32)).astype(BF)
            return 0

        lax.fori_loop(0, SR // ADD_ROWS, rows_add, 0)

    def line_event(j, e, h=None):
        zp = order(e)
        w = widths[j]
        d = jnp.where(zp > z, 0, 1)
        la, lb, lc = (ld.at[i, :, pl.ds(0, w)] for i in range(3))
        if h is None:
            zsrc, ri = zbs[j].at[d, zp], r_z[j] + d * NZ + zp
            si = s_z[j] + e
            o = claim_slot()
            dst = outs.at[o, :, pl.ds(0, w)]
            ca = local(gbs[j].at[zp, y], la, l_e)
            ca.start()
            wait_recv(ybs[j].at[zp], r_y[j] + e)
            cb = local(ybs[j].at[zp], lb, l_e + 1)
            cb.start()

            @pl.when(mid)
            def _():
                wait_recv(zsrc, ri)
                cc = local(zsrc, lc, l_e + 2)
                cc.start()
                ca.wait()
                cb.wait()
                cc.wait()
                add_into(dst, [la, lb, lc])

            @pl.when(end)
            def _():
                ca.wait()
                cb.wait()
                add_into(dst, [la, lb])

            z_send(j, dst, e, zp).start()
            slot_last[o] = lambda: wait_send(dst, si)
        else:
            zsrc, ri = zbs[j].at[d, zp, h], r_z[j] + (d * NZ + zp) * 2 + h
            si = s_z[j] + 2 * e + h
            o = claim_slot()
            dst = outs.at[o, :, pl.ds(0, w)]

            @pl.when(mid)
            def _():
                ca = local(gbs[j].at[zp, h], la, l_e)
                ca.start()
                wait_recv(zsrc, ri)
                cc = local(zsrc, lc, l_e + 2)
                cc.start()
                ca.wait()
                cc.wait()
                add_into(dst, [la, lc])
                z_send(j, dst, e, zp, h).start()

            def last():
                @pl.when(mid)
                def _():
                    wait_send(dst, si)

            slot_last[o] = last

    def gather_final(j, dst, own, with_y, h=None):
        w = widths[j]
        la, lb, lc, ldd = (ld.at[i, :, pl.ds(0, w)] for i in range(4))
        ca = local(own, la, l_e)
        ca.start()
        if with_y:
            wait_recv(ybs[j].at[z], r_y[j] + NZ - 1)
            cb = local(ybs[j].at[z], lb, l_e + 1)
            cb.start()

        def side(d):
            if h is None:
                return zbs[j].at[d, z], r_z[j] + d * NZ + z
            return zbs[j].at[d, z, h], r_z[j] + (d * NZ + z) * 2 + h

        def fetch(d, to, li):
            src, ri = side(d)
            wait_recv(src, ri)
            cp = local(src, to, li)
            cp.start()
            return cp

        base = [la, lb] if with_y else [la]

        def finish(cps, srcs):
            ca.wait()
            if with_y:
                cb.wait()
            for cp in cps:
                cp.wait()
            add_into(dst, srcs)

        @pl.when(mid)
        def _():
            c0 = fetch(0, lc, l_e + 2)
            c1 = fetch(1, ldd, l_e + 3)
            finish([c0, c1], base + [lc, ldd])

        @pl.when(z == 0)
        def _():
            c1 = fetch(1, ldd, l_e + 3)
            finish([c1], base + [ldd])

        @pl.when(z == NZ - 1)
        def _():
            c0 = fetch(0, lc, l_e + 2)
            finish([c0], base + [lc])

    finals = []

    def swap_pieces(j, dst):
        if j == 4:
            return [(None, m * CH, CH, g_conv.at[m], c * CH) for m in range(4)]
        mat = g_ffn.at[{0: 0, 1: 0, 2: 1, 3: 2}[j]]
        off = ZF_COLS if j == 1 else 0
        w = widths[j]
        if j == 1:
            return [(None, 0, w, mat, c * (FL - FW) + off)]
        return [(0, 0, w, mat, 0), (1, overlap, w - overlap, mat, FL - FW + overlap)]

    def final_out(j, dst):
        for cond, c0, w, mat, to in swap_pieces(j, dst):
            si, ri, li = take_s(), take_r(), take_l()
            to = pl.multiple_of(to, LANE) if not isinstance(to, int) else to
            keep = local(
                dst.at[pl.ds(pl.multiple_of(c * DR, DR), DR), pl.ds(c0, w)],
                mat.at[:, pl.ds(to, w)], li,
            )
            give = remote(
                dst.at[pl.ds(pl.multiple_of((1 - c) * DR, DR), DR), pl.ds(c0, w)],
                mat.at[:, pl.ds(to, w)], si, ri, core_dev,
            )
            if cond is None:
                keep.start()
                give.start()
                finals.append((None, keep, give, mat, w, ri))
            else:

                @pl.when(c == cond)
                def _():
                    keep.start()
                    give.start()

                finals.append((cond, keep, give, mat, w, ri))

    def drain_final(item):
        cond, keep, give, mat, w, ri = item
        got = mat.at[:, pl.ds(0, w)]
        if cond is None:
            keep.wait()
            give.wait_send()
            wait_recv(got, ri)
        else:

            @pl.when(c == cond)
            def _():
                keep.wait()
                give.wait_send()

            @pl.when(c != cond)
            def _():
                wait_recv(got, ri)

    def final_event(j):
        o = claim_slot()
        dst = outs.at[o, :, pl.ds(0, widths[j])]
        gather_final(j, dst, gbs[j].at[z, y], True)
        n0 = len(finals)
        final_out(j, dst)
        mine = finals[n0:]
        del finals[n0:]

        def last():
            for item in mine:
                drain_final(item)

        slot_last[o] = last

    s_f0, r_f0 = take_s(), take_r()

    def final0_send():
        o = claim_slot()
        dst = outs.at[o, :, pl.ds(0, widths[0])]
        w = widths[0]
        gather_final_h(dst, 1 - y)
        remote(dst, yb0, s_f0, r_f0, y_dev).start()
        slot_last[o] = lambda: wait_send(dst, s_f0)

    def gather_final_h(dst, h):
        gather_final(0, dst, gb0.at[z, h], False, h)

    def final0_finish():
        o = claim_slot()
        w = widths[0]
        dst = outs.at[o, :, pl.ds(0, w)]
        gather_final_h(dst, y)
        wait_recv(yb0, r_f0)
        cp = local(yb0, ld.at[0, :, pl.ds(0, w)], l_e)
        cp.start()
        cp.wait()
        add_more(dst, ld.at[0, :, pl.ds(0, w)])
        n0 = len(finals)
        final_out(0, dst)
        mine = finals[n0:]
        del finals[n0:]

        def last():
            for item in mine:
                drain_final(item)

        slot_last[o] = last

    HALF = 2 * ROWS_CHUNK

    def split_sum(product, cr, xr, base_a, base_d):
        s_c, r_c = take_s(2), take_r(2)
        s_x, r_x = take_s(NCH), take_r(NCH)
        l_c = take_l()

        def give(k, _):
            def tile(n, _):
                cols = pl.ds(pl.multiple_of(n * 512, 512), 512)
                v = product(1, k * HALF, n).astype(BF)
                ring[pl.ds(base_a + 2 * k, 2), :, cols] = v.reshape(2, ROWS_CHUNK, 512)
                return 0

            lax.fori_loop(0, D // 512, tile, 0)
            remote(
                ring.at[pl.ds(base_a + 2 * k, 2)], cr.at[pl.ds(2 * k, 2)], s_c + k, r_c + k, core_dev
            ).start()
            return 0

        lax.fori_loop(0, 2, give, 0)

        def keep(k, _):
            src = cr.at[pl.ds(2 * k, 2)]
            wait_recv(src, r_c + k)
            cp = local(src, rb, l_c)
            cp.start()
            cp.wait()

            def tile(n, _):
                cols = pl.ds(pl.multiple_of(n * 512, 512), 512)
                v = product(0, k * HALF, n) + rb[:, :, cols].reshape(HALF, 512).astype(F32)
                ring[pl.ds(base_d + 2 * k, 2), :, cols] = v.astype(BF).reshape(2, ROWS_CHUNK, 512)
                return 0

            lax.fori_loop(0, D // 512, tile, 0)
            for i in range(2):
                remote(
                    ring.at[base_d + 2 * k + i], xr.at[2 * k + i], s_x + 2 * k + i, r_x + 2 * k + i, x_dev
                ).start()
            return 0

        lax.fori_loop(0, 2, keep, 0)
        for k in range(2):
            wait_send(ring.at[pl.ds(base_a + 2 * k, 2)], s_c + k)
        return s_x, r_x

    def rows_at(ref, slot, r0):
        return ref[slot, pl.ds(pl.multiple_of(r0, HALF), HALF), :]

    def dh_product(slot, r0, n):
        cols = pl.ds(pl.multiple_of(n * 512, 512), 512)
        return nt(rows_at(dg, slot, r0), wg_v[cols, :]) + nt(rows_at(du, slot, r0), wu_v[cols, :])

    def dn_product(slot, r0, n):
        cols = pl.ds(pl.multiple_of(n * 512, 512), 512)
        return nn(rows_at(hid, slot, r0), wd_v[:, cols])

    s_xdh, r_xdh = split_sum(dh_product, cr_dh, xr_dh, 0, 4)
    for h in range(2):
        line_event(0, 0, h)
    s_xdn, r_xdn = split_sum(dn_product, cr_dn, xr_dn, 0, 8)
    for cp in load_w_in():
        cp.start()
    ld_wout.start()

    for j in (1, 2):
        line_event(j, 0)
    for h in range(2):
        line_event(0, 1, h)
    line_event(3, 0)

    l_x = take_l()
    s_do, r_do = take_s(NCH), take_r(NCH)
    xbuf = rb.at[0]

    def ffn_norm_back(k, _):
        rows = pl.ds(pl.multiple_of(k * ROWS_CHUNK, ROWS_CHUNK), ROWS_CHUNK)
        wait_recv(xr_dh.at[k], r_xdh + k)
        cp = local(xr_dh.at[k], xbuf, l_x)
        cp.start()
        cp.wait()
        d_h = ring[4 + k].astype(F32) + xbuf[...].astype(F32)
        res = resid[rows, :]
        s2 = inv_rms(res)
        n2 = res * s2
        sm[0, 1:2, :] += jnp.sum(d_h * n2, axis=0, keepdims=True)
        e2 = d_h * gain_ffn[...]
        d_res = dy_v[0, rows, :].astype(F32) + s2 * (
            e2 - n2 * jnp.mean(e2 * n2, axis=-1, keepdims=True)
        )
        h2_v[0, rows, :] = d_res.astype(BF)
        remote(h2_v.at[0, rows], h2_v.at[1, rows], s_do + k, r_do + k, core_dev).start()
        return 0

    lax.fori_loop(0, NCH, ffn_norm_back, 0)
    for k in range(NCH):
        wait_send(ring.at[4 + k], s_xdh + k)

    for cp in load_w_in():
        cp.wait()
    ld_wout.wait()
    for q in range(S):

        def conv_back(j, _, q=q):
            cols = pl.ds(pl.multiple_of(j * 256, 256), 256)
            rows = pl.ds(q * T, T)
            now, one, two = conv_terms(q, cols)
            k0, k1, k2 = tap_cols(cols)
            cv = k0 * two + k1 * one + k2 * now
            d_g = nt(h2_v[0, q * T : q * T + T, :], wd_v[cols, :])
            d_cv = d_g * pc[rows, cols].astype(F32)
            sm[0, 2:3, cols] += jnp.sum(d_cv * two, axis=0, keepdims=True)
            sm[0, 3:4, cols] += jnp.sum(d_cv * one, axis=0, keepdims=True)
            sm[0, 4:5, cols] += jnp.sum(d_cv * now, axis=0, keepdims=True)
            after1 = jnp.where(row_iota < T - 1, pltpu.roll(d_cv, T - 1, 0), 0.0)
            after2 = jnp.where(row_iota < T - 2, pltpu.roll(d_cv, T - 2, 0), 0.0)
            d_bx = k2 * d_cv + k1 * after1 + k0 * after2
            dhalo_s[q, :, cols] = d_cv[0:8]
            tail[q, :, cols] = d_bx[T - 16 : T]
            old_b = pb[rows, cols]
            old_x = px[rows, cols]
            pb_tail[q, :, cols] = old_b[T - 16 : T]
            px_tail[q, :, cols] = old_x[T - 16 : T]
            low = d_bx.astype(BF).astype(F32)
            pb[rows, cols] = (low * old_x.astype(F32)).astype(BF)
            px[rows, cols] = (low * old_b.astype(F32)).astype(BF)
            pc[rows, cols] = (d_g * cv).astype(BF)
            return 0

        lax.fori_loop(0, NC, conv_back, 0)

    s_dha, r_dha = take_s(), take_r()
    send_dhalo = remote(dhalo_s, dhalo_r, s_dha, r_dha, prev_dev)

    @pl.when(has_prev)
    def _():
        send_dhalo.start()

    @pl.when(has_next)
    def _():
        wait_recv(dhalo_r, r_dha)

    @pl.when(jnp.logical_not(has_next))
    def _():
        dhalo_r[...] = jnp.zeros_like(dhalo_r)

    tail_iota = lax.broadcasted_iota(jnp.int32, (16, CL), 0)
    for q in range(S):
        first = jnp.broadcast_to(dhalo_r[q, 0:1, :], (16, CL))
        second = jnp.broadcast_to(dhalo_r[q, 1:2, :], (16, CL))
        fix = jnp.where(
            tail_iota == 14,
            k_taps[0] * first,
            jnp.where(tail_iota == 15, k_taps[1] * first + k_taps[0] * second, 0.0),
        )
        low = (tail[q] + fix).astype(BF).astype(F32)
        rows = pl.ds(q * T + T - 16, 16)
        pb[rows, :] = (low * px_tail[q].astype(F32)).astype(BF)
        px[rows, :] = (low * pb_tail[q].astype(F32)).astype(BF)

    s_dp, r_dp = take_s(4), take_r(4)
    theirs = pl.ds(pl.multiple_of((1 - c) * CH, LANE), CH)
    ours = pl.ds(pl.multiple_of(c * CH, LANE), CH)
    dp_sends = [
        remote(ref.at[:, theirs], dy_v.at[1, :, pl.ds(m * CH, CH)], s_dp + m, r_dp + m, core_dev)
        for m, ref in enumerate((pb, pc, px, gated))
    ]
    for cp in dp_sends:
        cp.start()

    s_x1, r_x1 = take_s(NCH), take_r(NCH)

    def d1_half(k, _):
        r0 = pl.ds(pl.multiple_of(k * HALF, HALF), HALF)

        def tile(n, _):
            cols = pl.ds(pl.multiple_of(n * 512, 512), 512)
            v = (
                nt(pb[r0, :], wg_v[cols, 0:CL])
                + nt(pc[r0, :], wg_v[cols, CL : 2 * CL])
                + nt(px[r0, :], wu_v[cols, 0:CL])
            )
            ring[pl.ds(4 + 2 * k, 2), :, cols] = v.astype(BF).reshape(2, ROWS_CHUNK, 512)
            return 0

        lax.fori_loop(0, D // 512, tile, 0)
        for i in range(2):
            remote(
                ring.at[4 + 2 * k + i], xr_d1.at[2 * k + i], s_x1 + 2 * k + i, r_x1 + 2 * k + i, x_dev
            ).start()
        return 0

    lax.fori_loop(0, 2, d1_half, 0)

    wait_recv(h1_v.at[1], r_h1)
    for k in range(NCH):
        rows = pl.ds(k * ROWS_CHUNK, ROWS_CHUNK)
        wait_recv(h2_v.at[1, rows], r_do + k)
    for m in range(4):
        wait_recv(dy_v.at[1, :, pl.ds(m * CH, CH)], r_dp + m)
    W4 = widths[4]
    g4 = [dg.at[i, pl.ds(k * SR, SR), pl.ds(0, W4)] for i in range(2) for k in range(2)]

    def g_mixer(u, _):
        zp = order_dyn(u)
        zc = pl.ds(pl.multiple_of(zp * GR, GR), GR)
        for m, (mine, lhs) in enumerate(((pb, h1_v), (pc, h1_v), (px, h1_v), (gated, h2_v))):
            v = tn(lhs[0, :, zc], mine[:, ours]) + tn(
                lhs[1, :, zc], dy_v[1, :, m * CH : (m + 1) * CH]
            )
            v = v.astype(BF)
            g4[0][:, m * CH : (m + 1) * CH] = v[:SR]
            g4[1][:, m * CH : (m + 1) * CH] = v[SR:]
        cps = [local(g4[h], gb4.at[zp, h], l_g + h) for h in range(2)]
        for cp in cps:
            cp.start()
        for cp in cps:
            cp.wait()
        remote(gb4.at[zp, 1 - y], yb4.at[zp], s_y[4] + u, r_y[4] + u, y_dev).start()
        return 0

    lax.fori_loop(0, NZ, g_mixer, 0)

    for h in range(2):
        line_event(0, 2, h)
    for e in (1, 2):
        for j in (1, 2, 3):
            line_event(j, e)
    final0_send()

    l_o = take_l()

    def block_chunk(k, _):
        rows = pl.ds(pl.multiple_of(k * ROWS_CHUNK, ROWS_CHUNK), ROWS_CHUNK)
        wait_recv(xr_dn.at[k], r_xdn + k)
        cp = local(xr_dn.at[k], xbuf, l_x)
        cp.start()
        cp.wait()
        total = ring[8 + k].astype(F32) + xbuf[...].astype(F32)
        rb[1] = (resid[rows, :] + total).astype(BF)
        co = local(rb.at[1], block_out.at[rows, :], l_o)
        co.start()
        co.wait()
        return 0

    lax.fori_loop(0, NCH, block_chunk, 0)
    final0_finish()

    def mix_norm_back(k, _):
        rows = pl.ds(pl.multiple_of(k * ROWS_CHUNK, ROWS_CHUNK), ROWS_CHUNK)
        wait_recv(xr_d1.at[k], r_x1 + k)
        cp = local(xr_d1.at[k], xbuf, l_x)
        cp.start()
        cp.wait()
        d_h = ring[4 + k].astype(F32) + xbuf[...].astype(F32)
        xv = tok_v[rows, :].astype(F32)
        s1 = inv_rms(xv)
        n1 = xv * s1
        sm[0, 0:1, :] += jnp.sum(d_h * n1, axis=0, keepdims=True)
        e1 = d_h * gain_mix[...]
        out = h2_v[0, rows, :].astype(F32) + s1 * (
            e1 - n1 * jnp.mean(e1 * n1, axis=-1, keepdims=True)
        )
        rb[1] = out.astype(BF)
        co = local(rb.at[1], d_tokens.at[rows, :], l_o)
        co.start()
        co.wait()
        return 0

    lax.fori_loop(0, NCH, mix_norm_back, 0)

    for e in range(NZ - 1):
        line_event(4, e)

    s_sm, r_sm = take_s(2 + NZ), take_r(2 + NZ)
    a = remote(sm.at[0], sm_r.at[0], s_sm, r_sm, core_dev)
    a.start()
    a.wait()
    sm[1] = sm[0] + sm_r[0]
    b = remote(sm.at[1], sm_r.at[1], s_sm + 1, r_sm + 1, y_dev)
    b.start()
    b.wait()
    sm[2] = sm[1] + sm_r[1]
    for k in range(1, NZ):
        remote(
            sm.at[2], sm_r.at[1 + k], s_sm + 1 + k, r_sm + 1 + k, did((z + k) % NZ, y, c)
        ).start()
    total = sm[2]
    for k in range(1, NZ):
        wait_recv(sm_r.at[1 + k], r_sm + 1 + k)
        total = total + sm_r[1 + k]
    small_out[...] = total
    for k in range(1, NZ):
        wait_send(sm.at[2], s_sm + 1 + k)

    for j in (1, 2, 3, 4):
        final_event(j)

    for o in range(len(slot_last)):
        if slot_last[o] is not None:
            slot_last[o]()

    @pl.when(end)
    def _():
        for e in range(NZ - 1):
            for h in range(2):
                wait_send(gb0.at[0, h], s_z[0] + 2 * e + h)

    for j in range(1, 5):
        for u in range(NZ):
            wait_send(ybs[j].at[0], s_y[j] + u)
    send_h1.wait_send()
    for k in range(NCH):
        wait_send(h2_v.at[0, pl.ds(k * ROWS_CHUNK, ROWS_CHUNK)], s_do + k)
        wait_send(ring.at[4 + k], s_x1 + k)
        wait_send(ring.at[8 + k], s_xdn + k)
    for cp in dp_sends:
        cp.wait_send()

    @pl.when(has_next)
    def _():
        send_halo.wait_send()

    @pl.when(has_prev)
    def _():
        send_dhalo.wait_send()


def fused_body(tokens, gain_mix, w_in, kernel, w_out, gain_ffn, w_gate, w_up, w_down, cotangent):
    S, T, D = tokens.shape
    CL = w_out.shape[0]
    FL = w_gate.shape[1]
    R = S * T
    n_seq = lax.axis_size("seq")
    tiles = FL // LANE
    FW = -(-tiles // 2) * LANE
    GR = D // NZ
    SR = GR // 2
    DR = SR // 2
    widths = [ZF_COLS, FW - ZF_COLS, FW, FW, 2 * CL]
    NCH = R // ROWS_CHUNK

    def sds(shape, dtype=BF):
        return jax.ShapeDtypeStruct(shape, dtype)

    outs = [sds((R, D)), sds((R, D)), sds((3, DR, FL)), sds((4, DR, CL)), sds((8, D), F32)]
    outs += [sds((NZ, 2, SR, w)) for w in widths]
    outs += [sds((SR, widths[0]))] + [sds((NZ, SR, w)) for w in widths[1:]]
    outs += [sds((2, NZ, 2, SR, widths[0]))] + [sds((2, NZ, SR, w)) for w in widths[1:]]
    outs += [sds((NCH, ROWS_CHUNK, D))] * 5
    any_spec = pl.BlockSpec(memory_space=pl.ANY)
    vmem_spec = pl.BlockSpec(memory_space=pltpu.VMEM)
    V = pltpu.VMEM
    scratch = [
        V((R, D), BF),
        V((D, FW), BF),
        V((D, FW), BF),
        V((FW, D), BF),
        V((2, R, D), BF),
        V((2, R, D), BF),
        V((2, R, D), BF),
        V((2, R, FW), BF),
        V((2, R, FW), BF),
        V((2, R, FW), BF),
        V((R, CL), BF),
        V((R, CL), BF),
        V((R, CL), BF),
        V((R, CL), BF),
        V((R, CL), BF),
        V((R, D), F32),
        V((NCH, ROWS_CHUNK, D), BF),
        V((12, ROWS_CHUNK, D), BF),
        V((2, ROWS_CHUNK, D), BF),
        V((4, SR, FW), BF),
        V((4, SR, FW), BF),
        V((S, 16, CL), BF),
        V((S, 16, CL), BF),
        V((S, 8, CL), F32),
        V((S, 8, CL), F32),
        V((S, 16, CL), F32),
        V((S, 16, CL), BF),
        V((S, 16, CL), BF),
        V((3, 8, D), F32),
        V((1 + NZ, 8, D), F32),
        pltpu.SemaphoreType.DMA((N_SEND,)),
        pltpu.SemaphoreType.DMA((N_RECV,)),
        pltpu.SemaphoreType.DMA((N_LOCAL,)),
    ]
    flops = 2 * R * D * (4 * CL + 3 * FL) * 3
    res = pl.pallas_call(
        functools.partial(step_kernel, (R, T, D, CL, FL, FW)),
        out_shape=outs,
        in_specs=[
            any_spec, vmem_spec, any_spec, vmem_spec, any_spec, vmem_spec,
            any_spec, any_spec, any_spec, any_spec,
        ],
        out_specs=[any_spec] * 4 + [vmem_spec] + [any_spec] * (len(outs) - 5),
        scratch_shapes=scratch,
        compiler_params=pltpu.CompilerParams(
            collective_id=0, has_side_effects=True, vmem_limit_bytes=63 << 20
        ),
        cost_estimate=pl.CostEstimate(flops=flops, bytes_accessed=200 << 20, transcendentals=0),
        name="block_step",
    )(
        tokens.reshape(R, D), gain_mix.reshape(1, D), w_in, kernel, w_out,
        gain_ffn.reshape(1, D), w_gate, w_up, w_down, cotangent.reshape(R, D),
    )
    block_out, d_tokens, g_ffn, g_conv, small = res[:5]
    s = lax.axis_index("seq")
    per_d, per_c = D // n_seq, CL // n_seq
    gains = lax.dynamic_slice(small[0:2], (0, s * per_d), (2, per_d))
    g_taps = lax.dynamic_slice(small[2:5], (0, s * per_c), (3, per_c))
    return (
        block_out.reshape(S, T, D),
        d_tokens.reshape(S, T, D),
        gains[0],
        g_conv[0:3].astype(F32),
        g_taps.reshape(3, 1, per_c),
        g_conv[3].astype(F32).T,
        gains[1],
        g_ffn[1].astype(F32),
        g_ffn[2].astype(F32),
        g_ffn[0].astype(F32).T,
    )


def from_behind(value, axis, by):
    count = lax.axis_size(axis)
    pairs = [(i, i + by) for i in range(count) if 0 <= i + by < count]
    return lax.ppermute(value, axis, pairs)


def rms_scale(vector):
    return lax.rsqrt(jnp.mean(vector * vector, axis=-1, keepdims=True) + epsilon)


def norm_back(d_normout, normed, inv_scale, gain_vec):
    d_normed = d_normout * gain_vec
    return inv_scale * (d_normed - normed * jnp.mean(d_normed * normed, axis=-1, keepdims=True))


def matmul(lhs_mat, rhs_mat):
    return jnp.dot(lhs_mat, rhs_mat, preferred_element_type=jnp.float32)


def left_trans(lhs_mat, rhs_mat):
    return lax.dot_general(
        lhs_mat, rhs_mat, (((0,), (0,)), ((), ())), preferred_element_type=jnp.float32
    )


def right_trans(lhs_mat, rhs_mat):
    return lax.dot_general(
        lhs_mat, rhs_mat, (((1,), (1,)), ((), ())), preferred_element_type=jnp.float32
    )


def general_body(tokens, gain_mix, w_in, kernel, w_out, gain_ffn, w_gate, w_up, w_down, cotangent):
    seq_count, tok_rows, model_width = tokens.shape
    row_count = seq_count * tok_rows
    tokens_f = tokens.astype(jnp.float32).reshape(row_count, model_width)
    scale_mix = rms_scale(tokens_f)
    normed_mix = tokens_f * scale_mix
    h_mix = (normed_mix * gain_mix).astype(jnp.bfloat16)
    proj_b = matmul(h_mix, w_in[0])
    proj_c = matmul(h_mix, w_in[1])
    proj_x = matmul(h_mix, w_in[2])
    conv_in = (proj_b * proj_x).astype(jnp.bfloat16).reshape(seq_count, tok_rows, -1)
    before = from_behind(conv_in[:, tok_rows - 2 :, :], "seq", 1)
    extended = jnp.concatenate([before, conv_in], axis=1).astype(jnp.float32)
    conv_out = (
        kernel[0] * extended[:, :-2] + kernel[1] * extended[:, 1:-1] + kernel[2] * extended[:, 2:]
    )
    conv_flat = conv_out.reshape(row_count, -1)
    gated = (proj_c * conv_flat).astype(jnp.bfloat16)
    mixed_sum = lax.psum(matmul(gated, w_out).astype(jnp.bfloat16), "chan").astype(jnp.float32)
    residual = tokens_f + mixed_sum
    scale_ffn = rms_scale(residual)
    normed_ffn = residual * scale_ffn
    h_ffn = (normed_ffn * gain_ffn).astype(jnp.bfloat16)
    gate_pre = matmul(h_ffn, w_gate)
    up_value = matmul(h_ffn, w_up)
    sigmoid_gate = jax.nn.sigmoid(gate_pre)
    silu_gate = gate_pre * sigmoid_gate
    hidden = (silu_gate * up_value).astype(jnp.bfloat16)
    ffn_total = lax.psum(matmul(hidden, w_down).astype(jnp.bfloat16), "chan").astype(jnp.float32)
    block_out = (
        (residual + ffn_total).astype(jnp.bfloat16).reshape(seq_count, tok_rows, model_width)
    )
    grad_out = cotangent.reshape(row_count, model_width)
    g_w_down = left_trans(hidden, grad_out)
    d_hidden = right_trans(grad_out, w_down)
    d_gate = (d_hidden * up_value * sigmoid_gate * (1.0 + gate_pre * (1.0 - sigmoid_gate))).astype(
        jnp.bfloat16
    )
    d_up = (d_hidden * silu_gate).astype(jnp.bfloat16)
    g_w_gate = left_trans(h_ffn, d_gate)
    g_w_up = left_trans(h_ffn, d_up)
    d_h_ffn = lax.psum(
        (right_trans(d_gate, w_gate) + right_trans(d_up, w_up)).astype(jnp.bfloat16), "chan"
    ).astype(jnp.float32)
    g_gain_ffn = jnp.sum(d_h_ffn * normed_ffn, axis=0)
    d_resid = grad_out.astype(jnp.float32) + norm_back(d_h_ffn, normed_ffn, scale_ffn, gain_ffn)
    d_mixed = d_resid.astype(jnp.bfloat16)
    g_w_out = left_trans(gated, d_mixed)
    d_gated = right_trans(d_mixed, w_out)
    d_proj_c = (d_gated * conv_flat).astype(jnp.bfloat16)
    d_conv = (d_gated * proj_c).reshape(seq_count, tok_rows, -1)
    after_rows = from_behind(d_conv[:, :2, :], "seq", -1)
    ext_back = jnp.concatenate([d_conv, after_rows], axis=1)
    d_conv_in = (
        kernel[2] * ext_back[:, :-2] + kernel[1] * ext_back[:, 1:-1] + kernel[0] * ext_back[:, 2:]
    )
    g_kernel = jnp.stack(
        [
            jnp.sum(d_conv * extended[:, :-2], axis=(0, 1)),
            jnp.sum(d_conv * extended[:, 1:-1], axis=(0, 1)),
            jnp.sum(d_conv * extended[:, 2:], axis=(0, 1)),
        ]
    ).reshape(3, 1, -1)
    d_conv_low = d_conv_in.reshape(row_count, -1).astype(jnp.bfloat16)
    d_proj_b = (d_conv_low * proj_x).astype(jnp.bfloat16)
    d_proj_x = (d_conv_low * proj_b).astype(jnp.bfloat16)
    g_w_in = jnp.stack(
        [left_trans(h_mix, d_proj_b), left_trans(h_mix, d_proj_c), left_trans(h_mix, d_proj_x)]
    )
    d_h_mix = lax.psum(
        (
            right_trans(d_proj_b, w_in[0])
            + right_trans(d_proj_c, w_in[1])
            + right_trans(d_proj_x, w_in[2])
        ).astype(jnp.bfloat16),
        "chan",
    ).astype(jnp.float32)
    g_gain_mix = jnp.sum(d_h_mix * normed_mix, axis=0)
    d_tokens = (
        (d_resid + norm_back(d_h_mix, normed_mix, scale_mix, gain_mix))
        .astype(jnp.bfloat16)
        .reshape(seq_count, tok_rows, model_width)
    )
    summed = (
        lax.psum_scatter(g_w_in, "seq", scatter_dimension=1, tiled=True),
        lax.psum_scatter(g_w_out, "seq", scatter_dimension=1, tiled=True),
        lax.psum_scatter(g_kernel, "seq", scatter_dimension=2, tiled=True),
        lax.psum_scatter(g_gain_mix, "seq", scatter_dimension=0, tiled=True),
        lax.psum_scatter(g_w_gate, "seq", scatter_dimension=0, tiled=True),
        lax.psum_scatter(g_w_up, "seq", scatter_dimension=0, tiled=True),
        lax.psum_scatter(g_w_down, "seq", scatter_dimension=1, tiled=True),
        lax.psum_scatter(g_gain_ffn, "seq", scatter_dimension=0, tiled=True),
    )
    sum_in, sum_out, sum_kernel, sum_gain_mix, sum_gate, sum_up, sum_down, sum_gain_ffn = summed
    return (
        block_out,
        d_tokens,
        sum_gain_mix,
        sum_in,
        sum_kernel,
        sum_out,
        sum_gain_ffn,
        sum_gate,
        sum_up,
        sum_down,
    )


def solution(mesh):
    body = fused_body if mesh.shape["seq"] == 4 * NZ else general_body
    placed = (
        P(None, "seq", None),
        P(),
        P(None, None, "chan"),
        P(None, "chan"),
        P("chan", None),
        P(),
        P(None, "chan"),
        P(None, "chan"),
        P("chan", None),
        P(None, "seq", None),
    )
    return jax.shard_map(
        body,
        mesh=mesh,
        in_specs=placed,
        out_specs=(
            P(None, "seq", None),
            P(None, "seq", None),
            P("seq"),
            P(None, "seq", "chan"),
            P(None, "chan", "seq"),
            P("chan", "seq"),
            P("seq"),
            P("seq", "chan"),
            P("seq", "chan"),
            P("chan", "seq"),
        ),
        check_vma=False,
    )
```

```python
import functools

import jax
import jax.numpy as jnp
from jax import lax
from jax.experimental import pallas as pl
from jax.experimental.pallas import tpu as pltpu
from jax.sharding import PartitionSpec as P

epsilon = 1e-05
BF = jnp.bfloat16
F32 = jnp.float32
MESH = pl.DeviceIdType.MESH
LANE = 128
NZ = 4
ROWS_CHUNK = 128
ZF_COLS = 1152


def nn(a, b):
    return jnp.dot(a, b, preferred_element_type=F32)


def tn(a, b):
    return lax.dot_general(a, b, (((0,), (0,)), ((), ())), preferred_element_type=F32)


def nt(a, b):
    return lax.dot_general(a, b, (((1,), (1,)), ((), ())), preferred_element_type=F32)


def inv_rms(v):
    return lax.rsqrt(jnp.mean(v * v, axis=-1, keepdims=True) + epsilon)


class Take:
    def __init__(self, limit):
        self.used, self.limit = 0, limit

    def __call__(self, count=1):
        base = self.used
        self.used += count
        assert self.used <= self.limit
        return base


N_SEND, N_RECV, N_LOCAL = 128, 192, 64

SCHEDULE = {
    "dhA": (("mid", (0, 0)),),
    "dhD": (("mid", (0, 2)),),
    "dnA": (("end", (3, 0)), ("end", (2, 0)),),
    "dnD": (("mid", (0, 1)),),
    "nb0": (("end", (1, 0)),),
    "nb2": (("end", (2, 1)), ("mid", "pair"),),
    "d1a": (("mid", (2, 0)),),
    "tail": (("mid", (3, 0)),),
    "d1b": (("end", (3, 1)), ("mid", (2, 2)),),
    "gc0": (("mid", (3, 1)), ("mid", (1, 2)),),
    "gc2": (("end", "pair"), ("mid", "pair sum"),),
    "blk1": (("mid", (1, 0)), ("mid", (1, 3)),),
    "blk3": (("mid", (2, 1)), ("mid", (3, 2)), ("mid", (2, 3)),),
    "dt0": (("end", (1, 1)), ("end", (2, 2)), ("end", (1, 2)), ("end", (3, 2)),),
    "dt2": (("end", (4, 0)), ("end", (4, 1)), ("mid", (4, 0)), ("mid", (1, 1)), ("mid", (4, 2)), ("mid", (4, 1)),),
    "sm": (("end", (4, 2)), ("end", (2, 3)), ("end", (3, 3)), ("end", (1, 3)), ("end", "pair sum"), ("end", (4, 3)), ("mid", (3, 3)), ("mid", (4, 3)),),
}


def step_kernel(
    dims,
    tokens, gain_mix, w_in, taps, w_out, gain_ffn, w_gate, w_up, w_down, cot,
    block_out, d_tokens, g_ffn, g_conv, g_gain_mix, g_taps, g_gain_ffn,
    gb0, gb1, gb2, gb3, gb4, yb0, yb1, yb2, yb3, yb4, zb0, zb1, zb2, zb3, zb4,
    cr_dh, cr_dn, xr_dh, xr_dn, xr_d1,
    tok_v, wg_v, wu_v, wd_v, dy_v, h2_v, h1_v, hid, dg, du, pb, pc, px, bx, gated, resid, mix_r,
    ring, rb, ld, outs, halo_s, halo_r, dhalo_s, dhalo_r, tail, pb_tail, px_tail,
    sm, sm_r, ss, rs, ls,
):
    R, T, D, CL, FL, FW = dims
    S = R // T
    CH = CL // 2
    GR = D // NZ
    SR = GR // 2
    DR = SR // 2
    NCH = R // ROWS_CHUNK
    take_s, take_r, take_l = Take(N_SEND), Take(N_RECV), Take(N_LOCAL)

    s = lax.axis_index("seq")
    x = lax.axis_index("chan")
    n_seq = 4 * NZ
    z, y, c = s // 4, (s // 2) % 2, s % 2

    def did(z_, y_, c_):
        return ((z_ * 2 + y_) * 2 + c_, x)

    core_dev = did(z, y, 1 - c)
    y_dev = did(z, 1 - y, c)
    x_dev = (s, 1 - x)
    mid = jnp.logical_and(z > 0, z < NZ - 1)
    end = jnp.logical_not(mid)

    def remote(src, dst, si, ri, dev):
        return pltpu.make_async_remote_copy(
            src_ref=src, dst_ref=dst, send_sem=ss.at[si], recv_sem=rs.at[ri],
            device_id=dev, device_id_type=MESH,
        )

    def wait_recv(dst, ri):
        remote(dst, dst, 0, ri, core_dev).wait_recv()

    def wait_send(src, si):
        remote(src, src, si, 0, core_dev).wait_send()

    def local(src, dst, li):
        return pltpu.make_async_copy(src, dst, ls.at[li])

    l_tok, l_win, l_wout, l_dy = take_l(), take_l(3), take_l(), take_l()
    ld_tok = local(tokens, tok_v, l_tok)
    ld_tok.start()
    win_views = [wg_v.at[:, pl.ds(0, CL)], wg_v.at[:, pl.ds(CL, CL)], wu_v.at[:, pl.ds(0, CL)]]
    wout_view = wd_v.at[pl.ds(0, CL), :]

    def load_w_in():
        return [local(w_in.at[m], win_views[m], l_win + m) for m in range(3)]

    for cp in load_w_in():
        cp.start()
    ld_wout = local(w_out, wout_view, l_wout)
    ld_wout.start()
    ld_dy = local(cot, dy_v.at[0], l_dy)

    bar = pltpu.get_barrier_semaphore()

    def greet(dev):
        pl.semaphore_signal(bar, inc=1, device_id=dev, device_id_type=MESH)

    greet(core_dev)
    greet(x_dev)
    others = [(k, did((z + k // 2) % NZ, (y + k % 2) % 2, c)) for k in range(1, 2 * NZ)]
    for _, dev in others:
        greet(dev)
    has_prev = s > 0
    has_next = s < n_seq - 1
    prev_dev = ((s + n_seq - 1) % n_seq, x)
    next_dev = ((s + 1) % n_seq, x)
    greet(prev_dev)
    greet(next_dev)
    l_w = take_l(3)
    win_start = pl.multiple_of(c * (FL - FW), LANE)
    ld_wg = local(w_gate.at[:, pl.ds(win_start, FW)], wg_v, l_w)
    ld_wu = local(w_up.at[:, pl.ds(win_start, FW)], wu_v, l_w + 1)
    ld_wd = local(w_down.at[pl.ds(win_start, FW), :], wd_v, l_w + 2)

    sm[...] = jnp.zeros_like(sm)
    gain_mix_row = gain_mix[...].reshape(1, D)
    gain_ffn_row = gain_ffn[...].reshape(1, D)
    k_taps = [taps[t : t + 1, :] for t in range(3)]

    ld_tok.wait()

    CPS = T // ROWS_CHUNK
    NC = CL // 256
    s_h1, r_h1 = take_s(S), take_r(S)
    s_ha, r_ha = take_s(S), take_r(S)
    s_mx, r_mx = take_s(NCH), take_r(NCH)
    row_iota = lax.broadcasted_iota(jnp.int32, (T, 256), 0)
    top_iota = row_iota[0:16]

    def conv_terms(now, h, iota):
        h14 = jnp.broadcast_to(h[14:15], now.shape)
        h15 = jnp.broadcast_to(h[15:16], now.shape)
        one = jnp.where(iota == 0, h15, pltpu.roll(now, 1, 0))
        two = jnp.where(iota == 0, h14, jnp.where(iota == 1, h15, pltpu.roll(now, 2, 0)))
        return now, one, two

    def tap_cols(cols):
        return [taps[t : t + 1, cols] for t in range(3)]

    def convolve(terms, cols):
        now, one, two = terms
        k0, k1, k2 = tap_cols(cols)
        return k0 * two + k1 * one + k2 * now

    def h1_send(q):
        rows = pl.ds(q * T, T)
        return remote(h1_v.at[0, rows], h1_v.at[1, rows], s_h1 + q, r_h1 + q, core_dev)

    def halo_send(q):
        return remote(halo_s.at[q], halo_r.at[q], s_ha + q, r_ha + q, next_dev)

    def mixer_out(k):
        rows = slice(k * ROWS_CHUNK, (k + 1) * ROWS_CHUNK)

        def out_tile(j, _):
            cols = pl.ds(pl.multiple_of(j * 512, 512), 512)
            ring[k, :, cols] = nn(gated[rows, :], wd_v[0:CL, cols]).astype(BF)
            return 0

        lax.fori_loop(0, D // 512, out_tile, 0)
        remote(ring.at[k], mix_r.at[k], s_mx + k, r_mx + k, x_dev).start()

    for q in range(S):
        rows = pl.ds(q * T, T)

        def norm_rows(k, _, q=q):
            chunk = pl.ds(pl.multiple_of(q * T + k * ROWS_CHUNK, ROWS_CHUNK), ROWS_CHUNK)
            xv = tok_v[chunk, :].astype(F32)
            h1_v[0, chunk, :] = (xv * inv_rms(xv) * gain_mix_row).astype(BF)
            return 0

        lax.fori_loop(0, CPS, norm_rows, 0)
        if q == 0:
            for cp in load_w_in():
                cp.wait()

        def in_proj(j, _, q=q, rows=rows):
            cols = pl.ds(pl.multiple_of(j * 256, 256), 256)
            cols1 = pl.ds(pl.multiple_of(CL + j * 256, 256), 256)
            h = h1_v[0, rows, :]
            b = nn(h, wg_v[:, cols])
            pb[rows, cols] = b.astype(BF)
            xx = nn(h, wu_v[:, cols])
            px[rows, cols] = xx.astype(BF)
            inner = (b * xx).astype(BF)
            bx[rows, cols] = inner
            halo_s[q, :, cols] = inner[T - 16 : T]
            pcv = nn(h, wg_v[:, cols1])
            pc[rows, cols] = pcv.astype(BF)
            now = inner.astype(F32)
            cv = convolve(conv_terms(now, jnp.zeros_like(now[0:16]), row_iota), cols)
            gated[rows, cols] = (pcv * cv).astype(BF)
            return 0

        lax.fori_loop(0, NC, in_proj, 0)
        if q == 0:
            pl.semaphore_wait(bar, 3 + 2 * NZ)
        if q == S - 1:
            ld_wg.start()
            ld_wu.start()

        @pl.when(has_next)
        def _(q=q):
            halo_send(q).start()

        if q == 0:
            ld_wout.wait()
        for k in range(CPS - 1, 0, -1):
            mixer_out(q * CPS + k)

        @pl.when(has_prev)
        def _(q=q):
            wait_recv(halo_r.at[q], r_ha + q)

        @pl.when(jnp.logical_not(has_prev))
        def _(q=q):
            halo_r[q] = jnp.zeros_like(halo_r[q])

        def conv_top(j, _, q=q):
            cols = pl.ds(pl.multiple_of(j * 256, 256), 256)
            top = pl.ds(q * T, 16)
            now = bx[top, cols].astype(F32)
            cv = convolve(conv_terms(now, halo_r[q, :, cols].astype(F32), top_iota), cols)
            gated[top, cols] = (pc[top, cols].astype(F32) * cv).astype(BF)
            return 0

        lax.fori_loop(0, NC, conv_top, 0)
        mixer_out(q * CPS)
        h1_send(q).start()
        if q == 0:
            ld_dy.start()
            s_dy, r_dy = take_s(), take_r()
            send_dy = remote(cot, dy_v.at[1], s_dy, r_dy, core_dev)
            send_dy.start()
    ld_wd.start()

    s_h2, r_h2 = take_s(NCH), take_r(NCH)
    ld_dy.wait()
    send_dy.wait()
    ld_wg.wait()
    ld_wu.wait()
    ld_wd.wait()
    NF = FW // 256
    overlap = 2 * FW - FL
    col_iota = lax.broadcasted_iota(jnp.int32, (2 * ROWS_CHUNK, 256), 1)

    def residual_chunk(k):
        rows = pl.ds(pl.multiple_of(k * ROWS_CHUNK, ROWS_CHUNK), ROWS_CHUNK)
        wait_recv(mix_r.at[k], r_mx + k)
        res = tok_v[rows, :].astype(F32) + (ring[k].astype(F32) + mix_r[k].astype(F32))
        resid[rows, :] = res
        h2_v[0, rows, :] = (res * inv_rms(res) * gain_ffn_row).astype(BF)
        remote(h2_v.at[0, rows], h2_v.at[1, rows], s_h2 + k, r_h2 + k, core_dev).start()

    def ffn_chunk(k):
        rows = pl.ds(pl.multiple_of(k * ROWS_CHUNK, ROWS_CHUNK), ROWS_CHUNK)
        wait_recv(h2_v.at[1, rows], r_h2 + k)

        def tile(j, _):
            cols = pl.ds(pl.multiple_of(j * 256, 256), 256)
            h = h2_v[:, rows, :].reshape(2 * ROWS_CHUNK, D)
            e = dy_v[:, rows, :].reshape(2 * ROWS_CHUNK, D)
            g = nn(h, wg_v[:, cols])
            u = nn(h, wu_v[:, cols])
            dh = nt(e, wd_v[cols, :])
            keep = col_iota + j * 256 >= c * overlap
            sg = jax.nn.sigmoid(g)
            si = g * sg
            dh = jnp.where(keep, dh, 0.0)
            shape = (2, ROWS_CHUNK, 256)
            hid[:, rows, cols] = jnp.where(keep, si * u, 0.0).astype(BF).reshape(shape)
            dg[:, rows, cols] = (dh * u * sg * (1.0 + g * (1.0 - sg))).astype(BF).reshape(shape)
            du[:, rows, cols] = (dh * si).astype(BF).reshape(shape)
            return 0

        lax.fori_loop(0, NF, tile, 0)

    def sent(k):
        return (k // CPS) * CPS + (CPS - 1 - k % CPS)

    residual_chunk(sent(0))

    def chunk_loop(k, _):
        @pl.when(k + 1 < NCH)
        def _():
            residual_chunk(sent(k + 1))

        ffn_chunk(sent(k))
        return 0

    lax.fori_loop(0, NCH, chunk_loop, 0)
    for k in range(NCH):
        wait_send(ring.at[k], s_mx + k)
        wait_send(h2_v.at[0, pl.ds(k * ROWS_CHUNK, ROWS_CHUNK)], s_h2 + k)

    gbs = [gb0, gb1, gb2, gb3, gb4]
    ybs = [yb0, yb1, yb2, yb3, yb4]
    zbs = [zb0, zb1, zb2, zb3, zb4]
    widths = [ZF_COLS, FW - ZF_COLS, FW, FW, 2 * CL]
    s_y = [None] + [take_s(NZ) for _ in range(4)]
    r_y = [None] + [take_r(NZ) for _ in range(4)]
    s_z = [take_s(2 * NZ)] + [take_s(NZ) for _ in range(4)]
    r_z = [take_r(4 * NZ)] + [take_r(2 * NZ) for _ in range(4)]

    def order(e):
        if e == NZ - 1:
            return z
        per_z = {0: (3, 2, 1), 1: (3, 0, 2), 2: (0, 3, 1), 3: (0, 1, 2)}
        v = per_z[3][e]
        for zz in range(3):
            v = jnp.where(z == zz, per_z[zz][e], v)
        return v

    def order_dyn(u):
        v = order(NZ - 1)
        for e in range(NZ - 1):
            v = jnp.where(u == e, order(e), v)
        return v

    def z_send(j, src, e, zp, h=None):
        to_right = zp > z
        d = jnp.where(to_right, 0, 1)
        dev = did(jnp.clip(jnp.where(to_right, z + 1, z - 1), 0, NZ - 1), y, c)
        if h is None:
            return remote(src, zbs[j].at[d, zp], s_z[j] + e, r_z[j] + d * NZ + zp, dev)
        return remote(
            src, zbs[j].at[d, zp, h], s_z[j] + 2 * e + h, r_z[j] + (d * NZ + zp) * 2 + h, dev
        )

    l_g = take_l(12)

    def y_send(j, u):
        zp = order_dyn(u) if not isinstance(u, int) else order(u)
        return remote(gbs[j].at[zp, 1 - y], ybs[j].at[zp], s_y[j] + u, r_y[j] + u, y_dev)

    def g_block(lhs_ref, rhs_ref, zp, pair, parts=(0, 1)):
        lhs = lhs_ref[:, :, pl.ds(pl.multiple_of(zp * GR, GR), GR)].reshape(2 * R, GR)
        half = FW // 2
        for n in parts:
            v = tn(lhs, rhs_ref[:, :, n * half : (n + 1) * half].reshape(2 * R, half)).astype(BF)
            outs[2 * pair, :, n * half : (n + 1) * half] = v[:SR]
            outs[2 * pair + 1, :, n * half : (n + 1) * half] = v[SR:]

    def g_step(u, _):
        zp = order_dyn(u)

        def down_copies():
            return [
                cp
                for h in range(2)
                for cp in (
                    local(outs.at[h, :, pl.ds(0, ZF_COLS)], gb0.at[zp, h], l_g + 2 * h),
                    local(
                        outs.at[h, :, pl.ds(ZF_COLS, FW - ZF_COLS)], gb1.at[zp, h], l_g + 2 * h + 1
                    ),
                )
            ]

        def plain_copies(gb, pair, li):
            return [local(outs.at[2 * pair + h], gb.at[zp, h], li + h) for h in range(2)]

        g_block(dy_v, hid, zp, 0)
        for cp in down_copies():
            cp.start()
        g_block(h2_v, dg, zp, 1, (0,))
        for cp in down_copies():
            cp.wait()

        @pl.when(u < 3)
        def _():
            y_send(1, u).start()

        @pl.when(jnp.logical_and(end, u < NZ - 1))
        def _():
            for h in range(2):
                z_send(0, gb0.at[zp, h], u, zp, h).start()

        g_block(h2_v, dg, zp, 1, (1,))
        for cp in plain_copies(gb2, 1, l_g + 4):
            cp.start()
        g_block(h2_v, du, zp, 0)
        for cp in plain_copies(gb3, 0, l_g + 6):
            cp.start()
        for cp in plain_copies(gb2, 1, l_g + 4):
            cp.wait()

        @pl.when(u < 2)
        def _():
            y_send(2, u).start()

        for cp in plain_copies(gb3, 0, l_g + 6):
            cp.wait()

        @pl.when(u < 2)
        def _():
            y_send(3, u).start()

        return 0

    lax.fori_loop(0, NZ, g_step, 0)

    l_e = take_l(4)
    is_role = {"end": end, "mid": mid}
    slot_last = {role: [None] * outs.shape[0] for role in is_role}
    slot_next = {role: 0 for role in is_role}

    def claim_slot(role):
        o = slot_next[role]
        slot_next[role] = (o + 1) % outs.shape[0]
        if slot_last[role][o] is not None:
            slot_last[role][o]()
            slot_last[role][o] = None
        return o

    ADD_ROWS = 32

    def add_into(dst, srcs):
        def rows_add(k, _):
            rows = pl.ds(pl.multiple_of(k * ADD_ROWS, ADD_ROWS), ADD_ROWS)
            acc = srcs[0][rows, :].astype(F32)
            for src in srcs[1:]:
                acc = acc + src[rows, :].astype(F32)
            dst[rows, :] = acc.astype(BF)
            return 0

        lax.fori_loop(0, SR // ADD_ROWS, rows_add, 0)

    def fetch(srcs, w):
        views, copies = [], []
        for i, (src, ri) in enumerate(srcs):
            if ri is not None:
                wait_recv(src, ri)
            views.append(ld.at[i, :, pl.ds(0, w)])
            copies.append(local(src, views[-1], l_e + i))
            copies[-1].start()
        for cp in copies:
            cp.wait()
        return views

    def from_line(j, d, zp, h=None):
        if h is None:
            return zbs[j].at[d, zp], r_z[j] + d * NZ + zp
        return zbs[j].at[d, zp, h], r_z[j] + (d * NZ + zp) * 2 + h

    def line_event(role, j, e):
        @pl.when(is_role[role])
        def _():
            zp = order(e)
            w = widths[j]
            d = jnp.where(zp > z, 0, 1)
            for h in (0, 1) if j == 0 else (None,):
                o = claim_slot(role)
                dst = outs.at[o, :, pl.ds(0, w)]
                if h is None:
                    srcs = [(gbs[j].at[zp, y], None), (ybs[j].at[zp], r_y[j] + e)]
                    si = s_z[j] + e
                else:
                    srcs = [(gbs[j].at[zp, h], None)]
                    si = s_z[j] + 2 * e + h
                if role == "mid":
                    srcs.append(from_line(j, d, zp, h))
                add_into(dst, fetch(srcs, w))
                z_send(j, dst, e, zp, h).start()
                slot_last[role][o] = functools.partial(sent_slot, o, w, si)

    def sent_slot(o, w, si):
        wait_send(outs.at[o, :, pl.ds(0, w)], si)

    def own_shard(role, j, h=None):
        if h is None:
            srcs = [(gbs[j].at[z, y], None), (ybs[j].at[z], r_y[j] + NZ - 1)]
        else:
            srcs = [(gbs[j].at[z, h], None)]
        if role == "mid":
            return srcs + [from_line(j, 0, z, h), from_line(j, 1, z, h)]
        return srcs + [from_line(j, jnp.where(z == 0, 1, 0), z, h)]

    def swap_pieces(j):
        if j == 4:
            return [(None, m * CH, CH, g_conv.at[m], c * CH) for m in range(4)]
        mat = g_ffn.at[{0: 0, 1: 0, 2: 1, 3: 2}[j]]
        w = widths[j]
        if j == 1:
            return [(None, 0, w, mat, c * (FL - FW) + ZF_COLS)]
        return [(0, 0, w, mat, 0), (1, overlap, w - overlap, mat, FL - FW + overlap)]

    swap_sems = [[(take_s(), take_r(), take_l()) for _ in swap_pieces(j)] for j in range(5)]

    def swap(j, o):
        items = []
        for (core, c0, w, mat, to), (si, ri, li) in zip(swap_pieces(j), swap_sems[j]):
            to = to if isinstance(to, int) else pl.multiple_of(to, LANE)
            target = mat.at[:, pl.ds(to, w)]
            mine = outs.at[o, pl.ds(pl.multiple_of(c * DR, DR), DR), pl.ds(c0, w)]
            other = outs.at[o, pl.ds(pl.multiple_of((1 - c) * DR, DR), DR), pl.ds(c0, w)]
            items.append((core, local(mine, target, li), remote(other, target, si, ri, core_dev), target))
        return items

    def swap_start(j, o):
        for core, keep, give, _ in swap(j, o):
            if core is None:
                keep.start()
                give.start()
            else:

                @pl.when(c == core)
                def _():
                    keep.start()
                    give.start()

    def swap_finish(j, o):
        for (core, keep, give, target), (_, ri, _) in zip(swap(j, o), swap_sems[j]):
            if core is None:
                keep.wait()
                give.wait_send()
                wait_recv(target, ri)
            else:

                @pl.when(c == core)
                def _():
                    keep.wait()
                    give.wait_send()

                @pl.when(c != core)
                def _():
                    wait_recv(target, ri)

    def final_event(role, j):
        @pl.when(is_role[role])
        def _():
            o = claim_slot(role)
            w = widths[j]
            add_into(outs.at[o, :, pl.ds(0, w)], fetch(own_shard(role, j), w))
            swap_start(j, o)
            slot_last[role][o] = functools.partial(swap_finish, j, o)

    s_f0, r_f0 = take_s(), take_r()
    w0 = widths[0]

    def final0_send(role):
        @pl.when(is_role[role])
        def _():
            o = claim_slot(role)
            dst = outs.at[o, :, pl.ds(0, w0)]
            add_into(dst, fetch(own_shard(role, 0, 1 - y), w0))
            cp = local(dst, gb0.at[z, 1 - y], l_e)
            cp.start()
            cp.wait()
            remote(gb0.at[z, 1 - y], yb0, s_f0, r_f0, y_dev).start()

    def final0_finish(role):
        @pl.when(is_role[role])
        def _():
            o = claim_slot(role)
            dst = outs.at[o, :, pl.ds(0, w0)]
            add_into(dst, fetch(own_shard(role, 0, y), w0))
            add_into(dst, [dst] + fetch([(yb0, r_f0)], w0))
            swap_start(0, o)
            slot_last[role][o] = functools.partial(swap_finish, 0, o)

    def hook(name):
        for role, event in SCHEDULE.get(name, ()):
            if event == "pair":
                final0_send(role)
            elif event == "pair sum":
                final0_finish(role)
            elif event[1] == NZ - 1:
                final_event(role, event[0])
            else:
                line_event(role, *event)

    def chunks(name, count, body):
        first = 0
        for k in range(count):
            if SCHEDULE.get(name + str(k)) or k == count - 1:
                lax.fori_loop(first, k + 1, body, 0)
                first = k + 1
                hook(name + str(k))

    HALF = 2 * ROWS_CHUNK

    def split_sum(name, product, cr, xr, base_a, base_d):
        s_c, r_c = take_s(2), take_r(2)
        s_x, r_x = take_s(NCH), take_r(NCH)
        l_c = take_l()

        def give(k, _):
            def tile(n, _):
                cols = pl.ds(pl.multiple_of(n * 512, 512), 512)
                v = product(1, k * HALF, n).astype(BF)
                ring[pl.ds(base_a + 2 * k, 2), :, cols] = v.reshape(2, ROWS_CHUNK, 512)
                return 0

            lax.fori_loop(0, D // 512, tile, 0)
            remote(
                ring.at[pl.ds(base_a + 2 * k, 2)], cr.at[pl.ds(2 * k, 2)], s_c + k, r_c + k, core_dev
            ).start()
            return 0

        lax.fori_loop(0, 2, give, 0)
        hook(name + "A")

        def keep(k, _):
            src = cr.at[pl.ds(2 * k, 2)]
            wait_recv(src, r_c + k)
            cp = local(src, rb, l_c)
            cp.start()
            cp.wait()

            def tile(n, _):
                cols = pl.ds(pl.multiple_of(n * 512, 512), 512)
                v = product(0, k * HALF, n) + rb[:, :, cols].reshape(HALF, 512).astype(F32)
                ring[pl.ds(base_d + 2 * k, 2), :, cols] = v.astype(BF).reshape(2, ROWS_CHUNK, 512)
                return 0

            lax.fori_loop(0, D // 512, tile, 0)
            for i in range(2):
                remote(
                    ring.at[base_d + 2 * k + i], xr.at[2 * k + i], s_x + 2 * k + i, r_x + 2 * k + i, x_dev
                ).start()
            return 0

        lax.fori_loop(0, 2, keep, 0)
        for k in range(2):
            wait_send(ring.at[pl.ds(base_a + 2 * k, 2)], s_c + k)
        hook(name + "D")
        return s_x, r_x

    def rows_at(ref, slot, r0):
        return ref[slot, pl.ds(pl.multiple_of(r0, HALF), HALF), :]

    def dh_product(slot, r0, n):
        cols = pl.ds(pl.multiple_of(n * 512, 512), 512)
        return nt(rows_at(dg, slot, r0), wg_v[cols, :]) + nt(rows_at(du, slot, r0), wu_v[cols, :])

    def dn_product(slot, r0, n):
        cols = pl.ds(pl.multiple_of(n * 512, 512), 512)
        return nn(rows_at(hid, slot, r0), wd_v[:, cols])

    s_xdh, r_xdh = split_sum("dh", dh_product, cr_dh, xr_dh, 0, 4)
    s_xdn, r_xdn = split_sum("dn", dn_product, cr_dn, xr_dn, 0, 8)
    for cp in load_w_in():
        cp.start()
    ld_wout.start()

    l_x = take_l()
    s_do, r_do = take_s(NCH), take_r(NCH)
    xbuf = rb.at[0]

    def ffn_norm_back(k, _):
        rows = pl.ds(pl.multiple_of(k * ROWS_CHUNK, ROWS_CHUNK), ROWS_CHUNK)
        wait_recv(xr_dh.at[k], r_xdh + k)
        cp = local(xr_dh.at[k], xbuf, l_x)
        cp.start()
        cp.wait()
        d_h = ring[4 + k].astype(F32) + xbuf[...].astype(F32)
        res = resid[rows, :]
        s2 = inv_rms(res)
        n2 = res * s2
        sm[0, 1:2, :] += jnp.sum(d_h * n2, axis=0, keepdims=True)
        e2 = d_h * gain_ffn_row
        d_res = dy_v[0, rows, :].astype(F32) + s2 * (
            e2 - n2 * jnp.mean(e2 * n2, axis=-1, keepdims=True)
        )
        h2_v[0, rows, :] = d_res.astype(BF)
        remote(h2_v.at[0, rows], h2_v.at[1, rows], s_do + k, r_do + k, core_dev).start()
        return 0

    chunks("nb", NCH, ffn_norm_back)
    for k in range(NCH):
        wait_send(ring.at[4 + k], s_xdh + k)

    for cp in load_w_in():
        cp.wait()
    ld_wout.wait()
    for q in range(S):

        def conv_back(j, _, q=q):
            cols = pl.ds(pl.multiple_of(j * 256, 256), 256)
            rows = pl.ds(q * T, T)
            now, one, two = conv_terms(
                bx[rows, cols].astype(F32), halo_r[q, :, cols].astype(F32), row_iota
            )
            k0, k1, k2 = tap_cols(cols)
            cv = k0 * two + k1 * one + k2 * now
            d_g = nt(h2_v[0, q * T : q * T + T, :], wd_v[cols, :])
            d_cv = d_g * pc[rows, cols].astype(F32)
            sm[0, 2:3, cols] += jnp.sum(d_cv * two, axis=0, keepdims=True)
            sm[0, 3:4, cols] += jnp.sum(d_cv * one, axis=0, keepdims=True)
            sm[0, 4:5, cols] += jnp.sum(d_cv * now, axis=0, keepdims=True)
            after1 = jnp.where(row_iota < T - 1, pltpu.roll(d_cv, T - 1, 0), 0.0)
            after2 = jnp.where(row_iota < T - 2, pltpu.roll(d_cv, T - 2, 0), 0.0)
            d_bx = k2 * d_cv + k1 * after1 + k0 * after2
            dhalo_s[q, :, cols] = d_cv[0:8]
            tail[q, :, cols] = d_bx[T - 16 : T]
            old_b = pb[rows, cols]
            old_x = px[rows, cols]
            pb_tail[q, :, cols] = old_b[T - 16 : T]
            px_tail[q, :, cols] = old_x[T - 16 : T]
            low = d_bx.astype(BF).astype(F32)
            pb[rows, cols] = (low * old_x.astype(F32)).astype(BF)
            px[rows, cols] = (low * old_b.astype(F32)).astype(BF)
            pc[rows, cols] = (d_g * cv).astype(BF)
            return 0

        lax.fori_loop(0, NC, conv_back, 0)

    s_dha, r_dha = take_s(), take_r()
    send_dhalo = remote(dhalo_s, dhalo_r, s_dha, r_dha, prev_dev)

    @pl.when(has_prev)
    def _():
        send_dhalo.start()

    for j, u in ((2, 2), (3, 2), (1, 3), (2, 3), (3, 3)):
        y_send(j, u).start()

    hook("cb")

    s_x1, r_x1 = take_s(NCH), take_r(NCH)

    def d1_part(name, ids):
        def tile(n, _):
            cols = pl.ds(pl.multiple_of(n * 512, 512), 512)

            def rows_of(ref):
                return jnp.concatenate(
                    [ref[k * ROWS_CHUNK : (k + 1) * ROWS_CHUNK, :] for k in ids], axis=0
                )

            v = (
                nt(rows_of(pb), wg_v[cols, 0:CL])
                + nt(rows_of(pc), wg_v[cols, CL : 2 * CL])
                + nt(rows_of(px), wu_v[cols, 0:CL])
            ).astype(BF)
            for i, k in enumerate(ids):
                ring[4 + k, :, cols] = v[i * ROWS_CHUNK : (i + 1) * ROWS_CHUNK]
            return 0

        lax.fori_loop(0, D // 512, tile, 0)
        for k in ids:
            remote(ring.at[4 + k], xr_d1.at[k], s_x1 + k, r_x1 + k, x_dev).start()
        hook(name)

    d1_part("d1a", [q * CPS + k for q in range(S) for k in range(CPS - 1)])

    @pl.when(has_next)
    def _():
        wait_recv(dhalo_r, r_dha)

    @pl.when(jnp.logical_not(has_next))
    def _():
        dhalo_r[...] = jnp.zeros_like(dhalo_r)

    tail_iota = lax.broadcasted_iota(jnp.int32, (16, CL), 0)
    for q in range(S):
        first = jnp.broadcast_to(dhalo_r[q, 0:1, :], (16, CL))
        second = jnp.broadcast_to(dhalo_r[q, 1:2, :], (16, CL))
        fix = jnp.where(
            tail_iota == 14,
            k_taps[0] * first,
            jnp.where(tail_iota == 15, k_taps[1] * first + k_taps[0] * second, 0.0),
        )
        low = (tail[q] + fix).astype(BF).astype(F32)
        rows = pl.ds(q * T + T - 16, 16)
        pb[rows, :] = (low * px_tail[q].astype(F32)).astype(BF)
        px[rows, :] = (low * pb_tail[q].astype(F32)).astype(BF)

    s_dp, r_dp = take_s(4), take_r(4)
    theirs = pl.ds(pl.multiple_of((1 - c) * CH, LANE), CH)
    ours = pl.ds(pl.multiple_of(c * CH, LANE), CH)
    dp_sends = [
        remote(ref.at[:, theirs], dy_v.at[1, :, pl.ds(m * CH, CH)], s_dp + m, r_dp + m, core_dev)
        for m, ref in enumerate((pb, pc, px, gated))
    ]
    for cp in dp_sends:
        cp.start()
    hook("tail")

    d1_part("d1b", [q * CPS + k for q in range(S) for k in range(1, CPS)])

    for q in range(S):
        wait_recv(h1_v.at[1, pl.ds(q * T, T)], r_h1 + q)
    for k in range(NCH):
        rows = pl.ds(k * ROWS_CHUNK, ROWS_CHUNK)
        wait_recv(h2_v.at[1, rows], r_do + k)
    for m in range(4):
        wait_recv(dy_v.at[1, :, pl.ds(m * CH, CH)], r_dp + m)
    W4 = widths[4]
    g4 = [dg.at[i, pl.ds(k * SR, SR), pl.ds(0, W4)] for i in range(2) for k in range(2)]

    def g_mixer(u, _):
        zp = order_dyn(u)
        zc = pl.ds(pl.multiple_of(zp * GR, GR), GR)
        for m, (mine, lhs) in enumerate(((pb, h1_v), (pc, h1_v), (px, h1_v), (gated, h2_v))):
            v = tn(lhs[0, :, zc], mine[:, ours]) + tn(
                lhs[1, :, zc], dy_v[1, :, m * CH : (m + 1) * CH]
            )
            v = v.astype(BF)
            g4[0][:, m * CH : (m + 1) * CH] = v[:SR]
            g4[1][:, m * CH : (m + 1) * CH] = v[SR:]
        cps = [local(g4[h], gb4.at[zp, h], l_g + h) for h in range(2)]
        for cp in cps:
            cp.start()
        for cp in cps:
            cp.wait()
        y_send(4, u).start()
        return 0

    chunks("gc", NZ, g_mixer)

    l_o = take_l()

    def block_chunk(k, _):
        rows = pl.ds(pl.multiple_of(k * ROWS_CHUNK, ROWS_CHUNK), ROWS_CHUNK)
        wait_recv(xr_dn.at[k], r_xdn + k)
        cp = local(xr_dn.at[k], xbuf, l_x)
        cp.start()
        cp.wait()
        total = ring[8 + k].astype(F32) + xbuf[...].astype(F32)
        rb[1] = (resid[rows, :] + total).astype(BF)
        co = local(rb.at[1], block_out.at[rows, :], l_o)
        co.start()
        co.wait()
        return 0

    chunks("blk", NCH, block_chunk)

    def mix_norm_back(n, _):
        k = (n % S) * CPS + n // S
        rows = pl.ds(pl.multiple_of(k * ROWS_CHUNK, ROWS_CHUNK), ROWS_CHUNK)
        wait_recv(xr_d1.at[k], r_x1 + k)
        cp = local(xr_d1.at[k], xbuf, l_x)
        cp.start()
        cp.wait()
        d_h = ring[4 + k].astype(F32) + xbuf[...].astype(F32)
        xv = tok_v[rows, :].astype(F32)
        s1 = inv_rms(xv)
        n1 = xv * s1
        sm[0, 0:1, :] += jnp.sum(d_h * n1, axis=0, keepdims=True)
        e1 = d_h * gain_mix_row
        out = h2_v[0, rows, :].astype(F32) + s1 * (
            e1 - n1 * jnp.mean(e1 * n1, axis=-1, keepdims=True)
        )
        rb[1] = out.astype(BF)
        co = local(rb.at[1], d_tokens.at[rows, :], l_o)
        co.start()
        co.wait()
        return 0

    chunks("dt", NCH, mix_norm_back)

    s_sm, r_sm = take_s(2 * NZ), take_r(2 * NZ)
    a = remote(sm.at[0], sm_r.at[0], s_sm, r_sm, core_dev)
    a.start()
    a.wait()
    sm[1] = sm[0] + sm_r[0]
    for k, dev in others:
        remote(sm.at[1], sm_r.at[k], s_sm + k, r_sm + k, dev).start()
    hook("sm")

    total = sm[1]
    for k, _ in others:
        wait_recv(sm_r.at[k], r_sm + k)
        total = total + sm_r[k]
    for k, _ in others:
        wait_send(sm.at[1], s_sm + k)
    per_d, per_c = D // n_seq, CL // n_seq
    mine = pltpu.roll(total, D - s * per_d, 1)
    g_gain_mix[...] = mine[0, 0:per_d]
    g_gain_ffn[...] = mine[1, 0:per_d]
    mine = pltpu.roll(total, D - s * per_c, 1)
    for t in range(3):
        g_taps[t] = mine[2 + t : 3 + t, 0:per_c]

    for role, cond in is_role.items():

        @pl.when(cond)
        def _(role=role):
            for finish in slot_last[role]:
                if finish is not None:
                    finish()

    @pl.when(end)
    def _():
        for e in range(NZ - 1):
            for h in range(2):
                wait_send(gb0.at[0, h], s_z[0] + 2 * e + h)

    for j in range(1, 5):
        for u in range(NZ):
            wait_send(ybs[j].at[0], s_y[j] + u)
    wait_send(yb0, s_f0)
    for q in range(S):
        h1_send(q).wait_send()
    for k in range(NCH):
        wait_send(h2_v.at[0, pl.ds(k * ROWS_CHUNK, ROWS_CHUNK)], s_do + k)
        wait_send(ring.at[4 + k], s_x1 + k)
        wait_send(ring.at[8 + k], s_xdn + k)
    for cp in dp_sends:
        cp.wait_send()

    @pl.when(has_next)
    def _():
        for q in range(S):
            halo_send(q).wait_send()

    @pl.when(has_prev)
    def _():
        send_dhalo.wait_send()


def fused_body(tokens, gain_mix, w_in, kernel, w_out, gain_ffn, w_gate, w_up, w_down, cotangent):
    S, T, D = tokens.shape
    CL = w_out.shape[0]
    FL = w_gate.shape[1]
    R = S * T
    n_seq = lax.axis_size("seq")
    tiles = FL // LANE
    FW = -(-tiles // 2) * LANE
    GR = D // NZ
    SR = GR // 2
    DR = SR // 2
    widths = [ZF_COLS, FW - ZF_COLS, FW, FW, 2 * CL]
    NCH = R // ROWS_CHUNK

    def sds(shape, dtype=BF):
        return jax.ShapeDtypeStruct(shape, dtype)

    outs = [sds((R, D)), sds((R, D)), sds((3, DR, FL)), sds((4, DR, CL))]
    outs += [sds((D // n_seq,), F32), sds((3, 1, CL // n_seq), F32), sds((D // n_seq,), F32)]
    outs += [sds((NZ, 2, SR, w)) for w in widths]
    outs += [sds((SR, widths[0]))] + [sds((NZ, SR, w)) for w in widths[1:]]
    outs += [sds((2, NZ, 2, SR, widths[0]))] + [sds((2, NZ, SR, w)) for w in widths[1:]]
    outs += [sds((NCH, ROWS_CHUNK, D))] * 5
    any_spec = pl.BlockSpec(memory_space=pl.ANY)
    vmem_spec = pl.BlockSpec(memory_space=pltpu.VMEM)
    V = pltpu.VMEM
    scratch = [
        V((R, D), BF),
        V((D, FW), BF),
        V((D, FW), BF),
        V((FW, D), BF),
        V((2, R, D), BF),
        V((2, R, D), BF),
        V((2, R, D), BF),
        V((2, R, FW), BF),
        V((2, R, FW), BF),
        V((2, R, FW), BF),
        V((R, CL), BF),
        V((R, CL), BF),
        V((R, CL), BF),
        V((R, CL), BF),
        V((R, CL), BF),
        V((R, D), F32),
        V((NCH, ROWS_CHUNK, D), BF),
        V((12, ROWS_CHUNK, D), BF),
        V((2, ROWS_CHUNK, D), BF),
        V((4, SR, FW), BF),
        V((4, SR, FW), BF),
        V((S, 16, CL), BF),
        V((S, 16, CL), BF),
        V((S, 8, CL), F32),
        V((S, 8, CL), F32),
        V((S, 16, CL), F32),
        V((S, 16, CL), BF),
        V((S, 16, CL), BF),
        V((2, 8, D), F32),
        V((2 * NZ, 8, D), F32),
        pltpu.SemaphoreType.DMA((N_SEND,)),
        pltpu.SemaphoreType.DMA((N_RECV,)),
        pltpu.SemaphoreType.DMA((N_LOCAL,)),
    ]
    flops = 2 * R * D * (4 * CL + 3 * FL) * 3
    res = pl.pallas_call(
        functools.partial(step_kernel, (R, T, D, CL, FL, FW)),
        out_shape=outs,
        in_specs=[
            any_spec, vmem_spec, any_spec, vmem_spec, any_spec, vmem_spec,
            any_spec, any_spec, any_spec, any_spec,
        ],
        out_specs=[any_spec] * 4 + [vmem_spec] * 3 + [any_spec] * (len(outs) - 7),
        scratch_shapes=scratch,
        compiler_params=pltpu.CompilerParams(
            collective_id=0, has_side_effects=True, vmem_limit_bytes=63 << 20
        ),
        cost_estimate=pl.CostEstimate(flops=flops, bytes_accessed=200 << 20, transcendentals=0),
        name="block_step",
    )(
        tokens.reshape(R, D), gain_mix, w_in, kernel, w_out,
        gain_ffn, w_gate, w_up, w_down, cotangent.reshape(R, D),
    )
    block_out, d_tokens, g_ffn, g_conv, g_gain_mix, g_taps, g_gain_ffn = res[:7]
    return (
        block_out.reshape(S, T, D),
        d_tokens.reshape(S, T, D),
        g_gain_mix,
        g_conv[0:3].astype(F32),
        g_taps,
        g_conv[3].astype(F32).T,
        g_gain_ffn,
        g_ffn[1].astype(F32),
        g_ffn[2].astype(F32),
        g_ffn[0].astype(F32).T,
    )


def from_behind(value, axis, by):
    count = lax.axis_size(axis)
    pairs = [(i, i + by) for i in range(count) if 0 <= i + by < count]
    return lax.ppermute(value, axis, pairs)


def rms_scale(vector):
    return lax.rsqrt(jnp.mean(vector * vector, axis=-1, keepdims=True) + epsilon)


def norm_back(d_normout, normed, inv_scale, gain_vec):
    d_normed = d_normout * gain_vec
    return inv_scale * (d_normed - normed * jnp.mean(d_normed * normed, axis=-1, keepdims=True))


def matmul(lhs_mat, rhs_mat):
    return jnp.dot(lhs_mat, rhs_mat, preferred_element_type=jnp.float32)


def left_trans(lhs_mat, rhs_mat):
    return lax.dot_general(
        lhs_mat, rhs_mat, (((0,), (0,)), ((), ())), preferred_element_type=jnp.float32
    )


def right_trans(lhs_mat, rhs_mat):
    return lax.dot_general(
        lhs_mat, rhs_mat, (((1,), (1,)), ((), ())), preferred_element_type=jnp.float32
    )


def general_body(tokens, gain_mix, w_in, kernel, w_out, gain_ffn, w_gate, w_up, w_down, cotangent):
    seq_count, tok_rows, model_width = tokens.shape
    row_count = seq_count * tok_rows
    tokens_f = tokens.astype(jnp.float32).reshape(row_count, model_width)
    scale_mix = rms_scale(tokens_f)
    normed_mix = tokens_f * scale_mix
    h_mix = (normed_mix * gain_mix).astype(jnp.bfloat16)
    proj_b = matmul(h_mix, w_in[0])
    proj_c = matmul(h_mix, w_in[1])
    proj_x = matmul(h_mix, w_in[2])
    conv_in = (proj_b * proj_x).astype(jnp.bfloat16).reshape(seq_count, tok_rows, -1)
    before = from_behind(conv_in[:, tok_rows - 2 :, :], "seq", 1)
    extended = jnp.concatenate([before, conv_in], axis=1).astype(jnp.float32)
    conv_out = (
        kernel[0] * extended[:, :-2] + kernel[1] * extended[:, 1:-1] + kernel[2] * extended[:, 2:]
    )
    conv_flat = conv_out.reshape(row_count, -1)
    gated = (proj_c * conv_flat).astype(jnp.bfloat16)
    mixed_sum = lax.psum(matmul(gated, w_out).astype(jnp.bfloat16), "chan").astype(jnp.float32)
    residual = tokens_f + mixed_sum
    scale_ffn = rms_scale(residual)
    normed_ffn = residual * scale_ffn
    h_ffn = (normed_ffn * gain_ffn).astype(jnp.bfloat16)
    gate_pre = matmul(h_ffn, w_gate)
    up_value = matmul(h_ffn, w_up)
    sigmoid_gate = jax.nn.sigmoid(gate_pre)
    silu_gate = gate_pre * sigmoid_gate
    hidden = (silu_gate * up_value).astype(jnp.bfloat16)
    ffn_total = lax.psum(matmul(hidden, w_down).astype(jnp.bfloat16), "chan").astype(jnp.float32)
    block_out = (
        (residual + ffn_total).astype(jnp.bfloat16).reshape(seq_count, tok_rows, model_width)
    )
    grad_out = cotangent.reshape(row_count, model_width)
    g_w_down = left_trans(hidden, grad_out)
    d_hidden = right_trans(grad_out, w_down)
    d_gate = (d_hidden * up_value * sigmoid_gate * (1.0 + gate_pre * (1.0 - sigmoid_gate))).astype(
        jnp.bfloat16
    )
    d_up = (d_hidden * silu_gate).astype(jnp.bfloat16)
    g_w_gate = left_trans(h_ffn, d_gate)
    g_w_up = left_trans(h_ffn, d_up)
    d_h_ffn = lax.psum(
        (right_trans(d_gate, w_gate) + right_trans(d_up, w_up)).astype(jnp.bfloat16), "chan"
    ).astype(jnp.float32)
    g_gain_ffn = jnp.sum(d_h_ffn * normed_ffn, axis=0)
    d_resid = grad_out.astype(jnp.float32) + norm_back(d_h_ffn, normed_ffn, scale_ffn, gain_ffn)
    d_mixed = d_resid.astype(jnp.bfloat16)
    g_w_out = left_trans(gated, d_mixed)
    d_gated = right_trans(d_mixed, w_out)
    d_proj_c = (d_gated * conv_flat).astype(jnp.bfloat16)
    d_conv = (d_gated * proj_c).reshape(seq_count, tok_rows, -1)
    after_rows = from_behind(d_conv[:, :2, :], "seq", -1)
    ext_back = jnp.concatenate([d_conv, after_rows], axis=1)
    d_conv_in = (
        kernel[2] * ext_back[:, :-2] + kernel[1] * ext_back[:, 1:-1] + kernel[0] * ext_back[:, 2:]
    )
    g_kernel = jnp.stack(
        [
            jnp.sum(d_conv * extended[:, :-2], axis=(0, 1)),
            jnp.sum(d_conv * extended[:, 1:-1], axis=(0, 1)),
            jnp.sum(d_conv * extended[:, 2:], axis=(0, 1)),
        ]
    ).reshape(3, 1, -1)
    d_conv_low = d_conv_in.reshape(row_count, -1).astype(jnp.bfloat16)
    d_proj_b = (d_conv_low * proj_x).astype(jnp.bfloat16)
    d_proj_x = (d_conv_low * proj_b).astype(jnp.bfloat16)
    g_w_in = jnp.stack(
        [left_trans(h_mix, d_proj_b), left_trans(h_mix, d_proj_c), left_trans(h_mix, d_proj_x)]
    )
    d_h_mix = lax.psum(
        (
            right_trans(d_proj_b, w_in[0])
            + right_trans(d_proj_c, w_in[1])
            + right_trans(d_proj_x, w_in[2])
        ).astype(jnp.bfloat16),
        "chan",
    ).astype(jnp.float32)
    g_gain_mix = jnp.sum(d_h_mix * normed_mix, axis=0)
    d_tokens = (
        (d_resid + norm_back(d_h_mix, normed_mix, scale_mix, gain_mix))
        .astype(jnp.bfloat16)
        .reshape(seq_count, tok_rows, model_width)
    )
    summed = (
        lax.psum_scatter(g_w_in, "seq", scatter_dimension=1, tiled=True),
        lax.psum_scatter(g_w_out, "seq", scatter_dimension=1, tiled=True),
        lax.psum_scatter(g_kernel, "seq", scatter_dimension=2, tiled=True),
        lax.psum_scatter(g_gain_mix, "seq", scatter_dimension=0, tiled=True),
        lax.psum_scatter(g_w_gate, "seq", scatter_dimension=0, tiled=True),
        lax.psum_scatter(g_w_up, "seq", scatter_dimension=0, tiled=True),
        lax.psum_scatter(g_w_down, "seq", scatter_dimension=1, tiled=True),
        lax.psum_scatter(g_gain_ffn, "seq", scatter_dimension=0, tiled=True),
    )
    sum_in, sum_out, sum_kernel, sum_gain_mix, sum_gate, sum_up, sum_down, sum_gain_ffn = summed
    return (
        block_out,
        d_tokens,
        sum_gain_mix,
        sum_in,
        sum_kernel,
        sum_out,
        sum_gain_ffn,
        sum_gate,
        sum_up,
        sum_down,
    )


def solution(mesh):
    body = fused_body if mesh.shape["seq"] == 4 * NZ else general_body
    placed = (
        P(None, "seq", None),
        P(),
        P(None, None, "chan"),
        P(None, "chan"),
        P("chan", None),
        P(),
        P(None, "chan"),
        P(None, "chan"),
        P("chan", None),
        P(None, "seq", None),
    )
    return jax.shard_map(
        body,
        mesh=mesh,
        in_specs=placed,
        out_specs=(
            P(None, "seq", None),
            P(None, "seq", None),
            P("seq"),
            P(None, "seq", "chan"),
            P(None, "chan", "seq"),
            P("chan", "seq"),
            P("seq"),
            P("seq", "chan"),
            P("seq", "chan"),
            P("chan", "seq"),
        ),
        check_vma=False,
    )
```

```python
import functools

import jax
import jax.numpy as jnp
from jax import lax
from jax.experimental import pallas as pl
from jax.experimental.pallas import tpu as pltpu
from jax.sharding import PartitionSpec as P

epsilon = 1e-05
BF = jnp.bfloat16
F32 = jnp.float32
MESH = pl.DeviceIdType.MESH
LANE = 128
NZ = 4
ROWS_CHUNK = 128
ZF_COLS = 1152


def nn(a, b):
    return jnp.dot(a, b, preferred_element_type=F32)


def tn(a, b):
    return lax.dot_general(a, b, (((0,), (0,)), ((), ())), preferred_element_type=F32)


def nt(a, b):
    return lax.dot_general(a, b, (((1,), (1,)), ((), ())), preferred_element_type=F32)


def inv_rms(v):
    return lax.rsqrt(jnp.mean(v * v, axis=-1, keepdims=True) + epsilon)


class Take:
    def __init__(self, limit):
        self.used, self.limit = 0, limit

    def __call__(self, count=1):
        base = self.used
        self.used += count
        assert self.used <= self.limit
        return base


N_SEND, N_RECV, N_LOCAL = 128, 192, 64

SCHEDULE = {
    "dhA": (("end", (1, 1)), ("mid", (0, 0)),),
    "dhD": (("mid", (0, 2)), ("mid", (0, 1)),),
    "dnD": (("end", (2, 0)),),
    "nb1": (("end", "pair"), ("end", (2, 1)), ("mid", "pair"),),
    "cb": (("mid", (2, 0)),),
    "d1a": (("end", (3, 0)),),
    "tail": (("mid", (1, 2)),),
    "d1b": (("end", (1, 0)), ("end", (1, 2)), ("end", (3, 1)),),
    "gc0": (("mid", (3, 0)),),
    "gc1": (("end", (3, 2)),),
    "blk1": (("end", (4, 0)), ("end", (2, 2)),),
    "blk2": (("end", "pair sum"), ("end", (4, 1)), ("end", (4, 2)), ("end", (1, 3)),),
    "blk3": (("mid", (1, 0)), ("mid", (2, 2)),),
    "dt0": (("mid", (3, 1)),),
    "dt2": (("mid", (2, 1)), ("mid", (3, 2)), ("mid", (1, 1)), ("mid", (4, 0)), ("mid", "pair sum"),),
    "dt3": (("end", (3, 3)), ("mid", (2, 3)), ("mid", (4, 1)),),
    "sm": (("end", (2, 3)), ("end", (4, 3)), ("mid", (1, 3)), ("mid", (4, 2)), ("mid", (3, 3)), ("mid", (4, 3)),),
}


def step_kernel(
    dims,
    tokens, gain_mix_hbm, w_in, taps_hbm, w_out, gain_ffn_hbm, w_gate, w_up, w_down, cot,
    block_out, d_tokens, g_ffn, g_conv, small_out,
    gb0, gb1, gb2, gb3, gb4, yb0, yb1, yb2, yb3, yb4, zb0, zb1, zb2, zb3, zb4,
    cr_dh, cr_dn, xr_dh, xr_dn, xr_d1,
    gain_mix, taps, gain_ffn, tok_v, wg_v, wu_v, wd_v, dy_v, h2_v, h1_v, hid, dg, du, pb, pc, px, bx, gated, resid, mix_r,
    ring, rb, ld, outs, halo_s, halo_r, dhalo_s, dhalo_r, tail, pb_tail, px_tail,
    sm, sm_r, ss, rs, ls,
):
    R, T, D, CL, FL, FW = dims
    S = R // T
    CH = CL // 2
    GR = D // NZ
    SR = GR // 2
    DR = SR // 2
    NCH = R // ROWS_CHUNK
    take_s, take_r, take_l = Take(N_SEND), Take(N_RECV), Take(N_LOCAL)

    s = lax.axis_index("seq")
    x = lax.axis_index("chan")
    n_seq = 4 * NZ
    z, y, c = s // 4, (s // 2) % 2, s % 2

    def did(z_, y_, c_):
        return ((z_ * 2 + y_) * 2 + c_, x)

    core_dev = did(z, y, 1 - c)
    y_dev = did(z, 1 - y, c)
    x_dev = (s, 1 - x)
    mid = jnp.logical_and(z > 0, z < NZ - 1)
    end = jnp.logical_not(mid)

    def remote(src, dst, si, ri, dev):
        return pltpu.make_async_remote_copy(
            src_ref=src, dst_ref=dst, send_sem=ss.at[si], recv_sem=rs.at[ri],
            device_id=dev, device_id_type=MESH,
        )

    def wait_recv(dst, ri):
        remote(dst, dst, 0, ri, core_dev).wait_recv()

    def wait_send(src, si):
        remote(src, src, si, 0, core_dev).wait_send()

    def local(src, dst, li):
        return pltpu.make_async_copy(src, dst, ls.at[li])

    l_tok, l_win, l_wout, l_dy, l_small = take_l(), take_l(3), take_l(), take_l(), take_l(3)
    ld_tok = local(tokens, tok_v, l_tok)
    ld_tok.start()
    win_views = [wg_v.at[:, pl.ds(0, CL)], wg_v.at[:, pl.ds(CL, CL)], wu_v.at[:, pl.ds(0, CL)]]
    wout_view = wd_v.at[pl.ds(0, CL), :]

    def load_w_in():
        return [local(w_in.at[m], win_views[m], l_win + m) for m in range(3)]

    for cp in load_w_in():
        cp.start()
    ld_small = [
        local(src, dst, l_small + i)
        for i, (src, dst) in enumerate(
            ((gain_mix_hbm, gain_mix), (taps_hbm, taps), (gain_ffn_hbm, gain_ffn))
        )
    ]
    for cp in ld_small:
        cp.start()
    ld_wout = local(w_out, wout_view, l_wout)
    ld_wout.start()
    ld_dy = local(cot, dy_v.at[0], l_dy)

    bar = pltpu.get_barrier_semaphore()

    def greet(dev):
        pl.semaphore_signal(bar, inc=1, device_id=dev, device_id_type=MESH)

    greet(core_dev)
    greet(x_dev)
    others = [(k, did((z + k // 2) % NZ, (y + k % 2) % 2, c)) for k in range(1, 2 * NZ)]
    for _, dev in others:
        greet(dev)
    has_prev = s > 0
    has_next = s < n_seq - 1
    prev_dev = ((s + n_seq - 1) % n_seq, x)
    next_dev = ((s + 1) % n_seq, x)
    greet(prev_dev)
    greet(next_dev)
    l_w = take_l(3)
    win_start = pl.multiple_of(c * (FL - FW), LANE)
    ld_wg = local(w_gate.at[:, pl.ds(win_start, FW)], wg_v, l_w)
    ld_wu = local(w_up.at[:, pl.ds(win_start, FW)], wu_v, l_w + 1)
    ld_wd = local(w_down.at[pl.ds(win_start, FW), :], wd_v, l_w + 2)

    sm[...] = jnp.zeros_like(sm)
    for cp in ld_small:
        cp.wait()
    gain_mix_row = gain_mix[...].reshape(1, D)
    gain_ffn_row = gain_ffn[...].reshape(1, D)
    k_taps = [taps[t : t + 1, :] for t in range(3)]

    ld_tok.wait()

    CPS = T // ROWS_CHUNK
    NC = CL // 256
    s_h1, r_h1 = take_s(S), take_r(S)
    s_ha, r_ha = take_s(S), take_r(S)
    s_mx, r_mx = take_s(NCH), take_r(NCH)
    row_iota = lax.broadcasted_iota(jnp.int32, (T, 256), 0)
    top_iota = row_iota[0:16]

    def conv_terms(now, h, iota):
        h14 = jnp.broadcast_to(h[14:15], now.shape)
        h15 = jnp.broadcast_to(h[15:16], now.shape)
        one = jnp.where(iota == 0, h15, pltpu.roll(now, 1, 0))
        two = jnp.where(iota == 0, h14, jnp.where(iota == 1, h15, pltpu.roll(now, 2, 0)))
        return now, one, two

    def tap_cols(cols):
        return [taps[t : t + 1, cols] for t in range(3)]

    def convolve(terms, cols):
        now, one, two = terms
        k0, k1, k2 = tap_cols(cols)
        return k0 * two + k1 * one + k2 * now

    def h1_send(q):
        rows = pl.ds(q * T, T)
        return remote(h1_v.at[0, rows], h1_v.at[1, rows], s_h1 + q, r_h1 + q, core_dev)

    def halo_send(q):
        return remote(halo_s.at[q], halo_r.at[q], s_ha + q, r_ha + q, next_dev)

    def mixer_out(k):
        rows = slice(k * ROWS_CHUNK, (k + 1) * ROWS_CHUNK)

        def out_tile(j, _):
            cols = pl.ds(pl.multiple_of(j * 512, 512), 512)
            ring[k, :, cols] = nn(gated[rows, :], wd_v[0:CL, cols]).astype(BF)
            return 0

        lax.fori_loop(0, D // 512, out_tile, 0)
        remote(ring.at[k], mix_r.at[k], s_mx + k, r_mx + k, x_dev).start()

    for q in range(S):
        rows = pl.ds(q * T, T)

        def norm_rows(k, _, q=q):
            chunk = pl.ds(pl.multiple_of(q * T + k * ROWS_CHUNK, ROWS_CHUNK), ROWS_CHUNK)
            xv = tok_v[chunk, :].astype(F32)
            h1_v[0, chunk, :] = (xv * inv_rms(xv) * gain_mix_row).astype(BF)
            return 0

        lax.fori_loop(0, CPS, norm_rows, 0)
        if q == 0:
            for cp in load_w_in():
                cp.wait()

        def in_proj(j, _, q=q, rows=rows):
            cols = pl.ds(pl.multiple_of(j * 256, 256), 256)
            cols1 = pl.ds(pl.multiple_of(CL + j * 256, 256), 256)
            h = h1_v[0, rows, :]
            b = nn(h, wg_v[:, cols])
            pb[rows, cols] = b.astype(BF)
            xx = nn(h, wu_v[:, cols])
            px[rows, cols] = xx.astype(BF)
            inner = (b * xx).astype(BF)
            bx[rows, cols] = inner
            halo_s[q, :, cols] = inner[T - 16 : T]
            pcv = nn(h, wg_v[:, cols1])
            pc[rows, cols] = pcv.astype(BF)
            now = inner.astype(F32)
            cv = convolve(conv_terms(now, jnp.zeros_like(now[0:16]), row_iota), cols)
            gated[rows, cols] = (pcv * cv).astype(BF)
            return 0

        lax.fori_loop(0, NC, in_proj, 0)
        if q == 0:
            pl.semaphore_wait(bar, 3 + 2 * NZ)
        if q == S - 1:
            ld_wg.start()
            ld_wu.start()

        @pl.when(has_next)
        def _(q=q):
            halo_send(q).start()

        if q == 0:
            ld_wout.wait()
        for k in range(CPS - 1, 0, -1):
            mixer_out(q * CPS + k)

        @pl.when(has_prev)
        def _(q=q):
            wait_recv(halo_r.at[q], r_ha + q)

        @pl.when(jnp.logical_not(has_prev))
        def _(q=q):
            halo_r[q] = jnp.zeros_like(halo_r[q])

        def conv_top(j, _, q=q):
            cols = pl.ds(pl.multiple_of(j * 256, 256), 256)
            top = pl.ds(q * T, 16)
            now = bx[top, cols].astype(F32)
            cv = convolve(conv_terms(now, halo_r[q, :, cols].astype(F32), top_iota), cols)
            gated[top, cols] = (pc[top, cols].astype(F32) * cv).astype(BF)
            return 0

        lax.fori_loop(0, NC, conv_top, 0)
        mixer_out(q * CPS)
        h1_send(q).start()
        if q == 0:
            ld_dy.start()
            s_dy, r_dy = take_s(), take_r()
            send_dy = remote(cot, dy_v.at[1], s_dy, r_dy, core_dev)
            send_dy.start()
    ld_wd.start()

    s_h2, r_h2 = take_s(NCH), take_r(NCH)
    ld_wg.wait()
    ld_wu.wait()
    NF = FW // 256
    overlap = 2 * FW - FL
    col_iota = lax.broadcasted_iota(jnp.int32, (2 * ROWS_CHUNK, 256), 1)

    def forward_chunk(n, _):
        k = (n // CPS) * CPS + (CPS - 1 - n % CPS)
        rows = pl.ds(pl.multiple_of(k * ROWS_CHUNK, ROWS_CHUNK), ROWS_CHUNK)
        wait_recv(mix_r.at[k], r_mx + k)
        res = tok_v[rows, :].astype(F32) + (ring[k].astype(F32) + mix_r[k].astype(F32))
        resid[rows, :] = res
        h2_v[0, rows, :] = (res * inv_rms(res) * gain_ffn_row).astype(BF)
        remote(h2_v.at[0, rows], h2_v.at[1, rows], s_h2 + k, r_h2 + k, core_dev).start()
        wait_recv(h2_v.at[1, rows], r_h2 + k)

        def tile(j, _):
            cols = pl.ds(pl.multiple_of(j * 256, 256), 256)
            h = h2_v[:, rows, :].reshape(2 * ROWS_CHUNK, D)
            g = nn(h, wg_v[:, cols])
            u = nn(h, wu_v[:, cols])
            keep = col_iota + j * 256 >= c * overlap
            sg = jax.nn.sigmoid(g)
            si = jnp.where(keep, g * sg, 0.0)
            shape = (2, ROWS_CHUNK, 256)
            hid[:, rows, cols] = (si * u).astype(BF).reshape(shape)
            slope = jnp.where(keep, u * sg * (1.0 + g * (1.0 - sg)), 0.0)
            dg[:, rows, cols] = slope.astype(BF).reshape(shape)
            du[:, rows, cols] = si.astype(BF).reshape(shape)
            return 0

        lax.fori_loop(0, NF, tile, 0)
        return 0

    lax.fori_loop(0, NCH, forward_chunk, 0)
    ld_dy.wait()
    send_dy.wait()
    for k in range(NCH):
        wait_send(ring.at[k], s_mx + k)
        wait_send(h2_v.at[0, pl.ds(k * ROWS_CHUNK, ROWS_CHUNK)], s_h2 + k)

    gbs = [gb0, gb1, gb2, gb3, gb4]
    ybs = [yb0, yb1, yb2, yb3, yb4]
    zbs = [zb0, zb1, zb2, zb3, zb4]
    widths = [ZF_COLS, FW - ZF_COLS, FW, FW, 2 * CL]
    s_y = [None] + [take_s(NZ) for _ in range(4)]
    r_y = [None] + [take_r(NZ) for _ in range(4)]
    s_z = [take_s(2 * NZ)] + [take_s(NZ) for _ in range(4)]
    r_z = [take_r(4 * NZ)] + [take_r(2 * NZ) for _ in range(4)]

    def order(e):
        if e == NZ - 1:
            return z
        per_z = {0: (3, 2, 1), 1: (3, 0, 2), 2: (0, 3, 1), 3: (0, 1, 2)}
        v = per_z[3][e]
        for zz in range(3):
            v = jnp.where(z == zz, per_z[zz][e], v)
        return v

    def order_dyn(u):
        v = order(NZ - 1)
        for e in range(NZ - 1):
            v = jnp.where(u == e, order(e), v)
        return v

    def per_core(j, act):
        if j in (1, 4):
            act(lambda ref: ref)
            return

        @pl.when(c == 0)
        def _():
            act(lambda ref: ref)

        @pl.when(c == 1)
        def _():
            act(lambda ref: ref.at[:, pl.ds(overlap, widths[j] - overlap)])

    def z_send(j, src, e, zp, h=None):
        to_right = zp > z
        d = jnp.where(to_right, 0, 1)
        dev = did(jnp.clip(jnp.where(to_right, z + 1, z - 1), 0, NZ - 1), y, c)
        if h is None:
            dst, si, ri = zbs[j].at[d, zp], s_z[j] + e, r_z[j] + d * NZ + zp
        else:
            dst, si, ri = zbs[j].at[d, zp, h], s_z[j] + 2 * e + h, r_z[j] + (d * NZ + zp) * 2 + h
        per_core(j, lambda cut: remote(cut(src), cut(dst), si, ri, dev).start())

    l_g = take_l(12)

    def y_send(j, u):
        zp = order_dyn(u) if not isinstance(u, int) else order(u)
        src, dst = gbs[j].at[zp, 1 - y], ybs[j].at[zp]
        per_core(j, lambda cut: remote(cut(src), cut(dst), s_y[j] + u, r_y[j] + u, y_dev).start())

    def g_block(lhs_ref, rhs_ref, zp, pair, parts=(0, 1)):
        lhs = lhs_ref[:, :, pl.ds(pl.multiple_of(zp * GR, GR), GR)].reshape(2 * R, GR)
        half = FW // 2
        for n in parts:
            v = tn(lhs, rhs_ref[:, :, n * half : (n + 1) * half].reshape(2 * R, half)).astype(BF)
            outs[2 * pair, :, n * half : (n + 1) * half] = v[:SR]
            outs[2 * pair + 1, :, n * half : (n + 1) * half] = v[SR:]

    def down_copies(zp, pair):
        return [
            cp
            for h in range(2)
            for cp in (
                local(outs.at[2 * pair + h, :, pl.ds(0, ZF_COLS)], gb0.at[zp, h], l_g + 4 * pair + 2 * h),
                local(
                    outs.at[2 * pair + h, :, pl.ds(ZF_COLS, FW - ZF_COLS)],
                    gb1.at[zp, h], l_g + 4 * pair + 2 * h + 1,
                ),
            )
        ]

    def down_sends(u):
        zp = order(u)
        for cp in down_copies(zp, u % 2):
            cp.wait()
        if u < NZ - 1:

            @pl.when(end)
            def _():
                for h in range(2):
                    z_send(0, gb0.at[zp, h], u, zp, h)

            y_send(1, u)

    for u in range(NZ):
        g_block(dy_v, hid, order(u), u % 2, (0,))
        if u > 0:
            down_sends(u - 1)
        g_block(dy_v, hid, order(u), u % 2, (1,))
        for cp in down_copies(order(u), u % 2):
            cp.start()
    down_sends(NZ - 1)

    ld_wd.wait()

    def hid_back(n, _):
        slot, j = n // NF, n % NF
        cols = pl.ds(pl.multiple_of(j * 256, 256), 256)
        dh = nt(dy_v[slot], wd_v[cols, :])
        dg[slot, :, cols] = (dh * dg[slot, :, cols].astype(F32)).astype(BF)
        du[slot, :, cols] = (dh * du[slot, :, cols].astype(F32)).astype(BF)
        return 0

    lax.fori_loop(0, 2 * NF, hid_back, 0)

    def plain_copies(gb, zp, pair):
        return [local(outs.at[2 * pair + h], gb.at[zp, h], l_g + 2 * pair + h) for h in range(2)]

    def gate_up(u, _):
        zp = order_dyn(u)

        def up_sends(u):
            for cp in plain_copies(gb3, order_dyn(u), 1):
                cp.wait()

            @pl.when(u < 2)
            def _():
                y_send(3, u)

        g_block(h2_v, dg, zp, 0, (0,))

        @pl.when(u > 0)
        def _():
            up_sends(u - 1)

        g_block(h2_v, dg, zp, 0, (1,))
        for cp in plain_copies(gb2, zp, 0):
            cp.start()
        g_block(h2_v, du, zp, 1, (0,))
        for cp in plain_copies(gb2, zp, 0):
            cp.wait()

        @pl.when(u < 2)
        def _():
            y_send(2, u)

        g_block(h2_v, du, zp, 1, (1,))
        for cp in plain_copies(gb3, zp, 1):
            cp.start()
        return 0

    lax.fori_loop(0, NZ, gate_up, 0)
    for cp in plain_copies(gb3, order(NZ - 1), 1):
        cp.wait()

    l_e = take_l(4)
    is_role = {"end": end, "mid": mid}
    slot_last = {role: [None] * outs.shape[0] for role in is_role}
    slot_next = {role: 0 for role in is_role}

    def claim_slot(role):
        o = slot_next[role]
        slot_next[role] = (o + 1) % outs.shape[0]
        if slot_last[role][o] is not None:
            slot_last[role][o]()
            slot_last[role][o] = None
        return o

    ADD_ROWS = 32

    def add_into(dst, srcs):
        def rows_add(k, _):
            rows = pl.ds(pl.multiple_of(k * ADD_ROWS, ADD_ROWS), ADD_ROWS)
            acc = srcs[0][rows, :].astype(F32)
            for src in srcs[1:]:
                acc = acc + src[rows, :].astype(F32)
            dst[rows, :] = acc.astype(BF)
            return 0

        lax.fori_loop(0, SR // ADD_ROWS, rows_add, 0)

    def fetch(j, srcs):
        w = widths[j]
        views, copies = [], []
        for i, (src, ri) in enumerate(srcs):
            if ri is not None:
                per_core(j, lambda cut: wait_recv(cut(src), ri))
            views.append(ld.at[i, :, pl.ds(0, w)])
            copies.append(local(src, views[-1], l_e + i))
            copies[-1].start()
        for cp in copies:
            cp.wait()
        return views

    def from_line(j, d, zp, h=None):
        if h is None:
            return zbs[j].at[d, zp], r_z[j] + d * NZ + zp
        return zbs[j].at[d, zp, h], r_z[j] + (d * NZ + zp) * 2 + h

    def line_event(role, j, e):
        @pl.when(is_role[role])
        def _():
            zp = order(e)
            w = widths[j]
            d = jnp.where(zp > z, 0, 1)
            for h in (0, 1) if j == 0 else (None,):
                o = claim_slot(role)
                dst = outs.at[o, :, pl.ds(0, w)]
                if h is None:
                    srcs = [(gbs[j].at[zp, y], None), (ybs[j].at[zp], r_y[j] + e)]
                    si = s_z[j] + e
                else:
                    srcs = [(gbs[j].at[zp, h], None)]
                    si = s_z[j] + 2 * e + h
                if role == "mid":
                    srcs.append(from_line(j, d, zp, h))
                add_into(dst, fetch(j, srcs))
                z_send(j, dst, e, zp, h)
                slot_last[role][o] = functools.partial(sent_slot, j, o, si)

    def sent_slot(j, o, si):
        per_core(j, lambda cut: wait_send(cut(outs.at[o, :, pl.ds(0, widths[j])]), si))

    def own_shard(role, j, h=None):
        if h is None:
            srcs = [(gbs[j].at[z, y], None), (ybs[j].at[z], r_y[j] + NZ - 1)]
        else:
            srcs = [(gbs[j].at[z, h], None)]
        if role == "mid":
            return srcs + [from_line(j, 0, z, h), from_line(j, 1, z, h)]
        return srcs + [from_line(j, jnp.where(z == 0, 1, 0), z, h)]

    def swap_pieces(j):
        if j == 4:
            return [(None, m * CH, CH, g_conv.at[m], c * CH) for m in range(4)]
        mat = g_ffn.at[{0: 0, 1: 0, 2: 1, 3: 2}[j]]
        w = widths[j]
        if j == 1:
            return [(None, 0, w, mat, c * (FL - FW) + ZF_COLS)]
        return [(0, 0, w, mat, 0), (1, overlap, w - overlap, mat, FL - FW + overlap)]

    swap_sems = [[(take_s(), take_r(), take_l()) for _ in swap_pieces(j)] for j in range(5)]

    def swap(j, o):
        items = []
        for (core, c0, w, mat, to), (si, ri, li) in zip(swap_pieces(j), swap_sems[j]):
            to = to if isinstance(to, int) else pl.multiple_of(to, LANE)
            target = mat.at[:, pl.ds(to, w)]
            mine = outs.at[o, pl.ds(pl.multiple_of(c * DR, DR), DR), pl.ds(c0, w)]
            other = outs.at[o, pl.ds(pl.multiple_of((1 - c) * DR, DR), DR), pl.ds(c0, w)]
            items.append((core, local(mine, target, li), remote(other, target, si, ri, core_dev), target))
        return items

    def swap_start(j, o):
        for core, keep, give, _ in swap(j, o):
            if core is None:
                keep.start()
                give.start()
            else:

                @pl.when(c == core)
                def _():
                    keep.start()
                    give.start()

    def swap_finish(j, o):
        for (core, keep, give, target), (_, ri, _) in zip(swap(j, o), swap_sems[j]):
            if core is None:
                keep.wait()
                give.wait_send()
                wait_recv(target, ri)
            else:

                @pl.when(c == core)
                def _():
                    keep.wait()
                    give.wait_send()

                @pl.when(c != core)
                def _():
                    wait_recv(target, ri)

    def final_event(role, j):
        @pl.when(is_role[role])
        def _():
            o = claim_slot(role)
            w = widths[j]
            add_into(outs.at[o, :, pl.ds(0, w)], fetch(j, own_shard(role, j)))
            swap_start(j, o)
            slot_last[role][o] = functools.partial(swap_finish, j, o)

    s_f0, r_f0 = take_s(), take_r()
    w0 = widths[0]

    def final0_send(role):
        @pl.when(is_role[role])
        def _():
            o = claim_slot(role)
            dst = outs.at[o, :, pl.ds(0, w0)]
            add_into(dst, fetch(0, own_shard(role, 0, 1 - y)))
            cp = local(dst, gb0.at[z, 1 - y], l_e)
            cp.start()
            cp.wait()
            src = gb0.at[z, 1 - y]
            per_core(0, lambda cut: remote(cut(src), cut(yb0), s_f0, r_f0, y_dev).start())

    def final0_finish(role):
        @pl.when(is_role[role])
        def _():
            o = claim_slot(role)
            dst = outs.at[o, :, pl.ds(0, w0)]
            add_into(dst, fetch(0, own_shard(role, 0, y)))
            add_into(dst, [dst] + fetch(0, [(yb0, r_f0)]))
            swap_start(0, o)
            slot_last[role][o] = functools.partial(swap_finish, 0, o)

    def hook(name):
        for role, event in SCHEDULE.get(name, ()):
            if event == "pair":
                final0_send(role)
            elif event == "pair sum":
                final0_finish(role)
            elif event[1] == NZ - 1:
                final_event(role, event[0])
            else:
                line_event(role, *event)

    def chunks(name, count, body):
        first = 0
        for k in range(count):
            if SCHEDULE.get(name + str(k)) or k == count - 1:
                lax.fori_loop(first, k + 1, body, 0)
                first = k + 1
                hook(name + str(k))

    HALF = 2 * ROWS_CHUNK

    def split_sum(name, product, cr, xr, base_a, base_d):
        s_c, r_c = take_s(2), take_r(2)
        s_x, r_x = take_s(NCH), take_r(NCH)
        l_c = take_l()

        def give(k, _):
            def tile(n, _):
                cols = pl.ds(pl.multiple_of(n * 512, 512), 512)
                v = product(1, k * HALF, n).astype(BF)
                ring[pl.ds(base_a + 2 * k, 2), :, cols] = v.reshape(2, ROWS_CHUNK, 512)
                return 0

            lax.fori_loop(0, D // 512, tile, 0)
            remote(
                ring.at[pl.ds(base_a + 2 * k, 2)], cr.at[pl.ds(2 * k, 2)], s_c + k, r_c + k, core_dev
            ).start()
            return 0

        lax.fori_loop(0, 2, give, 0)
        hook(name + "A")

        def keep(k, _):
            src = cr.at[pl.ds(2 * k, 2)]
            wait_recv(src, r_c + k)
            cp = local(src, rb, l_c)
            cp.start()
            cp.wait()

            def tile(n, _):
                cols = pl.ds(pl.multiple_of(n * 512, 512), 512)
                v = product(0, k * HALF, n) + rb[:, :, cols].reshape(HALF, 512).astype(F32)
                ring[pl.ds(base_d + 2 * k, 2), :, cols] = v.astype(BF).reshape(2, ROWS_CHUNK, 512)
                return 0

            lax.fori_loop(0, D // 512, tile, 0)
            for i in range(2):
                remote(
                    ring.at[base_d + 2 * k + i], xr.at[2 * k + i], s_x + 2 * k + i, r_x + 2 * k + i, x_dev
                ).start()
            return 0

        lax.fori_loop(0, 2, keep, 0)
        for k in range(2):
            wait_send(ring.at[pl.ds(base_a + 2 * k, 2)], s_c + k)
        hook(name + "D")
        return s_x, r_x

    def rows_at(ref, slot, r0):
        return ref[slot, pl.ds(pl.multiple_of(r0, HALF), HALF), :]

    def dh_product(slot, r0, n):
        cols = pl.ds(pl.multiple_of(n * 512, 512), 512)
        return nt(rows_at(dg, slot, r0), wg_v[cols, :]) + nt(rows_at(du, slot, r0), wu_v[cols, :])

    def dn_product(slot, r0, n):
        cols = pl.ds(pl.multiple_of(n * 512, 512), 512)
        return nn(rows_at(hid, slot, r0), wd_v[:, cols])

    s_xdh, r_xdh = split_sum("dh", dh_product, cr_dh, xr_dh, 0, 4)
    s_xdn, r_xdn = split_sum("dn", dn_product, cr_dn, xr_dn, 0, 8)
    for cp in load_w_in():
        cp.start()
    ld_wout.start()

    l_x = take_l()
    s_do, r_do = take_s(NCH), take_r(NCH)
    xbuf = rb.at[0]

    def ffn_norm_back(k, _):
        rows = pl.ds(pl.multiple_of(k * ROWS_CHUNK, ROWS_CHUNK), ROWS_CHUNK)
        wait_recv(xr_dh.at[k], r_xdh + k)
        cp = local(xr_dh.at[k], xbuf, l_x)
        cp.start()
        cp.wait()
        d_h = ring[4 + k].astype(F32) + xbuf[...].astype(F32)
        res = resid[rows, :]
        s2 = inv_rms(res)
        n2 = res * s2
        sm[0, 1:2, :] += jnp.sum(d_h * n2, axis=0, keepdims=True)
        e2 = d_h * gain_ffn_row
        d_res = dy_v[0, rows, :].astype(F32) + s2 * (
            e2 - n2 * jnp.mean(e2 * n2, axis=-1, keepdims=True)
        )
        h2_v[0, rows, :] = d_res.astype(BF)
        remote(h2_v.at[0, rows], h2_v.at[1, rows], s_do + k, r_do + k, core_dev).start()
        return 0

    chunks("nb", NCH, ffn_norm_back)
    for k in range(NCH):
        wait_send(ring.at[4 + k], s_xdh + k)

    for cp in load_w_in():
        cp.wait()
    ld_wout.wait()
    for q in range(S):

        def conv_back(j, _, q=q):
            cols = pl.ds(pl.multiple_of(j * 256, 256), 256)
            rows = pl.ds(q * T, T)
            now, one, two = conv_terms(
                bx[rows, cols].astype(F32), halo_r[q, :, cols].astype(F32), row_iota
            )
            k0, k1, k2 = tap_cols(cols)
            cv = k0 * two + k1 * one + k2 * now
            d_g = nt(h2_v[0, q * T : q * T + T, :], wd_v[cols, :])
            d_cv = d_g * pc[rows, cols].astype(F32)
            sm[0, 2:3, cols] += jnp.sum(d_cv * two, axis=0, keepdims=True)
            sm[0, 3:4, cols] += jnp.sum(d_cv * one, axis=0, keepdims=True)
            sm[0, 4:5, cols] += jnp.sum(d_cv * now, axis=0, keepdims=True)
            after1 = jnp.where(row_iota < T - 1, pltpu.roll(d_cv, T - 1, 0), 0.0)
            after2 = jnp.where(row_iota < T - 2, pltpu.roll(d_cv, T - 2, 0), 0.0)
            d_bx = k2 * d_cv + k1 * after1 + k0 * after2
            dhalo_s[q, :, cols] = d_cv[0:8]
            tail[q, :, cols] = d_bx[T - 16 : T]
            old_b = pb[rows, cols]
            old_x = px[rows, cols]
            pb_tail[q, :, cols] = old_b[T - 16 : T]
            px_tail[q, :, cols] = old_x[T - 16 : T]
            low = d_bx.astype(BF).astype(F32)
            pb[rows, cols] = (low * old_x.astype(F32)).astype(BF)
            px[rows, cols] = (low * old_b.astype(F32)).astype(BF)
            pc[rows, cols] = (d_g * cv).astype(BF)
            return 0

        lax.fori_loop(0, NC, conv_back, 0)

    s_dha, r_dha = take_s(), take_r()
    send_dhalo = remote(dhalo_s, dhalo_r, s_dha, r_dha, prev_dev)

    @pl.when(has_prev)
    def _():
        send_dhalo.start()

    for j, u in ((2, 2), (3, 2)):
        y_send(j, u)

    hook("cb")

    s_x1, r_x1 = take_s(NCH), take_r(NCH)

    def d1_part(name, ids):
        def tile(n, _):
            cols = pl.ds(pl.multiple_of(n * 512, 512), 512)

            def rows_of(ref):
                return jnp.concatenate(
                    [ref[k * ROWS_CHUNK : (k + 1) * ROWS_CHUNK, :] for k in ids], axis=0
                )

            v = (
                nt(rows_of(pb), wg_v[cols, 0:CL])
                + nt(rows_of(pc), wg_v[cols, CL : 2 * CL])
                + nt(rows_of(px), wu_v[cols, 0:CL])
            ).astype(BF)
            for i, k in enumerate(ids):
                ring[4 + k, :, cols] = v[i * ROWS_CHUNK : (i + 1) * ROWS_CHUNK]
            return 0

        lax.fori_loop(0, D // 512, tile, 0)
        for k in ids:
            remote(ring.at[4 + k], xr_d1.at[k], s_x1 + k, r_x1 + k, x_dev).start()
        hook(name)

    d1_part("d1a", [q * CPS + k for q in range(S) for k in range(CPS - 1)])

    @pl.when(has_next)
    def _():
        wait_recv(dhalo_r, r_dha)

    @pl.when(jnp.logical_not(has_next))
    def _():
        dhalo_r[...] = jnp.zeros_like(dhalo_r)

    tail_iota = lax.broadcasted_iota(jnp.int32, (16, CL), 0)
    for q in range(S):
        first = jnp.broadcast_to(dhalo_r[q, 0:1, :], (16, CL))
        second = jnp.broadcast_to(dhalo_r[q, 1:2, :], (16, CL))
        fix = jnp.where(
            tail_iota == 14,
            k_taps[0] * first,
            jnp.where(tail_iota == 15, k_taps[1] * first + k_taps[0] * second, 0.0),
        )
        low = (tail[q] + fix).astype(BF).astype(F32)
        rows = pl.ds(q * T + T - 16, 16)
        pb[rows, :] = (low * px_tail[q].astype(F32)).astype(BF)
        px[rows, :] = (low * pb_tail[q].astype(F32)).astype(BF)

    s_dp, r_dp = take_s(4), take_r(4)
    theirs = pl.ds(pl.multiple_of((1 - c) * CH, LANE), CH)
    ours = pl.ds(pl.multiple_of(c * CH, LANE), CH)
    dp_sends = [
        remote(ref.at[:, theirs], dy_v.at[1, :, pl.ds(m * CH, CH)], s_dp + m, r_dp + m, core_dev)
        for m, ref in enumerate((pb, pc, px, gated))
    ]
    for cp in dp_sends:
        cp.start()
    hook("tail")

    d1_part("d1b", [q * CPS + k for q in range(S) for k in range(1, CPS)])

    for q in range(S):
        wait_recv(h1_v.at[1, pl.ds(q * T, T)], r_h1 + q)
    for k in range(NCH):
        rows = pl.ds(k * ROWS_CHUNK, ROWS_CHUNK)
        wait_recv(h2_v.at[1, rows], r_do + k)
    for m in range(4):
        wait_recv(dy_v.at[1, :, pl.ds(m * CH, CH)], r_dp + m)
    W4 = widths[4]
    g4 = [dg.at[i, pl.ds(k * SR, SR), pl.ds(0, W4)] for i in range(2) for k in range(2)]

    def g_mixer(u, _):
        zp = order_dyn(u)
        zc = pl.ds(pl.multiple_of(zp * GR, GR), GR)
        for m, (mine, lhs) in enumerate(((pb, h1_v), (pc, h1_v), (px, h1_v), (gated, h2_v))):
            v = tn(lhs[0, :, zc], mine[:, ours]) + tn(
                lhs[1, :, zc], dy_v[1, :, m * CH : (m + 1) * CH]
            )
            v = v.astype(BF)
            g4[0][:, m * CH : (m + 1) * CH] = v[:SR]
            g4[1][:, m * CH : (m + 1) * CH] = v[SR:]
        cps = [local(g4[h], gb4.at[zp, h], l_g + h) for h in range(2)]
        for cp in cps:
            cp.start()
        for cp in cps:
            cp.wait()

        @pl.when(u < NZ - 1)
        def _():
            y_send(4, u)

        return 0

    chunks("gc", NZ, g_mixer)
    for j in (1, 2, 3, 4):
        y_send(j, NZ - 1)

    l_o = take_l()

    def block_chunk(k, _):
        rows = pl.ds(pl.multiple_of(k * ROWS_CHUNK, ROWS_CHUNK), ROWS_CHUNK)
        wait_recv(xr_dn.at[k], r_xdn + k)
        cp = local(xr_dn.at[k], xbuf, l_x)
        cp.start()
        cp.wait()
        total = ring[8 + k].astype(F32) + xbuf[...].astype(F32)
        rb[1] = (resid[rows, :] + total).astype(BF)
        co = local(rb.at[1], block_out.at[rows, :], l_o)
        co.start()
        co.wait()
        return 0

    chunks("blk", NCH, block_chunk)

    def mix_norm_back(n, _):
        k = (n % S) * CPS + n // S
        rows = pl.ds(pl.multiple_of(k * ROWS_CHUNK, ROWS_CHUNK), ROWS_CHUNK)
        wait_recv(xr_d1.at[k], r_x1 + k)
        cp = local(xr_d1.at[k], xbuf, l_x)
        cp.start()
        cp.wait()
        d_h = ring[4 + k].astype(F32) + xbuf[...].astype(F32)
        xv = tok_v[rows, :].astype(F32)
        s1 = inv_rms(xv)
        n1 = xv * s1
        sm[0, 0:1, :] += jnp.sum(d_h * n1, axis=0, keepdims=True)
        e1 = d_h * gain_mix_row
        out = h2_v[0, rows, :].astype(F32) + s1 * (
            e1 - n1 * jnp.mean(e1 * n1, axis=-1, keepdims=True)
        )
        rb[1] = out.astype(BF)
        co = local(rb.at[1], d_tokens.at[rows, :], l_o)
        co.start()
        co.wait()
        return 0

    chunks("dt", NCH, mix_norm_back)

    s_sm, r_sm = take_s(2 * NZ), take_r(2 * NZ)
    a = remote(sm.at[0], sm_r.at[0], s_sm, r_sm, core_dev)
    a.start()
    a.wait()
    sm[1] = sm[0] + sm_r[0]
    for k, dev in others:
        remote(sm.at[1], sm_r.at[k], s_sm + k, r_sm + k, dev).start()
    hook("sm")

    total = sm[1]
    for k, _ in others:
        wait_recv(sm_r.at[k], r_sm + k)
        total = total + sm_r[k]
    for k, _ in others:
        wait_send(sm.at[1], s_sm + k)
    sm[0] = total
    out_small = local(sm.at[0], small_out, l_small)
    out_small.start()
    out_small.wait()

    for role, cond in is_role.items():

        @pl.when(cond)
        def _(role=role):
            for finish in slot_last[role]:
                if finish is not None:
                    finish()

    @pl.when(end)
    def _():
        for e in range(NZ - 1):
            for h in range(2):
                per_core(0, lambda cut: wait_send(cut(gb0.at[0, h]), s_z[0] + 2 * e + h))

    for j in range(1, 5):
        for u in range(NZ):
            per_core(j, lambda cut: wait_send(cut(ybs[j].at[0]), s_y[j] + u))
    per_core(0, lambda cut: wait_send(cut(yb0), s_f0))
    for q in range(S):
        h1_send(q).wait_send()
    for k in range(NCH):
        wait_send(h2_v.at[0, pl.ds(k * ROWS_CHUNK, ROWS_CHUNK)], s_do + k)
        wait_send(ring.at[4 + k], s_x1 + k)
        wait_send(ring.at[8 + k], s_xdn + k)
    for cp in dp_sends:
        cp.wait_send()

    @pl.when(has_next)
    def _():
        for q in range(S):
            halo_send(q).wait_send()

    @pl.when(has_prev)
    def _():
        send_dhalo.wait_send()


def fused_body(tokens, gain_mix, w_in, kernel, w_out, gain_ffn, w_gate, w_up, w_down, cotangent):
    S, T, D = tokens.shape
    CL = w_out.shape[0]
    FL = w_gate.shape[1]
    R = S * T
    n_seq = lax.axis_size("seq")
    tiles = FL // LANE
    FW = -(-tiles // 2) * LANE
    GR = D // NZ
    SR = GR // 2
    DR = SR // 2
    widths = [ZF_COLS, FW - ZF_COLS, FW, FW, 2 * CL]
    NCH = R // ROWS_CHUNK

    def sds(shape, dtype=BF):
        return jax.ShapeDtypeStruct(shape, dtype)

    outs = [sds((R, D)), sds((R, D)), sds((3, DR, FL)), sds((4, DR, CL)), sds((8, D), F32)]
    outs += [sds((NZ, 2, SR, w)) for w in widths]
    outs += [sds((SR, widths[0]))] + [sds((NZ, SR, w)) for w in widths[1:]]
    outs += [sds((2, NZ, 2, SR, widths[0]))] + [sds((2, NZ, SR, w)) for w in widths[1:]]
    outs += [sds((NCH, ROWS_CHUNK, D))] * 5
    any_spec = pl.BlockSpec(memory_space=pl.ANY)
    V = pltpu.VMEM
    scratch = [
        V((D,), F32),
        V((3, CL), F32),
        V((D,), F32),
        V((R, D), BF),
        V((D, FW), BF),
        V((D, FW), BF),
        V((FW, D), BF),
        V((2, R, D), BF),
        V((2, R, D), BF),
        V((2, R, D), BF),
        V((2, R, FW), BF),
        V((2, R, FW), BF),
        V((2, R, FW), BF),
        V((R, CL), BF),
        V((R, CL), BF),
        V((R, CL), BF),
        V((R, CL), BF),
        V((R, CL), BF),
        V((R, D), F32),
        V((NCH, ROWS_CHUNK, D), BF),
        V((12, ROWS_CHUNK, D), BF),
        V((2, ROWS_CHUNK, D), BF),
        V((4, SR, FW), BF),
        V((4, SR, FW), BF),
        V((S, 16, CL), BF),
        V((S, 16, CL), BF),
        V((S, 8, CL), F32),
        V((S, 8, CL), F32),
        V((S, 16, CL), F32),
        V((S, 16, CL), BF),
        V((S, 16, CL), BF),
        V((2, 8, D), F32),
        V((2 * NZ, 8, D), F32),
        pltpu.SemaphoreType.DMA((N_SEND,)),
        pltpu.SemaphoreType.DMA((N_RECV,)),
        pltpu.SemaphoreType.DMA((N_LOCAL,)),
    ]
    flops = 2 * R * D * (4 * CL + 3 * FL) * 3
    res = pl.pallas_call(
        functools.partial(step_kernel, (R, T, D, CL, FL, FW)),
        out_shape=outs,
        in_specs=[any_spec] * 10,
        out_specs=[any_spec] * len(outs),
        scratch_shapes=scratch,
        compiler_params=pltpu.CompilerParams(
            collective_id=0, has_side_effects=True, vmem_limit_bytes=63 << 20
        ),
        cost_estimate=pl.CostEstimate(flops=flops, bytes_accessed=200 << 20, transcendentals=0),
        name="block_step",
    )(
        tokens.reshape(R, D), gain_mix, w_in, kernel, w_out,
        gain_ffn, w_gate, w_up, w_down, cotangent.reshape(R, D),
    )
    block_out, d_tokens, g_mix, g_in, g_taps, g_out, g_gain, g_gate, g_up, g_down = finish(
        n_seq, *res[:5]
    )
    return (
        block_out.reshape(S, T, D),
        d_tokens.reshape(S, T, D),
        g_mix, g_in, g_taps, g_out.T, g_gain, g_gate, g_up, g_down.T,
    )


def finish_kernel(
    n_seq, block_in, d_in, ffn_in, conv_in, small_in,
    block_out, d_out, g_mix, g_in, g_taps, g_out, g_gain, g_gate, g_up, g_down,
    block_v, d_v, ffn, conv, small, gate_v, up_v, down_v, in_v, out_v, mix_v, taps_v, gain_v, sem,
):
    D = d_in.shape[1]
    CL = conv_in.shape[2]
    s = lax.axis_index("seq")
    count = [0]

    def copy(src, dst):
        count[0] += 1
        cp = pltpu.make_async_copy(src, dst, sem.at[count[0] - 1])
        cp.start()
        return cp

    loads = [copy(ffn_in.at[0], ffn.at[0]), copy(conv_in, conv), copy(small_in, small)]
    loads += [copy(ffn_in.at[m], ffn.at[m]) for m in (1, 2)]
    passing = [copy(block_in, block_v), copy(d_in, d_v)]
    stores = []
    loads[0].wait()
    down_v[...] = ffn[0].astype(F32)
    stores.append(copy(down_v, g_down))
    loads[1].wait()
    in_v[...] = conv[0:3].astype(F32)
    stores.append(copy(in_v, g_in))
    out_v[...] = conv[3].astype(F32)
    stores.append(copy(out_v, g_out))
    passing[0].wait()
    stores.append(copy(block_v, block_out))
    passing[1].wait()
    stores.append(copy(d_v, d_out))
    loads[3].wait()
    gate_v[...] = ffn[1].astype(F32)
    stores.append(copy(gate_v, g_gate))
    loads[4].wait()
    up_v[...] = ffn[2].astype(F32)
    stores.append(copy(up_v, g_up))
    loads[2].wait()
    per_d, per_c = D // n_seq, CL // n_seq
    mine = pltpu.roll(small[...], D - s * per_d, 1)
    mix_v[...] = mine[0, 0:per_d]
    gain_v[...] = mine[1, 0:per_d]
    mine = pltpu.roll(small[...], D - s * per_c, 1)
    for t in range(3):
        taps_v[t] = mine[2 + t : 3 + t, 0:per_c]
    stores += [copy(mix_v, g_mix), copy(gain_v, g_gain), copy(taps_v, g_taps)]
    for cp in stores:
        cp.wait()


def finish(n_seq, block_out, d_tokens, g_ffn, g_conv, small):
    R, D = block_out.shape
    _, DR, FL = g_ffn.shape
    CL = g_conv.shape[2]
    any_spec = pl.BlockSpec(memory_space=pl.ANY)
    V = pltpu.VMEM
    tails = [
        (DR, FL), (DR, FL), (DR, FL), (3, DR, CL), (DR, CL),
        (D // n_seq,), (3, 1, CL // n_seq), (D // n_seq,),
    ]
    gate, up, down, inp, out, mix, taps, gain = [jax.ShapeDtypeStruct(t, F32) for t in tails]
    low = jax.ShapeDtypeStruct((R, D), BF)
    return pl.pallas_call(
        functools.partial(finish_kernel, n_seq),
        out_shape=[low, low, mix, inp, taps, out, gain, gate, up, down],
        in_specs=[any_spec] * 5,
        out_specs=[any_spec] * 10,
        scratch_shapes=[V((R, D), BF), V((R, D), BF), V(g_ffn.shape, BF), V(g_conv.shape, BF), V(small.shape, F32)]
        + [V(t, F32) for t in tails]
        + [pltpu.SemaphoreType.DMA((20,))],
        compiler_params=pltpu.CompilerParams(vmem_limit_bytes=63 << 20),
        name="finish",
    )(block_out, d_tokens, g_ffn, g_conv, small)


def from_behind(value, axis, by):
    count = lax.axis_size(axis)
    pairs = [(i, i + by) for i in range(count) if 0 <= i + by < count]
    return lax.ppermute(value, axis, pairs)


def rms_scale(vector):
    return lax.rsqrt(jnp.mean(vector * vector, axis=-1, keepdims=True) + epsilon)


def norm_back(d_normout, normed, inv_scale, gain_vec):
    d_normed = d_normout * gain_vec
    return inv_scale * (d_normed - normed * jnp.mean(d_normed * normed, axis=-1, keepdims=True))


def matmul(lhs_mat, rhs_mat):
    return jnp.dot(lhs_mat, rhs_mat, preferred_element_type=jnp.float32)


def left_trans(lhs_mat, rhs_mat):
    return lax.dot_general(
        lhs_mat, rhs_mat, (((0,), (0,)), ((), ())), preferred_element_type=jnp.float32
    )


def right_trans(lhs_mat, rhs_mat):
    return lax.dot_general(
        lhs_mat, rhs_mat, (((1,), (1,)), ((), ())), preferred_element_type=jnp.float32
    )


def general_body(tokens, gain_mix, w_in, kernel, w_out, gain_ffn, w_gate, w_up, w_down, cotangent):
    seq_count, tok_rows, model_width = tokens.shape
    row_count = seq_count * tok_rows
    tokens_f = tokens.astype(jnp.float32).reshape(row_count, model_width)
    scale_mix = rms_scale(tokens_f)
    normed_mix = tokens_f * scale_mix
    h_mix = (normed_mix * gain_mix).astype(jnp.bfloat16)
    proj_b = matmul(h_mix, w_in[0])
    proj_c = matmul(h_mix, w_in[1])
    proj_x = matmul(h_mix, w_in[2])
    conv_in = (proj_b * proj_x).astype(jnp.bfloat16).reshape(seq_count, tok_rows, -1)
    before = from_behind(conv_in[:, tok_rows - 2 :, :], "seq", 1)
    extended = jnp.concatenate([before, conv_in], axis=1).astype(jnp.float32)
    conv_out = (
        kernel[0] * extended[:, :-2] + kernel[1] * extended[:, 1:-1] + kernel[2] * extended[:, 2:]
    )
    conv_flat = conv_out.reshape(row_count, -1)
    gated = (proj_c * conv_flat).astype(jnp.bfloat16)
    mixed_sum = lax.psum(matmul(gated, w_out).astype(jnp.bfloat16), "chan").astype(jnp.float32)
    residual = tokens_f + mixed_sum
    scale_ffn = rms_scale(residual)
    normed_ffn = residual * scale_ffn
    h_ffn = (normed_ffn * gain_ffn).astype(jnp.bfloat16)
    gate_pre = matmul(h_ffn, w_gate)
    up_value = matmul(h_ffn, w_up)
    sigmoid_gate = jax.nn.sigmoid(gate_pre)
    silu_gate = gate_pre * sigmoid_gate
    hidden = (silu_gate * up_value).astype(jnp.bfloat16)
    ffn_total = lax.psum(matmul(hidden, w_down).astype(jnp.bfloat16), "chan").astype(jnp.float32)
    block_out = (
        (residual + ffn_total).astype(jnp.bfloat16).reshape(seq_count, tok_rows, model_width)
    )
    grad_out = cotangent.reshape(row_count, model_width)
    g_w_down = left_trans(hidden, grad_out)
    d_hidden = right_trans(grad_out, w_down)
    d_gate = (d_hidden * up_value * sigmoid_gate * (1.0 + gate_pre * (1.0 - sigmoid_gate))).astype(
        jnp.bfloat16
    )
    d_up = (d_hidden * silu_gate).astype(jnp.bfloat16)
    g_w_gate = left_trans(h_ffn, d_gate)
    g_w_up = left_trans(h_ffn, d_up)
    d_h_ffn = lax.psum(
        (right_trans(d_gate, w_gate) + right_trans(d_up, w_up)).astype(jnp.bfloat16), "chan"
    ).astype(jnp.float32)
    g_gain_ffn = jnp.sum(d_h_ffn * normed_ffn, axis=0)
    d_resid = grad_out.astype(jnp.float32) + norm_back(d_h_ffn, normed_ffn, scale_ffn, gain_ffn)
    d_mixed = d_resid.astype(jnp.bfloat16)
    g_w_out = left_trans(gated, d_mixed)
    d_gated = right_trans(d_mixed, w_out)
    d_proj_c = (d_gated * conv_flat).astype(jnp.bfloat16)
    d_conv = (d_gated * proj_c).reshape(seq_count, tok_rows, -1)
    after_rows = from_behind(d_conv[:, :2, :], "seq", -1)
    ext_back = jnp.concatenate([d_conv, after_rows], axis=1)
    d_conv_in = (
        kernel[2] * ext_back[:, :-2] + kernel[1] * ext_back[:, 1:-1] + kernel[0] * ext_back[:, 2:]
    )
    g_kernel = jnp.stack(
        [
            jnp.sum(d_conv * extended[:, :-2], axis=(0, 1)),
            jnp.sum(d_conv * extended[:, 1:-1], axis=(0, 1)),
            jnp.sum(d_conv * extended[:, 2:], axis=(0, 1)),
        ]
    ).reshape(3, 1, -1)
    d_conv_low = d_conv_in.reshape(row_count, -1).astype(jnp.bfloat16)
    d_proj_b = (d_conv_low * proj_x).astype(jnp.bfloat16)
    d_proj_x = (d_conv_low * proj_b).astype(jnp.bfloat16)
    g_w_in = jnp.stack(
        [left_trans(h_mix, d_proj_b), left_trans(h_mix, d_proj_c), left_trans(h_mix, d_proj_x)]
    )
    d_h_mix = lax.psum(
        (
            right_trans(d_proj_b, w_in[0])
            + right_trans(d_proj_c, w_in[1])
            + right_trans(d_proj_x, w_in[2])
        ).astype(jnp.bfloat16),
        "chan",
    ).astype(jnp.float32)
    g_gain_mix = jnp.sum(d_h_mix * normed_mix, axis=0)
    d_tokens = (
        (d_resid + norm_back(d_h_mix, normed_mix, scale_mix, gain_mix))
        .astype(jnp.bfloat16)
        .reshape(seq_count, tok_rows, model_width)
    )
    summed = (
        lax.psum_scatter(g_w_in, "seq", scatter_dimension=1, tiled=True),
        lax.psum_scatter(g_w_out, "seq", scatter_dimension=1, tiled=True),
        lax.psum_scatter(g_kernel, "seq", scatter_dimension=2, tiled=True),
        lax.psum_scatter(g_gain_mix, "seq", scatter_dimension=0, tiled=True),
        lax.psum_scatter(g_w_gate, "seq", scatter_dimension=0, tiled=True),
        lax.psum_scatter(g_w_up, "seq", scatter_dimension=0, tiled=True),
        lax.psum_scatter(g_w_down, "seq", scatter_dimension=1, tiled=True),
        lax.psum_scatter(g_gain_ffn, "seq", scatter_dimension=0, tiled=True),
    )
    sum_in, sum_out, sum_kernel, sum_gain_mix, sum_gate, sum_up, sum_down, sum_gain_ffn = summed
    return (
        block_out,
        d_tokens,
        sum_gain_mix,
        sum_in,
        sum_kernel,
        sum_out,
        sum_gain_ffn,
        sum_gate,
        sum_up,
        sum_down,
    )


def solution(mesh):
    body = fused_body if mesh.shape["seq"] == 4 * NZ else general_body
    placed = (
        P(None, "seq", None),
        P(),
        P(None, None, "chan"),
        P(None, "chan"),
        P("chan", None),
        P(),
        P(None, "chan"),
        P(None, "chan"),
        P("chan", None),
        P(None, "seq", None),
    )
    return jax.shard_map(
        body,
        mesh=mesh,
        in_specs=placed,
        out_specs=(
            P(None, "seq", None),
            P(None, "seq", None),
            P("seq"),
            P(None, "seq", "chan"),
            P(None, "chan", "seq"),
            P("chan", "seq"),
            P("seq"),
            P("seq", "chan"),
            P("seq", "chan"),
            P("chan", "seq"),
        ),
        check_vma=False,
    )
```

```python
import functools

import jax
import jax.numpy as jnp
from jax import lax
from jax.experimental import pallas as pl
from jax.experimental.pallas import tpu as pltpu
from jax.sharding import PartitionSpec as P

epsilon = 1e-05
BF = jnp.bfloat16
F32 = jnp.float32
MESH = pl.DeviceIdType.MESH
LANE = 128
NZ = 4
ROWS_CHUNK = 128
ZF_COLS = 1152


def nn(a, b):
    return jnp.dot(a, b, preferred_element_type=F32)


def tn(a, b):
    return lax.dot_general(a, b, (((0,), (0,)), ((), ())), preferred_element_type=F32)


def nt(a, b):
    return lax.dot_general(a, b, (((1,), (1,)), ((), ())), preferred_element_type=F32)


def inv_rms(v):
    return lax.rsqrt(jnp.mean(v * v, axis=-1, keepdims=True) + epsilon)


class Take:
    def __init__(self, limit):
        self.used, self.limit = 0, limit

    def __call__(self, count=1):
        base = self.used
        self.used += count
        assert self.used <= self.limit
        return base


N_SEND, N_RECV, N_LOCAL = 128, 192, 64

SCHEDULE = {
    "dhA": (("end", (2, 0)), ("mid", (0, 0)),),
    "dhD": (("mid", (0, 2)), ("mid", (0, 1)),),
    "nb0": (("end", (3, 0)),),
    "nb1": (("end", "pair"), ("mid", "pair"),),
    "nb2": (("end", (1, 1)),),
    "cb": (("end", (2, 1)),),
    "d1a": (("end", "pair sum"),),
    "tail": (("end", (2, 2)), ("mid", (3, 0)), ("mid", (2, 0)),),
    "d1b": (("mid", (2, 2)),),
    "gc0": (("end", (1, 0)), ("mid", (3, 1)),),
    "blk1": (("end", (3, 1)),),
    "blk2": (("end", (4, 0)), ("mid", "pair sum"), ("mid", (1, 0)), ("mid", (1, 1)), ("mid", (1, 2)),),
    "blk3": (("mid", (2, 1)), ("mid", (4, 0)),),
    "dt0": (("end", (4, 1)), ("end", (1, 2)),),
    "dt1": (("end", (3, 2)), ("end", (2, 3)), ("mid", (3, 2)), ("mid", (4, 1)),),
    "dt2": (("end", (4, 2)),),
    "dt3": (("mid", (2, 3)),),
    "sm": (("end", (1, 3)), ("end", (3, 3)), ("end", (4, 3)), ("mid", (4, 2)), ("mid", (3, 3)), ("mid", (1, 3)), ("mid", (4, 3)),),
}


def step_kernel(
    dims,
    tokens, gain_mix_hbm, w_in, taps_hbm, w_out, gain_ffn_hbm, w_gate, w_up, w_down, cot,
    block_out, d_tokens, g_ffn, g_conv, small_out,
    gb0, gb1, gb2, gb3, gb4, yb0, yb1, yb2, yb3, yb4, zb0, zb1, zb2, zb3, zb4,
    cr_dh, cr_dn,
    gain_mix, taps, gain_ffn, tok_v, wg_v, wu_v, wd_v, dy_v, h2_v, h1_v, hid, dg, du, pb, pc, px, bx, gated, resid, gall,
    ring, xr_dh, xr_dn, xr_d1, rb, ld, outs, halo_s, halo_r, dhalo_s, dhalo_r, tail, pb_tail, px_tail,
    sm, sm_r, ss, rs, ls,
):
    R, T, D, CL, FL, FW = dims
    S = R // T
    CH = CL // 2
    GR = D // NZ
    SR = GR // 2
    DR = SR // 2
    NCH = R // ROWS_CHUNK
    take_s, take_r, take_l = Take(N_SEND), Take(N_RECV), Take(N_LOCAL)

    s = lax.axis_index("seq")
    x = lax.axis_index("chan")
    n_seq = 4 * NZ
    z, y, c = s // 4, (s // 2) % 2, s % 2

    def did(z_, y_, c_):
        return ((z_ * 2 + y_) * 2 + c_, x)

    core_dev = did(z, y, 1 - c)
    y_dev = did(z, 1 - y, c)
    x_dev = (s, 1 - x)
    mid = jnp.logical_and(z > 0, z < NZ - 1)
    end = jnp.logical_not(mid)

    def remote(src, dst, si, ri, dev):
        return pltpu.make_async_remote_copy(
            src_ref=src, dst_ref=dst, send_sem=ss.at[si], recv_sem=rs.at[ri],
            device_id=dev, device_id_type=MESH,
        )

    def wait_recv(dst, ri):
        remote(dst, dst, 0, ri, core_dev).wait_recv()

    def wait_send(src, si):
        remote(src, src, si, 0, core_dev).wait_send()

    def local(src, dst, li):
        return pltpu.make_async_copy(src, dst, ls.at[li])

    l_tok, l_win, l_wout, l_dy, l_small = take_l(), take_l(3), take_l(), take_l(), take_l(3)
    ld_tok = local(tokens, tok_v, l_tok)
    ld_tok.start()
    win_views = [wg_v.at[:, pl.ds(0, CL)], wg_v.at[:, pl.ds(CL, CL)], wu_v.at[:, pl.ds(0, CL)]]
    wout_view = wd_v.at[pl.ds(pl.multiple_of(x * CL, CL), CL), :]

    def load_w_in():
        return [local(w_in.at[m], win_views[m], l_win + m) for m in range(3)]

    for cp in load_w_in():
        cp.start()
    ld_small = [
        local(src, dst, l_small + i)
        for i, (src, dst) in enumerate(
            ((gain_mix_hbm, gain_mix), (taps_hbm, taps), (gain_ffn_hbm, gain_ffn))
        )
    ]
    for cp in ld_small:
        cp.start()
    ld_wout = local(w_out, wout_view, l_wout)
    ld_wout.start()
    ld_dy = local(cot, dy_v.at[0], l_dy)

    bar = pltpu.get_barrier_semaphore()

    def greet(dev):
        pl.semaphore_signal(bar, inc=1, device_id=dev, device_id_type=MESH)

    greet(core_dev)
    greet(x_dev)
    others = [(k, did((z + k // 2) % NZ, (y + k % 2) % 2, c)) for k in range(1, 2 * NZ)]
    for _, dev in others:
        greet(dev)
    has_prev = s > 0
    has_next = s < n_seq - 1
    prev_dev = ((s + n_seq - 1) % n_seq, x)
    next_dev = ((s + 1) % n_seq, x)
    greet(prev_dev)
    greet(next_dev)
    pl.semaphore_wait(bar, 3 + 2 * NZ)

    QR, SUBS = CL // 4, 4
    PR = QR // SUBS
    s_w, r_w = [take_s(SUBS) for _ in range(4)], [take_r(SUBS) for _ in range(4)]

    def w_rows(half, quarter, sub):
        return wd_v.at[pl.ds(pl.multiple_of(half * CL + quarter * QR + sub * PR, PR), PR), :]

    mine_q, pair_q = y * 2 + c, (1 - y) * 2 + c
    core_q, far_q = y * 2 + (1 - c), (1 - y) * 2 + (1 - c)

    def w_over_x(sub):
        src = w_out.at[pl.ds(pl.multiple_of(mine_q * QR + sub * PR, PR), PR), :]
        return remote(src, w_rows(x, mine_q, sub), s_w[0] + sub, r_w[0] + sub, x_dev)

    def w_over_y(sub):
        ref = w_rows(1 - x, mine_q, sub)
        return remote(ref, ref, s_w[1] + sub, r_w[1] + sub, y_dev)

    def w_over_core(sub):
        ref = w_rows(1 - x, mine_q, sub)
        return remote(ref, ref, s_w[2] + sub, r_w[2] + sub, core_dev)

    def w_far_over_core(sub):
        ref = w_rows(1 - x, pair_q, sub)
        return remote(ref, ref, s_w[3] + sub, r_w[3] + sub, core_dev)

    def w_pass_on(sub):
        wait_recv(w_rows(1 - x, mine_q, sub), r_w[0] + sub)
        w_over_y(sub).start()
        w_over_core(sub).start()

    def w_pass_far(sub):
        wait_recv(w_rows(1 - x, pair_q, sub), r_w[1] + sub)
        w_far_over_core(sub).start()

    for sub in range(SUBS):
        w_over_x(sub).start()

    l_w = take_l(3)
    win_start = pl.multiple_of(c * (FL - FW), LANE)
    ld_wg = local(w_gate.at[:, pl.ds(win_start, FW)], wg_v, l_w)
    ld_wu = local(w_up.at[:, pl.ds(win_start, FW)], wu_v, l_w + 1)
    ld_wd = local(w_down.at[pl.ds(win_start, FW), :], wd_v, l_w + 2)

    sm[...] = jnp.zeros_like(sm)
    for cp in ld_small:
        cp.wait()
    gain_mix_row = gain_mix[...].reshape(1, D)
    gain_ffn_row = gain_ffn[...].reshape(1, D)
    k_taps = [taps[t : t + 1, :] for t in range(3)]

    ld_tok.wait()

    CPS = T // ROWS_CHUNK
    NC = CL // 256
    s_h1, r_h1 = take_s(S), take_r(S)
    s_ha, r_ha = take_s(S), take_r(S)
    s_mx, r_mx = take_s(NCH), take_r(NCH)
    row_iota = lax.broadcasted_iota(jnp.int32, (T, 256), 0)
    top_iota = row_iota[0:16]

    def conv_terms(now, h, iota):
        h14 = jnp.broadcast_to(h[14:15], now.shape)
        h15 = jnp.broadcast_to(h[15:16], now.shape)
        one = jnp.where(iota == 0, h15, pltpu.roll(now, 1, 0))
        two = jnp.where(iota == 0, h14, jnp.where(iota == 1, h15, pltpu.roll(now, 2, 0)))
        return now, one, two

    def tap_cols(cols):
        return [taps[t : t + 1, cols] for t in range(3)]

    def convolve(terms, cols):
        now, one, two = terms
        k0, k1, k2 = tap_cols(cols)
        return k0 * two + k1 * one + k2 * now

    def h1_send(q):
        rows = pl.ds(q * T, T)
        return remote(h1_v.at[0, rows], h1_v.at[1, rows], s_h1 + q, r_h1 + q, core_dev)

    def halo_send(q):
        return remote(halo_s.at[q], halo_r.at[q], s_ha + q, r_ha + q, next_dev)

    own_cols = pl.ds(pl.multiple_of(x * CL, CL), CL)
    other_cols = pl.ds(pl.multiple_of((1 - x) * CL, CL), CL)

    def gated_send(k):
        ref = gall.at[k, :, own_cols]
        return remote(ref, ref, s_mx + k, r_mx + k, x_dev)

    def mixer_out(k):
        gall[k, :, own_cols] = gated[k * ROWS_CHUNK : (k + 1) * ROWS_CHUNK, :]
        gated_send(k).start()

    for q in range(S):
        rows = pl.ds(q * T, T)

        def norm_rows(k, _, q=q):
            chunk = pl.ds(pl.multiple_of(q * T + k * ROWS_CHUNK, ROWS_CHUNK), ROWS_CHUNK)
            xv = tok_v[chunk, :].astype(F32)
            h1_v[0, chunk, :] = (xv * inv_rms(xv) * gain_mix_row).astype(BF)
            return 0

        lax.fori_loop(0, CPS, norm_rows, 0)
        if q > 0:
            w_pass_on(1)
        if q == 0:
            for cp in load_w_in():
                cp.wait()

        def in_proj(j, _, q=q, rows=rows):
            cols = pl.ds(pl.multiple_of(j * 256, 256), 256)
            cols1 = pl.ds(pl.multiple_of(CL + j * 256, 256), 256)
            h = h1_v[0, rows, :]
            b = nn(h, wg_v[:, cols])
            pb[rows, cols] = b.astype(BF)
            xx = nn(h, wu_v[:, cols])
            px[rows, cols] = xx.astype(BF)
            inner = (b * xx).astype(BF)
            bx[rows, cols] = inner
            halo_s[q, :, cols] = inner[T - 16 : T]
            pcv = nn(h, wg_v[:, cols1])
            pc[rows, cols] = pcv.astype(BF)
            now = inner.astype(F32)
            cv = convolve(conv_terms(now, jnp.zeros_like(now[0:16]), row_iota), cols)
            gated[rows, cols] = (pcv * cv).astype(BF)
            return 0

        lax.fori_loop(0, NC, in_proj, 0, unroll=True)
        if q == S - 1:
            ld_wg.start()
            ld_wu.start()

        @pl.when(has_next)
        def _(q=q):
            halo_send(q).start()

        for k in range(CPS - 1, 0, -1):
            mixer_out(q * CPS + k)
        if q == 0:
            w_pass_on(0)
        else:
            w_pass_on(2)
            w_pass_far(0)

        @pl.when(has_prev)
        def _(q=q):
            wait_recv(halo_r.at[q], r_ha + q)

        @pl.when(jnp.logical_not(has_prev))
        def _(q=q):
            halo_r[q] = jnp.zeros_like(halo_r[q])

        def conv_top(j, _, q=q):
            cols = pl.ds(pl.multiple_of(j * 256, 256), 256)
            top = pl.ds(q * T, 16)
            now = bx[top, cols].astype(F32)
            cv = convolve(conv_terms(now, halo_r[q, :, cols].astype(F32), top_iota), cols)
            gated[top, cols] = (pc[top, cols].astype(F32) * cv).astype(BF)
            return 0

        lax.fori_loop(0, NC, conv_top, 0)
        mixer_out(q * CPS)
        h1_send(q).start()
        if q == 0:
            ld_dy.start()
            s_dy, r_dy = take_s(), take_r()
            send_dy = remote(cot, dy_v.at[1], s_dy, r_dy, core_dev)
            send_dy.start()
    w_pass_on(3)
    w_pass_far(1)

    s_h2, r_h2 = take_s(NCH), take_r(NCH)
    ld_wg.wait()
    ld_wu.wait()
    NF = FW // 256
    overlap = 2 * FW - FL
    col_iota = lax.broadcasted_iota(jnp.int32, (2 * ROWS_CHUNK, 256), 1)

    def sent(n):
        return (n // CPS) * CPS + (CPS - 1 - n % CPS)

    def residual_chunk(k):
        rows = pl.ds(pl.multiple_of(k * ROWS_CHUNK, ROWS_CHUNK), ROWS_CHUNK)
        wait_recv(gall.at[k, :, other_cols], r_mx + k)

        def out_tile(j, _):
            cols = pl.ds(pl.multiple_of(j * 512, 512), 512)
            resid[rows, cols] = tok_v[rows, cols].astype(F32) + nn(gall[k], wd_v[0 : 2 * CL, cols])
            return 0

        lax.fori_loop(0, D // 512, out_tile, 0, unroll=True)
        res = resid[rows, :]
        h2_v[0, rows, :] = (res * inv_rms(res) * gain_ffn_row).astype(BF)
        remote(h2_v.at[0, rows], h2_v.at[1, rows], s_h2 + k, r_h2 + k, core_dev).start()

    def forward_chunk(k):
        rows = pl.ds(pl.multiple_of(k * ROWS_CHUNK, ROWS_CHUNK), ROWS_CHUNK)
        wait_recv(h2_v.at[1, rows], r_h2 + k)

        def tile(j, _):
            cols = pl.ds(pl.multiple_of(j * 256, 256), 256)
            h = h2_v[:, rows, :].reshape(2 * ROWS_CHUNK, D)
            g = nn(h, wg_v[:, cols])
            u = nn(h, wu_v[:, cols])
            keep = col_iota + j * 256 >= c * overlap
            sg = jax.nn.sigmoid(g)
            si = jnp.where(keep, g * sg, 0.0)
            shape = (2, ROWS_CHUNK, 256)
            hid[:, rows, cols] = (si * u).astype(BF).reshape(shape)
            slope = jnp.where(keep, u * sg * (1.0 + g * (1.0 - sg)), 0.0)
            dg[:, rows, cols] = slope.astype(BF).reshape(shape)
            du[:, rows, cols] = si.astype(BF).reshape(shape)
            return 0

        lax.fori_loop(0, NF, tile, 0, unroll=True)

    w_pass_far(2)
    w_pass_far(3)
    ld_wout.wait()
    for sub in range(SUBS):
        wait_recv(w_rows(1 - x, core_q, sub), r_w[2] + sub)
        wait_recv(w_rows(1 - x, far_q, sub), r_w[3] + sub)
    residual_chunk(sent(0))

    def chunk_loop(n, _):
        @pl.when(n + 1 < NCH)
        def _():
            residual_chunk(sent(n + 1))

        forward_chunk(sent(n))
        return 0

    lax.fori_loop(0, NCH, chunk_loop, 0)
    for sub in range(SUBS):
        w_over_x(sub).wait_send()
        for send in (w_over_y, w_over_core, w_far_over_core):
            send(sub).wait_send()
    ld_wd.start()
    ld_dy.wait()
    send_dy.wait()
    for k in range(NCH):
        gated_send(k).wait_send()
        wait_send(h2_v.at[0, pl.ds(k * ROWS_CHUNK, ROWS_CHUNK)], s_h2 + k)

    gbs = [gb0, gb1, gb2, gb3, gb4]
    ybs = [yb0, yb1, yb2, yb3, yb4]
    zbs = [zb0, zb1, zb2, zb3, zb4]
    widths = [ZF_COLS, FW - ZF_COLS, FW, FW, 2 * CL]
    s_y = [None] + [take_s(NZ) for _ in range(4)]
    r_y = [None] + [take_r(NZ) for _ in range(4)]
    s_z = [take_s(2 * NZ)] + [take_s(NZ) for _ in range(4)]
    r_z = [take_r(4 * NZ)] + [take_r(2 * NZ) for _ in range(4)]

    def order(e):
        if e == NZ - 1:
            return z
        per_z = {0: (3, 2, 1), 1: (3, 0, 2), 2: (0, 3, 1), 3: (0, 1, 2)}
        v = per_z[3][e]
        for zz in range(3):
            v = jnp.where(z == zz, per_z[zz][e], v)
        return v

    def order_dyn(u):
        v = order(NZ - 1)
        for e in range(NZ - 1):
            v = jnp.where(u == e, order(e), v)
        return v

    def per_core(j, act):
        if j in (1, 4):
            act(lambda ref: ref)
            return

        @pl.when(c == 0)
        def _():
            act(lambda ref: ref)

        @pl.when(c == 1)
        def _():
            act(lambda ref: ref.at[:, pl.ds(overlap, widths[j] - overlap)])

    def z_send(j, src, e, zp, h=None):
        to_right = zp > z
        d = jnp.where(to_right, 0, 1)
        dev = did(jnp.clip(jnp.where(to_right, z + 1, z - 1), 0, NZ - 1), y, c)
        if h is None:
            dst, si, ri = zbs[j].at[d, zp], s_z[j] + e, r_z[j] + d * NZ + zp
        else:
            dst, si, ri = zbs[j].at[d, zp, h], s_z[j] + 2 * e + h, r_z[j] + (d * NZ + zp) * 2 + h
        per_core(j, lambda cut: remote(cut(src), cut(dst), si, ri, dev).start())

    l_g = take_l(12)

    def y_send(j, u):
        zp = order_dyn(u) if not isinstance(u, int) else order(u)
        src, dst = gbs[j].at[zp, 1 - y], ybs[j].at[zp]
        per_core(j, lambda cut: remote(cut(src), cut(dst), s_y[j] + u, r_y[j] + u, y_dev).start())

    def g_block(lhs_ref, rhs_ref, zp, pair, parts=(0, 1)):
        lhs = lhs_ref[:, :, pl.ds(pl.multiple_of(zp * GR, GR), GR)].reshape(2 * R, GR)
        cut = -(-FW // 512) * 256
        for n in parts:
            cols = slice(0, cut) if n == 0 else slice(cut, FW)
            v = tn(lhs, rhs_ref[:, :, cols].reshape(2 * R, cols.stop - cols.start)).astype(BF)
            outs[2 * pair, :, cols] = v[:SR]
            outs[2 * pair + 1, :, cols] = v[SR:]

    def down_copies(zp, pair):
        return [
            cp
            for h in range(2)
            for cp in (
                local(outs.at[2 * pair + h, :, pl.ds(0, ZF_COLS)], gb0.at[zp, h], l_g + 4 * pair + 2 * h),
                local(
                    outs.at[2 * pair + h, :, pl.ds(ZF_COLS, FW - ZF_COLS)],
                    gb1.at[zp, h], l_g + 4 * pair + 2 * h + 1,
                ),
            )
        ]

    def down_sends(u):
        zp = order(u)
        for cp in down_copies(zp, u % 2):
            cp.wait()
        if u < NZ - 1:

            @pl.when(end)
            def _():
                for h in range(2):
                    z_send(0, gb0.at[zp, h], u, zp, h)

            y_send(1, u)

    for u in range(NZ):
        g_block(dy_v, hid, order(u), u % 2, (0,))
        if u > 0:
            down_sends(u - 1)
        g_block(dy_v, hid, order(u), u % 2, (1,))
        for cp in down_copies(order(u), u % 2):
            cp.start()
    down_sends(NZ - 1)

    ld_wd.wait()

    def hid_back(slot, _):
        for j in range(NF):
            cols = slice(j * 256, (j + 1) * 256)
            dh = nt(dy_v[slot], wd_v[cols, :])
            dg[slot, :, cols] = (dh * dg[slot, :, cols].astype(F32)).astype(BF)
            du[slot, :, cols] = (dh * du[slot, :, cols].astype(F32)).astype(BF)
        return 0

    lax.fori_loop(0, 2, hid_back, 0)

    def plain_copies(gb, zp, pair):
        return [local(outs.at[2 * pair + h], gb.at[zp, h], l_g + 2 * pair + h) for h in range(2)]

    def gate_up(u, _):
        zp = order_dyn(u)

        def up_sends(u):
            for cp in plain_copies(gb3, order_dyn(u), 1):
                cp.wait()

            @pl.when(u < 2)
            def _():
                y_send(3, u)

        g_block(h2_v, dg, zp, 0, (0,))

        @pl.when(u > 0)
        def _():
            up_sends(u - 1)

        g_block(h2_v, dg, zp, 0, (1,))
        for cp in plain_copies(gb2, zp, 0):
            cp.start()
        g_block(h2_v, du, zp, 1, (0,))
        for cp in plain_copies(gb2, zp, 0):
            cp.wait()

        @pl.when(u < 2)
        def _():
            y_send(2, u)

        g_block(h2_v, du, zp, 1, (1,))
        for cp in plain_copies(gb3, zp, 1):
            cp.start()
        return 0

    lax.fori_loop(0, NZ, gate_up, 0)
    for cp in plain_copies(gb3, order(NZ - 1), 1):
        cp.wait()

    l_e = take_l(4)
    is_role = {"end": end, "mid": mid}
    slot_last = {role: [None] * outs.shape[0] for role in is_role}
    slot_next = {role: 0 for role in is_role}

    def claim_slot(role):
        o = slot_next[role]
        slot_next[role] = (o + 1) % outs.shape[0]
        if slot_last[role][o] is not None:
            slot_last[role][o]()
            slot_last[role][o] = None
        return o

    ADD_ROWS = 32

    def add_into(dst, srcs):
        def rows_add(k, _):
            rows = pl.ds(pl.multiple_of(k * ADD_ROWS, ADD_ROWS), ADD_ROWS)
            acc = srcs[0][rows, :].astype(F32)
            for src in srcs[1:]:
                acc = acc + src[rows, :].astype(F32)
            dst[rows, :] = acc.astype(BF)
            return 0

        lax.fori_loop(0, SR // ADD_ROWS, rows_add, 0)

    def fetch(j, srcs):
        w = widths[j]
        views, copies = [], []
        for i, (src, ri) in enumerate(srcs):
            if ri is not None:
                per_core(j, lambda cut: wait_recv(cut(src), ri))
            views.append(ld.at[i, :, pl.ds(0, w)])
            copies.append(local(src, views[-1], l_e + i))
            copies[-1].start()
        for cp in copies:
            cp.wait()
        return views

    def from_line(j, d, zp, h=None):
        if h is None:
            return zbs[j].at[d, zp], r_z[j] + d * NZ + zp
        return zbs[j].at[d, zp, h], r_z[j] + (d * NZ + zp) * 2 + h

    def line_event(role, j, e):
        @pl.when(is_role[role])
        def _():
            zp = order(e)
            w = widths[j]
            d = jnp.where(zp > z, 0, 1)
            for h in (0, 1) if j == 0 else (None,):
                o = claim_slot(role)
                dst = outs.at[o, :, pl.ds(0, w)]
                if h is None:
                    srcs = [(gbs[j].at[zp, y], None), (ybs[j].at[zp], r_y[j] + e)]
                    si = s_z[j] + e
                else:
                    srcs = [(gbs[j].at[zp, h], None)]
                    si = s_z[j] + 2 * e + h
                if role == "mid":
                    srcs.append(from_line(j, d, zp, h))
                add_into(dst, fetch(j, srcs))
                z_send(j, dst, e, zp, h)
                slot_last[role][o] = functools.partial(sent_slot, j, o, si)

    def sent_slot(j, o, si):
        per_core(j, lambda cut: wait_send(cut(outs.at[o, :, pl.ds(0, widths[j])]), si))

    def own_shard(role, j, h=None):
        if h is None:
            srcs = [(gbs[j].at[z, y], None), (ybs[j].at[z], r_y[j] + NZ - 1)]
        else:
            srcs = [(gbs[j].at[z, h], None)]
        if role == "mid":
            return srcs + [from_line(j, 0, z, h), from_line(j, 1, z, h)]
        return srcs + [from_line(j, jnp.where(z == 0, 1, 0), z, h)]

    def swap_pieces(j):
        if j == 4:
            return [(None, m * CH, CH, g_conv.at[m], c * CH) for m in range(4)]
        mat = g_ffn.at[{0: 0, 1: 0, 2: 1, 3: 2}[j]]
        w = widths[j]
        if j == 1:
            return [(None, 0, w, mat, c * (FL - FW) + ZF_COLS)]
        return [(0, 0, w, mat, 0), (1, overlap, w - overlap, mat, FL - FW + overlap)]

    swap_sems = [[(take_s(), take_r(), take_l()) for _ in swap_pieces(j)] for j in range(5)]

    def swap(j, o):
        items = []
        for (core, c0, w, mat, to), (si, ri, li) in zip(swap_pieces(j), swap_sems[j]):
            to = to if isinstance(to, int) else pl.multiple_of(to, LANE)
            target = mat.at[:, pl.ds(to, w)]
            mine = outs.at[o, pl.ds(pl.multiple_of(c * DR, DR), DR), pl.ds(c0, w)]
            other = outs.at[o, pl.ds(pl.multiple_of((1 - c) * DR, DR), DR), pl.ds(c0, w)]
            items.append((core, local(mine, target, li), remote(other, target, si, ri, core_dev), target))
        return items

    def swap_start(j, o):
        for core, keep, give, _ in swap(j, o):
            if core is None:
                keep.start()
                give.start()
            else:

                @pl.when(c == core)
                def _():
                    keep.start()
                    give.start()

    def swap_finish(j, o):
        for (core, keep, give, target), (_, ri, _) in zip(swap(j, o), swap_sems[j]):
            if core is None:
                keep.wait()
                give.wait_send()
                wait_recv(target, ri)
            else:

                @pl.when(c == core)
                def _():
                    keep.wait()
                    give.wait_send()

                @pl.when(c != core)
                def _():
                    wait_recv(target, ri)

    def final_event(role, j):
        @pl.when(is_role[role])
        def _():
            o = claim_slot(role)
            w = widths[j]
            add_into(outs.at[o, :, pl.ds(0, w)], fetch(j, own_shard(role, j)))
            swap_start(j, o)
            slot_last[role][o] = functools.partial(swap_finish, j, o)

    s_f0, r_f0 = take_s(), take_r()
    w0 = widths[0]

    def final0_send(role):
        @pl.when(is_role[role])
        def _():
            o = claim_slot(role)
            dst = outs.at[o, :, pl.ds(0, w0)]
            add_into(dst, fetch(0, own_shard(role, 0, 1 - y)))
            cp = local(dst, gb0.at[z, 1 - y], l_e)
            cp.start()
            cp.wait()
            src = gb0.at[z, 1 - y]
            per_core(0, lambda cut: remote(cut(src), cut(yb0), s_f0, r_f0, y_dev).start())

    def final0_finish(role):
        @pl.when(is_role[role])
        def _():
            o = claim_slot(role)
            dst = outs.at[o, :, pl.ds(0, w0)]
            add_into(dst, fetch(0, own_shard(role, 0, y)))
            add_into(dst, [dst] + fetch(0, [(yb0, r_f0)]))
            swap_start(0, o)
            slot_last[role][o] = functools.partial(swap_finish, 0, o)

    def hook(name):
        for role, event in SCHEDULE.get(name, ()):
            if event == "pair":
                final0_send(role)
            elif event == "pair sum":
                final0_finish(role)
            elif event[1] == NZ - 1:
                final_event(role, event[0])
            else:
                line_event(role, *event)

    def chunks(name, count, body):
        first = 0
        for k in range(count):
            if SCHEDULE.get(name + str(k)) or k == count - 1:
                lax.fori_loop(first, k + 1, body, 0)
                first = k + 1
                hook(name + str(k))

    HALF = 2 * ROWS_CHUNK

    def split_sum(name, product, cr, xr, base_d):
        s_c, r_c = take_s(2), take_r(2)
        s_x, r_x = take_s(NCH), take_r(NCH)
        l_c = take_l()

        def give(k, _):
            def tile(n, _):
                cols = pl.ds(pl.multiple_of(n * 512, 512), 512)
                v = product(1, k * HALF, n).astype(BF)
                gall[pl.ds(2 * k, 2), :, cols] = v.reshape(2, ROWS_CHUNK, 512)
                return 0

            lax.fori_loop(0, D // 512, tile, 0, unroll=True)
            remote(
                gall.at[pl.ds(2 * k, 2)], cr.at[pl.ds(2 * k, 2)], s_c + k, r_c + k, core_dev
            ).start()
            return 0

        lax.fori_loop(0, 2, give, 0)
        hook(name + "A")

        def keep(k, _):
            src = cr.at[pl.ds(2 * k, 2)]
            wait_recv(src, r_c + k)
            cp = local(src, rb, l_c)
            cp.start()
            cp.wait()

            def tile(n, _):
                cols = pl.ds(pl.multiple_of(n * 512, 512), 512)
                v = product(0, k * HALF, n) + rb[:, :, cols].reshape(HALF, 512).astype(F32)
                ring[pl.ds(base_d + 2 * k, 2), :, cols] = v.astype(BF).reshape(2, ROWS_CHUNK, 512)
                return 0

            lax.fori_loop(0, D // 512, tile, 0, unroll=True)
            for i in range(2):
                remote(
                    ring.at[base_d + 2 * k + i], xr.at[2 * k + i], s_x + 2 * k + i, r_x + 2 * k + i, x_dev
                ).start()
            return 0

        lax.fori_loop(0, 2, keep, 0)
        for k in range(2):
            wait_send(gall.at[pl.ds(2 * k, 2)], s_c + k)
        hook(name + "D")
        return s_x, r_x

    def rows_at(ref, slot, r0):
        return ref[slot, pl.ds(pl.multiple_of(r0, HALF), HALF), :]

    def dh_product(slot, r0, n):
        cols = pl.ds(pl.multiple_of(n * 512, 512), 512)
        return nt(rows_at(dg, slot, r0), wg_v[cols, :]) + nt(rows_at(du, slot, r0), wu_v[cols, :])

    def dn_product(slot, r0, n):
        cols = pl.ds(pl.multiple_of(n * 512, 512), 512)
        return nn(rows_at(hid, slot, r0), wd_v[:, cols])

    s_xdh, r_xdh = split_sum("dh", dh_product, cr_dh, xr_dh, 0)
    s_xdn, r_xdn = split_sum("dn", dn_product, cr_dn, xr_dn, 4)
    for cp in load_w_in():
        cp.start()
    ld_wout = local(w_out, wd_v.at[pl.ds(0, CL), :], l_wout)
    ld_wout.start()

    s_do, r_do = take_s(NCH), take_r(NCH)

    def ffn_norm_back(k, _):
        rows = pl.ds(pl.multiple_of(k * ROWS_CHUNK, ROWS_CHUNK), ROWS_CHUNK)
        wait_recv(xr_dh.at[k], r_xdh + k)
        d_h = ring[k].astype(F32) + xr_dh[k].astype(F32)
        res = resid[rows, :]
        s2 = inv_rms(res)
        n2 = res * s2
        sm[0, 1:2, :] += jnp.sum(d_h * n2, axis=0, keepdims=True)
        e2 = d_h * gain_ffn_row
        d_res = dy_v[0, rows, :].astype(F32) + s2 * (
            e2 - n2 * jnp.mean(e2 * n2, axis=-1, keepdims=True)
        )
        h2_v[0, rows, :] = d_res.astype(BF)
        remote(h2_v.at[0, rows], h2_v.at[1, rows], s_do + k, r_do + k, core_dev).start()
        return 0

    chunks("nb", NCH, ffn_norm_back)
    for k in range(NCH):
        wait_send(ring.at[k], s_xdh + k)

    for cp in load_w_in():
        cp.wait()
    ld_wout.wait()
    for q in range(S):

        def conv_back(j, _, q=q):
            cols = pl.ds(pl.multiple_of(j * 256, 256), 256)
            rows = pl.ds(q * T, T)
            now, one, two = conv_terms(
                bx[rows, cols].astype(F32), halo_r[q, :, cols].astype(F32), row_iota
            )
            k0, k1, k2 = tap_cols(cols)
            cv = k0 * two + k1 * one + k2 * now
            d_g = nt(h2_v[0, q * T : q * T + T, :], wd_v[cols, :])
            d_cv = d_g * pc[rows, cols].astype(F32)
            sm[0, 2:3, cols] += jnp.sum(d_cv * two, axis=0, keepdims=True)
            sm[0, 3:4, cols] += jnp.sum(d_cv * one, axis=0, keepdims=True)
            sm[0, 4:5, cols] += jnp.sum(d_cv * now, axis=0, keepdims=True)
            after1 = jnp.where(row_iota < T - 1, pltpu.roll(d_cv, T - 1, 0), 0.0)
            after2 = jnp.where(row_iota < T - 2, pltpu.roll(d_cv, T - 2, 0), 0.0)
            d_bx = k2 * d_cv + k1 * after1 + k0 * after2
            dhalo_s[q, :, cols] = d_cv[0:8]
            tail[q, :, cols] = d_bx[T - 16 : T]
            old_b = pb[rows, cols]
            old_x = px[rows, cols]
            pb_tail[q, :, cols] = old_b[T - 16 : T]
            px_tail[q, :, cols] = old_x[T - 16 : T]
            low = d_bx.astype(BF).astype(F32)
            pb[rows, cols] = (low * old_x.astype(F32)).astype(BF)
            px[rows, cols] = (low * old_b.astype(F32)).astype(BF)
            pc[rows, cols] = (d_g * cv).astype(BF)
            return 0

        lax.fori_loop(0, NC, conv_back, 0, unroll=True)

    s_dha, r_dha = take_s(), take_r()
    send_dhalo = remote(dhalo_s, dhalo_r, s_dha, r_dha, prev_dev)

    @pl.when(has_prev)
    def _():
        send_dhalo.start()

    for j, u in ((2, 2), (3, 2)):
        y_send(j, u)

    hook("cb")

    s_x1, r_x1 = take_s(NCH), take_r(NCH)

    def d1_part(name, ids):
        def tile(n, _):
            cols = pl.ds(pl.multiple_of(n * 512, 512), 512)

            def rows_of(ref):
                return jnp.concatenate(
                    [ref[k * ROWS_CHUNK : (k + 1) * ROWS_CHUNK, :] for k in ids], axis=0
                )

            v = (
                nt(rows_of(pb), wg_v[cols, 0:CL])
                + nt(rows_of(pc), wg_v[cols, CL : 2 * CL])
                + nt(rows_of(px), wu_v[cols, 0:CL])
            ).astype(BF)
            for i, k in enumerate(ids):
                ring[k, :, cols] = v[i * ROWS_CHUNK : (i + 1) * ROWS_CHUNK]
            return 0

        lax.fori_loop(0, D // 512, tile, 0, unroll=True)
        for k in ids:
            remote(ring.at[k], xr_d1.at[k], s_x1 + k, r_x1 + k, x_dev).start()
        hook(name)

    d1_part("d1a", [q * CPS + k for q in range(S) for k in range(CPS - 1)])

    @pl.when(has_next)
    def _():
        wait_recv(dhalo_r, r_dha)

    @pl.when(jnp.logical_not(has_next))
    def _():
        dhalo_r[...] = jnp.zeros_like(dhalo_r)

    tail_iota = lax.broadcasted_iota(jnp.int32, (16, CL), 0)
    for q in range(S):
        first = jnp.broadcast_to(dhalo_r[q, 0:1, :], (16, CL))
        second = jnp.broadcast_to(dhalo_r[q, 1:2, :], (16, CL))
        fix = jnp.where(
            tail_iota == 14,
            k_taps[0] * first,
            jnp.where(tail_iota == 15, k_taps[1] * first + k_taps[0] * second, 0.0),
        )
        low = (tail[q] + fix).astype(BF).astype(F32)
        rows = pl.ds(q * T + T - 16, 16)
        pb[rows, :] = (low * px_tail[q].astype(F32)).astype(BF)
        px[rows, :] = (low * pb_tail[q].astype(F32)).astype(BF)

    s_dp, r_dp = take_s(4), take_r(4)
    theirs = pl.ds(pl.multiple_of((1 - c) * CH, LANE), CH)
    ours = pl.ds(pl.multiple_of(c * CH, LANE), CH)
    dp_sends = [
        remote(ref.at[:, theirs], dy_v.at[1, :, pl.ds(m * CH, CH)], s_dp + m, r_dp + m, core_dev)
        for m, ref in enumerate((pb, pc, px, gated))
    ]
    for cp in dp_sends:
        cp.start()
    hook("tail")

    d1_part("d1b", [q * CPS + k for q in range(S) for k in range(1, CPS)])

    for q in range(S):
        wait_recv(h1_v.at[1, pl.ds(q * T, T)], r_h1 + q)
    for k in range(NCH):
        rows = pl.ds(k * ROWS_CHUNK, ROWS_CHUNK)
        wait_recv(h2_v.at[1, rows], r_do + k)
    for m in range(4):
        wait_recv(dy_v.at[1, :, pl.ds(m * CH, CH)], r_dp + m)
    W4 = widths[4]
    g4 = [dg.at[i, pl.ds(k * SR, SR), pl.ds(0, W4)] for i in range(2) for k in range(2)]

    def g_mixer(u, _):
        zp = order_dyn(u)
        zc = pl.ds(pl.multiple_of(zp * GR, GR), GR)
        for m, (mine, lhs) in enumerate(((pb, h1_v), (pc, h1_v), (px, h1_v), (gated, h2_v))):
            v = tn(lhs[0, :, zc], mine[:, ours]) + tn(
                lhs[1, :, zc], dy_v[1, :, m * CH : (m + 1) * CH]
            )
            v = v.astype(BF)
            g4[0][:, m * CH : (m + 1) * CH] = v[:SR]
            g4[1][:, m * CH : (m + 1) * CH] = v[SR:]
        cps = [local(g4[h], gb4.at[zp, h], l_g + h) for h in range(2)]
        for cp in cps:
            cp.start()
        for cp in cps:
            cp.wait()

        @pl.when(u < NZ - 1)
        def _():
            y_send(4, u)

        return 0

    chunks("gc", NZ, g_mixer)
    for j in (1, 2, 3, 4):
        y_send(j, NZ - 1)

    l_o = take_l(2)

    def put_rows(v, out, rows, n):
        slot = n % 2
        cp = local(rb.at[slot], out.at[rows, :], l_o + slot)

        @pl.when(n >= 2)
        def _():
            cp.wait()

        rb[slot] = v
        cp.start()

    def put_done(out):
        for slot in range(2):
            local(rb.at[slot], out.at[pl.ds(0, ROWS_CHUNK), :], l_o + slot).wait()

    def block_chunk(k, _):
        rows = pl.ds(pl.multiple_of(k * ROWS_CHUNK, ROWS_CHUNK), ROWS_CHUNK)
        wait_recv(xr_dn.at[k], r_xdn + k)
        total = ring[4 + k].astype(F32) + xr_dn[k].astype(F32)
        put_rows((resid[rows, :] + total).astype(BF), block_out, rows, k)
        return 0

    chunks("blk", NCH, block_chunk)
    put_done(block_out)

    def mix_norm_back(n, _):
        k = (n % S) * CPS + n // S
        rows = pl.ds(pl.multiple_of(k * ROWS_CHUNK, ROWS_CHUNK), ROWS_CHUNK)
        wait_recv(xr_d1.at[k], r_x1 + k)
        d_h = ring[k].astype(F32) + xr_d1[k].astype(F32)
        xv = tok_v[rows, :].astype(F32)
        s1 = inv_rms(xv)
        n1 = xv * s1
        sm[0, 0:1, :] += jnp.sum(d_h * n1, axis=0, keepdims=True)
        e1 = d_h * gain_mix_row
        out = h2_v[0, rows, :].astype(F32) + s1 * (
            e1 - n1 * jnp.mean(e1 * n1, axis=-1, keepdims=True)
        )
        put_rows(out.astype(BF), d_tokens, rows, n)
        return 0

    chunks("dt", NCH, mix_norm_back)
    put_done(d_tokens)

    s_sm, r_sm = take_s(2 * NZ), take_r(2 * NZ)
    a = remote(sm.at[0], sm_r.at[0], s_sm, r_sm, core_dev)
    a.start()
    a.wait()
    sm[1] = sm[0] + sm_r[0]
    for k, dev in others:
        remote(sm.at[1], sm_r.at[k], s_sm + k, r_sm + k, dev).start()
    hook("sm")

    total = sm[1]
    for k, _ in others:
        wait_recv(sm_r.at[k], r_sm + k)
        total = total + sm_r[k]
    for k, _ in others:
        wait_send(sm.at[1], s_sm + k)
    sm[0] = total
    out_small = local(sm.at[0], small_out, l_small)
    out_small.start()
    out_small.wait()

    for role, cond in is_role.items():

        @pl.when(cond)
        def _(role=role):
            for finish in slot_last[role]:
                if finish is not None:
                    finish()

    @pl.when(end)
    def _():
        for e in range(NZ - 1):
            for h in range(2):
                per_core(0, lambda cut: wait_send(cut(gb0.at[0, h]), s_z[0] + 2 * e + h))

    for j in range(1, 5):
        for u in range(NZ):
            per_core(j, lambda cut: wait_send(cut(ybs[j].at[0]), s_y[j] + u))
    per_core(0, lambda cut: wait_send(cut(yb0), s_f0))
    for q in range(S):
        h1_send(q).wait_send()
    for k in range(NCH):
        wait_send(h2_v.at[0, pl.ds(k * ROWS_CHUNK, ROWS_CHUNK)], s_do + k)
        wait_send(ring.at[k], s_x1 + k)
        wait_send(ring.at[4 + k], s_xdn + k)
    for cp in dp_sends:
        cp.wait_send()

    @pl.when(has_next)
    def _():
        for q in range(S):
            halo_send(q).wait_send()

    @pl.when(has_prev)
    def _():
        send_dhalo.wait_send()


def fused_body(tokens, gain_mix, w_in, kernel, w_out, gain_ffn, w_gate, w_up, w_down, cotangent):
    S, T, D = tokens.shape
    CL = w_out.shape[0]
    FL = w_gate.shape[1]
    R = S * T
    n_seq = lax.axis_size("seq")
    tiles = FL // LANE
    FW = -(-tiles // 2) * LANE
    GR = D // NZ
    SR = GR // 2
    DR = SR // 2
    widths = [ZF_COLS, FW - ZF_COLS, FW, FW, 2 * CL]
    NCH = R // ROWS_CHUNK

    def sds(shape, dtype=BF):
        return jax.ShapeDtypeStruct(shape, dtype)

    outs = [sds((R, D)), sds((R, D)), sds((3, DR, FL)), sds((4, DR, CL)), sds((8, D), F32)]
    outs += [sds((NZ, 2, SR, w)) for w in widths]
    outs += [sds((SR, widths[0]))] + [sds((NZ, SR, w)) for w in widths[1:]]
    outs += [sds((2, NZ, 2, SR, widths[0]))] + [sds((2, NZ, SR, w)) for w in widths[1:]]
    outs += [sds((NCH, ROWS_CHUNK, D))] * 2
    any_spec = pl.BlockSpec(memory_space=pl.ANY)
    V = pltpu.VMEM
    scratch = [
        V((D,), F32),
        V((3, CL), F32),
        V((D,), F32),
        V((R, D), BF),
        V((D, FW), BF),
        V((D, FW), BF),
        V((FW, D), BF),
        V((2, R, D), BF),
        V((2, R, D), BF),
        V((2, R, D), BF),
        V((2, R, FW), BF),
        V((2, R, FW), BF),
        V((2, R, FW), BF),
        V((R, CL), BF),
        V((R, CL), BF),
        V((R, CL), BF),
        V((R, CL), BF),
        V((R, CL), BF),
        V((R, D), F32),
        V((NCH, ROWS_CHUNK, D), BF),
        V((8, ROWS_CHUNK, D), BF),
        V((NCH, ROWS_CHUNK, D), BF),
        V((NCH, ROWS_CHUNK, D), BF),
        V((NCH, ROWS_CHUNK, D), BF),
        V((2, ROWS_CHUNK, D), BF),
        V((4, SR, FW), BF),
        V((4, SR, FW), BF),
        V((S, 16, CL), BF),
        V((S, 16, CL), BF),
        V((S, 8, CL), F32),
        V((S, 8, CL), F32),
        V((S, 16, CL), F32),
        V((S, 16, CL), BF),
        V((S, 16, CL), BF),
        V((2, 8, D), F32),
        V((2 * NZ, 8, D), F32),
        pltpu.SemaphoreType.DMA((N_SEND,)),
        pltpu.SemaphoreType.DMA((N_RECV,)),
        pltpu.SemaphoreType.DMA((N_LOCAL,)),
    ]
    flops = 2 * R * D * (4 * CL + 3 * FL) * 3
    res = pl.pallas_call(
        functools.partial(step_kernel, (R, T, D, CL, FL, FW)),
        out_shape=outs,
        in_specs=[any_spec] * 10,
        out_specs=[any_spec] * len(outs),
        scratch_shapes=scratch,
        compiler_params=pltpu.CompilerParams(
            collective_id=0, has_side_effects=True, vmem_limit_bytes=63 << 20
        ),
        cost_estimate=pl.CostEstimate(flops=flops, bytes_accessed=200 << 20, transcendentals=0),
        name="block_step",
    )(
        tokens.reshape(R, D), gain_mix, w_in, kernel, w_out,
        gain_ffn, w_gate, w_up, w_down, cotangent.reshape(R, D),
    )
    block_out, d_tokens, g_mix, g_in, g_taps, g_out, g_gain, g_gate, g_up, g_down = finish(
        n_seq, *res[:5]
    )
    return (
        block_out.reshape(S, T, D),
        d_tokens.reshape(S, T, D),
        g_mix, g_in, g_taps, g_out.T, g_gain, g_gate, g_up, g_down.T,
    )


def finish_kernel(
    n_seq, block_in, d_in, ffn_in, conv_in, small_in,
    block_out, d_out, g_mix, g_in, g_taps, g_out, g_gain, g_gate, g_up, g_down,
    block_v, d_v, ffn, conv, small, gate_v, up_v, down_v, in_v, out_v, mix_v, taps_v, gain_v, sem,
):
    D = d_in.shape[1]
    CL = conv_in.shape[2]
    s = lax.axis_index("seq")
    count = [0]

    def copy(src, dst):
        count[0] += 1
        cp = pltpu.make_async_copy(src, dst, sem.at[count[0] - 1])
        cp.start()
        return cp

    loads = [copy(ffn_in.at[0], ffn.at[0]), copy(conv_in, conv), copy(small_in, small)]
    loads += [copy(ffn_in.at[m], ffn.at[m]) for m in (1, 2)]
    passing = [copy(block_in, block_v), copy(d_in, d_v)]
    stores = []
    loads[0].wait()
    down_v[...] = ffn[0].astype(F32)
    stores.append(copy(down_v, g_down))
    loads[1].wait()
    in_v[...] = conv[0:3].astype(F32)
    stores.append(copy(in_v, g_in))
    out_v[...] = conv[3].astype(F32)
    stores.append(copy(out_v, g_out))
    passing[0].wait()
    stores.append(copy(block_v, block_out))
    passing[1].wait()
    stores.append(copy(d_v, d_out))
    loads[3].wait()
    gate_v[...] = ffn[1].astype(F32)
    stores.append(copy(gate_v, g_gate))
    loads[4].wait()
    up_v[...] = ffn[2].astype(F32)
    stores.append(copy(up_v, g_up))
    loads[2].wait()
    per_d, per_c = D // n_seq, CL // n_seq
    mine = pltpu.roll(small[...], D - s * per_d, 1)
    mix_v[...] = mine[0, 0:per_d]
    gain_v[...] = mine[1, 0:per_d]
    mine = pltpu.roll(small[...], D - s * per_c, 1)
    for t in range(3):
        taps_v[t] = mine[2 + t : 3 + t, 0:per_c]
    stores += [copy(mix_v, g_mix), copy(gain_v, g_gain), copy(taps_v, g_taps)]
    for cp in stores:
        cp.wait()


def finish(n_seq, block_out, d_tokens, g_ffn, g_conv, small):
    R, D = block_out.shape
    _, DR, FL = g_ffn.shape
    CL = g_conv.shape[2]
    any_spec = pl.BlockSpec(memory_space=pl.ANY)
    V = pltpu.VMEM
    tails = [
        (DR, FL), (DR, FL), (DR, FL), (3, DR, CL), (DR, CL),
        (D // n_seq,), (3, 1, CL // n_seq), (D // n_seq,),
    ]
    gate, up, down, inp, out, mix, taps, gain = [jax.ShapeDtypeStruct(t, F32) for t in tails]
    low = jax.ShapeDtypeStruct((R, D), BF)
    return pl.pallas_call(
        functools.partial(finish_kernel, n_seq),
        out_shape=[low, low, mix, inp, taps, out, gain, gate, up, down],
        in_specs=[any_spec] * 5,
        out_specs=[any_spec] * 10,
        scratch_shapes=[V((R, D), BF), V((R, D), BF), V(g_ffn.shape, BF), V(g_conv.shape, BF), V(small.shape, F32)]
        + [V(t, F32) for t in tails]
        + [pltpu.SemaphoreType.DMA((20,))],
        compiler_params=pltpu.CompilerParams(vmem_limit_bytes=63 << 20),
        name="finish",
    )(block_out, d_tokens, g_ffn, g_conv, small)


def from_behind(value, axis, by):
    count = lax.axis_size(axis)
    pairs = [(i, i + by) for i in range(count) if 0 <= i + by < count]
    return lax.ppermute(value, axis, pairs)


def rms_scale(vector):
    return lax.rsqrt(jnp.mean(vector * vector, axis=-1, keepdims=True) + epsilon)


def norm_back(d_normout, normed, inv_scale, gain_vec):
    d_normed = d_normout * gain_vec
    return inv_scale * (d_normed - normed * jnp.mean(d_normed * normed, axis=-1, keepdims=True))


def matmul(lhs_mat, rhs_mat):
    return jnp.dot(lhs_mat, rhs_mat, preferred_element_type=jnp.float32)


def left_trans(lhs_mat, rhs_mat):
    return lax.dot_general(
        lhs_mat, rhs_mat, (((0,), (0,)), ((), ())), preferred_element_type=jnp.float32
    )


def right_trans(lhs_mat, rhs_mat):
    return lax.dot_general(
        lhs_mat, rhs_mat, (((1,), (1,)), ((), ())), preferred_element_type=jnp.float32
    )


def general_body(tokens, gain_mix, w_in, kernel, w_out, gain_ffn, w_gate, w_up, w_down, cotangent):
    seq_count, tok_rows, model_width = tokens.shape
    row_count = seq_count * tok_rows
    tokens_f = tokens.astype(jnp.float32).reshape(row_count, model_width)
    scale_mix = rms_scale(tokens_f)
    normed_mix = tokens_f * scale_mix
    h_mix = (normed_mix * gain_mix).astype(jnp.bfloat16)
    proj_b = matmul(h_mix, w_in[0])
    proj_c = matmul(h_mix, w_in[1])
    proj_x = matmul(h_mix, w_in[2])
    conv_in = (proj_b * proj_x).astype(jnp.bfloat16).reshape(seq_count, tok_rows, -1)
    before = from_behind(conv_in[:, tok_rows - 2 :, :], "seq", 1)
    extended = jnp.concatenate([before, conv_in], axis=1).astype(jnp.float32)
    conv_out = (
        kernel[0] * extended[:, :-2] + kernel[1] * extended[:, 1:-1] + kernel[2] * extended[:, 2:]
    )
    conv_flat = conv_out.reshape(row_count, -1)
    gated = (proj_c * conv_flat).astype(jnp.bfloat16)
    mixed_sum = lax.psum(matmul(gated, w_out).astype(jnp.bfloat16), "chan").astype(jnp.float32)
    residual = tokens_f + mixed_sum
    scale_ffn = rms_scale(residual)
    normed_ffn = residual * scale_ffn
    h_ffn = (normed_ffn * gain_ffn).astype(jnp.bfloat16)
    gate_pre = matmul(h_ffn, w_gate)
    up_value = matmul(h_ffn, w_up)
    sigmoid_gate = jax.nn.sigmoid(gate_pre)
    silu_gate = gate_pre * sigmoid_gate
    hidden = (silu_gate * up_value).astype(jnp.bfloat16)
    ffn_total = lax.psum(matmul(hidden, w_down).astype(jnp.bfloat16), "chan").astype(jnp.float32)
    block_out = (
        (residual + ffn_total).astype(jnp.bfloat16).reshape(seq_count, tok_rows, model_width)
    )
    grad_out = cotangent.reshape(row_count, model_width)
    g_w_down = left_trans(hidden, grad_out)
    d_hidden = right_trans(grad_out, w_down)
    d_gate = (d_hidden * up_value * sigmoid_gate * (1.0 + gate_pre * (1.0 - sigmoid_gate))).astype(
        jnp.bfloat16
    )
    d_up = (d_hidden * silu_gate).astype(jnp.bfloat16)
    g_w_gate = left_trans(h_ffn, d_gate)
    g_w_up = left_trans(h_ffn, d_up)
    d_h_ffn = lax.psum(
        (right_trans(d_gate, w_gate) + right_trans(d_up, w_up)).astype(jnp.bfloat16), "chan"
    ).astype(jnp.float32)
    g_gain_ffn = jnp.sum(d_h_ffn * normed_ffn, axis=0)
    d_resid = grad_out.astype(jnp.float32) + norm_back(d_h_ffn, normed_ffn, scale_ffn, gain_ffn)
    d_mixed = d_resid.astype(jnp.bfloat16)
    g_w_out = left_trans(gated, d_mixed)
    d_gated = right_trans(d_mixed, w_out)
    d_proj_c = (d_gated * conv_flat).astype(jnp.bfloat16)
    d_conv = (d_gated * proj_c).reshape(seq_count, tok_rows, -1)
    after_rows = from_behind(d_conv[:, :2, :], "seq", -1)
    ext_back = jnp.concatenate([d_conv, after_rows], axis=1)
    d_conv_in = (
        kernel[2] * ext_back[:, :-2] + kernel[1] * ext_back[:, 1:-1] + kernel[0] * ext_back[:, 2:]
    )
    g_kernel = jnp.stack(
        [
            jnp.sum(d_conv * extended[:, :-2], axis=(0, 1)),
            jnp.sum(d_conv * extended[:, 1:-1], axis=(0, 1)),
            jnp.sum(d_conv * extended[:, 2:], axis=(0, 1)),
        ]
    ).reshape(3, 1, -1)
    d_conv_low = d_conv_in.reshape(row_count, -1).astype(jnp.bfloat16)
    d_proj_b = (d_conv_low * proj_x).astype(jnp.bfloat16)
    d_proj_x = (d_conv_low * proj_b).astype(jnp.bfloat16)
    g_w_in = jnp.stack(
        [left_trans(h_mix, d_proj_b), left_trans(h_mix, d_proj_c), left_trans(h_mix, d_proj_x)]
    )
    d_h_mix = lax.psum(
        (
            right_trans(d_proj_b, w_in[0])
            + right_trans(d_proj_c, w_in[1])
            + right_trans(d_proj_x, w_in[2])
        ).astype(jnp.bfloat16),
        "chan",
    ).astype(jnp.float32)
    g_gain_mix = jnp.sum(d_h_mix * normed_mix, axis=0)
    d_tokens = (
        (d_resid + norm_back(d_h_mix, normed_mix, scale_mix, gain_mix))
        .astype(jnp.bfloat16)
        .reshape(seq_count, tok_rows, model_width)
    )
    summed = (
        lax.psum_scatter(g_w_in, "seq", scatter_dimension=1, tiled=True),
        lax.psum_scatter(g_w_out, "seq", scatter_dimension=1, tiled=True),
        lax.psum_scatter(g_kernel, "seq", scatter_dimension=2, tiled=True),
        lax.psum_scatter(g_gain_mix, "seq", scatter_dimension=0, tiled=True),
        lax.psum_scatter(g_w_gate, "seq", scatter_dimension=0, tiled=True),
        lax.psum_scatter(g_w_up, "seq", scatter_dimension=0, tiled=True),
        lax.psum_scatter(g_w_down, "seq", scatter_dimension=1, tiled=True),
        lax.psum_scatter(g_gain_ffn, "seq", scatter_dimension=0, tiled=True),
    )
    sum_in, sum_out, sum_kernel, sum_gain_mix, sum_gate, sum_up, sum_down, sum_gain_ffn = summed
    return (
        block_out,
        d_tokens,
        sum_gain_mix,
        sum_in,
        sum_kernel,
        sum_out,
        sum_gain_ffn,
        sum_gate,
        sum_up,
        sum_down,
    )


def solution(mesh):
    body = fused_body if mesh.shape["seq"] == 4 * NZ else general_body
    placed = (
        P(None, "seq", None),
        P(),
        P(None, None, "chan"),
        P(None, "chan"),
        P("chan", None),
        P(),
        P(None, "chan"),
        P(None, "chan"),
        P("chan", None),
        P(None, "seq", None),
    )
    return jax.shard_map(
        body,
        mesh=mesh,
        in_specs=placed,
        out_specs=(
            P(None, "seq", None),
            P(None, "seq", None),
            P("seq"),
            P(None, "seq", "chan"),
            P(None, "chan", "seq"),
            P("chan", "seq"),
            P("seq"),
            P("seq", "chan"),
            P("seq", "chan"),
            P("chan", "seq"),
        ),
        check_vma=False,
    )
```

```python
import functools

import jax
import jax.numpy as jnp
from jax import lax
from jax.experimental import pallas as pl
from jax.experimental.pallas import tpu as pltpu
from jax.sharding import PartitionSpec as P

epsilon = 1e-05
BF = jnp.bfloat16
F32 = jnp.float32
MESH = pl.DeviceIdType.MESH
LANE = 128
NZ = 4
ROWS_CHUNK = 128
ZF_COLS = 1152


def nn(a, b):
    return jnp.dot(a, b, preferred_element_type=F32)


def tn(a, b):
    return lax.dot_general(a, b, (((0,), (0,)), ((), ())), preferred_element_type=F32)


def nt(a, b):
    return lax.dot_general(a, b, (((1,), (1,)), ((), ())), preferred_element_type=F32)


def inv_rms(v):
    return lax.rsqrt(jnp.mean(v * v, axis=-1, keepdims=True) + epsilon)


class Take:
    def __init__(self, limit):
        self.used, self.limit = 0, limit

    def __call__(self, count=1):
        base = self.used
        self.used += count
        assert self.used <= self.limit
        return base


N_SEND, N_RECV, N_LOCAL = 128, 192, 64

SCHEDULE = {
    "dhA": (("end", (1, 0)), ("mid", (0, 2)),),
    "dnD": (("mid", (0, 0)),),
    "nb0": (("end", (3, 0)), ("end", (1, 2)), ("end", (2, 1)),),
    "nb1": (("mid", (0, 1)), ("mid", (3, 0)),),
    "cb": (("end", (2, 0)), ("mid", "pair"),),
    "tail": (("end", (3, 1)), ("mid", (2, 2)), ("mid", (1, 0)),),
    "gc2": (("mid", (2, 0)), ("mid", (1, 1)), ("mid", (3, 1)),),
    "gc3": (("mid", (1, 2)), ("mid", (3, 2)),),
    "blk1": (("end", (1, 1)),),
    "blk3": (("mid", (2, 1)), ("mid", "pair sum"), ("mid", (4, 0)), ("mid", (1, 3)), ("mid", (4, 2)),),
    "dt0": (("end", (4, 0)), ("end", (4, 1)), ("end", (3, 2)), ("end", (2, 2)), ("end", (1, 3)),),
    "dt1": (("end", "pair"), ("mid", (4, 1)), ("mid", (2, 3)),),
    "dt3": (("end", (4, 2)), ("end", (2, 3)), ("end", (3, 3)), ("mid", (3, 3)),),
    "sm": (("end", (4, 3)), ("end", "pair sum"), ("mid", (4, 3)),),
}


def step_kernel(
    dims,
    tokens, gain_mix_hbm, w_in, taps_hbm, w_out, gain_ffn_hbm, w_gate, w_up, w_down, cot,
    block_out, d_tokens, g_ffn, g_conv, small_out,
    gb0, gb1, gb2, gb3, gb4, yb0, yb1, yb2, yb3, yb4, zb0, zb1, zb2, zb3, zb4,
    cr_dh, cr_dn,
    gain_mix, taps, gain_ffn, tok_v, wg_v, wu_v, wd_v, dy_v, h2_v, h1_v, hid, dg, du, pb, pc, px, bx, gated, resid, gall,
    ring, xr_dh, xr_dn, xr_d1, rb, ld, outs, halo_s, halo_r, dhalo_s, dhalo_r, tail, pb_tail, px_tail,
    sm, sm_r, ss, rs, ls,
):
    R, T, D, CL, FL, FW = dims
    S = R // T
    CH = CL // 2
    GR = D // NZ
    SR = GR // 2
    DR = SR // 2
    NCH = R // ROWS_CHUNK
    take_s, take_r, take_l = Take(N_SEND), Take(N_RECV), Take(N_LOCAL)

    s = lax.axis_index("seq")
    x = lax.axis_index("chan")
    n_seq = 4 * NZ
    z, y, c = s // 4, (s // 2) % 2, s % 2

    def did(z_, y_, c_):
        return ((z_ * 2 + y_) * 2 + c_, x)

    core_dev = did(z, y, 1 - c)
    y_dev = did(z, 1 - y, c)
    x_dev = (s, 1 - x)
    mid = jnp.logical_and(z > 0, z < NZ - 1)
    end = jnp.logical_not(mid)

    def remote(src, dst, si, ri, dev):
        return pltpu.make_async_remote_copy(
            src_ref=src, dst_ref=dst, send_sem=ss.at[si], recv_sem=rs.at[ri],
            device_id=dev, device_id_type=MESH,
        )

    def wait_recv(dst, ri):
        remote(dst, dst, 0, ri, core_dev).wait_recv()

    def wait_send(src, si):
        remote(src, src, si, 0, core_dev).wait_send()

    def local(src, dst, li):
        return pltpu.make_async_copy(src, dst, ls.at[li])

    l_tok, l_win, l_wout, l_dy, l_small = take_l(), take_l(3), take_l(), take_l(), take_l(3)
    ld_tok = local(tokens, tok_v, l_tok)
    ld_tok.start()
    win_views = [wg_v.at[:, pl.ds(0, CL)], wg_v.at[:, pl.ds(CL, CL)], wu_v.at[:, pl.ds(0, CL)]]
    wout_view = wd_v.at[pl.ds(pl.multiple_of(x * CL, CL), CL), :]

    def load_w_in():
        return [local(w_in.at[m], win_views[m], l_win + m) for m in range(3)]

    for cp in load_w_in():
        cp.start()
    ld_small = [
        local(src, dst, l_small + i)
        for i, (src, dst) in enumerate(
            ((gain_mix_hbm, gain_mix), (taps_hbm, taps), (gain_ffn_hbm, gain_ffn))
        )
    ]
    for cp in ld_small:
        cp.start()
    ld_wout = local(w_out, wout_view, l_wout)
    ld_wout.start()
    ld_dy = local(cot, dy_v.at[0], l_dy)

    bar = pltpu.get_barrier_semaphore()

    def greet(dev):
        pl.semaphore_signal(bar, inc=1, device_id=dev, device_id_type=MESH)

    greet(core_dev)
    greet(x_dev)
    others = [(k, did((z + k // 2) % NZ, (y + k % 2) % 2, c)) for k in range(1, 2 * NZ)]
    for _, dev in others:
        greet(dev)
    has_prev = s > 0
    has_next = s < n_seq - 1
    prev_dev = ((s + n_seq - 1) % n_seq, x)
    next_dev = ((s + 1) % n_seq, x)
    greet(prev_dev)
    greet(next_dev)
    pl.semaphore_wait(bar, 3 + 2 * NZ)

    QR, SUBS = CL // 4, 4
    PR = QR // SUBS
    s_w, r_w = [take_s(SUBS) for _ in range(4)], [take_r(SUBS) for _ in range(4)]

    def w_rows(half, quarter, sub):
        return wd_v.at[pl.ds(pl.multiple_of(half * CL + quarter * QR + sub * PR, PR), PR), :]

    mine_q, pair_q = y * 2 + c, (1 - y) * 2 + c
    core_q, far_q = y * 2 + (1 - c), (1 - y) * 2 + (1 - c)

    def w_over_x(sub):
        src = w_out.at[pl.ds(pl.multiple_of(mine_q * QR + sub * PR, PR), PR), :]
        return remote(src, w_rows(x, mine_q, sub), s_w[0] + sub, r_w[0] + sub, x_dev)

    def w_over_y(sub):
        ref = w_rows(1 - x, mine_q, sub)
        return remote(ref, ref, s_w[1] + sub, r_w[1] + sub, y_dev)

    def w_over_core(sub):
        ref = w_rows(1 - x, mine_q, sub)
        return remote(ref, ref, s_w[2] + sub, r_w[2] + sub, core_dev)

    def w_far_over_core(sub):
        ref = w_rows(1 - x, pair_q, sub)
        return remote(ref, ref, s_w[3] + sub, r_w[3] + sub, core_dev)

    def w_pass_on(sub):
        wait_recv(w_rows(1 - x, mine_q, sub), r_w[0] + sub)
        w_over_y(sub).start()
        w_over_core(sub).start()

    def w_pass_far(sub):
        wait_recv(w_rows(1 - x, pair_q, sub), r_w[1] + sub)
        w_far_over_core(sub).start()

    for sub in range(SUBS):
        w_over_x(sub).start()

    l_w = take_l(3)
    win_start = pl.multiple_of(c * (FL - FW), LANE)
    ld_wg = local(w_gate.at[:, pl.ds(win_start, FW)], wg_v, l_w)
    ld_wu = local(w_up.at[:, pl.ds(win_start, FW)], wu_v, l_w + 1)
    ld_wd = local(w_down.at[pl.ds(win_start, FW), :], wd_v, l_w + 2)

    sm[...] = jnp.zeros_like(sm)
    for cp in ld_small:
        cp.wait()
    gain_mix_row = gain_mix[...].reshape(1, D)
    gain_ffn_row = gain_ffn[...].reshape(1, D)
    k_taps = [taps[t : t + 1, :] for t in range(3)]

    ld_tok.wait()

    CPS = T // ROWS_CHUNK
    NC = CL // 256
    s_h1, r_h1 = take_s(S), take_r(S)
    s_ha, r_ha = take_s(S), take_r(S)
    s_mx, r_mx = take_s(NCH), take_r(NCH)
    row_iota = lax.broadcasted_iota(jnp.int32, (T, 256), 0)
    top_iota = row_iota[0:16]

    def conv_terms(now, h, iota):
        h14 = jnp.broadcast_to(h[14:15], now.shape)
        h15 = jnp.broadcast_to(h[15:16], now.shape)
        one = jnp.where(iota == 0, h15, pltpu.roll(now, 1, 0))
        two = jnp.where(iota == 0, h14, jnp.where(iota == 1, h15, pltpu.roll(now, 2, 0)))
        return now, one, two

    def tap_cols(cols):
        return [taps[t : t + 1, cols] for t in range(3)]

    def convolve(terms, cols):
        now, one, two = terms
        k0, k1, k2 = tap_cols(cols)
        return k0 * two + k1 * one + k2 * now

    def h1_send(q):
        rows = pl.ds(q * T, T)
        return remote(h1_v.at[0, rows], h1_v.at[1, rows], s_h1 + q, r_h1 + q, core_dev)

    def halo_send(q):
        return remote(halo_s.at[q], halo_r.at[q], s_ha + q, r_ha + q, next_dev)

    own_cols = pl.ds(pl.multiple_of(x * CL, CL), CL)
    other_cols = pl.ds(pl.multiple_of((1 - x) * CL, CL), CL)

    def gated_send(k):
        ref = gall.at[k, :, own_cols]
        return remote(ref, ref, s_mx + k, r_mx + k, x_dev)

    def mixer_out(k):
        gall[k, :, own_cols] = gated[k * ROWS_CHUNK : (k + 1) * ROWS_CHUNK, :]
        gated_send(k).start()

    for q in range(S):
        rows = pl.ds(q * T, T)

        def norm_rows(k, _, q=q):
            chunk = pl.ds(pl.multiple_of(q * T + k * ROWS_CHUNK, ROWS_CHUNK), ROWS_CHUNK)
            xv = tok_v[chunk, :].astype(F32)
            h1_v[0, chunk, :] = (xv * inv_rms(xv) * gain_mix_row).astype(BF)
            return 0

        lax.fori_loop(0, CPS, norm_rows, 0)
        if q > 0:
            w_pass_on(1)
        if q == 0:
            for cp in load_w_in():
                cp.wait()

        def in_proj(j, _, q=q, rows=rows):
            cols = pl.ds(pl.multiple_of(j * 256, 256), 256)
            cols1 = pl.ds(pl.multiple_of(CL + j * 256, 256), 256)
            h = h1_v[0, rows, :]
            b = nn(h, wg_v[:, cols])
            pb[rows, cols] = b.astype(BF)
            xx = nn(h, wu_v[:, cols])
            px[rows, cols] = xx.astype(BF)
            inner = (b * xx).astype(BF)
            bx[rows, cols] = inner
            halo_s[q, :, cols] = inner[T - 16 : T]
            pcv = nn(h, wg_v[:, cols1])
            pc[rows, cols] = pcv.astype(BF)
            now = inner.astype(F32)
            cv = convolve(conv_terms(now, jnp.zeros_like(now[0:16]), row_iota), cols)
            gated[rows, cols] = (pcv * cv).astype(BF)
            return 0

        lax.fori_loop(0, NC, in_proj, 0)
        if q == S - 1:
            ld_wg.start()
            ld_wu.start()

        @pl.when(has_next)
        def _(q=q):
            halo_send(q).start()

        for k in range(CPS - 1, 0, -1):
            mixer_out(q * CPS + k)
        if q == 0:
            w_pass_on(0)
        else:
            w_pass_on(2)
            w_pass_far(0)

        @pl.when(has_prev)
        def _(q=q):
            wait_recv(halo_r.at[q], r_ha + q)

        @pl.when(jnp.logical_not(has_prev))
        def _(q=q):
            halo_r[q] = jnp.zeros_like(halo_r[q])

        def conv_top(j, _, q=q):
            cols = pl.ds(pl.multiple_of(j * 256, 256), 256)
            top = pl.ds(q * T, 16)
            now = bx[top, cols].astype(F32)
            cv = convolve(conv_terms(now, halo_r[q, :, cols].astype(F32), top_iota), cols)
            gated[top, cols] = (pc[top, cols].astype(F32) * cv).astype(BF)
            return 0

        lax.fori_loop(0, NC, conv_top, 0)
        mixer_out(q * CPS)
        h1_send(q).start()
        if q == 0:
            ld_dy.start()
            s_dy, r_dy = take_s(), take_r()
            send_dy = remote(cot, dy_v.at[1], s_dy, r_dy, core_dev)
            send_dy.start()
    w_pass_on(3)
    w_pass_far(1)

    s_h2, r_h2 = take_s(NCH), take_r(NCH)
    ld_wg.wait()
    ld_wu.wait()
    NF = FW // 256
    overlap = 2 * FW - FL
    col_iota = lax.broadcasted_iota(jnp.int32, (2 * ROWS_CHUNK, 256), 1)

    def sent(n):
        return (n // CPS) * CPS + (CPS - 1 - n % CPS)

    def residual_chunk(k):
        rows = pl.ds(pl.multiple_of(k * ROWS_CHUNK, ROWS_CHUNK), ROWS_CHUNK)
        wait_recv(gall.at[k, :, other_cols], r_mx + k)

        def out_tile(j, _):
            cols = pl.ds(pl.multiple_of(j * 512, 512), 512)
            resid[rows, cols] = tok_v[rows, cols].astype(F32) + nn(gall[k], wd_v[0 : 2 * CL, cols])
            return 0

        lax.fori_loop(0, D // 512, out_tile, 0, unroll=True)
        res = resid[rows, :]
        h2_v[0, rows, :] = (res * inv_rms(res) * gain_ffn_row).astype(BF)
        remote(h2_v.at[0, rows], h2_v.at[1, rows], s_h2 + k, r_h2 + k, core_dev).start()

    def forward_chunk(k):
        rows = pl.ds(pl.multiple_of(k * ROWS_CHUNK, ROWS_CHUNK), ROWS_CHUNK)
        wait_recv(h2_v.at[1, rows], r_h2 + k)

        def tile(j, _):
            cols = pl.ds(pl.multiple_of(j * 256, 256), 256)
            h = h2_v[:, rows, :].reshape(2 * ROWS_CHUNK, D)
            g = nn(h, wg_v[:, cols])
            u = nn(h, wu_v[:, cols])
            keep = col_iota + j * 256 >= c * overlap
            sg = jax.nn.sigmoid(g)
            si = jnp.where(keep, g * sg, 0.0)
            shape = (2, ROWS_CHUNK, 256)
            hid[:, rows, cols] = (si * u).astype(BF).reshape(shape)
            slope = jnp.where(keep, u * sg * (1.0 + g * (1.0 - sg)), 0.0)
            dg[:, rows, cols] = slope.astype(BF).reshape(shape)
            du[:, rows, cols] = si.astype(BF).reshape(shape)
            return 0

        lax.fori_loop(0, NF, tile, 0, unroll=True)

    w_pass_far(2)
    w_pass_far(3)
    ld_wout.wait()
    for sub in range(SUBS):
        wait_recv(w_rows(1 - x, core_q, sub), r_w[2] + sub)
        wait_recv(w_rows(1 - x, far_q, sub), r_w[3] + sub)
    residual_chunk(sent(0))

    def chunk_loop(n, _):
        @pl.when(n + 1 < NCH)
        def _():
            residual_chunk(sent(n + 1))

        forward_chunk(sent(n))
        return 0

    lax.fori_loop(0, NCH, chunk_loop, 0)
    for sub in range(SUBS):
        w_over_x(sub).wait_send()
        for send in (w_over_y, w_over_core, w_far_over_core):
            send(sub).wait_send()
    ld_wd.start()
    ld_dy.wait()
    send_dy.wait()
    for k in range(NCH):
        gated_send(k).wait_send()
        wait_send(h2_v.at[0, pl.ds(k * ROWS_CHUNK, ROWS_CHUNK)], s_h2 + k)

    gbs = [gb0, gb1, gb2, gb3, gb4]
    ybs = [yb0, yb1, yb2, yb3, yb4]
    zbs = [zb0, zb1, zb2, zb3, zb4]
    widths = [ZF_COLS, FW - ZF_COLS, FW, FW, 2 * CL]
    s_y = [None] + [take_s(NZ) for _ in range(4)]
    r_y = [None] + [take_r(NZ) for _ in range(4)]
    s_z = [take_s(2 * NZ)] + [take_s(NZ) for _ in range(4)]
    r_z = [take_r(4 * NZ)] + [take_r(2 * NZ) for _ in range(4)]

    def order(e):
        if e == NZ - 1:
            return z
        per_z = {0: (3, 2, 1), 1: (3, 0, 2), 2: (0, 3, 1), 3: (0, 1, 2)}
        v = per_z[3][e]
        for zz in range(3):
            v = jnp.where(z == zz, per_z[zz][e], v)
        return v

    def order_dyn(u):
        v = order(NZ - 1)
        for e in range(NZ - 1):
            v = jnp.where(u == e, order(e), v)
        return v

    def per_core(j, act):
        if j in (1, 4):
            act(lambda ref: ref)
            return

        @pl.when(c == 0)
        def _():
            act(lambda ref: ref)

        @pl.when(c == 1)
        def _():
            act(lambda ref: ref.at[:, pl.ds(overlap, widths[j] - overlap)])

    def z_send(j, src, e, zp, h=None):
        to_right = zp > z
        d = jnp.where(to_right, 0, 1)
        dev = did(jnp.clip(jnp.where(to_right, z + 1, z - 1), 0, NZ - 1), y, c)
        if h is None:
            dst, si, ri = zbs[j].at[d, zp], s_z[j] + e, r_z[j] + d * NZ + zp
        else:
            dst, si, ri = zbs[j].at[d, zp, h], s_z[j] + 2 * e + h, r_z[j] + (d * NZ + zp) * 2 + h
        per_core(j, lambda cut: remote(cut(src), cut(dst), si, ri, dev).start())

    l_g = take_l(12)

    def y_send(j, u):
        zp = order_dyn(u) if not isinstance(u, int) else order(u)
        src, dst = gbs[j].at[zp, 1 - y], ybs[j].at[zp]
        per_core(j, lambda cut: remote(cut(src), cut(dst), s_y[j] + u, r_y[j] + u, y_dev).start())

    def g_block(lhs_ref, rhs_ref, zp, pair, parts=(0, 1)):
        lhs = lhs_ref[:, :, pl.ds(pl.multiple_of(zp * GR, GR), GR)].reshape(2 * R, GR)
        cut = -(-FW // 512) * 256
        for n in parts:
            cols = slice(0, cut) if n == 0 else slice(cut, FW)
            v = tn(lhs, rhs_ref[:, :, cols].reshape(2 * R, cols.stop - cols.start)).astype(BF)
            outs[2 * pair, :, cols] = v[:SR]
            outs[2 * pair + 1, :, cols] = v[SR:]

    def down_copies(zp, pair):
        return [
            cp
            for h in range(2)
            for cp in (
                local(outs.at[2 * pair + h, :, pl.ds(0, ZF_COLS)], gb0.at[zp, h], l_g + 4 * pair + 2 * h),
                local(
                    outs.at[2 * pair + h, :, pl.ds(ZF_COLS, FW - ZF_COLS)],
                    gb1.at[zp, h], l_g + 4 * pair + 2 * h + 1,
                ),
            )
        ]

    def down_sends(u):
        zp = order(u)
        for cp in down_copies(zp, u % 2):
            cp.wait()
        if u < NZ - 1:

            @pl.when(end)
            def _():
                for h in range(2):
                    z_send(0, gb0.at[zp, h], u, zp, h)

            y_send(1, u)

    for u in range(NZ):
        g_block(dy_v, hid, order(u), u % 2, (0,))
        if u > 0:
            down_sends(u - 1)
        g_block(dy_v, hid, order(u), u % 2, (1,))
        for cp in down_copies(order(u), u % 2):
            cp.start()
    down_sends(NZ - 1)

    ld_wd.wait()

    def hid_back(slot, _):
        for j in range(NF):
            cols = slice(j * 256, (j + 1) * 256)
            dh = nt(dy_v[slot], wd_v[cols, :])
            dg[slot, :, cols] = (dh * dg[slot, :, cols].astype(F32)).astype(BF)
            du[slot, :, cols] = (dh * du[slot, :, cols].astype(F32)).astype(BF)
        return 0

    lax.fori_loop(0, 2, hid_back, 0)

    def plain_copies(gb, zp, pair):
        return [local(outs.at[2 * pair + h], gb.at[zp, h], l_g + 2 * pair + h) for h in range(2)]

    def gate_up(u, _):
        zp = order_dyn(u)

        def up_sends(u):
            for cp in plain_copies(gb3, order_dyn(u), 1):
                cp.wait()

            @pl.when(u < 2)
            def _():
                y_send(3, u)

        g_block(h2_v, dg, zp, 0, (0,))

        @pl.when(u > 0)
        def _():
            up_sends(u - 1)

        g_block(h2_v, dg, zp, 0, (1,))
        for cp in plain_copies(gb2, zp, 0):
            cp.start()
        g_block(h2_v, du, zp, 1, (0,))
        for cp in plain_copies(gb2, zp, 0):
            cp.wait()

        @pl.when(u < 3)
        def _():
            y_send(2, u)

        g_block(h2_v, du, zp, 1, (1,))
        for cp in plain_copies(gb3, zp, 1):
            cp.start()
        return 0

    lax.fori_loop(0, NZ, gate_up, 0)
    for cp in plain_copies(gb3, order(NZ - 1), 1):
        cp.wait()

    l_e = take_l(4)
    is_role = {"end": end, "mid": mid}
    slot_last = {role: [None] * outs.shape[0] for role in is_role}
    slot_next = {role: 0 for role in is_role}

    def claim_slot(role):
        o = slot_next[role]
        slot_next[role] = (o + 1) % outs.shape[0]
        if slot_last[role][o] is not None:
            slot_last[role][o]()
            slot_last[role][o] = None
        return o

    ADD_ROWS = 32

    def add_into(dst, srcs):
        def rows_add(k, _):
            rows = pl.ds(pl.multiple_of(k * ADD_ROWS, ADD_ROWS), ADD_ROWS)
            acc = srcs[0][rows, :].astype(F32)
            for src in srcs[1:]:
                acc = acc + src[rows, :].astype(F32)
            dst[rows, :] = acc.astype(BF)
            return 0

        lax.fori_loop(0, SR // ADD_ROWS, rows_add, 0)

    def fetch(j, srcs):
        w = widths[j]
        views, copies = [], []
        for i, (src, ri) in enumerate(srcs):
            if ri is not None:
                per_core(j, lambda cut: wait_recv(cut(src), ri))
            views.append(ld.at[i, :, pl.ds(0, w)])
            copies.append(local(src, views[-1], l_e + i))
            copies[-1].start()
        for cp in copies:
            cp.wait()
        return views

    def from_line(j, d, zp, h=None):
        if h is None:
            return zbs[j].at[d, zp], r_z[j] + d * NZ + zp
        return zbs[j].at[d, zp, h], r_z[j] + (d * NZ + zp) * 2 + h

    def line_event(role, j, e):
        @pl.when(is_role[role])
        def _():
            zp = order(e)
            w = widths[j]
            d = jnp.where(zp > z, 0, 1)
            for h in (0, 1) if j == 0 else (None,):
                o = claim_slot(role)
                dst = outs.at[o, :, pl.ds(0, w)]
                if h is None:
                    srcs = [(gbs[j].at[zp, y], None), (ybs[j].at[zp], r_y[j] + e)]
                    si = s_z[j] + e
                else:
                    srcs = [(gbs[j].at[zp, h], None)]
                    si = s_z[j] + 2 * e + h
                if role == "mid":
                    srcs.append(from_line(j, d, zp, h))
                add_into(dst, fetch(j, srcs))
                z_send(j, dst, e, zp, h)
                slot_last[role][o] = functools.partial(sent_slot, j, o, si)

    def sent_slot(j, o, si):
        per_core(j, lambda cut: wait_send(cut(outs.at[o, :, pl.ds(0, widths[j])]), si))

    def own_shard(role, j, h=None):
        if h is None:
            srcs = [(gbs[j].at[z, y], None), (ybs[j].at[z], r_y[j] + NZ - 1)]
        else:
            srcs = [(gbs[j].at[z, h], None)]
        if role == "mid":
            return srcs + [from_line(j, 0, z, h), from_line(j, 1, z, h)]
        return srcs + [from_line(j, jnp.where(z == 0, 1, 0), z, h)]

    def swap_pieces(j):
        if j == 4:
            return [(None, m * CH, CH, g_conv.at[m], c * CH) for m in range(4)]
        mat = g_ffn.at[{0: 0, 1: 0, 2: 1, 3: 2}[j]]
        w = widths[j]
        if j == 1:
            return [(None, 0, w, mat, c * (FL - FW) + ZF_COLS)]
        return [(0, 0, w, mat, 0), (1, overlap, w - overlap, mat, FL - FW + overlap)]

    swap_sems = [[(take_s(), take_r(), take_l()) for _ in swap_pieces(j)] for j in range(5)]

    def swap(j, o):
        items = []
        for (core, c0, w, mat, to), (si, ri, li) in zip(swap_pieces(j), swap_sems[j]):
            to = to if isinstance(to, int) else pl.multiple_of(to, LANE)
            target = mat.at[:, pl.ds(to, w)]
            mine = outs.at[o, pl.ds(pl.multiple_of(c * DR, DR), DR), pl.ds(c0, w)]
            other = outs.at[o, pl.ds(pl.multiple_of((1 - c) * DR, DR), DR), pl.ds(c0, w)]
            items.append((core, local(mine, target, li), remote(other, target, si, ri, core_dev), target))
        return items

    def swap_start(j, o):
        for core, keep, give, _ in swap(j, o):
            if core is None:
                keep.start()
                give.start()
            else:

                @pl.when(c == core)
                def _():
                    keep.start()
                    give.start()

    def swap_finish(j, o):
        for (core, keep, give, target), (_, ri, _) in zip(swap(j, o), swap_sems[j]):
            if core is None:
                keep.wait()
                give.wait_send()
                wait_recv(target, ri)
            else:

                @pl.when(c == core)
                def _():
                    keep.wait()
                    give.wait_send()

                @pl.when(c != core)
                def _():
                    wait_recv(target, ri)

    def final_event(role, j):
        @pl.when(is_role[role])
        def _():
            o = claim_slot(role)
            w = widths[j]
            add_into(outs.at[o, :, pl.ds(0, w)], fetch(j, own_shard(role, j)))
            swap_start(j, o)
            slot_last[role][o] = functools.partial(swap_finish, j, o)

    s_f0, r_f0 = take_s(), take_r()
    w0 = widths[0]

    def final0_send(role):
        @pl.when(is_role[role])
        def _():
            o = claim_slot(role)
            dst = outs.at[o, :, pl.ds(0, w0)]
            add_into(dst, fetch(0, own_shard(role, 0, 1 - y)))
            cp = local(dst, gb0.at[z, 1 - y], l_e)
            cp.start()
            cp.wait()
            src = gb0.at[z, 1 - y]
            per_core(0, lambda cut: remote(cut(src), cut(yb0), s_f0, r_f0, y_dev).start())

    def final0_finish(role):
        @pl.when(is_role[role])
        def _():
            o = claim_slot(role)
            dst = outs.at[o, :, pl.ds(0, w0)]
            add_into(dst, fetch(0, own_shard(role, 0, y)))
            add_into(dst, [dst] + fetch(0, [(yb0, r_f0)]))
            swap_start(0, o)
            slot_last[role][o] = functools.partial(swap_finish, 0, o)

    def hook(name):
        for role, event in SCHEDULE.get(name, ()):
            if event == "pair":
                final0_send(role)
            elif event == "pair sum":
                final0_finish(role)
            elif event[1] == NZ - 1:
                final_event(role, event[0])
            else:
                line_event(role, *event)

    def chunks(name, count, body):
        first = 0
        for k in range(count):
            if SCHEDULE.get(name + str(k)) or k == count - 1:
                lax.fori_loop(first, k + 1, body, 0)
                first = k + 1
                hook(name + str(k))

    HALF = 2 * ROWS_CHUNK

    def split_sum(name, product, cr, xr, base_d):
        s_c, r_c = take_s(2), take_r(2)
        s_x, r_x = take_s(NCH), take_r(NCH)
        l_c = take_l()

        def give(k, _):
            def tile(n, _):
                cols = pl.ds(pl.multiple_of(n * 512, 512), 512)
                v = product(1, k * HALF, n).astype(BF)
                gall[pl.ds(2 * k, 2), :, cols] = v.reshape(2, ROWS_CHUNK, 512)
                return 0

            lax.fori_loop(0, D // 512, tile, 0)
            remote(
                gall.at[pl.ds(2 * k, 2)], cr.at[pl.ds(2 * k, 2)], s_c + k, r_c + k, core_dev
            ).start()
            return 0

        lax.fori_loop(0, 2, give, 0)
        hook(name + "A")

        def keep(k, _):
            src = cr.at[pl.ds(2 * k, 2)]
            wait_recv(src, r_c + k)
            cp = local(src, rb, l_c)
            cp.start()
            cp.wait()

            def tile(n, _):
                cols = pl.ds(pl.multiple_of(n * 512, 512), 512)
                v = product(0, k * HALF, n) + rb[:, :, cols].reshape(HALF, 512).astype(F32)
                ring[pl.ds(base_d + 2 * k, 2), :, cols] = v.astype(BF).reshape(2, ROWS_CHUNK, 512)
                return 0

            lax.fori_loop(0, D // 512, tile, 0)
            for i in range(2):
                remote(
                    ring.at[base_d + 2 * k + i], xr.at[2 * k + i], s_x + 2 * k + i, r_x + 2 * k + i, x_dev
                ).start()
            return 0

        lax.fori_loop(0, 2, keep, 0)
        for k in range(2):
            wait_send(gall.at[pl.ds(2 * k, 2)], s_c + k)
        hook(name + "D")
        return s_x, r_x

    def rows_at(ref, slot, r0):
        return ref[slot, pl.ds(pl.multiple_of(r0, HALF), HALF), :]

    def dh_product(slot, r0, n):
        cols = pl.ds(pl.multiple_of(n * 512, 512), 512)
        return nt(rows_at(dg, slot, r0), wg_v[cols, :]) + nt(rows_at(du, slot, r0), wu_v[cols, :])

    def dn_product(slot, r0, n):
        cols = pl.ds(pl.multiple_of(n * 512, 512), 512)
        return nn(rows_at(hid, slot, r0), wd_v[:, cols])

    s_xdh, r_xdh = split_sum("dh", dh_product, cr_dh, xr_dh, 0)
    s_xdn, r_xdn = split_sum("dn", dn_product, cr_dn, xr_dn, 4)
    for cp in load_w_in():
        cp.start()
    ld_wout = local(w_out, wd_v.at[pl.ds(0, CL), :], l_wout)
    ld_wout.start()

    s_do, r_do = take_s(NCH), take_r(NCH)

    def ffn_norm_back(k, _):
        rows = pl.ds(pl.multiple_of(k * ROWS_CHUNK, ROWS_CHUNK), ROWS_CHUNK)
        wait_recv(xr_dh.at[k], r_xdh + k)
        d_h = ring[k].astype(F32) + xr_dh[k].astype(F32)
        res = resid[rows, :]
        s2 = inv_rms(res)
        n2 = res * s2
        sm[0, 1:2, :] += jnp.sum(d_h * n2, axis=0, keepdims=True)
        e2 = d_h * gain_ffn_row
        d_res = dy_v[0, rows, :].astype(F32) + s2 * (
            e2 - n2 * jnp.mean(e2 * n2, axis=-1, keepdims=True)
        )
        h2_v[0, rows, :] = d_res.astype(BF)
        remote(h2_v.at[0, rows], h2_v.at[1, rows], s_do + k, r_do + k, core_dev).start()
        return 0

    chunks("nb", NCH, ffn_norm_back)
    for k in range(NCH):
        wait_send(ring.at[k], s_xdh + k)

    for cp in load_w_in():
        cp.wait()
    ld_wout.wait()
    for q in range(S):

        def conv_back(j, _, q=q):
            cols = pl.ds(pl.multiple_of(j * 256, 256), 256)
            rows = pl.ds(q * T, T)
            now, one, two = conv_terms(
                bx[rows, cols].astype(F32), halo_r[q, :, cols].astype(F32), row_iota
            )
            k0, k1, k2 = tap_cols(cols)
            cv = k0 * two + k1 * one + k2 * now
            d_g = nt(h2_v[0, q * T : q * T + T, :], wd_v[cols, :])
            d_cv = d_g * pc[rows, cols].astype(F32)
            sm[0, 2:3, cols] += jnp.sum(d_cv * two, axis=0, keepdims=True)
            sm[0, 3:4, cols] += jnp.sum(d_cv * one, axis=0, keepdims=True)
            sm[0, 4:5, cols] += jnp.sum(d_cv * now, axis=0, keepdims=True)
            after1 = jnp.where(row_iota < T - 1, pltpu.roll(d_cv, T - 1, 0), 0.0)
            after2 = jnp.where(row_iota < T - 2, pltpu.roll(d_cv, T - 2, 0), 0.0)
            d_bx = k2 * d_cv + k1 * after1 + k0 * after2
            dhalo_s[q, :, cols] = d_cv[0:8]
            tail[q, :, cols] = d_bx[T - 16 : T]
            old_b = pb[rows, cols]
            old_x = px[rows, cols]
            pb_tail[q, :, cols] = old_b[T - 16 : T]
            px_tail[q, :, cols] = old_x[T - 16 : T]
            low = d_bx.astype(BF).astype(F32)
            pb[rows, cols] = (low * old_x.astype(F32)).astype(BF)
            px[rows, cols] = (low * old_b.astype(F32)).astype(BF)
            pc[rows, cols] = (d_g * cv).astype(BF)
            return 0

        lax.fori_loop(0, NC, conv_back, 0)

    s_dha, r_dha = take_s(), take_r()
    send_dhalo = remote(dhalo_s, dhalo_r, s_dha, r_dha, prev_dev)

    @pl.when(has_prev)
    def _():
        send_dhalo.start()

    y_send(3, 2)

    hook("cb")

    s_x1, r_x1 = take_s(NCH), take_r(NCH)

    def d1_part(name, ids):
        def tile(n, _):
            cols = pl.ds(pl.multiple_of(n * 512, 512), 512)

            def rows_of(ref):
                return jnp.concatenate(
                    [ref[k * ROWS_CHUNK : (k + 1) * ROWS_CHUNK, :] for k in ids], axis=0
                )

            v = (
                nt(rows_of(pb), wg_v[cols, 0:CL])
                + nt(rows_of(pc), wg_v[cols, CL : 2 * CL])
                + nt(rows_of(px), wu_v[cols, 0:CL])
            ).astype(BF)
            for i, k in enumerate(ids):
                ring[k, :, cols] = v[i * ROWS_CHUNK : (i + 1) * ROWS_CHUNK]
            return 0

        lax.fori_loop(0, D // 512, tile, 0)
        for k in ids:
            remote(ring.at[k], xr_d1.at[k], s_x1 + k, r_x1 + k, x_dev).start()
        hook(name)

    d1_part("d1a", [q * CPS + k for q in range(S) for k in range(CPS - 1)])

    @pl.when(has_next)
    def _():
        wait_recv(dhalo_r, r_dha)

    @pl.when(jnp.logical_not(has_next))
    def _():
        dhalo_r[...] = jnp.zeros_like(dhalo_r)

    tail_iota = lax.broadcasted_iota(jnp.int32, (16, CL), 0)
    for q in range(S):
        first = jnp.broadcast_to(dhalo_r[q, 0:1, :], (16, CL))
        second = jnp.broadcast_to(dhalo_r[q, 1:2, :], (16, CL))
        fix = jnp.where(
            tail_iota == 14,
            k_taps[0] * first,
            jnp.where(tail_iota == 15, k_taps[1] * first + k_taps[0] * second, 0.0),
        )
        low = (tail[q] + fix).astype(BF).astype(F32)
        rows = pl.ds(q * T + T - 16, 16)
        pb[rows, :] = (low * px_tail[q].astype(F32)).astype(BF)
        px[rows, :] = (low * pb_tail[q].astype(F32)).astype(BF)

    s_dp, r_dp = take_s(4), take_r(4)
    theirs = pl.ds(pl.multiple_of((1 - c) * CH, LANE), CH)
    ours = pl.ds(pl.multiple_of(c * CH, LANE), CH)
    dp_sends = [
        remote(ref.at[:, theirs], dy_v.at[1, :, pl.ds(m * CH, CH)], s_dp + m, r_dp + m, core_dev)
        for m, ref in enumerate((pb, pc, px, gated))
    ]
    for cp in dp_sends:
        cp.start()
    hook("tail")

    d1_part("d1b", [q * CPS + k for q in range(S) for k in range(1, CPS)])

    for q in range(S):
        wait_recv(h1_v.at[1, pl.ds(q * T, T)], r_h1 + q)
    for k in range(NCH):
        rows = pl.ds(k * ROWS_CHUNK, ROWS_CHUNK)
        wait_recv(h2_v.at[1, rows], r_do + k)
    for m in range(4):
        wait_recv(dy_v.at[1, :, pl.ds(m * CH, CH)], r_dp + m)
    W4 = widths[4]
    g4 = [dg.at[i, pl.ds(k * SR, SR), pl.ds(0, W4)] for i in range(2) for k in range(2)]

    def g_mixer(u, _):
        zp = order_dyn(u)
        zc = pl.ds(pl.multiple_of(zp * GR, GR), GR)
        for m, (mine, lhs) in enumerate(((pb, h1_v), (pc, h1_v), (px, h1_v), (gated, h2_v))):
            v = tn(lhs[0, :, zc], mine[:, ours]) + tn(
                lhs[1, :, zc], dy_v[1, :, m * CH : (m + 1) * CH]
            )
            v = v.astype(BF)
            g4[0][:, m * CH : (m + 1) * CH] = v[:SR]
            g4[1][:, m * CH : (m + 1) * CH] = v[SR:]
        cps = [local(g4[h], gb4.at[zp, h], l_g + h) for h in range(2)]
        for cp in cps:
            cp.start()
        for cp in cps:
            cp.wait()

        @pl.when(u < NZ - 1)
        def _():
            y_send(4, u)

        return 0

    chunks("gc", NZ, g_mixer)
    for j in (1, 2, 3, 4):
        y_send(j, NZ - 1)

    l_o = take_l(2)

    def put_rows(v, out, rows, n):
        slot = n % 2
        cp = local(rb.at[slot], out.at[rows, :], l_o + slot)

        @pl.when(n >= 2)
        def _():
            cp.wait()

        rb[slot] = v
        cp.start()

    def put_done(out):
        for slot in range(2):
            local(rb.at[slot], out.at[pl.ds(0, ROWS_CHUNK), :], l_o + slot).wait()

    def block_chunk(k, _):
        rows = pl.ds(pl.multiple_of(k * ROWS_CHUNK, ROWS_CHUNK), ROWS_CHUNK)
        wait_recv(xr_dn.at[k], r_xdn + k)
        total = ring[4 + k].astype(F32) + xr_dn[k].astype(F32)
        put_rows((resid[rows, :] + total).astype(BF), block_out, rows, k)
        return 0

    chunks("blk", NCH, block_chunk)
    put_done(block_out)

    def mix_norm_back(n, _):
        k = (n % S) * CPS + n // S
        rows = pl.ds(pl.multiple_of(k * ROWS_CHUNK, ROWS_CHUNK), ROWS_CHUNK)
        wait_recv(xr_d1.at[k], r_x1 + k)
        d_h = ring[k].astype(F32) + xr_d1[k].astype(F32)
        xv = tok_v[rows, :].astype(F32)
        s1 = inv_rms(xv)
        n1 = xv * s1
        sm[0, 0:1, :] += jnp.sum(d_h * n1, axis=0, keepdims=True)
        e1 = d_h * gain_mix_row
        out = h2_v[0, rows, :].astype(F32) + s1 * (
            e1 - n1 * jnp.mean(e1 * n1, axis=-1, keepdims=True)
        )
        put_rows(out.astype(BF), d_tokens, rows, n)
        return 0

    chunks("dt", NCH, mix_norm_back)
    put_done(d_tokens)

    s_sm, r_sm = take_s(2 * NZ), take_r(2 * NZ)
    a = remote(sm.at[0], sm_r.at[0], s_sm, r_sm, core_dev)
    a.start()
    a.wait()
    sm[1] = sm[0] + sm_r[0]
    for k, dev in others:
        remote(sm.at[1], sm_r.at[k], s_sm + k, r_sm + k, dev).start()
    hook("sm")

    total = sm[1]
    for k, _ in others:
        wait_recv(sm_r.at[k], r_sm + k)
        total = total + sm_r[k]
    for k, _ in others:
        wait_send(sm.at[1], s_sm + k)
    sm[0] = total
    out_small = local(sm.at[0], small_out, l_small)
    out_small.start()
    out_small.wait()

    for role, cond in is_role.items():

        @pl.when(cond)
        def _(role=role):
            for finish in slot_last[role]:
                if finish is not None:
                    finish()

    @pl.when(end)
    def _():
        for e in range(NZ - 1):
            for h in range(2):
                per_core(0, lambda cut: wait_send(cut(gb0.at[0, h]), s_z[0] + 2 * e + h))

    for j in range(1, 5):
        for u in range(NZ):
            per_core(j, lambda cut: wait_send(cut(ybs[j].at[0]), s_y[j] + u))
    per_core(0, lambda cut: wait_send(cut(yb0), s_f0))
    for q in range(S):
        h1_send(q).wait_send()
    for k in range(NCH):
        wait_send(h2_v.at[0, pl.ds(k * ROWS_CHUNK, ROWS_CHUNK)], s_do + k)
        wait_send(ring.at[k], s_x1 + k)
        wait_send(ring.at[4 + k], s_xdn + k)
    for cp in dp_sends:
        cp.wait_send()

    @pl.when(has_next)
    def _():
        for q in range(S):
            halo_send(q).wait_send()

    @pl.when(has_prev)
    def _():
        send_dhalo.wait_send()


def fused_body(tokens, gain_mix, w_in, kernel, w_out, gain_ffn, w_gate, w_up, w_down, cotangent):
    S, T, D = tokens.shape
    CL = w_out.shape[0]
    FL = w_gate.shape[1]
    R = S * T
    n_seq = lax.axis_size("seq")
    tiles = FL // LANE
    FW = -(-tiles // 2) * LANE
    GR = D // NZ
    SR = GR // 2
    DR = SR // 2
    widths = [ZF_COLS, FW - ZF_COLS, FW, FW, 2 * CL]
    NCH = R // ROWS_CHUNK

    def sds(shape, dtype=BF):
        return jax.ShapeDtypeStruct(shape, dtype)

    outs = [sds((R, D)), sds((R, D)), sds((3, DR, FL)), sds((4, DR, CL)), sds((8, D), F32)]
    outs += [sds((NZ, 2, SR, w)) for w in widths]
    outs += [sds((SR, widths[0]))] + [sds((NZ, SR, w)) for w in widths[1:]]
    outs += [sds((2, NZ, 2, SR, widths[0]))] + [sds((2, NZ, SR, w)) for w in widths[1:]]
    outs += [sds((NCH, ROWS_CHUNK, D))] * 2
    any_spec = pl.BlockSpec(memory_space=pl.ANY)
    V = pltpu.VMEM
    scratch = [
        V((D,), F32),
        V((3, CL), F32),
        V((D,), F32),
        V((R, D), BF),
        V((D, FW), BF),
        V((D, FW), BF),
        V((FW, D), BF),
        V((2, R, D), BF),
        V((2, R, D), BF),
        V((2, R, D), BF),
        V((2, R, FW), BF),
        V((2, R, FW), BF),
        V((2, R, FW), BF),
        V((R, CL), BF),
        V((R, CL), BF),
        V((R, CL), BF),
        V((R, CL), BF),
        V((R, CL), BF),
        V((R, D), F32),
        V((NCH, ROWS_CHUNK, D), BF),
        V((8, ROWS_CHUNK, D), BF),
        V((NCH, ROWS_CHUNK, D), BF),
        V((NCH, ROWS_CHUNK, D), BF),
        V((NCH, ROWS_CHUNK, D), BF),
        V((2, ROWS_CHUNK, D), BF),
        V((4, SR, FW), BF),
        V((4, SR, FW), BF),
        V((S, 16, CL), BF),
        V((S, 16, CL), BF),
        V((S, 8, CL), F32),
        V((S, 8, CL), F32),
        V((S, 16, CL), F32),
        V((S, 16, CL), BF),
        V((S, 16, CL), BF),
        V((2, 8, D), F32),
        V((2 * NZ, 8, D), F32),
        pltpu.SemaphoreType.DMA((N_SEND,)),
        pltpu.SemaphoreType.DMA((N_RECV,)),
        pltpu.SemaphoreType.DMA((N_LOCAL,)),
    ]
    flops = 2 * R * D * (4 * CL + 3 * FL) * 3
    res = pl.pallas_call(
        functools.partial(step_kernel, (R, T, D, CL, FL, FW)),
        out_shape=outs,
        in_specs=[any_spec] * 10,
        out_specs=[any_spec] * len(outs),
        scratch_shapes=scratch,
        compiler_params=pltpu.CompilerParams(
            collective_id=0, has_side_effects=True, vmem_limit_bytes=63 << 20
        ),
        cost_estimate=pl.CostEstimate(flops=flops, bytes_accessed=200 << 20, transcendentals=0),
        name="block_step",
    )(
        tokens.reshape(R, D), gain_mix, w_in, kernel, w_out,
        gain_ffn, w_gate, w_up, w_down, cotangent.reshape(R, D),
    )
    block_out, d_tokens, g_mix, g_in, g_taps, g_out, g_gain, g_gate, g_up, g_down = finish(
        n_seq, *res[:5]
    )
    return (
        block_out.reshape(S, T, D),
        d_tokens.reshape(S, T, D),
        g_mix, g_in, g_taps, g_out.T, g_gain, g_gate, g_up, g_down.T,
    )


def finish_kernel(
    n_seq, block_in, d_in, ffn_in, conv_in, small_in,
    block_out, d_out, g_mix, g_in, g_taps, g_out, g_gain, g_gate, g_up, g_down,
    block_v, d_v, ffn, conv, small, gate_v, up_v, down_v, in_v, out_v, mix_v, taps_v, gain_v, sem,
):
    D = d_in.shape[1]
    CL = conv_in.shape[2]
    s = lax.axis_index("seq")
    count = [0]

    def copy(src, dst):
        count[0] += 1
        cp = pltpu.make_async_copy(src, dst, sem.at[count[0] - 1])
        cp.start()
        return cp

    loads = [copy(ffn_in.at[0], ffn.at[0]), copy(conv_in, conv), copy(small_in, small)]
    loads += [copy(ffn_in.at[m], ffn.at[m]) for m in (1, 2)]
    passing = [copy(block_in, block_v), copy(d_in, d_v)]
    stores = []
    loads[0].wait()
    down_v[...] = ffn[0].astype(F32)
    stores.append(copy(down_v, g_down))
    loads[1].wait()
    in_v[...] = conv[0:3].astype(F32)
    stores.append(copy(in_v, g_in))
    out_v[...] = conv[3].astype(F32)
    stores.append(copy(out_v, g_out))
    passing[0].wait()
    stores.append(copy(block_v, block_out))
    passing[1].wait()
    stores.append(copy(d_v, d_out))
    loads[3].wait()
    gate_v[...] = ffn[1].astype(F32)
    stores.append(copy(gate_v, g_gate))
    loads[4].wait()
    up_v[...] = ffn[2].astype(F32)
    stores.append(copy(up_v, g_up))
    loads[2].wait()
    per_d, per_c = D // n_seq, CL // n_seq
    mine = pltpu.roll(small[...], D - s * per_d, 1)
    mix_v[...] = mine[0, 0:per_d]
    gain_v[...] = mine[1, 0:per_d]
    mine = pltpu.roll(small[...], D - s * per_c, 1)
    for t in range(3):
        taps_v[t] = mine[2 + t : 3 + t, 0:per_c]
    stores += [copy(mix_v, g_mix), copy(gain_v, g_gain), copy(taps_v, g_taps)]
    for cp in stores:
        cp.wait()


def finish(n_seq, block_out, d_tokens, g_ffn, g_conv, small):
    R, D = block_out.shape
    _, DR, FL = g_ffn.shape
    CL = g_conv.shape[2]
    any_spec = pl.BlockSpec(memory_space=pl.ANY)
    V = pltpu.VMEM
    tails = [
        (DR, FL), (DR, FL), (DR, FL), (3, DR, CL), (DR, CL),
        (D // n_seq,), (3, 1, CL // n_seq), (D // n_seq,),
    ]
    gate, up, down, inp, out, mix, taps, gain = [jax.ShapeDtypeStruct(t, F32) for t in tails]
    low = jax.ShapeDtypeStruct((R, D), BF)
    return pl.pallas_call(
        functools.partial(finish_kernel, n_seq),
        out_shape=[low, low, mix, inp, taps, out, gain, gate, up, down],
        in_specs=[any_spec] * 5,
        out_specs=[any_spec] * 10,
        scratch_shapes=[V((R, D), BF), V((R, D), BF), V(g_ffn.shape, BF), V(g_conv.shape, BF), V(small.shape, F32)]
        + [V(t, F32) for t in tails]
        + [pltpu.SemaphoreType.DMA((20,))],
        compiler_params=pltpu.CompilerParams(vmem_limit_bytes=63 << 20),
        name="finish",
    )(block_out, d_tokens, g_ffn, g_conv, small)


def from_behind(value, axis, by):
    count = lax.axis_size(axis)
    pairs = [(i, i + by) for i in range(count) if 0 <= i + by < count]
    return lax.ppermute(value, axis, pairs)


def rms_scale(vector):
    return lax.rsqrt(jnp.mean(vector * vector, axis=-1, keepdims=True) + epsilon)


def norm_back(d_normout, normed, inv_scale, gain_vec):
    d_normed = d_normout * gain_vec
    return inv_scale * (d_normed - normed * jnp.mean(d_normed * normed, axis=-1, keepdims=True))


def matmul(lhs_mat, rhs_mat):
    return jnp.dot(lhs_mat, rhs_mat, preferred_element_type=jnp.float32)


def left_trans(lhs_mat, rhs_mat):
    return lax.dot_general(
        lhs_mat, rhs_mat, (((0,), (0,)), ((), ())), preferred_element_type=jnp.float32
    )


def right_trans(lhs_mat, rhs_mat):
    return lax.dot_general(
        lhs_mat, rhs_mat, (((1,), (1,)), ((), ())), preferred_element_type=jnp.float32
    )


def general_body(tokens, gain_mix, w_in, kernel, w_out, gain_ffn, w_gate, w_up, w_down, cotangent):
    seq_count, tok_rows, model_width = tokens.shape
    row_count = seq_count * tok_rows
    tokens_f = tokens.astype(jnp.float32).reshape(row_count, model_width)
    scale_mix = rms_scale(tokens_f)
    normed_mix = tokens_f * scale_mix
    h_mix = (normed_mix * gain_mix).astype(jnp.bfloat16)
    proj_b = matmul(h_mix, w_in[0])
    proj_c = matmul(h_mix, w_in[1])
    proj_x = matmul(h_mix, w_in[2])
    conv_in = (proj_b * proj_x).astype(jnp.bfloat16).reshape(seq_count, tok_rows, -1)
    before = from_behind(conv_in[:, tok_rows - 2 :, :], "seq", 1)
    extended = jnp.concatenate([before, conv_in], axis=1).astype(jnp.float32)
    conv_out = (
        kernel[0] * extended[:, :-2] + kernel[1] * extended[:, 1:-1] + kernel[2] * extended[:, 2:]
    )
    conv_flat = conv_out.reshape(row_count, -1)
    gated = (proj_c * conv_flat).astype(jnp.bfloat16)
    mixed_sum = lax.psum(matmul(gated, w_out).astype(jnp.bfloat16), "chan").astype(jnp.float32)
    residual = tokens_f + mixed_sum
    scale_ffn = rms_scale(residual)
    normed_ffn = residual * scale_ffn
    h_ffn = (normed_ffn * gain_ffn).astype(jnp.bfloat16)
    gate_pre = matmul(h_ffn, w_gate)
    up_value = matmul(h_ffn, w_up)
    sigmoid_gate = jax.nn.sigmoid(gate_pre)
    silu_gate = gate_pre * sigmoid_gate
    hidden = (silu_gate * up_value).astype(jnp.bfloat16)
    ffn_total = lax.psum(matmul(hidden, w_down).astype(jnp.bfloat16), "chan").astype(jnp.float32)
    block_out = (
        (residual + ffn_total).astype(jnp.bfloat16).reshape(seq_count, tok_rows, model_width)
    )
    grad_out = cotangent.reshape(row_count, model_width)
    g_w_down = left_trans(hidden, grad_out)
    d_hidden = right_trans(grad_out, w_down)
    d_gate = (d_hidden * up_value * sigmoid_gate * (1.0 + gate_pre * (1.0 - sigmoid_gate))).astype(
        jnp.bfloat16
    )
    d_up = (d_hidden * silu_gate).astype(jnp.bfloat16)
    g_w_gate = left_trans(h_ffn, d_gate)
    g_w_up = left_trans(h_ffn, d_up)
    d_h_ffn = lax.psum(
        (right_trans(d_gate, w_gate) + right_trans(d_up, w_up)).astype(jnp.bfloat16), "chan"
    ).astype(jnp.float32)
    g_gain_ffn = jnp.sum(d_h_ffn * normed_ffn, axis=0)
    d_resid = grad_out.astype(jnp.float32) + norm_back(d_h_ffn, normed_ffn, scale_ffn, gain_ffn)
    d_mixed = d_resid.astype(jnp.bfloat16)
    g_w_out = left_trans(gated, d_mixed)
    d_gated = right_trans(d_mixed, w_out)
    d_proj_c = (d_gated * conv_flat).astype(jnp.bfloat16)
    d_conv = (d_gated * proj_c).reshape(seq_count, tok_rows, -1)
    after_rows = from_behind(d_conv[:, :2, :], "seq", -1)
    ext_back = jnp.concatenate([d_conv, after_rows], axis=1)
    d_conv_in = (
        kernel[2] * ext_back[:, :-2] + kernel[1] * ext_back[:, 1:-1] + kernel[0] * ext_back[:, 2:]
    )
    g_kernel = jnp.stack(
        [
            jnp.sum(d_conv * extended[:, :-2], axis=(0, 1)),
            jnp.sum(d_conv * extended[:, 1:-1], axis=(0, 1)),
            jnp.sum(d_conv * extended[:, 2:], axis=(0, 1)),
        ]
    ).reshape(3, 1, -1)
    d_conv_low = d_conv_in.reshape(row_count, -1).astype(jnp.bfloat16)
    d_proj_b = (d_conv_low * proj_x).astype(jnp.bfloat16)
    d_proj_x = (d_conv_low * proj_b).astype(jnp.bfloat16)
    g_w_in = jnp.stack(
        [left_trans(h_mix, d_proj_b), left_trans(h_mix, d_proj_c), left_trans(h_mix, d_proj_x)]
    )
    d_h_mix = lax.psum(
        (
            right_trans(d_proj_b, w_in[0])
            + right_trans(d_proj_c, w_in[1])
            + right_trans(d_proj_x, w_in[2])
        ).astype(jnp.bfloat16),
        "chan",
    ).astype(jnp.float32)
    g_gain_mix = jnp.sum(d_h_mix * normed_mix, axis=0)
    d_tokens = (
        (d_resid + norm_back(d_h_mix, normed_mix, scale_mix, gain_mix))
        .astype(jnp.bfloat16)
        .reshape(seq_count, tok_rows, model_width)
    )
    summed = (
        lax.psum_scatter(g_w_in, "seq", scatter_dimension=1, tiled=True),
        lax.psum_scatter(g_w_out, "seq", scatter_dimension=1, tiled=True),
        lax.psum_scatter(g_kernel, "seq", scatter_dimension=2, tiled=True),
        lax.psum_scatter(g_gain_mix, "seq", scatter_dimension=0, tiled=True),
        lax.psum_scatter(g_w_gate, "seq", scatter_dimension=0, tiled=True),
        lax.psum_scatter(g_w_up, "seq", scatter_dimension=0, tiled=True),
        lax.psum_scatter(g_w_down, "seq", scatter_dimension=1, tiled=True),
        lax.psum_scatter(g_gain_ffn, "seq", scatter_dimension=0, tiled=True),
    )
    sum_in, sum_out, sum_kernel, sum_gain_mix, sum_gate, sum_up, sum_down, sum_gain_ffn = summed
    return (
        block_out,
        d_tokens,
        sum_gain_mix,
        sum_in,
        sum_kernel,
        sum_out,
        sum_gain_ffn,
        sum_gate,
        sum_up,
        sum_down,
    )


def solution(mesh):
    body = fused_body if mesh.shape["seq"] == 4 * NZ else general_body
    placed = (
        P(None, "seq", None),
        P(),
        P(None, None, "chan"),
        P(None, "chan"),
        P("chan", None),
        P(),
        P(None, "chan"),
        P(None, "chan"),
        P("chan", None),
        P(None, "seq", None),
    )
    return jax.shard_map(
        body,
        mesh=mesh,
        in_specs=placed,
        out_specs=(
            P(None, "seq", None),
            P(None, "seq", None),
            P("seq"),
            P(None, "seq", "chan"),
            P(None, "chan", "seq"),
            P("chan", "seq"),
            P("seq"),
            P("seq", "chan"),
            P("seq", "chan"),
            P("chan", "seq"),
        ),
        check_vma=False,
    )
```

```python
import functools

import jax
import jax.numpy as jnp
from jax import lax
from jax.experimental import pallas as pl
from jax.experimental.pallas import tpu as pltpu
from jax.sharding import PartitionSpec as P

epsilon = 1e-05
BF = jnp.bfloat16
F32 = jnp.float32
MESH = pl.DeviceIdType.MESH
LANE = 128
NZ = 4
ROWS_CHUNK = 128
SMALL = 256
ZF_COLS = 1152


def nn(a, b):
    return jnp.dot(a, b, preferred_element_type=F32)


def tn(a, b):
    return lax.dot_general(a, b, (((0,), (0,)), ((), ())), preferred_element_type=F32)


def nt(a, b):
    return lax.dot_general(a, b, (((1,), (1,)), ((), ())), preferred_element_type=F32)


def inv_rms(v):
    return lax.rsqrt(jnp.mean(v * v, axis=-1, keepdims=True) + epsilon)


class Take:
    def __init__(self, limit):
        self.used, self.limit = 0, limit

    def __call__(self, count=1):
        base = self.used
        self.used += count
        assert self.used <= self.limit
        return base


N_SEND, N_RECV, N_LOCAL = 128, 192, 64

SCHEDULE = {
    "dhA": (("end", (1, 0)), ("mid", (0, 2)),),
    "dnD": (("mid", (0, 0)),),
    "nb0": (("end", (3, 0)), ("end", (1, 2)), ("end", (2, 1)),),
    "nb1": (("mid", (0, 1)), ("mid", (3, 0)),),
    "cb": (("end", (2, 0)), ("mid", "pair"),),
    "tail": (("end", (3, 1)), ("mid", (2, 2)), ("mid", (1, 0)),),
    "gc2": (("mid", (2, 0)), ("mid", (1, 1)), ("mid", (3, 1)),),
    "gc3": (("mid", (1, 2)), ("mid", (3, 2)),),
    "blk1": (("end", (1, 1)),),
    "blk3": (("mid", (2, 1)), ("mid", "pair sum"), ("mid", (4, 0)), ("mid", (1, 3)), ("mid", (4, 2)),),
    "dt0": (("end", (4, 0)), ("end", (4, 1)), ("end", (3, 2)), ("end", (2, 2)), ("end", (1, 3)),),
    "dt1": (("end", "pair"), ("mid", (4, 1)), ("mid", (2, 3)),),
    "dt3": (("end", (4, 2)), ("end", (2, 3)), ("end", (3, 3)), ("mid", (3, 3)),),
    "sm": (("end", (4, 3)), ("end", "pair sum"), ("mid", (4, 3)),),
}


def step_kernel(
    dims,
    tokens, gain_mix_hbm, w_in, taps_hbm, w_out, gain_ffn_hbm, w_gate, w_up, w_down, cot,
    block_out, d_tokens, g_ffn, g_conv, small_out,
    gb0, gb1, gb2, gb3, gb4, yb0, yb1, yb2, yb3, yb4, zb0, zb1, zb2, zb3, zb4,
    cr_dh, cr_dn,
    gain_mix, taps, gain_ffn, tok_v, wg_v, wu_v, wd_v, dy_v, h2_v, h1_v, hid, dg, du, pb, pc, px, bx, gated, resid, gall,
    ring, xr_dh, xr_dn, xr_d1, rb, ld, outs, halo_s, halo_r, dhalo_s, dhalo_r, tail, pb_tail, px_tail,
    sm, sm_o, sm_t, sm_r, ss, rs, ls,
):
    R, T, D, CL, FL, FW = dims
    S = R // T
    CH = CL // 2
    GR = D // NZ
    SR = GR // 2
    DR = SR // 2
    NCH = R // ROWS_CHUNK
    take_s, take_r, take_l = Take(N_SEND), Take(N_RECV), Take(N_LOCAL)

    s = lax.axis_index("seq")
    x = lax.axis_index("chan")
    n_seq = 4 * NZ
    z, y, c = s // 4, (s // 2) % 2, s % 2

    def did(z_, y_, c_):
        return ((z_ * 2 + y_) * 2 + c_, x)

    core_dev = did(z, y, 1 - c)
    y_dev = did(z, 1 - y, c)
    x_dev = (s, 1 - x)
    mid = jnp.logical_and(z > 0, z < NZ - 1)
    end = jnp.logical_not(mid)

    def remote(src, dst, si, ri, dev):
        return pltpu.make_async_remote_copy(
            src_ref=src, dst_ref=dst, send_sem=ss.at[si], recv_sem=rs.at[ri],
            device_id=dev, device_id_type=MESH,
        )

    def wait_recv(dst, ri):
        remote(dst, dst, 0, ri, core_dev).wait_recv()

    def wait_send(src, si):
        remote(src, src, si, 0, core_dev).wait_send()

    def local(src, dst, li):
        return pltpu.make_async_copy(src, dst, ls.at[li])

    l_tok, l_win, l_wout, l_dy, l_small = take_l(), take_l(3), take_l(), take_l(), take_l(3)
    ld_tok = local(tokens, tok_v, l_tok)
    ld_tok.start()
    win_views = [wg_v.at[:, pl.ds(0, CL)], wg_v.at[:, pl.ds(CL, CL)], wu_v.at[:, pl.ds(0, CL)]]
    wout_view = wd_v.at[pl.ds(pl.multiple_of(x * CL, CL), CL), :]

    def load_w_in():
        return [local(w_in.at[m], win_views[m], l_win + m) for m in range(3)]

    for cp in load_w_in():
        cp.start()
    ld_small = [
        local(src, dst, l_small + i)
        for i, (src, dst) in enumerate(
            ((gain_mix_hbm, gain_mix), (taps_hbm, taps), (gain_ffn_hbm, gain_ffn))
        )
    ]
    for cp in ld_small:
        cp.start()
    ld_wout = local(w_out, wout_view, l_wout)
    ld_wout.start()
    ld_dy = local(cot, dy_v.at[0], l_dy)

    bar = pltpu.get_barrier_semaphore()

    def greet(dev):
        pl.semaphore_signal(bar, inc=1, device_id=dev, device_id_type=MESH)

    greet(core_dev)
    greet(x_dev)
    others = [(k, did((z + k // 2) % NZ, (y + k % 2) % 2, c)) for k in range(1, 2 * NZ)]
    for _, dev in others:
        greet(dev)
    has_prev = s > 0
    has_next = s < n_seq - 1
    prev_dev = ((s + n_seq - 1) % n_seq, x)
    next_dev = ((s + 1) % n_seq, x)
    greet(prev_dev)
    greet(next_dev)
    pl.semaphore_wait(bar, 3 + 2 * NZ)

    SUBS = 2
    ER = CL // 8
    PR = ER // SUBS
    zi = z % 2
    z_dev = did(z + 1 - 2 * zi, y, c)
    mine_e = zi * 4 + y * 2 + c
    pair_e = zi * 4 + (1 - y) * 2 + c
    line_e = (1 - zi) * 4 + y * 2 + c
    far_e = (1 - zi) * 4 + (1 - y) * 2 + c
    w_sems = {}

    def w_rows(half, eighth, sub):
        return wd_v.at[pl.ds(pl.multiple_of(half * CL + eighth * ER + sub * PR, PR), PR), :]

    def w_copy(name, eighth, sub, dev):
        if (name, sub) not in w_sems:
            w_sems[name, sub] = take_s(), take_r()
        ref = w_rows(1 - x, eighth, sub)
        return remote(ref, ref, *w_sems[name, sub], dev)

    def w_came(name, eighth, sub):
        wait_recv(w_rows(1 - x, eighth, sub), w_sems[name, sub][1])

    def w_over_x(sub):
        if ("x", sub) not in w_sems:
            w_sems["x", sub] = take_s(), take_r()
        src = w_out.at[pl.ds(pl.multiple_of(mine_e * ER + sub * PR, PR), PR), :]
        return remote(src, w_rows(x, mine_e, sub), *w_sems["x", sub], x_dev)

    w_sent = []

    def w_pass(name, eighth, sub, targets):
        w_came(name, eighth, sub)
        for to, dev in targets:
            w_copy(to, eighth, sub, dev).start()
            w_sent.append((to, eighth, sub, dev))

    def w_mine(sub):
        w_pass("x", mine_e, sub, (("z", z_dev), ("y", y_dev), ("core", core_dev)))

    def w_pair(sub):
        to = (("zy", z_dev),) if sub == 0 else ()
        w_pass("y", pair_e, sub, to + (("core pair", core_dev),))

    def w_line(sub):
        to = (("zy", y_dev),) if sub == 1 else ()
        w_pass("z", line_e, sub, to + (("core line", core_dev),))

    def w_far(sub):
        w_pass("zy", far_e, sub, (("core far", core_dev),))

    for sub in range(SUBS):
        w_over_x(sub).start()

    l_w = take_l(3)
    win_start = pl.multiple_of(c * (FL - FW), LANE)
    ld_wg = local(w_gate.at[:, pl.ds(win_start, FW)], wg_v, l_w)
    ld_wu = local(w_up.at[:, pl.ds(win_start, FW)], wu_v, l_w + 1)
    ld_wd = local(w_down.at[pl.ds(win_start, FW), :], wd_v, l_w + 2)

    sm[...] = jnp.zeros_like(sm)
    for cp in ld_small:
        cp.wait()
    gain_mix_row = gain_mix[...].reshape(1, D)
    gain_ffn_row = gain_ffn[...].reshape(1, D)
    k_taps = [taps[t : t + 1, :] for t in range(3)]

    ld_tok.wait()

    CPS = T // ROWS_CHUNK
    NC = CL // 256
    s_h1, r_h1 = take_s(S), take_r(S)
    s_ha, r_ha = take_s(S), take_r(S)
    s_mx, r_mx = take_s(NCH), take_r(NCH)
    row_iota = lax.broadcasted_iota(jnp.int32, (T, 256), 0)
    top_iota = row_iota[0:16]

    def conv_terms(now, h, iota):
        h14 = jnp.broadcast_to(h[14:15], now.shape)
        h15 = jnp.broadcast_to(h[15:16], now.shape)
        one = jnp.where(iota == 0, h15, pltpu.roll(now, 1, 0))
        two = jnp.where(iota == 0, h14, jnp.where(iota == 1, h15, pltpu.roll(now, 2, 0)))
        return now, one, two

    def tap_cols(cols):
        return [taps[t : t + 1, cols] for t in range(3)]

    def convolve(terms, cols):
        now, one, two = terms
        k0, k1, k2 = tap_cols(cols)
        return k0 * two + k1 * one + k2 * now

    def h1_send(q):
        rows = pl.ds(q * T, T)
        return remote(h1_v.at[0, rows], h1_v.at[1, rows], s_h1 + q, r_h1 + q, core_dev)

    def halo_send(q):
        return remote(halo_s.at[q], halo_r.at[q], s_ha + q, r_ha + q, next_dev)

    own_cols = pl.ds(pl.multiple_of(x * CL, CL), CL)
    other_cols = pl.ds(pl.multiple_of((1 - x) * CL, CL), CL)

    def gated_send(k):
        ref = gall.at[k, :, own_cols]
        return remote(ref, ref, s_mx + k, r_mx + k, x_dev)

    def mixer_out(k):
        gall[k, :, own_cols] = gated[k * ROWS_CHUNK : (k + 1) * ROWS_CHUNK, :]
        gated_send(k).start()

    for q in range(S):
        rows = pl.ds(q * T, T)

        def norm_rows(k, _, q=q):
            chunk = pl.ds(pl.multiple_of(q * T + k * ROWS_CHUNK, ROWS_CHUNK), ROWS_CHUNK)
            xv = tok_v[chunk, :].astype(F32)
            h1_v[0, chunk, :] = (xv * inv_rms(xv) * gain_mix_row).astype(BF)
            return 0

        lax.fori_loop(0, CPS, norm_rows, 0)
        if q == 0:
            for cp in load_w_in():
                cp.wait()

        def in_proj(j, _, q=q, rows=rows):
            cols = pl.ds(pl.multiple_of(j * 256, 256), 256)
            cols1 = pl.ds(pl.multiple_of(CL + j * 256, 256), 256)
            h = h1_v[0, rows, :]
            b = nn(h, wg_v[:, cols])
            pb[rows, cols] = b.astype(BF)
            xx = nn(h, wu_v[:, cols])
            px[rows, cols] = xx.astype(BF)
            inner = (b * xx).astype(BF)
            bx[rows, cols] = inner
            halo_s[q, :, cols] = inner[T - 16 : T]
            pcv = nn(h, wg_v[:, cols1])
            pc[rows, cols] = pcv.astype(BF)
            now = inner.astype(F32)
            cv = convolve(conv_terms(now, jnp.zeros_like(now[0:16]), row_iota), cols)
            gated[rows, cols] = (pcv * cv).astype(BF)
            return 0

        lax.fori_loop(0, NC, in_proj, 0)
        if q == S - 1:
            ld_wg.start()
            ld_wu.start()

        @pl.when(has_next)
        def _(q=q):
            halo_send(q).start()

        for k in range(CPS - 1, 0, -1):
            mixer_out(q * CPS + k)
        if q > 0:
            w_mine(1)

        @pl.when(has_prev)
        def _(q=q):
            wait_recv(halo_r.at[q], r_ha + q)

        @pl.when(jnp.logical_not(has_prev))
        def _(q=q):
            halo_r[q] = jnp.zeros_like(halo_r[q])

        def conv_top(j, _, q=q):
            cols = pl.ds(pl.multiple_of(j * 256, 256), 256)
            top = pl.ds(q * T, 16)
            now = bx[top, cols].astype(F32)
            cv = convolve(conv_terms(now, halo_r[q, :, cols].astype(F32), top_iota), cols)
            gated[top, cols] = (pc[top, cols].astype(F32) * cv).astype(BF)
            return 0

        lax.fori_loop(0, NC, conv_top, 0)
        mixer_out(q * CPS)
        if q == 0:
            w_mine(0)
        h1_send(q).start()
        if q == 0:
            ld_dy.start()
            s_dy, r_dy = take_s(), take_r()
            send_dy = remote(cot, dy_v.at[1], s_dy, r_dy, core_dev)
            send_dy.start()
    w_line(0)
    w_pair(0)
    w_line(1)
    w_pair(1)

    s_h2, r_h2 = take_s(NCH), take_r(NCH)
    ld_wg.wait()
    ld_wu.wait()
    NF = FW // 256
    overlap = 2 * FW - FL
    col_iota = lax.broadcasted_iota(jnp.int32, (2 * ROWS_CHUNK, 256), 1)

    def sent(n):
        return (n // CPS) * CPS + (CPS - 1 - n % CPS)

    def residual_chunk(k):
        rows = pl.ds(pl.multiple_of(k * ROWS_CHUNK, ROWS_CHUNK), ROWS_CHUNK)
        wait_recv(gall.at[k, :, other_cols], r_mx + k)

        def out_tile(j, _):
            cols = pl.ds(pl.multiple_of(j * 512, 512), 512)
            resid[rows, cols] = tok_v[rows, cols].astype(F32) + nn(gall[k], wd_v[0 : 2 * CL, cols])
            return 0

        lax.fori_loop(0, D // 512, out_tile, 0, unroll=True)
        res = resid[rows, :]
        h2_v[0, rows, :] = (res * inv_rms(res) * gain_ffn_row).astype(BF)
        remote(h2_v.at[0, rows], h2_v.at[1, rows], s_h2 + k, r_h2 + k, core_dev).start()

    def forward_chunk(k):
        rows = pl.ds(pl.multiple_of(k * ROWS_CHUNK, ROWS_CHUNK), ROWS_CHUNK)
        wait_recv(h2_v.at[1, rows], r_h2 + k)

        def tile(j, _):
            cols = pl.ds(pl.multiple_of(j * 256, 256), 256)
            h = h2_v[:, rows, :].reshape(2 * ROWS_CHUNK, D)
            g = nn(h, wg_v[:, cols])
            u = nn(h, wu_v[:, cols])
            keep = col_iota + j * 256 >= c * overlap
            sg = jax.nn.sigmoid(g)
            si = jnp.where(keep, g * sg, 0.0)
            shape = (2, ROWS_CHUNK, 256)
            hid[:, rows, cols] = (si * u).astype(BF).reshape(shape)
            slope = jnp.where(keep, u * sg * (1.0 + g * (1.0 - sg)), 0.0)
            dg[:, rows, cols] = slope.astype(BF).reshape(shape)
            du[:, rows, cols] = si.astype(BF).reshape(shape)
            return 0

        lax.fori_loop(0, NF, tile, 0, unroll=True)

    for sub in range(SUBS):
        w_far(sub)
    ld_wout.wait()
    for sub in range(SUBS):
        for name, eighth in (("core", mine_e), ("core pair", pair_e), ("core line", line_e), ("core far", far_e)):
            w_came(name, eighth + 1 - 2 * c, sub)
    residual_chunk(sent(0))

    def chunk_loop(n, _):
        @pl.when(n + 1 < NCH)
        def _():
            residual_chunk(sent(n + 1))

        forward_chunk(sent(n))
        return 0

    lax.fori_loop(0, NCH, chunk_loop, 0)
    for sub in range(SUBS):
        w_over_x(sub).wait_send()
    for item in w_sent:
        w_copy(*item).wait_send()
    ld_wd.start()
    ld_dy.wait()
    send_dy.wait()
    for k in range(NCH):
        gated_send(k).wait_send()
        wait_send(h2_v.at[0, pl.ds(k * ROWS_CHUNK, ROWS_CHUNK)], s_h2 + k)

    gbs = [gb0, gb1, gb2, gb3, gb4]
    ybs = [yb0, yb1, yb2, yb3, yb4]
    zbs = [zb0, zb1, zb2, zb3, zb4]
    widths = [ZF_COLS, FW - ZF_COLS, FW, FW, 2 * CL]
    s_y = [None] + [take_s(NZ) for _ in range(4)]
    r_y = [None] + [take_r(NZ) for _ in range(4)]
    s_z = [take_s(2 * NZ)] + [take_s(NZ) for _ in range(4)]
    r_z = [take_r(4 * NZ)] + [take_r(2 * NZ) for _ in range(4)]

    def order(e):
        if e == NZ - 1:
            return z
        per_z = {0: (3, 2, 1), 1: (3, 0, 2), 2: (0, 3, 1), 3: (0, 1, 2)}
        v = per_z[3][e]
        for zz in range(3):
            v = jnp.where(z == zz, per_z[zz][e], v)
        return v

    def order_dyn(u):
        v = order(NZ - 1)
        for e in range(NZ - 1):
            v = jnp.where(u == e, order(e), v)
        return v

    def per_core(j, act):
        if j in (1, 4):
            act(lambda ref: ref)
            return

        @pl.when(c == 0)
        def _():
            act(lambda ref: ref)

        @pl.when(c == 1)
        def _():
            act(lambda ref: ref.at[:, pl.ds(overlap, widths[j] - overlap)])

    def z_send(j, src, e, zp, h=None):
        to_right = zp > z
        d = jnp.where(to_right, 0, 1)
        dev = did(jnp.clip(jnp.where(to_right, z + 1, z - 1), 0, NZ - 1), y, c)
        if h is None:
            dst, si, ri = zbs[j].at[d, zp], s_z[j] + e, r_z[j] + d * NZ + zp
        else:
            dst, si, ri = zbs[j].at[d, zp, h], s_z[j] + 2 * e + h, r_z[j] + (d * NZ + zp) * 2 + h
        per_core(j, lambda cut: remote(cut(src), cut(dst), si, ri, dev).start())

    l_g = take_l(12)

    def y_send(j, u):
        zp = order_dyn(u) if not isinstance(u, int) else order(u)
        src, dst = gbs[j].at[zp, 1 - y], ybs[j].at[zp]
        per_core(j, lambda cut: remote(cut(src), cut(dst), s_y[j] + u, r_y[j] + u, y_dev).start())

    def g_block(lhs_ref, rhs_ref, zp, pair, parts=(0, 1)):
        lhs = lhs_ref[:, :, pl.ds(pl.multiple_of(zp * GR, GR), GR)].reshape(2 * R, GR)
        cut = -(-FW // 512) * 256
        for n in parts:
            cols = slice(0, cut) if n == 0 else slice(cut, FW)
            v = tn(lhs, rhs_ref[:, :, cols].reshape(2 * R, cols.stop - cols.start)).astype(BF)
            outs[2 * pair, :, cols] = v[:SR]
            outs[2 * pair + 1, :, cols] = v[SR:]

    def down_copies(zp, pair):
        return [
            cp
            for h in range(2)
            for cp in (
                local(outs.at[2 * pair + h, :, pl.ds(0, ZF_COLS)], gb0.at[zp, h], l_g + 4 * pair + 2 * h),
                local(
                    outs.at[2 * pair + h, :, pl.ds(ZF_COLS, FW - ZF_COLS)],
                    gb1.at[zp, h], l_g + 4 * pair + 2 * h + 1,
                ),
            )
        ]

    def down_sends(u):
        zp = order(u)
        for cp in down_copies(zp, u % 2):
            cp.wait()
        if u < NZ - 1:

            @pl.when(end)
            def _():
                for h in range(2):
                    z_send(0, gb0.at[zp, h], u, zp, h)

            y_send(1, u)

    for u in range(NZ):
        g_block(dy_v, hid, order(u), u % 2, (0,))
        if u > 0:
            down_sends(u - 1)
        g_block(dy_v, hid, order(u), u % 2, (1,))
        for cp in down_copies(order(u), u % 2):
            cp.start()
    down_sends(NZ - 1)

    ld_wd.wait()

    def hid_back(slot, _):
        for j in range(NF):
            cols = slice(j * 256, (j + 1) * 256)
            dh = nt(dy_v[slot], wd_v[cols, :])
            dg[slot, :, cols] = (dh * dg[slot, :, cols].astype(F32)).astype(BF)
            du[slot, :, cols] = (dh * du[slot, :, cols].astype(F32)).astype(BF)
        return 0

    lax.fori_loop(0, 2, hid_back, 0)

    def plain_copies(gb, zp, pair):
        return [local(outs.at[2 * pair + h], gb.at[zp, h], l_g + 2 * pair + h) for h in range(2)]

    def gate_up(u, _):
        zp = order_dyn(u)

        def up_sends(u):
            for cp in plain_copies(gb3, order_dyn(u), 1):
                cp.wait()

            @pl.when(u < 2)
            def _():
                y_send(3, u)

        g_block(h2_v, dg, zp, 0, (0,))

        @pl.when(u > 0)
        def _():
            up_sends(u - 1)

        g_block(h2_v, dg, zp, 0, (1,))
        for cp in plain_copies(gb2, zp, 0):
            cp.start()
        g_block(h2_v, du, zp, 1, (0,))
        for cp in plain_copies(gb2, zp, 0):
            cp.wait()

        @pl.when(u < 3)
        def _():
            y_send(2, u)

        g_block(h2_v, du, zp, 1, (1,))
        for cp in plain_copies(gb3, zp, 1):
            cp.start()
        return 0

    lax.fori_loop(0, NZ, gate_up, 0)
    for cp in plain_copies(gb3, order(NZ - 1), 1):
        cp.wait()

    l_e = take_l(4)
    is_role = {"end": end, "mid": mid}
    slot_last = {role: [None] * outs.shape[0] for role in is_role}
    slot_next = {role: 0 for role in is_role}

    def claim_slot(role):
        o = slot_next[role]
        slot_next[role] = (o + 1) % outs.shape[0]
        if slot_last[role][o] is not None:
            slot_last[role][o]()
            slot_last[role][o] = None
        return o

    ADD_ROWS = 32

    def add_into(dst, srcs):
        def rows_add(k, _):
            rows = pl.ds(pl.multiple_of(k * ADD_ROWS, ADD_ROWS), ADD_ROWS)
            acc = srcs[0][rows, :].astype(F32)
            for src in srcs[1:]:
                acc = acc + src[rows, :].astype(F32)
            dst[rows, :] = acc.astype(BF)
            return 0

        lax.fori_loop(0, SR // ADD_ROWS, rows_add, 0)

    def fetch(j, srcs):
        w = widths[j]
        views, copies = [], []
        for i, (src, ri) in enumerate(srcs):
            if ri is not None:
                per_core(j, lambda cut: wait_recv(cut(src), ri))
            views.append(ld.at[i, :, pl.ds(0, w)])
            copies.append(local(src, views[-1], l_e + i))
            copies[-1].start()
        for cp in copies:
            cp.wait()
        return views

    def from_line(j, d, zp, h=None):
        if h is None:
            return zbs[j].at[d, zp], r_z[j] + d * NZ + zp
        return zbs[j].at[d, zp, h], r_z[j] + (d * NZ + zp) * 2 + h

    def line_event(role, j, e):
        @pl.when(is_role[role])
        def _():
            zp = order(e)
            w = widths[j]
            d = jnp.where(zp > z, 0, 1)
            for h in (0, 1) if j == 0 else (None,):
                o = claim_slot(role)
                dst = outs.at[o, :, pl.ds(0, w)]
                if h is None:
                    srcs = [(gbs[j].at[zp, y], None), (ybs[j].at[zp], r_y[j] + e)]
                    si = s_z[j] + e
                else:
                    srcs = [(gbs[j].at[zp, h], None)]
                    si = s_z[j] + 2 * e + h
                if role == "mid":
                    srcs.append(from_line(j, d, zp, h))
                add_into(dst, fetch(j, srcs))
                z_send(j, dst, e, zp, h)
                slot_last[role][o] = functools.partial(sent_slot, j, o, si)

    def sent_slot(j, o, si):
        per_core(j, lambda cut: wait_send(cut(outs.at[o, :, pl.ds(0, widths[j])]), si))

    def own_shard(role, j, h=None):
        if h is None:
            srcs = [(gbs[j].at[z, y], None), (ybs[j].at[z], r_y[j] + NZ - 1)]
        else:
            srcs = [(gbs[j].at[z, h], None)]
        if role == "mid":
            return srcs + [from_line(j, 0, z, h), from_line(j, 1, z, h)]
        return srcs + [from_line(j, jnp.where(z == 0, 1, 0), z, h)]

    def swap_pieces(j):
        if j == 4:
            return [(None, m * CH, CH, g_conv.at[m], c * CH) for m in range(4)]
        mat = g_ffn.at[{0: 0, 1: 0, 2: 1, 3: 2}[j]]
        w = widths[j]
        if j == 1:
            return [(None, 0, w, mat, c * (FL - FW) + ZF_COLS)]
        return [(0, 0, w, mat, 0), (1, overlap, w - overlap, mat, FL - FW + overlap)]

    swap_sems = [[(take_s(), take_r(), take_l()) for _ in swap_pieces(j)] for j in range(5)]

    def swap(j, o):
        items = []
        for (core, c0, w, mat, to), (si, ri, li) in zip(swap_pieces(j), swap_sems[j]):
            to = to if isinstance(to, int) else pl.multiple_of(to, LANE)
            target = mat.at[:, pl.ds(to, w)]
            mine = outs.at[o, pl.ds(pl.multiple_of(c * DR, DR), DR), pl.ds(c0, w)]
            other = outs.at[o, pl.ds(pl.multiple_of((1 - c) * DR, DR), DR), pl.ds(c0, w)]
            items.append((core, local(mine, target, li), remote(other, target, si, ri, core_dev), target))
        return items

    def swap_start(j, o):
        for core, keep, give, _ in swap(j, o):
            if core is None:
                keep.start()
                give.start()
            else:

                @pl.when(c == core)
                def _():
                    keep.start()
                    give.start()

    def swap_finish(j, o):
        for (core, keep, give, target), (_, ri, _) in zip(swap(j, o), swap_sems[j]):
            if core is None:
                keep.wait()
                give.wait_send()
                wait_recv(target, ri)
            else:

                @pl.when(c == core)
                def _():
                    keep.wait()
                    give.wait_send()

                @pl.when(c != core)
                def _():
                    wait_recv(target, ri)

    def final_event(role, j):
        @pl.when(is_role[role])
        def _():
            o = claim_slot(role)
            w = widths[j]
            add_into(outs.at[o, :, pl.ds(0, w)], fetch(j, own_shard(role, j)))
            swap_start(j, o)
            slot_last[role][o] = functools.partial(swap_finish, j, o)

    s_f0, r_f0 = take_s(), take_r()
    w0 = widths[0]

    def final0_send(role):
        @pl.when(is_role[role])
        def _():
            o = claim_slot(role)
            dst = outs.at[o, :, pl.ds(0, w0)]
            add_into(dst, fetch(0, own_shard(role, 0, 1 - y)))
            cp = local(dst, gb0.at[z, 1 - y], l_e)
            cp.start()
            cp.wait()
            src = gb0.at[z, 1 - y]
            per_core(0, lambda cut: remote(cut(src), cut(yb0), s_f0, r_f0, y_dev).start())

    def final0_finish(role):
        @pl.when(is_role[role])
        def _():
            o = claim_slot(role)
            dst = outs.at[o, :, pl.ds(0, w0)]
            add_into(dst, fetch(0, own_shard(role, 0, y)))
            add_into(dst, [dst] + fetch(0, [(yb0, r_f0)]))
            swap_start(0, o)
            slot_last[role][o] = functools.partial(swap_finish, 0, o)

    def hook(name):
        for role, event in SCHEDULE.get(name, ()):
            if event == "pair":
                final0_send(role)
            elif event == "pair sum":
                final0_finish(role)
            elif event[1] == NZ - 1:
                final_event(role, event[0])
            else:
                line_event(role, *event)

    def chunks(name, count, body):
        first = 0
        for k in range(count):
            if SCHEDULE.get(name + str(k)) or k == count - 1:
                lax.fori_loop(first, k + 1, body, 0)
                first = k + 1
                hook(name + str(k))

    HALF = 2 * ROWS_CHUNK

    def split_sum(name, product, cr, xr, base_d):
        s_c, r_c = take_s(2), take_r(2)
        s_x, r_x = take_s(NCH), take_r(NCH)
        l_c = take_l()

        def give(k, _):
            def tile(n, _):
                cols = pl.ds(pl.multiple_of(n * 512, 512), 512)
                v = product(1, k * HALF, n).astype(BF)
                gall[pl.ds(2 * k, 2), :, cols] = v.reshape(2, ROWS_CHUNK, 512)
                return 0

            lax.fori_loop(0, D // 512, tile, 0)
            remote(
                gall.at[pl.ds(2 * k, 2)], cr.at[pl.ds(2 * k, 2)], s_c + k, r_c + k, core_dev
            ).start()
            return 0

        lax.fori_loop(0, 2, give, 0)
        hook(name + "A")

        def keep(k, _):
            src = cr.at[pl.ds(2 * k, 2)]
            wait_recv(src, r_c + k)
            cp = local(src, rb, l_c)
            cp.start()
            cp.wait()

            def tile(n, _):
                cols = pl.ds(pl.multiple_of(n * 512, 512), 512)
                v = product(0, k * HALF, n) + rb[:, :, cols].reshape(HALF, 512).astype(F32)
                ring[pl.ds(base_d + 2 * k, 2), :, cols] = v.astype(BF).reshape(2, ROWS_CHUNK, 512)
                return 0

            lax.fori_loop(0, D // 512, tile, 0)
            for i in range(2):
                remote(
                    ring.at[base_d + 2 * k + i], xr.at[2 * k + i], s_x + 2 * k + i, r_x + 2 * k + i, x_dev
                ).start()
            return 0

        lax.fori_loop(0, 2, keep, 0)
        for k in range(2):
            wait_send(gall.at[pl.ds(2 * k, 2)], s_c + k)
        hook(name + "D")
        return s_x, r_x

    def rows_at(ref, slot, r0):
        return ref[slot, pl.ds(pl.multiple_of(r0, HALF), HALF), :]

    def dh_product(slot, r0, n):
        cols = pl.ds(pl.multiple_of(n * 512, 512), 512)
        return nt(rows_at(dg, slot, r0), wg_v[cols, :]) + nt(rows_at(du, slot, r0), wu_v[cols, :])

    def dn_product(slot, r0, n):
        cols = pl.ds(pl.multiple_of(n * 512, 512), 512)
        return nn(rows_at(hid, slot, r0), wd_v[:, cols])

    s_xdh, r_xdh = split_sum("dh", dh_product, cr_dh, xr_dh, 0)
    s_xdn, r_xdn = split_sum("dn", dn_product, cr_dn, xr_dn, 4)
    for cp in load_w_in():
        cp.start()
    ld_wout = local(w_out, wd_v.at[pl.ds(0, CL), :], l_wout)
    ld_wout.start()

    s_do, r_do = take_s(NCH), take_r(NCH)

    def ffn_norm_back(k, _):
        rows = pl.ds(pl.multiple_of(k * ROWS_CHUNK, ROWS_CHUNK), ROWS_CHUNK)
        wait_recv(xr_dh.at[k], r_xdh + k)
        d_h = ring[k].astype(F32) + xr_dh[k].astype(F32)
        res = resid[rows, :]
        s2 = inv_rms(res)
        n2 = res * s2
        sm[0, 1:2, :] += jnp.sum(d_h * n2, axis=0, keepdims=True)
        e2 = d_h * gain_ffn_row
        d_res = dy_v[0, rows, :].astype(F32) + s2 * (
            e2 - n2 * jnp.mean(e2 * n2, axis=-1, keepdims=True)
        )
        h2_v[0, rows, :] = d_res.astype(BF)
        remote(h2_v.at[0, rows], h2_v.at[1, rows], s_do + k, r_do + k, core_dev).start()
        return 0

    chunks("nb", NCH, ffn_norm_back)
    for k in range(NCH):
        wait_send(ring.at[k], s_xdh + k)

    for cp in load_w_in():
        cp.wait()
    ld_wout.wait()
    for q in range(S):

        def conv_back(j, _, q=q):
            cols = pl.ds(pl.multiple_of(j * 256, 256), 256)
            rows = pl.ds(q * T, T)
            now, one, two = conv_terms(
                bx[rows, cols].astype(F32), halo_r[q, :, cols].astype(F32), row_iota
            )
            k0, k1, k2 = tap_cols(cols)
            cv = k0 * two + k1 * one + k2 * now
            d_g = nt(h2_v[0, q * T : q * T + T, :], wd_v[cols, :])
            d_cv = d_g * pc[rows, cols].astype(F32)
            sm[0, 2:3, cols] += jnp.sum(d_cv * two, axis=0, keepdims=True)
            sm[0, 3:4, cols] += jnp.sum(d_cv * one, axis=0, keepdims=True)
            sm[0, 4:5, cols] += jnp.sum(d_cv * now, axis=0, keepdims=True)
            after1 = jnp.where(row_iota < T - 1, pltpu.roll(d_cv, T - 1, 0), 0.0)
            after2 = jnp.where(row_iota < T - 2, pltpu.roll(d_cv, T - 2, 0), 0.0)
            d_bx = k2 * d_cv + k1 * after1 + k0 * after2
            dhalo_s[q, :, cols] = d_cv[0:8]
            tail[q, :, cols] = d_bx[T - 16 : T]
            old_b = pb[rows, cols]
            old_x = px[rows, cols]
            pb_tail[q, :, cols] = old_b[T - 16 : T]
            px_tail[q, :, cols] = old_x[T - 16 : T]
            low = d_bx.astype(BF).astype(F32)
            pb[rows, cols] = (low * old_x.astype(F32)).astype(BF)
            px[rows, cols] = (low * old_b.astype(F32)).astype(BF)
            pc[rows, cols] = (d_g * cv).astype(BF)
            return 0

        lax.fori_loop(0, NC, conv_back, 0)

    s_dha, r_dha = take_s(), take_r()
    send_dhalo = remote(dhalo_s, dhalo_r, s_dha, r_dha, prev_dev)

    @pl.when(has_prev)
    def _():
        send_dhalo.start()

    y_send(3, 2)

    hook("cb")

    s_x1, r_x1 = take_s(NCH), take_r(NCH)

    def d1_part(name, ids):
        def tile(n, _):
            cols = pl.ds(pl.multiple_of(n * 512, 512), 512)

            def rows_of(ref):
                return jnp.concatenate(
                    [ref[k * ROWS_CHUNK : (k + 1) * ROWS_CHUNK, :] for k in ids], axis=0
                )

            v = (
                nt(rows_of(pb), wg_v[cols, 0:CL])
                + nt(rows_of(pc), wg_v[cols, CL : 2 * CL])
                + nt(rows_of(px), wu_v[cols, 0:CL])
            ).astype(BF)
            for i, k in enumerate(ids):
                ring[k, :, cols] = v[i * ROWS_CHUNK : (i + 1) * ROWS_CHUNK]
            return 0

        lax.fori_loop(0, D // 512, tile, 0)
        for k in ids:
            remote(ring.at[k], xr_d1.at[k], s_x1 + k, r_x1 + k, x_dev).start()
        hook(name)

    d1_part("d1a", [q * CPS + k for q in range(S) for k in range(CPS - 1)])

    @pl.when(has_next)
    def _():
        wait_recv(dhalo_r, r_dha)

    @pl.when(jnp.logical_not(has_next))
    def _():
        dhalo_r[...] = jnp.zeros_like(dhalo_r)

    tail_iota = lax.broadcasted_iota(jnp.int32, (16, CL), 0)
    for q in range(S):
        first = jnp.broadcast_to(dhalo_r[q, 0:1, :], (16, CL))
        second = jnp.broadcast_to(dhalo_r[q, 1:2, :], (16, CL))
        fix = jnp.where(
            tail_iota == 14,
            k_taps[0] * first,
            jnp.where(tail_iota == 15, k_taps[1] * first + k_taps[0] * second, 0.0),
        )
        low = (tail[q] + fix).astype(BF).astype(F32)
        rows = pl.ds(q * T + T - 16, 16)
        pb[rows, :] = (low * px_tail[q].astype(F32)).astype(BF)
        px[rows, :] = (low * pb_tail[q].astype(F32)).astype(BF)

    s_dp, r_dp = take_s(4), take_r(4)
    theirs = pl.ds(pl.multiple_of((1 - c) * CH, LANE), CH)
    ours = pl.ds(pl.multiple_of(c * CH, LANE), CH)
    dp_sends = [
        remote(ref.at[:, theirs], dy_v.at[1, :, pl.ds(m * CH, CH)], s_dp + m, r_dp + m, core_dev)
        for m, ref in enumerate((pb, pc, px, gated))
    ]
    for cp in dp_sends:
        cp.start()
    hook("tail")

    d1_part("d1b", [q * CPS + k for q in range(S) for k in range(1, CPS)])

    for q in range(S):
        wait_recv(h1_v.at[1, pl.ds(q * T, T)], r_h1 + q)
    for k in range(NCH):
        rows = pl.ds(k * ROWS_CHUNK, ROWS_CHUNK)
        wait_recv(h2_v.at[1, rows], r_do + k)
    for m in range(4):
        wait_recv(dy_v.at[1, :, pl.ds(m * CH, CH)], r_dp + m)
    W4 = widths[4]
    g4 = [dg.at[i, pl.ds(k * SR, SR), pl.ds(0, W4)] for i in range(2) for k in range(2)]

    def g_mixer(u, _):
        zp = order_dyn(u)
        zc = pl.ds(pl.multiple_of(zp * GR, GR), GR)
        for m, (mine, lhs) in enumerate(((pb, h1_v), (pc, h1_v), (px, h1_v), (gated, h2_v))):
            v = tn(lhs[0, :, zc], mine[:, ours]) + tn(
                lhs[1, :, zc], dy_v[1, :, m * CH : (m + 1) * CH]
            )
            v = v.astype(BF)
            g4[0][:, m * CH : (m + 1) * CH] = v[:SR]
            g4[1][:, m * CH : (m + 1) * CH] = v[SR:]
        cps = [local(g4[h], gb4.at[zp, h], l_g + h) for h in range(2)]
        for cp in cps:
            cp.start()
        for cp in cps:
            cp.wait()

        @pl.when(u < NZ - 1)
        def _():
            y_send(4, u)

        return 0

    chunks("gc", NZ, g_mixer)
    for j in (1, 2, 3, 4):
        y_send(j, NZ - 1)

    l_o = take_l(2)

    def put_rows(v, out, rows, n):
        slot = n % 2
        cp = local(rb.at[slot], out.at[rows, :], l_o + slot)

        @pl.when(n >= 2)
        def _():
            cp.wait()

        rb[slot] = v
        cp.start()

    def put_done(out):
        for slot in range(2):
            local(rb.at[slot], out.at[pl.ds(0, ROWS_CHUNK), :], l_o + slot).wait()

    def block_chunk(k, _):
        rows = pl.ds(pl.multiple_of(k * ROWS_CHUNK, ROWS_CHUNK), ROWS_CHUNK)
        wait_recv(xr_dn.at[k], r_xdn + k)
        total = ring[4 + k].astype(F32) + xr_dn[k].astype(F32)
        put_rows((resid[rows, :] + total).astype(BF), block_out, rows, k)
        return 0

    chunks("blk", NCH, block_chunk)
    put_done(block_out)

    def mix_norm_back(n, _):
        k = (n % S) * CPS + n // S
        rows = pl.ds(pl.multiple_of(k * ROWS_CHUNK, ROWS_CHUNK), ROWS_CHUNK)
        wait_recv(xr_d1.at[k], r_x1 + k)
        d_h = ring[k].astype(F32) + xr_d1[k].astype(F32)
        xv = tok_v[rows, :].astype(F32)
        s1 = inv_rms(xv)
        n1 = xv * s1
        sm[0, 0:1, :] += jnp.sum(d_h * n1, axis=0, keepdims=True)
        e1 = d_h * gain_mix_row
        out = h2_v[0, rows, :].astype(F32) + s1 * (
            e1 - n1 * jnp.mean(e1 * n1, axis=-1, keepdims=True)
        )
        put_rows(out.astype(BF), d_tokens, rows, n)
        return 0

    chunks("dt", NCH, mix_norm_back)
    put_done(d_tokens)

    s_sm, r_sm = take_s(2 * NZ), take_r(2 * NZ)
    a = remote(sm.at[0], sm_o, s_sm, r_sm, core_dev)
    a.start()
    a.wait()
    chip_sum = sm[0] + sm_o[...]
    gain_w, tap_w = 2 * D // n_seq, 2 * CL // n_seq
    is_gain = lax.broadcasted_iota(jnp.int32, sm_t.shape[1:], 0) < 2
    for q in range(2 * NZ):
        gains = pltpu.roll(chip_sum, (D - q * gain_w) % D, 1)[:, 0:SMALL]
        tap_sums = pltpu.roll(chip_sum, (D - q * tap_w) % D, 1)[:, 0:SMALL]
        sm_t[q] = jnp.where(is_gain, gains, tap_sums)
    for k, dev in others:
        remote(sm_t.at[dev[0] // 2], sm_r.at[k], s_sm + k, r_sm + k, dev).start()
    hook("sm")

    total = sm_t[s // 2]
    for k, _ in others:
        wait_recv(sm_r.at[k], r_sm + k)
        total = total + sm_r[k]
    for k, _ in others:
        wait_send(sm_t.at[0], s_sm + k)
    sm_r[0] = total
    out_small = local(sm_r.at[0], small_out, l_small)
    out_small.start()
    out_small.wait()

    for role, cond in is_role.items():

        @pl.when(cond)
        def _(role=role):
            for finish in slot_last[role]:
                if finish is not None:
                    finish()

    @pl.when(end)
    def _():
        for e in range(NZ - 1):
            for h in range(2):
                per_core(0, lambda cut: wait_send(cut(gb0.at[0, h]), s_z[0] + 2 * e + h))

    for j in range(1, 5):
        for u in range(NZ):
            per_core(j, lambda cut: wait_send(cut(ybs[j].at[0]), s_y[j] + u))
    per_core(0, lambda cut: wait_send(cut(yb0), s_f0))
    for q in range(S):
        h1_send(q).wait_send()
    for k in range(NCH):
        wait_send(h2_v.at[0, pl.ds(k * ROWS_CHUNK, ROWS_CHUNK)], s_do + k)
        wait_send(ring.at[k], s_x1 + k)
        wait_send(ring.at[4 + k], s_xdn + k)
    for cp in dp_sends:
        cp.wait_send()

    @pl.when(has_next)
    def _():
        for q in range(S):
            halo_send(q).wait_send()

    @pl.when(has_prev)
    def _():
        send_dhalo.wait_send()


def fused_body(tokens, gain_mix, w_in, kernel, w_out, gain_ffn, w_gate, w_up, w_down, cotangent):
    S, T, D = tokens.shape
    CL = w_out.shape[0]
    FL = w_gate.shape[1]
    R = S * T
    n_seq = lax.axis_size("seq")
    tiles = FL // LANE
    FW = -(-tiles // 2) * LANE
    GR = D // NZ
    SR = GR // 2
    DR = SR // 2
    widths = [ZF_COLS, FW - ZF_COLS, FW, FW, 2 * CL]
    NCH = R // ROWS_CHUNK

    def sds(shape, dtype=BF):
        return jax.ShapeDtypeStruct(shape, dtype)

    outs = [sds((R, D)), sds((R, D)), sds((3, DR, FL)), sds((4, DR, CL)), sds((8, SMALL), F32)]
    outs += [sds((NZ, 2, SR, w)) for w in widths]
    outs += [sds((SR, widths[0]))] + [sds((NZ, SR, w)) for w in widths[1:]]
    outs += [sds((2, NZ, 2, SR, widths[0]))] + [sds((2, NZ, SR, w)) for w in widths[1:]]
    outs += [sds((NCH, ROWS_CHUNK, D))] * 2
    any_spec = pl.BlockSpec(memory_space=pl.ANY)
    V = pltpu.VMEM
    scratch = [
        V((D,), F32),
        V((3, CL), F32),
        V((D,), F32),
        V((R, D), BF),
        V((D, FW), BF),
        V((D, FW), BF),
        V((FW, D), BF),
        V((2, R, D), BF),
        V((2, R, D), BF),
        V((2, R, D), BF),
        V((2, R, FW), BF),
        V((2, R, FW), BF),
        V((2, R, FW), BF),
        V((R, CL), BF),
        V((R, CL), BF),
        V((R, CL), BF),
        V((R, CL), BF),
        V((R, CL), BF),
        V((R, D), F32),
        V((NCH, ROWS_CHUNK, D), BF),
        V((8, ROWS_CHUNK, D), BF),
        V((NCH, ROWS_CHUNK, D), BF),
        V((NCH, ROWS_CHUNK, D), BF),
        V((NCH, ROWS_CHUNK, D), BF),
        V((2, ROWS_CHUNK, D), BF),
        V((4, SR, FW), BF),
        V((4, SR, FW), BF),
        V((S, 16, CL), BF),
        V((S, 16, CL), BF),
        V((S, 8, CL), F32),
        V((S, 8, CL), F32),
        V((S, 16, CL), F32),
        V((S, 16, CL), BF),
        V((S, 16, CL), BF),
        V((1, 8, D), F32),
        V((8, D), F32),
        V((2 * NZ, 8, SMALL), F32),
        V((2 * NZ, 8, SMALL), F32),
        pltpu.SemaphoreType.DMA((N_SEND,)),
        pltpu.SemaphoreType.DMA((N_RECV,)),
        pltpu.SemaphoreType.DMA((N_LOCAL,)),
    ]
    flops = 2 * R * D * (4 * CL + 3 * FL) * 3
    res = pl.pallas_call(
        functools.partial(step_kernel, (R, T, D, CL, FL, FW)),
        out_shape=outs,
        in_specs=[any_spec] * 10,
        out_specs=[any_spec] * len(outs),
        scratch_shapes=scratch,
        compiler_params=pltpu.CompilerParams(
            collective_id=0, has_side_effects=True, vmem_limit_bytes=63 << 20
        ),
        cost_estimate=pl.CostEstimate(flops=flops, bytes_accessed=200 << 20, transcendentals=0),
        name="block_step",
    )(
        tokens.reshape(R, D), gain_mix, w_in, kernel, w_out,
        gain_ffn, w_gate, w_up, w_down, cotangent.reshape(R, D),
    )
    block_out, d_tokens, g_mix, g_in, g_taps, g_out, g_gain, g_gate, g_up, g_down = finish(
        n_seq, *res[:5]
    )
    return (
        block_out.reshape(S, T, D),
        d_tokens.reshape(S, T, D),
        g_mix, g_in, g_taps, g_out.T, g_gain, g_gate, g_up, g_down.T,
    )


def finish_kernel(
    n_seq, block_in, d_in, ffn_in, conv_in, small_in,
    block_out, d_out, g_mix, g_in, g_taps, g_out, g_gain, g_gate, g_up, g_down,
    block_v, d_v, ffn, conv, small, gate_v, up_v, down_v, in_v, out_v, mix_v, taps_v, gain_v, sem,
):
    D = d_in.shape[1]
    CL = conv_in.shape[2]
    s = lax.axis_index("seq")
    count = [0]

    def copy(src, dst):
        count[0] += 1
        cp = pltpu.make_async_copy(src, dst, sem.at[count[0] - 1])
        cp.start()
        return cp

    loads = [copy(ffn_in.at[0], ffn.at[0]), copy(conv_in, conv), copy(small_in, small)]
    loads += [copy(ffn_in.at[m], ffn.at[m]) for m in (1, 2)]
    passing = [copy(block_in, block_v), copy(d_in, d_v)]
    stores = []
    loads[0].wait()
    down_v[...] = ffn[0].astype(F32)
    stores.append(copy(down_v, g_down))
    loads[1].wait()
    in_v[...] = conv[0:3].astype(F32)
    stores.append(copy(in_v, g_in))
    out_v[...] = conv[3].astype(F32)
    stores.append(copy(out_v, g_out))
    passing[0].wait()
    stores.append(copy(block_v, block_out))
    passing[1].wait()
    stores.append(copy(d_v, d_out))
    loads[3].wait()
    gate_v[...] = ffn[1].astype(F32)
    stores.append(copy(gate_v, g_gate))
    loads[4].wait()
    up_v[...] = ffn[2].astype(F32)
    stores.append(copy(up_v, g_up))
    loads[2].wait()
    per_d, per_c = D // n_seq, CL // n_seq
    mine = pltpu.roll(small[...], SMALL - (s % 2) * per_d, 1)
    mix_v[...] = mine[0, 0:per_d]
    gain_v[...] = mine[1, 0:per_d]
    mine = pltpu.roll(small[...], SMALL - (s % 2) * per_c, 1)
    for t in range(3):
        taps_v[t] = mine[2 + t : 3 + t, 0:per_c]
    stores += [copy(mix_v, g_mix), copy(gain_v, g_gain), copy(taps_v, g_taps)]
    for cp in stores:
        cp.wait()


def finish(n_seq, block_out, d_tokens, g_ffn, g_conv, small):
    R, D = block_out.shape
    _, DR, FL = g_ffn.shape
    CL = g_conv.shape[2]
    any_spec = pl.BlockSpec(memory_space=pl.ANY)
    V = pltpu.VMEM
    tails = [
        (DR, FL), (DR, FL), (DR, FL), (3, DR, CL), (DR, CL),
        (D // n_seq,), (3, 1, CL // n_seq), (D // n_seq,),
    ]
    gate, up, down, inp, out, mix, taps, gain = [jax.ShapeDtypeStruct(t, F32) for t in tails]
    low = jax.ShapeDtypeStruct((R, D), BF)
    return pl.pallas_call(
        functools.partial(finish_kernel, n_seq),
        out_shape=[low, low, mix, inp, taps, out, gain, gate, up, down],
        in_specs=[any_spec] * 5,
        out_specs=[any_spec] * 10,
        scratch_shapes=[V((R, D), BF), V((R, D), BF), V(g_ffn.shape, BF), V(g_conv.shape, BF), V(small.shape, F32)]
        + [V(t, F32) for t in tails]
        + [pltpu.SemaphoreType.DMA((20,))],
        compiler_params=pltpu.CompilerParams(vmem_limit_bytes=63 << 20),
        name="finish",
    )(block_out, d_tokens, g_ffn, g_conv, small)


def from_behind(value, axis, by):
    count = lax.axis_size(axis)
    pairs = [(i, i + by) for i in range(count) if 0 <= i + by < count]
    return lax.ppermute(value, axis, pairs)


def rms_scale(vector):
    return lax.rsqrt(jnp.mean(vector * vector, axis=-1, keepdims=True) + epsilon)


def norm_back(d_normout, normed, inv_scale, gain_vec):
    d_normed = d_normout * gain_vec
    return inv_scale * (d_normed - normed * jnp.mean(d_normed * normed, axis=-1, keepdims=True))


def matmul(lhs_mat, rhs_mat):
    return jnp.dot(lhs_mat, rhs_mat, preferred_element_type=jnp.float32)


def left_trans(lhs_mat, rhs_mat):
    return lax.dot_general(
        lhs_mat, rhs_mat, (((0,), (0,)), ((), ())), preferred_element_type=jnp.float32
    )


def right_trans(lhs_mat, rhs_mat):
    return lax.dot_general(
        lhs_mat, rhs_mat, (((1,), (1,)), ((), ())), preferred_element_type=jnp.float32
    )


def general_body(tokens, gain_mix, w_in, kernel, w_out, gain_ffn, w_gate, w_up, w_down, cotangent):
    seq_count, tok_rows, model_width = tokens.shape
    row_count = seq_count * tok_rows
    tokens_f = tokens.astype(jnp.float32).reshape(row_count, model_width)
    scale_mix = rms_scale(tokens_f)
    normed_mix = tokens_f * scale_mix
    h_mix = (normed_mix * gain_mix).astype(jnp.bfloat16)
    proj_b = matmul(h_mix, w_in[0])
    proj_c = matmul(h_mix, w_in[1])
    proj_x = matmul(h_mix, w_in[2])
    conv_in = (proj_b * proj_x).astype(jnp.bfloat16).reshape(seq_count, tok_rows, -1)
    before = from_behind(conv_in[:, tok_rows - 2 :, :], "seq", 1)
    extended = jnp.concatenate([before, conv_in], axis=1).astype(jnp.float32)
    conv_out = (
        kernel[0] * extended[:, :-2] + kernel[1] * extended[:, 1:-1] + kernel[2] * extended[:, 2:]
    )
    conv_flat = conv_out.reshape(row_count, -1)
    gated = (proj_c * conv_flat).astype(jnp.bfloat16)
    mixed_sum = lax.psum(matmul(gated, w_out).astype(jnp.bfloat16), "chan").astype(jnp.float32)
    residual = tokens_f + mixed_sum
    scale_ffn = rms_scale(residual)
    normed_ffn = residual * scale_ffn
    h_ffn = (normed_ffn * gain_ffn).astype(jnp.bfloat16)
    gate_pre = matmul(h_ffn, w_gate)
    up_value = matmul(h_ffn, w_up)
    sigmoid_gate = jax.nn.sigmoid(gate_pre)
    silu_gate = gate_pre * sigmoid_gate
    hidden = (silu_gate * up_value).astype(jnp.bfloat16)
    ffn_total = lax.psum(matmul(hidden, w_down).astype(jnp.bfloat16), "chan").astype(jnp.float32)
    block_out = (
        (residual + ffn_total).astype(jnp.bfloat16).reshape(seq_count, tok_rows, model_width)
    )
    grad_out = cotangent.reshape(row_count, model_width)
    g_w_down = left_trans(hidden, grad_out)
    d_hidden = right_trans(grad_out, w_down)
    d_gate = (d_hidden * up_value * sigmoid_gate * (1.0 + gate_pre * (1.0 - sigmoid_gate))).astype(
        jnp.bfloat16
    )
    d_up = (d_hidden * silu_gate).astype(jnp.bfloat16)
    g_w_gate = left_trans(h_ffn, d_gate)
    g_w_up = left_trans(h_ffn, d_up)
    d_h_ffn = lax.psum(
        (right_trans(d_gate, w_gate) + right_trans(d_up, w_up)).astype(jnp.bfloat16), "chan"
    ).astype(jnp.float32)
    g_gain_ffn = jnp.sum(d_h_ffn * normed_ffn, axis=0)
    d_resid = grad_out.astype(jnp.float32) + norm_back(d_h_ffn, normed_ffn, scale_ffn, gain_ffn)
    d_mixed = d_resid.astype(jnp.bfloat16)
    g_w_out = left_trans(gated, d_mixed)
    d_gated = right_trans(d_mixed, w_out)
    d_proj_c = (d_gated * conv_flat).astype(jnp.bfloat16)
    d_conv = (d_gated * proj_c).reshape(seq_count, tok_rows, -1)
    after_rows = from_behind(d_conv[:, :2, :], "seq", -1)
    ext_back = jnp.concatenate([d_conv, after_rows], axis=1)
    d_conv_in = (
        kernel[2] * ext_back[:, :-2] + kernel[1] * ext_back[:, 1:-1] + kernel[0] * ext_back[:, 2:]
    )
    g_kernel = jnp.stack(
        [
            jnp.sum(d_conv * extended[:, :-2], axis=(0, 1)),
            jnp.sum(d_conv * extended[:, 1:-1], axis=(0, 1)),
            jnp.sum(d_conv * extended[:, 2:], axis=(0, 1)),
        ]
    ).reshape(3, 1, -1)
    d_conv_low = d_conv_in.reshape(row_count, -1).astype(jnp.bfloat16)
    d_proj_b = (d_conv_low * proj_x).astype(jnp.bfloat16)
    d_proj_x = (d_conv_low * proj_b).astype(jnp.bfloat16)
    g_w_in = jnp.stack(
        [left_trans(h_mix, d_proj_b), left_trans(h_mix, d_proj_c), left_trans(h_mix, d_proj_x)]
    )
    d_h_mix = lax.psum(
        (
            right_trans(d_proj_b, w_in[0])
            + right_trans(d_proj_c, w_in[1])
            + right_trans(d_proj_x, w_in[2])
        ).astype(jnp.bfloat16),
        "chan",
    ).astype(jnp.float32)
    g_gain_mix = jnp.sum(d_h_mix * normed_mix, axis=0)
    d_tokens = (
        (d_resid + norm_back(d_h_mix, normed_mix, scale_mix, gain_mix))
        .astype(jnp.bfloat16)
        .reshape(seq_count, tok_rows, model_width)
    )
    summed = (
        lax.psum_scatter(g_w_in, "seq", scatter_dimension=1, tiled=True),
        lax.psum_scatter(g_w_out, "seq", scatter_dimension=1, tiled=True),
        lax.psum_scatter(g_kernel, "seq", scatter_dimension=2, tiled=True),
        lax.psum_scatter(g_gain_mix, "seq", scatter_dimension=0, tiled=True),
        lax.psum_scatter(g_w_gate, "seq", scatter_dimension=0, tiled=True),
        lax.psum_scatter(g_w_up, "seq", scatter_dimension=0, tiled=True),
        lax.psum_scatter(g_w_down, "seq", scatter_dimension=1, tiled=True),
        lax.psum_scatter(g_gain_ffn, "seq", scatter_dimension=0, tiled=True),
    )
    sum_in, sum_out, sum_kernel, sum_gain_mix, sum_gate, sum_up, sum_down, sum_gain_ffn = summed
    return (
        block_out,
        d_tokens,
        sum_gain_mix,
        sum_in,
        sum_kernel,
        sum_out,
        sum_gain_ffn,
        sum_gate,
        sum_up,
        sum_down,
    )


def solution(mesh):
    body = fused_body if mesh.shape["seq"] == 4 * NZ else general_body
    placed = (
        P(None, "seq", None),
        P(),
        P(None, None, "chan"),
        P(None, "chan"),
        P("chan", None),
        P(),
        P(None, "chan"),
        P(None, "chan"),
        P("chan", None),
        P(None, "seq", None),
    )
    return jax.shard_map(
        body,
        mesh=mesh,
        in_specs=placed,
        out_specs=(
            P(None, "seq", None),
            P(None, "seq", None),
            P("seq"),
            P(None, "seq", "chan"),
            P(None, "chan", "seq"),
            P("chan", "seq"),
            P("seq"),
            P("seq", "chan"),
            P("seq", "chan"),
            P("chan", "seq"),
        ),
        check_vma=False,
    )
```

```python
import functools

import jax
import jax.numpy as jnp
from jax import lax
from jax.experimental import pallas as pl
from jax.experimental.pallas import tpu as pltpu
from jax.sharding import PartitionSpec as P

epsilon = 1e-05
BF = jnp.bfloat16
F32 = jnp.float32
MESH = pl.DeviceIdType.MESH
LANE = 128
NZ = 4
ROWS_CHUNK = 128
SMALL = 256
ZF_COLS = 1280


def nn(a, b):
    return jnp.dot(a, b, preferred_element_type=F32)


def tn(a, b):
    return lax.dot_general(a, b, (((0,), (0,)), ((), ())), preferred_element_type=F32)


def nt(a, b):
    return lax.dot_general(a, b, (((1,), (1,)), ((), ())), preferred_element_type=F32)


def inv_rms(v):
    return lax.rsqrt(jnp.mean(v * v, axis=-1, keepdims=True) + epsilon)


class Take:
    def __init__(self, limit):
        self.used, self.limit = 0, limit

    def __call__(self, count=1):
        base = self.used
        self.used += count
        assert self.used <= self.limit
        return base


N_SEND, N_RECV, N_LOCAL = 128, 192, 64

SCHEDULE = {
    "dhA": (("end", (1, 1)), ("end", (1, 0)), ("mid", (0, 2)), ("mid", (0, 0)),),
    "dhD": (("mid", "pair"),),
    "dnA": (("end", (2, 0)),),
    "dnD": (("end", (3, 0)),),
    "nb2": (("mid", (2, 0)), ("mid", (1, 0)),),
    "cb": (("end", (2, 1)), ("mid", (3, 0)), ("mid", (2, 1)),),
    "d1a": (("mid", (1, 1)), ("mid", (2, 2)),),
    "tail": (("end", (3, 1)),),
    "d1b": (("mid", (0, 1)),),
    "gc1": (("end", (3, 2)), ("end", (1, 3)), ("mid", (3, 1)),),
    "gc2": (("end", (4, 0)), ("end", (1, 2)),),
    "gc3": (("mid", (1, 2)),),
    "blk0": (("end", (4, 1)), ("end", "pair"),),
    "blk1": (("mid", (4, 0)), ("mid", (1, 3)),),
    "blk2": (("end", (2, 2)),),
    "blk3": (("mid", (3, 2)), ("mid", (4, 1)),),
    "dt0": (("end", (2, 3)),),
    "dt1": (("end", (4, 2)),),
    "dt2": (("mid", (4, 2)), ("mid", "pair sum"), ("mid", (2, 3)),),
    "dt3": (("mid", (3, 3)),),
    "sm": (("end", (3, 3)), ("end", (4, 3)), ("end", "pair sum"), ("mid", (4, 3)),),
}


def step_kernel(
    dims,
    tokens, gain_mix_hbm, w_in, taps_hbm, w_out, gain_ffn_hbm, w_gate, w_up, w_down, cot,
    block_out, d_tokens, g_ffn, g_conv, small_out,
    gb0, gb1, gb2, gb3, gb4, yb0, yb1, yb2, yb3, yb4, zb0, zb1, zb2, zb3, zb4,
    cr_dh, cr_dn,
    gain_mix, taps, gain_ffn, tok_v, wg_v, wu_v, wd_v, dy_v, h2_v, h1_v, hid, dg, du, pb, pc, px, bx, gated, resid, gall,
    ring, xr_dh, xr_dn, xr_d1, rb, ld, outs, halo_s, halo_r, dhalo_s, dhalo_r, tail, pb_tail, px_tail,
    sm, sm_o, sm_t, sm_r, ss, rs, ls,
):
    R, T, D, CL, FL, FW = dims
    S = R // T
    CH = CL // 2
    GR = D // NZ
    SR = GR // 2
    DR = SR // 2
    NCH = R // ROWS_CHUNK
    take_s, take_r, take_l = Take(N_SEND), Take(N_RECV), Take(N_LOCAL)

    s = lax.axis_index("seq")
    x = lax.axis_index("chan")
    n_seq = 4 * NZ
    z, y, c = s // 4, (s // 2) % 2, s % 2

    def did(z_, y_, c_):
        return ((z_ * 2 + y_) * 2 + c_, x)

    core_dev = did(z, y, 1 - c)
    y_dev = did(z, 1 - y, c)
    x_dev = (s, 1 - x)
    mid = jnp.logical_and(z > 0, z < NZ - 1)
    end = jnp.logical_not(mid)

    def remote(src, dst, si, ri, dev):
        return pltpu.make_async_remote_copy(
            src_ref=src, dst_ref=dst, send_sem=ss.at[si], recv_sem=rs.at[ri],
            device_id=dev, device_id_type=MESH,
        )

    def wait_recv(dst, ri):
        remote(dst, dst, 0, ri, core_dev).wait_recv()

    def wait_send(src, si):
        remote(src, src, si, 0, core_dev).wait_send()

    def local(src, dst, li):
        return pltpu.make_async_copy(src, dst, ls.at[li])

    l_tok, l_win, l_wout, l_dy, l_small = take_l(), take_l(3), take_l(), take_l(), take_l(3)
    ld_tok = local(tokens, tok_v, l_tok)
    ld_tok.start()
    win_views = [wg_v.at[:, pl.ds(0, CL)], wg_v.at[:, pl.ds(CL, CL)], wu_v.at[:, pl.ds(0, CL)]]
    wout_view = wd_v.at[pl.ds(pl.multiple_of(x * CL, CL), CL), :]

    def load_w_in():
        return [local(w_in.at[m], win_views[m], l_win + m) for m in range(3)]

    for cp in load_w_in():
        cp.start()
    ld_small = [
        local(src, dst, l_small + i)
        for i, (src, dst) in enumerate(
            ((gain_mix_hbm, gain_mix), (taps_hbm, taps), (gain_ffn_hbm, gain_ffn))
        )
    ]
    for cp in ld_small:
        cp.start()
    ld_wout = local(w_out, wout_view, l_wout)
    ld_wout.start()
    ld_dy = local(cot, dy_v.at[0], l_dy)

    bar = pltpu.get_barrier_semaphore()

    def greet(dev):
        pl.semaphore_signal(bar, inc=1, device_id=dev, device_id_type=MESH)

    greet(core_dev)
    greet(x_dev)
    others = [(k, did((z + k // 2) % NZ, (y + k % 2) % 2, c)) for k in range(1, 2 * NZ)]
    for _, dev in others:
        greet(dev)
    has_prev = s > 0
    has_next = s < n_seq - 1
    prev_dev = ((s + n_seq - 1) % n_seq, x)
    next_dev = ((s + 1) % n_seq, x)
    greet(prev_dev)
    greet(next_dev)
    pl.semaphore_wait(bar, 3 + 2 * NZ)

    SUBS = 2
    ER = CL // 8
    PR = ER // SUBS
    zi = z % 2
    z_dev = did(z + 1 - 2 * zi, y, c)
    mine_e = zi * 4 + y * 2 + c
    pair_e = zi * 4 + (1 - y) * 2 + c
    line_e = (1 - zi) * 4 + y * 2 + c
    far_e = (1 - zi) * 4 + (1 - y) * 2 + c
    w_sems = {}

    def w_rows(half, eighth, sub):
        return wd_v.at[pl.ds(pl.multiple_of(half * CL + eighth * ER + sub * PR, PR), PR), :]

    def w_copy(name, eighth, sub, dev):
        if (name, sub) not in w_sems:
            w_sems[name, sub] = take_s(), take_r()
        ref = w_rows(1 - x, eighth, sub)
        return remote(ref, ref, *w_sems[name, sub], dev)

    def w_came(name, eighth, sub):
        wait_recv(w_rows(1 - x, eighth, sub), w_sems[name, sub][1])

    def w_over_x(sub):
        if ("x", sub) not in w_sems:
            w_sems["x", sub] = take_s(), take_r()
        src = w_out.at[pl.ds(pl.multiple_of(mine_e * ER + sub * PR, PR), PR), :]
        return remote(src, w_rows(x, mine_e, sub), *w_sems["x", sub], x_dev)

    w_sent = []

    def w_pass(name, eighth, sub, targets):
        w_came(name, eighth, sub)
        for to, dev in targets:
            w_copy(to, eighth, sub, dev).start()
            w_sent.append((to, eighth, sub, dev))

    def w_mine(sub):
        w_pass("x", mine_e, sub, (("z", z_dev), ("y", y_dev), ("core", core_dev)))

    def w_pair(sub):
        to = (("zy", z_dev),) if sub == 0 else ()
        w_pass("y", pair_e, sub, to + (("core pair", core_dev),))

    def w_line(sub):
        to = (("zy", y_dev),) if sub == 1 else ()
        w_pass("z", line_e, sub, to + (("core line", core_dev),))

    def w_far(sub):
        w_pass("zy", far_e, sub, (("core far", core_dev),))

    for sub in range(SUBS):
        w_over_x(sub).start()

    l_w = take_l(3)
    win_start = pl.multiple_of(c * (FL - FW), LANE)
    ld_wg = local(w_gate.at[:, pl.ds(win_start, FW)], wg_v, l_w)
    ld_wu = local(w_up.at[:, pl.ds(win_start, FW)], wu_v, l_w + 1)
    ld_wd = local(w_down.at[pl.ds(win_start, FW), :], wd_v, l_w + 2)

    sm[...] = jnp.zeros_like(sm)
    for cp in ld_small:
        cp.wait()
    gain_mix_row = gain_mix[...].reshape(1, D)
    gain_ffn_row = gain_ffn[...].reshape(1, D)
    k_taps = [taps[t : t + 1, :] for t in range(3)]

    ld_tok.wait()

    CPS = T // ROWS_CHUNK
    NC = CL // 256
    s_h1, r_h1 = take_s(S), take_r(S)
    s_ha, r_ha = take_s(S), take_r(S)
    s_mx, r_mx = take_s(NCH), take_r(NCH)
    row_iota = lax.broadcasted_iota(jnp.int32, (T, 256), 0)
    top_iota = row_iota[0:16]

    def conv_terms(now, h, iota):
        h14 = jnp.broadcast_to(h[14:15], now.shape)
        h15 = jnp.broadcast_to(h[15:16], now.shape)
        one = jnp.where(iota == 0, h15, pltpu.roll(now, 1, 0))
        two = jnp.where(iota == 0, h14, jnp.where(iota == 1, h15, pltpu.roll(now, 2, 0)))
        return now, one, two

    def tap_cols(cols):
        return [taps[t : t + 1, cols] for t in range(3)]

    def convolve(terms, cols):
        now, one, two = terms
        k0, k1, k2 = tap_cols(cols)
        return k0 * two + k1 * one + k2 * now

    def h1_send(q):
        rows = pl.ds(q * T, T)
        return remote(h1_v.at[0, rows], h1_v.at[1, rows], s_h1 + q, r_h1 + q, core_dev)

    def halo_send(q):
        return remote(halo_s.at[q], halo_r.at[q], s_ha + q, r_ha + q, next_dev)

    own_cols = pl.ds(pl.multiple_of(x * CL, CL), CL)
    other_cols = pl.ds(pl.multiple_of((1 - x) * CL, CL), CL)

    def gated_send(k):
        ref = gall.at[k, :, own_cols]
        return remote(ref, ref, s_mx + k, r_mx + k, x_dev)

    def mixer_out(k):
        gall[k, :, own_cols] = gated[k * ROWS_CHUNK : (k + 1) * ROWS_CHUNK, :]
        gated_send(k).start()

    for q in range(S):
        rows = pl.ds(q * T, T)

        def norm_rows(k, _, q=q):
            chunk = pl.ds(pl.multiple_of(q * T + k * ROWS_CHUNK, ROWS_CHUNK), ROWS_CHUNK)
            xv = tok_v[chunk, :].astype(F32)
            h1_v[0, chunk, :] = (xv * inv_rms(xv) * gain_mix_row).astype(BF)
            return 0

        lax.fori_loop(0, CPS, norm_rows, 0)
        if q == 0:
            for cp in load_w_in():
                cp.wait()

        def in_proj(j, _, q=q, rows=rows):
            cols = pl.ds(pl.multiple_of(j * 256, 256), 256)
            cols1 = pl.ds(pl.multiple_of(CL + j * 256, 256), 256)
            h = h1_v[0, rows, :]
            b = nn(h, wg_v[:, cols])
            pb[rows, cols] = b.astype(BF)
            xx = nn(h, wu_v[:, cols])
            px[rows, cols] = xx.astype(BF)
            inner = (b * xx).astype(BF)
            bx[rows, cols] = inner
            halo_s[q, :, cols] = inner[T - 16 : T]
            pcv = nn(h, wg_v[:, cols1])
            pc[rows, cols] = pcv.astype(BF)
            now = inner.astype(F32)
            cv = convolve(conv_terms(now, jnp.zeros_like(now[0:16]), row_iota), cols)
            gated[rows, cols] = (pcv * cv).astype(BF)
            return 0

        lax.fori_loop(0, NC, in_proj, 0)
        if q == S - 1:
            ld_wg.start()
            ld_wu.start()

        @pl.when(has_next)
        def _(q=q):
            halo_send(q).start()

        for k in range(CPS - 1, 0, -1):
            mixer_out(q * CPS + k)
        if q > 0:
            w_mine(1)

        @pl.when(has_prev)
        def _(q=q):
            wait_recv(halo_r.at[q], r_ha + q)

        @pl.when(jnp.logical_not(has_prev))
        def _(q=q):
            halo_r[q] = jnp.zeros_like(halo_r[q])

        def conv_top(j, _, q=q):
            cols = pl.ds(pl.multiple_of(j * 256, 256), 256)
            top = pl.ds(q * T, 16)
            now = bx[top, cols].astype(F32)
            cv = convolve(conv_terms(now, halo_r[q, :, cols].astype(F32), top_iota), cols)
            gated[top, cols] = (pc[top, cols].astype(F32) * cv).astype(BF)
            return 0

        lax.fori_loop(0, NC, conv_top, 0)
        mixer_out(q * CPS)
        if q == 0:
            w_mine(0)
        h1_send(q).start()
        if q == 0:
            ld_dy.start()
            s_dy, r_dy = take_s(), take_r()
            send_dy = remote(cot, dy_v.at[1], s_dy, r_dy, core_dev)
            send_dy.start()
    w_line(0)
    w_pair(0)
    w_line(1)
    w_pair(1)

    s_h2, r_h2 = take_s(NCH), take_r(NCH)
    ld_wg.wait()
    ld_wu.wait()
    NF, NA = FW // 256, ZF_COLS // 256
    overlap = 2 * FW - FL
    col_iota = lax.broadcasted_iota(jnp.int32, (2 * ROWS_CHUNK, 256), 1)

    def sent(n):
        return (n // CPS) * CPS + (CPS - 1 - n % CPS)

    def ffn_tile(h, cols, keep):
        g = nn(h, wg_v[:, cols])
        u = nn(h, wu_v[:, cols])
        sg = jax.nn.sigmoid(g)
        si = g * sg
        slope = u * sg * (1.0 + g * (1.0 - sg))
        if keep is not None:
            si, slope = jnp.where(keep, si, 0.0), jnp.where(keep, slope, 0.0)
        return (si * u).astype(BF), slope.astype(BF), si.astype(BF)

    def residual_chunk(k):
        rows = pl.ds(pl.multiple_of(k * ROWS_CHUNK, ROWS_CHUNK), ROWS_CHUNK)
        wait_recv(gall.at[k, :, other_cols], r_mx + k)

        def out_tile(j, _):
            cols = pl.ds(pl.multiple_of(j * 512, 512), 512)
            resid[rows, cols] = tok_v[rows, cols].astype(F32) + nn(gall[k], wd_v[0 : 2 * CL, cols])
            return 0

        lax.fori_loop(0, D // 512, out_tile, 0, unroll=True)
        res = resid[rows, :]
        h2_v[0, rows, :] = (res * inv_rms(res) * gain_ffn_row).astype(BF)
        remote(h2_v.at[0, rows], h2_v.at[1, rows], s_h2 + k, r_h2 + k, core_dev).start()

    def forward_chunk(k):
        rows = pl.ds(pl.multiple_of(k * ROWS_CHUNK, ROWS_CHUNK), ROWS_CHUNK)
        wait_recv(h2_v.at[1, rows], r_h2 + k)

        def tile(j, _):
            cols = pl.ds(pl.multiple_of(j * 256, 256), 256)
            h = h2_v[:, rows, :].reshape(2 * ROWS_CHUNK, D)
            keep = col_iota + j * 256 >= c * overlap
            for ref, v in zip((hid, dg, du), ffn_tile(h, cols, keep)):
                ref[:, rows, cols] = v.reshape(2, ROWS_CHUNK, 256)
            return 0

        lax.fori_loop(0, NA, tile, 0, unroll=True)

    def forward_rest(slot):
        for j in range(NA, NF):
            cols = slice(j * 256, (j + 1) * 256)
            for ref, v in zip((hid, dg, du), ffn_tile(h2_v[slot], cols, None)):
                ref[slot, :, cols] = v

    for sub in range(SUBS):
        w_far(sub)
    ld_wout.wait()
    for sub in range(SUBS):
        for name, eighth in (("core", mine_e), ("core pair", pair_e), ("core line", line_e), ("core far", far_e)):
            w_came(name, eighth + 1 - 2 * c, sub)
    residual_chunk(sent(0))

    def chunk_loop(n, _):
        @pl.when(n + 1 < NCH)
        def _():
            residual_chunk(sent(n + 1))

        forward_chunk(sent(n))
        return 0

    lax.fori_loop(0, NCH, chunk_loop, 0)
    for sub in range(SUBS):
        w_over_x(sub).wait_send()
    for item in w_sent:
        w_copy(*item).wait_send()
    ld_wd.start()
    ld_dy.wait()
    send_dy.wait()
    for k in range(NCH):
        gated_send(k).wait_send()
        wait_send(h2_v.at[0, pl.ds(k * ROWS_CHUNK, ROWS_CHUNK)], s_h2 + k)

    gbs = [gb0, gb1, gb2, gb3, gb4]
    ybs = [yb0, yb1, yb2, yb3, yb4]
    zbs = [zb0, zb1, zb2, zb3, zb4]
    widths = [ZF_COLS, FW - ZF_COLS, FW, FW, 2 * CL]
    s_y = [None] + [take_s(NZ) for _ in range(4)]
    r_y = [None] + [take_r(NZ) for _ in range(4)]
    s_z = [take_s(2 * NZ)] + [take_s(NZ) for _ in range(4)]
    r_z = [take_r(4 * NZ)] + [take_r(2 * NZ) for _ in range(4)]

    def order(e):
        if e == NZ - 1:
            return z
        per_z = {0: (3, 2, 1), 1: (3, 0, 2), 2: (0, 3, 1), 3: (0, 1, 2)}
        v = per_z[3][e]
        for zz in range(3):
            v = jnp.where(z == zz, per_z[zz][e], v)
        return v

    def order_dyn(u):
        v = order(NZ - 1)
        for e in range(NZ - 1):
            v = jnp.where(u == e, order(e), v)
        return v

    def per_core(j, act):
        if j in (1, 4):
            act(lambda ref: ref)
            return

        @pl.when(c == 0)
        def _():
            act(lambda ref: ref)

        @pl.when(c == 1)
        def _():
            act(lambda ref: ref.at[:, pl.ds(overlap, widths[j] - overlap)])

    def z_send(j, src, e, zp, h=None):
        to_right = zp > z
        d = jnp.where(to_right, 0, 1)
        dev = did(jnp.clip(jnp.where(to_right, z + 1, z - 1), 0, NZ - 1), y, c)
        if h is None:
            dst, si, ri = zbs[j].at[d, zp], s_z[j] + e, r_z[j] + d * NZ + zp
        else:
            dst, si, ri = zbs[j].at[d, zp, h], s_z[j] + 2 * e + h, r_z[j] + (d * NZ + zp) * 2 + h
        per_core(j, lambda cut: remote(cut(src), cut(dst), si, ri, dev).start())

    l_g = take_l(12)

    def y_send(j, u):
        zp = order_dyn(u) if not isinstance(u, int) else order(u)
        src, dst = gbs[j].at[zp, 1 - y], ybs[j].at[zp]
        per_core(j, lambda cut: remote(cut(src), cut(dst), s_y[j] + u, r_y[j] + u, y_dev).start())

    def g_block(lhs_ref, rhs_ref, zp, pair, parts=(0, 1)):
        lhs = lhs_ref[:, :, pl.ds(pl.multiple_of(zp * GR, GR), GR)].reshape(2 * R, GR)
        cut = ZF_COLS
        for n in parts:
            cols = slice(0, cut) if n == 0 else slice(cut, FW)
            v = tn(lhs, rhs_ref[:, :, cols].reshape(2 * R, cols.stop - cols.start)).astype(BF)
            outs[2 * pair, :, cols] = v[:SR]
            outs[2 * pair + 1, :, cols] = v[SR:]

    def line_copies(u):
        zp = order(u)
        return [
            local(outs.at[2 * (u % 2) + h, :, pl.ds(0, ZF_COLS)], gb0.at[zp, h], l_g + 2 * (u % 2) + h)
            for h in range(2)
        ]

    def pair_copies(u):
        zp = order(u)
        return [
            local(
                outs.at[2 * (u % 2) + h, :, pl.ds(ZF_COLS, FW - ZF_COLS)],
                gb1.at[zp, h], l_g + 4 + 2 * (u % 2) + h,
            )
            for h in range(2)
        ]

    def start(copies):
        for cp in copies:
            cp.start()

    def wait(copies):
        for cp in copies:
            cp.wait()

    def line_sends(u):
        wait(line_copies(u))
        if u < NZ - 1:

            @pl.when(end)
            def _():
                for h in range(2):
                    z_send(0, gb0.at[order(u), h], u, order(u), h)

    def pair_sends(u):
        wait(pair_copies(u))
        y_send(1, u)

    for u in range(NZ):
        g_block(dy_v, hid, order(u), u % 2, (0,))
        start(line_copies(u))
        if u == 0:
            forward_rest(0)
            line_sends(0)
            forward_rest(1)
        else:
            pair_sends(u - 1)
        g_block(dy_v, hid, order(u), u % 2, (1,))
        start(pair_copies(u))
        if u > 0:
            line_sends(u)
    pair_sends(NZ - 1)

    ld_wd.wait()

    def hid_back(slot, _):
        for j in range(NF):
            cols = slice(j * 256, (j + 1) * 256)
            dh = nt(dy_v[slot], wd_v[cols, :])
            dg[slot, :, cols] = (dh * dg[slot, :, cols].astype(F32)).astype(BF)
            du[slot, :, cols] = (dh * du[slot, :, cols].astype(F32)).astype(BF)
        return 0

    lax.fori_loop(0, 2, hid_back, 0)

    def plain_copies(gb, zp, pair):
        return [local(outs.at[2 * pair + h], gb.at[zp, h], l_g + 2 * pair + h) for h in range(2)]

    def gate_up(u, _):
        zp = order_dyn(u)

        def up_sends(u):
            for cp in plain_copies(gb3, order_dyn(u), 1):
                cp.wait()

            @pl.when(u < 2)
            def _():
                y_send(3, u)

        g_block(h2_v, dg, zp, 0, (0,))

        @pl.when(u > 0)
        def _():
            up_sends(u - 1)

        g_block(h2_v, dg, zp, 0, (1,))
        for cp in plain_copies(gb2, zp, 0):
            cp.start()
        g_block(h2_v, du, zp, 1, (0,))
        for cp in plain_copies(gb2, zp, 0):
            cp.wait()

        @pl.when(u < 3)
        def _():
            y_send(2, u)

        g_block(h2_v, du, zp, 1, (1,))
        for cp in plain_copies(gb3, zp, 1):
            cp.start()
        return 0

    lax.fori_loop(0, NZ, gate_up, 0)
    for cp in plain_copies(gb3, order(NZ - 1), 1):
        cp.wait()

    l_e = take_l(4)
    is_role = {"end": end, "mid": mid}
    slot_last = {role: [None] * outs.shape[0] for role in is_role}
    slot_next = {role: 0 for role in is_role}

    def claim_slot(role):
        o = slot_next[role]
        slot_next[role] = (o + 1) % outs.shape[0]
        if slot_last[role][o] is not None:
            slot_last[role][o]()
            slot_last[role][o] = None
        return o

    ADD_ROWS = 32

    def add_into(dst, srcs):
        def rows_add(k, _):
            rows = pl.ds(pl.multiple_of(k * ADD_ROWS, ADD_ROWS), ADD_ROWS)
            acc = srcs[0][rows, :].astype(F32)
            for src in srcs[1:]:
                acc = acc + src[rows, :].astype(F32)
            dst[rows, :] = acc.astype(BF)
            return 0

        lax.fori_loop(0, SR // ADD_ROWS, rows_add, 0)

    def fetch(j, srcs):
        w = widths[j]
        views, copies = [], []
        for i, (src, ri) in enumerate(srcs):
            if ri is not None:
                per_core(j, lambda cut: wait_recv(cut(src), ri))
            views.append(ld.at[i, :, pl.ds(0, w)])
            copies.append(local(src, views[-1], l_e + i))
            copies[-1].start()
        for cp in copies:
            cp.wait()
        return views

    def from_line(j, d, zp, h=None):
        if h is None:
            return zbs[j].at[d, zp], r_z[j] + d * NZ + zp
        return zbs[j].at[d, zp, h], r_z[j] + (d * NZ + zp) * 2 + h

    def line_event(role, j, e):
        @pl.when(is_role[role])
        def _():
            zp = order(e)
            w = widths[j]
            d = jnp.where(zp > z, 0, 1)
            for h in (0, 1) if j == 0 else (None,):
                o = claim_slot(role)
                dst = outs.at[o, :, pl.ds(0, w)]
                if h is None:
                    srcs = [(gbs[j].at[zp, y], None), (ybs[j].at[zp], r_y[j] + e)]
                    si = s_z[j] + e
                else:
                    srcs = [(gbs[j].at[zp, h], None)]
                    si = s_z[j] + 2 * e + h
                if role == "mid":
                    srcs.append(from_line(j, d, zp, h))
                add_into(dst, fetch(j, srcs))
                z_send(j, dst, e, zp, h)
                slot_last[role][o] = functools.partial(sent_slot, j, o, si)

    def sent_slot(j, o, si):
        per_core(j, lambda cut: wait_send(cut(outs.at[o, :, pl.ds(0, widths[j])]), si))

    def own_shard(role, j, h=None):
        if h is None:
            srcs = [(gbs[j].at[z, y], None), (ybs[j].at[z], r_y[j] + NZ - 1)]
        else:
            srcs = [(gbs[j].at[z, h], None)]
        if role == "mid":
            near = jnp.where(z < NZ // 2, 0, 1)
            return srcs + [from_line(j, 1 - near, z, h), from_line(j, near, z, h)]
        return srcs + [from_line(j, jnp.where(z == 0, 1, 0), z, h)]

    def swap_pieces(j):
        if j == 4:
            return [(None, 0, 4 * CH, g_conv.at[c], 0)]
        mat = g_ffn.at[{0: 0, 1: 0, 2: 1, 3: 2}[j]]
        w = widths[j]
        if j == 1:
            return [(None, 0, w, mat, c * (FL - FW) + ZF_COLS)]
        return [(0, 0, w, mat, 0), (1, overlap, w - overlap, mat, FL - FW + overlap)]

    swap_sems = [[(take_s(), take_r(), take_l()) for _ in swap_pieces(j)] for j in range(5)]

    def swap(j, o):
        items = []
        for (core, c0, w, mat, to), (si, ri, li) in zip(swap_pieces(j), swap_sems[j]):
            to = to if isinstance(to, int) else pl.multiple_of(to, LANE)
            target = mat.at[:, pl.ds(to, w)]
            mine = outs.at[o, pl.ds(pl.multiple_of(c * DR, DR), DR), pl.ds(c0, w)]
            other = outs.at[o, pl.ds(pl.multiple_of((1 - c) * DR, DR), DR), pl.ds(c0, w)]
            items.append((core, local(mine, target, li), remote(other, target, si, ri, core_dev), target))
        return items

    def swap_start(j, o):
        for core, keep, give, _ in swap(j, o):
            if core is None:
                keep.start()
                give.start()
            else:

                @pl.when(c == core)
                def _():
                    keep.start()
                    give.start()

    def swap_finish(j, o):
        for (core, keep, give, target), (_, ri, _) in zip(swap(j, o), swap_sems[j]):
            if core is None:
                keep.wait()
                give.wait_send()
                wait_recv(target, ri)
            else:

                @pl.when(c == core)
                def _():
                    keep.wait()
                    give.wait_send()

                @pl.when(c != core)
                def _():
                    wait_recv(target, ri)

    def final_event(role, j):
        @pl.when(is_role[role])
        def _():
            o = claim_slot(role)
            w = widths[j]
            add_into(outs.at[o, :, pl.ds(0, w)], fetch(j, own_shard(role, j)))
            swap_start(j, o)
            slot_last[role][o] = functools.partial(swap_finish, j, o)

    s_f0, r_f0 = take_s(), take_r()
    w0 = widths[0]

    def final0_send(role):
        @pl.when(is_role[role])
        def _():
            o = claim_slot(role)
            dst = outs.at[o, :, pl.ds(0, w0)]
            add_into(dst, fetch(0, own_shard(role, 0, 1 - y)))
            cp = local(dst, gb0.at[z, 1 - y], l_e)
            cp.start()
            cp.wait()
            src = gb0.at[z, 1 - y]
            per_core(0, lambda cut: remote(cut(src), cut(yb0), s_f0, r_f0, y_dev).start())

    def final0_finish(role):
        @pl.when(is_role[role])
        def _():
            o = claim_slot(role)
            dst = outs.at[o, :, pl.ds(0, w0)]
            add_into(dst, fetch(0, own_shard(role, 0, y)))
            add_into(dst, [dst] + fetch(0, [(yb0, r_f0)]))
            swap_start(0, o)
            slot_last[role][o] = functools.partial(swap_finish, 0, o)

    def hook(name):
        for role, event in SCHEDULE.get(name, ()):
            if event == "pair":
                final0_send(role)
            elif event == "pair sum":
                final0_finish(role)
            elif event[1] == NZ - 1:
                final_event(role, event[0])
            else:
                line_event(role, *event)

    def chunks(name, count, body):
        first = 0
        for k in range(count):
            if SCHEDULE.get(name + str(k)) or k == count - 1:
                lax.fori_loop(first, k + 1, body, 0)
                first = k + 1
                hook(name + str(k))

    HALF = 2 * ROWS_CHUNK

    def split_sum(name, product, cr, xr, base_d):
        s_c, r_c = take_s(2), take_r(2)
        s_x, r_x = take_s(NCH), take_r(NCH)
        l_c = take_l()

        def give(k, _):
            def tile(n, _):
                cols = pl.ds(pl.multiple_of(n * 512, 512), 512)
                v = product(1, k * HALF, n).astype(BF)
                gall[pl.ds(2 * k, 2), :, cols] = v.reshape(2, ROWS_CHUNK, 512)
                return 0

            lax.fori_loop(0, D // 512, tile, 0)
            remote(
                gall.at[pl.ds(2 * k, 2)], cr.at[pl.ds(2 * k, 2)], s_c + k, r_c + k, core_dev
            ).start()
            return 0

        lax.fori_loop(0, 2, give, 0)
        hook(name + "A")

        def keep(k, _):
            src = cr.at[pl.ds(2 * k, 2)]
            wait_recv(src, r_c + k)
            cp = local(src, rb, l_c)
            cp.start()
            cp.wait()

            def tile(n, _):
                cols = pl.ds(pl.multiple_of(n * 512, 512), 512)
                v = product(0, k * HALF, n) + rb[:, :, cols].reshape(HALF, 512).astype(F32)
                ring[pl.ds(base_d + 2 * k, 2), :, cols] = v.astype(BF).reshape(2, ROWS_CHUNK, 512)
                return 0

            lax.fori_loop(0, D // 512, tile, 0)
            for i in range(2):
                remote(
                    ring.at[base_d + 2 * k + i], xr.at[2 * k + i], s_x + 2 * k + i, r_x + 2 * k + i, x_dev
                ).start()
            return 0

        lax.fori_loop(0, 2, keep, 0)
        for k in range(2):
            wait_send(gall.at[pl.ds(2 * k, 2)], s_c + k)
        hook(name + "D")
        return s_x, r_x

    def rows_at(ref, slot, r0):
        return ref[slot, pl.ds(pl.multiple_of(r0, HALF), HALF), :]

    def dh_product(slot, r0, n):
        cols = pl.ds(pl.multiple_of(n * 512, 512), 512)
        return nt(rows_at(dg, slot, r0), wg_v[cols, :]) + nt(rows_at(du, slot, r0), wu_v[cols, :])

    def dn_product(slot, r0, n):
        cols = pl.ds(pl.multiple_of(n * 512, 512), 512)
        return nn(rows_at(hid, slot, r0), wd_v[:, cols])

    s_xdh, r_xdh = split_sum("dh", dh_product, cr_dh, xr_dh, 0)
    s_xdn, r_xdn = split_sum("dn", dn_product, cr_dn, xr_dn, 4)
    for cp in load_w_in():
        cp.start()
    ld_wout = local(w_out, wd_v.at[pl.ds(0, CL), :], l_wout)
    ld_wout.start()

    s_do, r_do = take_s(NCH), take_r(NCH)

    def ffn_norm_back(k, _):
        rows = pl.ds(pl.multiple_of(k * ROWS_CHUNK, ROWS_CHUNK), ROWS_CHUNK)
        wait_recv(xr_dh.at[k], r_xdh + k)
        d_h = ring[k].astype(F32) + xr_dh[k].astype(F32)
        res = resid[rows, :]
        s2 = inv_rms(res)
        n2 = res * s2
        sm[0, 1:2, :] += jnp.sum(d_h * n2, axis=0, keepdims=True)
        e2 = d_h * gain_ffn_row
        d_res = dy_v[0, rows, :].astype(F32) + s2 * (
            e2 - n2 * jnp.mean(e2 * n2, axis=-1, keepdims=True)
        )
        h2_v[0, rows, :] = d_res.astype(BF)
        remote(h2_v.at[0, rows], h2_v.at[1, rows], s_do + k, r_do + k, core_dev).start()
        return 0

    chunks("nb", NCH, ffn_norm_back)
    for k in range(NCH):
        wait_send(ring.at[k], s_xdh + k)

    for cp in load_w_in():
        cp.wait()
    ld_wout.wait()
    for q in range(S):

        def conv_back(j, _, q=q):
            cols = pl.ds(pl.multiple_of(j * 256, 256), 256)
            rows = pl.ds(q * T, T)
            now, one, two = conv_terms(
                bx[rows, cols].astype(F32), halo_r[q, :, cols].astype(F32), row_iota
            )
            k0, k1, k2 = tap_cols(cols)
            cv = k0 * two + k1 * one + k2 * now
            d_g = nt(h2_v[0, q * T : q * T + T, :], wd_v[cols, :])
            d_cv = d_g * pc[rows, cols].astype(F32)
            sm[0, 2:3, cols] += jnp.sum(d_cv * two, axis=0, keepdims=True)
            sm[0, 3:4, cols] += jnp.sum(d_cv * one, axis=0, keepdims=True)
            sm[0, 4:5, cols] += jnp.sum(d_cv * now, axis=0, keepdims=True)
            after1 = jnp.where(row_iota < T - 1, pltpu.roll(d_cv, T - 1, 0), 0.0)
            after2 = jnp.where(row_iota < T - 2, pltpu.roll(d_cv, T - 2, 0), 0.0)
            d_bx = k2 * d_cv + k1 * after1 + k0 * after2
            dhalo_s[q, :, cols] = d_cv[0:8]
            tail[q, :, cols] = d_bx[T - 16 : T]
            old_b = pb[rows, cols]
            old_x = px[rows, cols]
            pb_tail[q, :, cols] = old_b[T - 16 : T]
            px_tail[q, :, cols] = old_x[T - 16 : T]
            low = d_bx.astype(BF).astype(F32)
            pb[rows, cols] = (low * old_x.astype(F32)).astype(BF)
            px[rows, cols] = (low * old_b.astype(F32)).astype(BF)
            pc[rows, cols] = (d_g * cv).astype(BF)
            return 0

        lax.fori_loop(0, NC, conv_back, 0)

    s_dha, r_dha = take_s(), take_r()
    send_dhalo = remote(dhalo_s, dhalo_r, s_dha, r_dha, prev_dev)

    @pl.when(has_prev)
    def _():
        send_dhalo.start()

    y_send(3, 2)
    y_send(2, 3)

    hook("cb")

    s_x1, r_x1 = take_s(NCH), take_r(NCH)

    def d1_part(name, ids):
        def tile(n, _):
            cols = pl.ds(pl.multiple_of(n * 512, 512), 512)

            def rows_of(ref):
                return jnp.concatenate(
                    [ref[k * ROWS_CHUNK : (k + 1) * ROWS_CHUNK, :] for k in ids], axis=0
                )

            v = (
                nt(rows_of(pb), wg_v[cols, 0:CL])
                + nt(rows_of(pc), wg_v[cols, CL : 2 * CL])
                + nt(rows_of(px), wu_v[cols, 0:CL])
            ).astype(BF)
            for i, k in enumerate(ids):
                ring[k, :, cols] = v[i * ROWS_CHUNK : (i + 1) * ROWS_CHUNK]
            return 0

        lax.fori_loop(0, D // 512, tile, 0)
        for k in ids:
            remote(ring.at[k], xr_d1.at[k], s_x1 + k, r_x1 + k, x_dev).start()
        hook(name)

    d1_part("d1a", [q * CPS + k for q in range(S) for k in range(CPS - 1)])

    @pl.when(has_next)
    def _():
        wait_recv(dhalo_r, r_dha)

    @pl.when(jnp.logical_not(has_next))
    def _():
        dhalo_r[...] = jnp.zeros_like(dhalo_r)

    tail_iota = lax.broadcasted_iota(jnp.int32, (16, CL), 0)
    for q in range(S):
        first = jnp.broadcast_to(dhalo_r[q, 0:1, :], (16, CL))
        second = jnp.broadcast_to(dhalo_r[q, 1:2, :], (16, CL))
        fix = jnp.where(
            tail_iota == 14,
            k_taps[0] * first,
            jnp.where(tail_iota == 15, k_taps[1] * first + k_taps[0] * second, 0.0),
        )
        low = (tail[q] + fix).astype(BF).astype(F32)
        rows = pl.ds(q * T + T - 16, 16)
        pb[rows, :] = (low * px_tail[q].astype(F32)).astype(BF)
        px[rows, :] = (low * pb_tail[q].astype(F32)).astype(BF)

    s_dp, r_dp = take_s(4), take_r(4)
    theirs = pl.ds(pl.multiple_of((1 - c) * CH, LANE), CH)
    ours = pl.ds(pl.multiple_of(c * CH, LANE), CH)
    dp_sends = [
        remote(ref.at[:, theirs], dy_v.at[1, :, pl.ds(m * CH, CH)], s_dp + m, r_dp + m, core_dev)
        for m, ref in enumerate((pb, pc, px, gated))
    ]
    for cp in dp_sends:
        cp.start()
    hook("tail")

    d1_part("d1b", [q * CPS + k for q in range(S) for k in range(1, CPS)])

    for q in range(S):
        wait_recv(h1_v.at[1, pl.ds(q * T, T)], r_h1 + q)
    for k in range(NCH):
        rows = pl.ds(k * ROWS_CHUNK, ROWS_CHUNK)
        wait_recv(h2_v.at[1, rows], r_do + k)
    for m in range(4):
        wait_recv(dy_v.at[1, :, pl.ds(m * CH, CH)], r_dp + m)
    W4 = widths[4]
    g4 = [dg.at[i, pl.ds(k * SR, SR), pl.ds(0, W4)] for i in range(2) for k in range(2)]

    def g_mixer(u, _):
        zp = order_dyn(u)
        zc = pl.ds(pl.multiple_of(zp * GR, GR), GR)
        for m, (mine, lhs) in enumerate(((pb, h1_v), (pc, h1_v), (px, h1_v), (gated, h2_v))):
            v = tn(lhs[0, :, zc], mine[:, ours]) + tn(
                lhs[1, :, zc], dy_v[1, :, m * CH : (m + 1) * CH]
            )
            v = v.astype(BF)
            g4[0][:, m * CH : (m + 1) * CH] = v[:SR]
            g4[1][:, m * CH : (m + 1) * CH] = v[SR:]
        cps = [local(g4[h], gb4.at[zp, h], l_g + h) for h in range(2)]
        for cp in cps:
            cp.start()
        for cp in cps:
            cp.wait()

        @pl.when(u < NZ - 1)
        def _():
            y_send(4, u)

        return 0

    chunks("gc", NZ, g_mixer)
    for j in (3, 4):
        y_send(j, NZ - 1)

    l_o = take_l(2)

    def put_rows(v, out, rows, n):
        slot = n % 2
        cp = local(rb.at[slot], out.at[rows, :], l_o + slot)

        @pl.when(n >= 2)
        def _():
            cp.wait()

        rb[slot] = v
        cp.start()

    def put_done(out):
        for slot in range(2):
            local(rb.at[slot], out.at[pl.ds(0, ROWS_CHUNK), :], l_o + slot).wait()

    def block_chunk(k, _):
        rows = pl.ds(pl.multiple_of(k * ROWS_CHUNK, ROWS_CHUNK), ROWS_CHUNK)
        wait_recv(xr_dn.at[k], r_xdn + k)
        total = ring[4 + k].astype(F32) + xr_dn[k].astype(F32)
        put_rows((resid[rows, :] + total).astype(BF), block_out, rows, k)
        return 0

    chunks("blk", NCH, block_chunk)
    put_done(block_out)

    def mix_norm_back(n, _):
        k = (n % S) * CPS + n // S
        rows = pl.ds(pl.multiple_of(k * ROWS_CHUNK, ROWS_CHUNK), ROWS_CHUNK)
        wait_recv(xr_d1.at[k], r_x1 + k)
        d_h = ring[k].astype(F32) + xr_d1[k].astype(F32)
        xv = tok_v[rows, :].astype(F32)
        s1 = inv_rms(xv)
        n1 = xv * s1
        sm[0, 0:1, :] += jnp.sum(d_h * n1, axis=0, keepdims=True)
        e1 = d_h * gain_mix_row
        out = h2_v[0, rows, :].astype(F32) + s1 * (
            e1 - n1 * jnp.mean(e1 * n1, axis=-1, keepdims=True)
        )
        put_rows(out.astype(BF), d_tokens, rows, n)
        return 0

    chunks("dt", NCH, mix_norm_back)
    put_done(d_tokens)

    s_sm, r_sm = take_s(2 * NZ), take_r(2 * NZ)
    a = remote(sm.at[0], sm_o, s_sm, r_sm, core_dev)
    a.start()
    a.wait()
    chip_sum = sm[0] + sm_o[...]
    gain_w, tap_w = 2 * D // n_seq, 2 * CL // n_seq
    is_gain = lax.broadcasted_iota(jnp.int32, sm_t.shape[1:], 0) < 2
    for q in range(2 * NZ):
        gains = pltpu.roll(chip_sum, (D - q * gain_w) % D, 1)[:, 0:SMALL]
        tap_sums = pltpu.roll(chip_sum, (D - q * tap_w) % D, 1)[:, 0:SMALL]
        sm_t[q] = jnp.where(is_gain, gains, tap_sums)
    for k, dev in others:
        remote(sm_t.at[dev[0] // 2], sm_r.at[k], s_sm + k, r_sm + k, dev).start()
    @pl.when(end)
    def _():
        for e in range(NZ - 1):
            for h in range(2):
                per_core(0, lambda cut: wait_send(cut(gb0.at[0, h]), s_z[0] + 2 * e + h))

    for j in range(1, 5):
        for u in range(NZ - 1):
            per_core(j, lambda cut: wait_send(cut(ybs[j].at[0]), s_y[j] + u))
    for q in range(S):
        h1_send(q).wait_send()
    for k in range(NCH):
        wait_send(h2_v.at[0, pl.ds(k * ROWS_CHUNK, ROWS_CHUNK)], s_do + k)
        wait_send(ring.at[k], s_x1 + k)
        wait_send(ring.at[4 + k], s_xdn + k)
    for cp in dp_sends:
        cp.wait_send()

    @pl.when(has_next)
    def _():
        for q in range(S):
            halo_send(q).wait_send()

    @pl.when(has_prev)
    def _():
        send_dhalo.wait_send()

    hook("sm")

    total = sm_t[s // 2]
    for k, _ in others:
        wait_recv(sm_r.at[k], r_sm + k)
        total = total + sm_r[k]
    for k, _ in others:
        wait_send(sm_t.at[0], s_sm + k)
    sm_r[0] = total
    out_small = local(sm_r.at[0], small_out, l_small)
    out_small.start()
    out_small.wait()

    for role, cond in is_role.items():

        @pl.when(cond)
        def _(role=role):
            for finish in slot_last[role]:
                if finish is not None:
                    finish()

    for j in range(1, 5):
        per_core(j, lambda cut: wait_send(cut(ybs[j].at[0]), s_y[j] + NZ - 1))
    per_core(0, lambda cut: wait_send(cut(yb0), s_f0))


def fused_body(tokens, gain_mix, w_in, kernel, w_out, gain_ffn, w_gate, w_up, w_down, cotangent):
    S, T, D = tokens.shape
    CL = w_out.shape[0]
    FL = w_gate.shape[1]
    R = S * T
    n_seq = lax.axis_size("seq")
    tiles = FL // LANE
    FW = -(-tiles // 2) * LANE
    GR = D // NZ
    SR = GR // 2
    DR = SR // 2
    widths = [ZF_COLS, FW - ZF_COLS, FW, FW, 2 * CL]
    NCH = R // ROWS_CHUNK

    def sds(shape, dtype=BF):
        return jax.ShapeDtypeStruct(shape, dtype)

    outs = [sds((R, D)), sds((R, D)), sds((3, DR, FL)), sds((2, DR, 2 * CL)), sds((8, SMALL), F32)]
    outs += [sds((NZ, 2, SR, w)) for w in widths]
    outs += [sds((SR, widths[0]))] + [sds((NZ, SR, w)) for w in widths[1:]]
    outs += [sds((2, NZ, 2, SR, widths[0]))] + [sds((2, NZ, SR, w)) for w in widths[1:]]
    outs += [sds((NCH, ROWS_CHUNK, D))] * 2
    any_spec = pl.BlockSpec(memory_space=pl.ANY)
    V = pltpu.VMEM
    scratch = [
        V((D,), F32),
        V((3, CL), F32),
        V((D,), F32),
        V((R, D), BF),
        V((D, FW), BF),
        V((D, FW), BF),
        V((FW, D), BF),
        V((2, R, D), BF),
        V((2, R, D), BF),
        V((2, R, D), BF),
        V((2, R, FW), BF),
        V((2, R, FW), BF),
        V((2, R, FW), BF),
        V((R, CL), BF),
        V((R, CL), BF),
        V((R, CL), BF),
        V((R, CL), BF),
        V((R, CL), BF),
        V((R, D), F32),
        V((NCH, ROWS_CHUNK, D), BF),
        V((8, ROWS_CHUNK, D), BF),
        V((NCH, ROWS_CHUNK, D), BF),
        V((NCH, ROWS_CHUNK, D), BF),
        V((NCH, ROWS_CHUNK, D), BF),
        V((2, ROWS_CHUNK, D), BF),
        V((4, SR, FW), BF),
        V((4, SR, FW), BF),
        V((S, 16, CL), BF),
        V((S, 16, CL), BF),
        V((S, 8, CL), F32),
        V((S, 8, CL), F32),
        V((S, 16, CL), F32),
        V((S, 16, CL), BF),
        V((S, 16, CL), BF),
        V((1, 8, D), F32),
        V((8, D), F32),
        V((2 * NZ, 8, SMALL), F32),
        V((2 * NZ, 8, SMALL), F32),
        pltpu.SemaphoreType.DMA((N_SEND,)),
        pltpu.SemaphoreType.DMA((N_RECV,)),
        pltpu.SemaphoreType.DMA((N_LOCAL,)),
    ]
    flops = 2 * R * D * (4 * CL + 3 * FL) * 3
    res = pl.pallas_call(
        functools.partial(step_kernel, (R, T, D, CL, FL, FW)),
        out_shape=outs,
        in_specs=[any_spec] * 10,
        out_specs=[any_spec] * len(outs),
        scratch_shapes=scratch,
        compiler_params=pltpu.CompilerParams(
            collective_id=0, has_side_effects=True, vmem_limit_bytes=63 << 20
        ),
        cost_estimate=pl.CostEstimate(flops=flops, bytes_accessed=200 << 20, transcendentals=0),
        name="block_step",
    )(
        tokens.reshape(R, D), gain_mix, w_in, kernel, w_out,
        gain_ffn, w_gate, w_up, w_down, cotangent.reshape(R, D),
    )
    block_out, d_tokens, g_mix, g_in, g_taps, g_out, g_gain, g_gate, g_up, g_down = finish(
        n_seq, *res[:5]
    )
    return (
        block_out.reshape(S, T, D),
        d_tokens.reshape(S, T, D),
        g_mix, g_in, g_taps, g_out.T, g_gain, g_gate, g_up, g_down.T,
    )


def finish_kernel(
    n_seq, block_in, d_in, ffn_in, conv_in, small_in,
    block_out, d_out, g_mix, g_in, g_taps, g_out, g_gain, g_gate, g_up, g_down,
    block_v, d_v, ffn, conv, small, gate_v, up_v, down_v, in_v, out_v, mix_v, taps_v, gain_v, sem,
):
    D = d_in.shape[1]
    CL = conv_in.shape[2] // 2
    s = lax.axis_index("seq")
    count = [0]

    def copy(src, dst):
        count[0] += 1
        cp = pltpu.make_async_copy(src, dst, sem.at[count[0] - 1])
        cp.start()
        return cp

    loads = [copy(ffn_in.at[0], ffn.at[0]), copy(conv_in, conv), copy(small_in, small)]
    loads += [copy(ffn_in.at[m], ffn.at[m]) for m in (1, 2)]
    passing = [copy(block_in, block_v), copy(d_in, d_v)]
    stores = []
    loads[0].wait()
    down_v[...] = ffn[0].astype(F32)
    stores.append(copy(down_v, g_down))
    loads[1].wait()
    half = CL // 2
    for core in range(2):
        for m in range(3):
            in_v[m, :, core * half : (core + 1) * half] = conv[core, :, m * half : (m + 1) * half].astype(F32)
    stores.append(copy(in_v, g_in))
    for core in range(2):
        out_v[:, core * half : (core + 1) * half] = conv[core, :, 3 * half : 4 * half].astype(F32)
    stores.append(copy(out_v, g_out))
    passing[0].wait()
    stores.append(copy(block_v, block_out))
    passing[1].wait()
    stores.append(copy(d_v, d_out))
    loads[3].wait()
    gate_v[...] = ffn[1].astype(F32)
    stores.append(copy(gate_v, g_gate))
    loads[4].wait()
    up_v[...] = ffn[2].astype(F32)
    stores.append(copy(up_v, g_up))
    loads[2].wait()
    per_d, per_c = D // n_seq, CL // n_seq
    mine = pltpu.roll(small[...], SMALL - (s % 2) * per_d, 1)
    mix_v[...] = mine[0, 0:per_d]
    gain_v[...] = mine[1, 0:per_d]
    mine = pltpu.roll(small[...], SMALL - (s % 2) * per_c, 1)
    for t in range(3):
        taps_v[t] = mine[2 + t : 3 + t, 0:per_c]
    stores += [copy(mix_v, g_mix), copy(gain_v, g_gain), copy(taps_v, g_taps)]
    for cp in stores:
        cp.wait()


def finish(n_seq, block_out, d_tokens, g_ffn, g_conv, small):
    R, D = block_out.shape
    _, DR, FL = g_ffn.shape
    CL = g_conv.shape[2] // 2
    any_spec = pl.BlockSpec(memory_space=pl.ANY)
    V = pltpu.VMEM
    tails = [
        (DR, FL), (DR, FL), (DR, FL), (3, DR, CL), (DR, CL),
        (D // n_seq,), (3, 1, CL // n_seq), (D // n_seq,),
    ]
    gate, up, down, inp, out, mix, taps, gain = [jax.ShapeDtypeStruct(t, F32) for t in tails]
    low = jax.ShapeDtypeStruct((R, D), BF)
    return pl.pallas_call(
        functools.partial(finish_kernel, n_seq),
        out_shape=[low, low, mix, inp, taps, out, gain, gate, up, down],
        in_specs=[any_spec] * 5,
        out_specs=[any_spec] * 10,
        scratch_shapes=[V((R, D), BF), V((R, D), BF), V(g_ffn.shape, BF), V(g_conv.shape, BF), V(small.shape, F32)]
        + [V(t, F32) for t in tails]
        + [pltpu.SemaphoreType.DMA((20,))],
        compiler_params=pltpu.CompilerParams(vmem_limit_bytes=63 << 20),
        name="finish",
    )(block_out, d_tokens, g_ffn, g_conv, small)


def from_behind(value, axis, by):
    count = lax.axis_size(axis)
    pairs = [(i, i + by) for i in range(count) if 0 <= i + by < count]
    return lax.ppermute(value, axis, pairs)


def rms_scale(vector):
    return lax.rsqrt(jnp.mean(vector * vector, axis=-1, keepdims=True) + epsilon)


def norm_back(d_normout, normed, inv_scale, gain_vec):
    d_normed = d_normout * gain_vec
    return inv_scale * (d_normed - normed * jnp.mean(d_normed * normed, axis=-1, keepdims=True))


def matmul(lhs_mat, rhs_mat):
    return jnp.dot(lhs_mat, rhs_mat, preferred_element_type=jnp.float32)


def left_trans(lhs_mat, rhs_mat):
    return lax.dot_general(
        lhs_mat, rhs_mat, (((0,), (0,)), ((), ())), preferred_element_type=jnp.float32
    )


def right_trans(lhs_mat, rhs_mat):
    return lax.dot_general(
        lhs_mat, rhs_mat, (((1,), (1,)), ((), ())), preferred_element_type=jnp.float32
    )


def general_body(tokens, gain_mix, w_in, kernel, w_out, gain_ffn, w_gate, w_up, w_down, cotangent):
    seq_count, tok_rows, model_width = tokens.shape
    row_count = seq_count * tok_rows
    tokens_f = tokens.astype(jnp.float32).reshape(row_count, model_width)
    scale_mix = rms_scale(tokens_f)
    normed_mix = tokens_f * scale_mix
    h_mix = (normed_mix * gain_mix).astype(jnp.bfloat16)
    proj_b = matmul(h_mix, w_in[0])
    proj_c = matmul(h_mix, w_in[1])
    proj_x = matmul(h_mix, w_in[2])
    conv_in = (proj_b * proj_x).astype(jnp.bfloat16).reshape(seq_count, tok_rows, -1)
    before = from_behind(conv_in[:, tok_rows - 2 :, :], "seq", 1)
    extended = jnp.concatenate([before, conv_in], axis=1).astype(jnp.float32)
    conv_out = (
        kernel[0] * extended[:, :-2] + kernel[1] * extended[:, 1:-1] + kernel[2] * extended[:, 2:]
    )
    conv_flat = conv_out.reshape(row_count, -1)
    gated = (proj_c * conv_flat).astype(jnp.bfloat16)
    mixed_sum = lax.psum(matmul(gated, w_out).astype(jnp.bfloat16), "chan").astype(jnp.float32)
    residual = tokens_f + mixed_sum
    scale_ffn = rms_scale(residual)
    normed_ffn = residual * scale_ffn
    h_ffn = (normed_ffn * gain_ffn).astype(jnp.bfloat16)
    gate_pre = matmul(h_ffn, w_gate)
    up_value = matmul(h_ffn, w_up)
    sigmoid_gate = jax.nn.sigmoid(gate_pre)
    silu_gate = gate_pre * sigmoid_gate
    hidden = (silu_gate * up_value).astype(jnp.bfloat16)
    ffn_total = lax.psum(matmul(hidden, w_down).astype(jnp.bfloat16), "chan").astype(jnp.float32)
    block_out = (
        (residual + ffn_total).astype(jnp.bfloat16).reshape(seq_count, tok_rows, model_width)
    )
    grad_out = cotangent.reshape(row_count, model_width)
    g_w_down = left_trans(hidden, grad_out)
    d_hidden = right_trans(grad_out, w_down)
    d_gate = (d_hidden * up_value * sigmoid_gate * (1.0 + gate_pre * (1.0 - sigmoid_gate))).astype(
        jnp.bfloat16
    )
    d_up = (d_hidden * silu_gate).astype(jnp.bfloat16)
    g_w_gate = left_trans(h_ffn, d_gate)
    g_w_up = left_trans(h_ffn, d_up)
    d_h_ffn = lax.psum(
        (right_trans(d_gate, w_gate) + right_trans(d_up, w_up)).astype(jnp.bfloat16), "chan"
    ).astype(jnp.float32)
    g_gain_ffn = jnp.sum(d_h_ffn * normed_ffn, axis=0)
    d_resid = grad_out.astype(jnp.float32) + norm_back(d_h_ffn, normed_ffn, scale_ffn, gain_ffn)
    d_mixed = d_resid.astype(jnp.bfloat16)
    g_w_out = left_trans(gated, d_mixed)
    d_gated = right_trans(d_mixed, w_out)
    d_proj_c = (d_gated * conv_flat).astype(jnp.bfloat16)
    d_conv = (d_gated * proj_c).reshape(seq_count, tok_rows, -1)
    after_rows = from_behind(d_conv[:, :2, :], "seq", -1)
    ext_back = jnp.concatenate([d_conv, after_rows], axis=1)
    d_conv_in = (
        kernel[2] * ext_back[:, :-2] + kernel[1] * ext_back[:, 1:-1] + kernel[0] * ext_back[:, 2:]
    )
    g_kernel = jnp.stack(
        [
            jnp.sum(d_conv * extended[:, :-2], axis=(0, 1)),
            jnp.sum(d_conv * extended[:, 1:-1], axis=(0, 1)),
            jnp.sum(d_conv * extended[:, 2:], axis=(0, 1)),
        ]
    ).reshape(3, 1, -1)
    d_conv_low = d_conv_in.reshape(row_count, -1).astype(jnp.bfloat16)
    d_proj_b = (d_conv_low * proj_x).astype(jnp.bfloat16)
    d_proj_x = (d_conv_low * proj_b).astype(jnp.bfloat16)
    g_w_in = jnp.stack(
        [left_trans(h_mix, d_proj_b), left_trans(h_mix, d_proj_c), left_trans(h_mix, d_proj_x)]
    )
    d_h_mix = lax.psum(
        (
            right_trans(d_proj_b, w_in[0])
            + right_trans(d_proj_c, w_in[1])
            + right_trans(d_proj_x, w_in[2])
        ).astype(jnp.bfloat16),
        "chan",
    ).astype(jnp.float32)
    g_gain_mix = jnp.sum(d_h_mix * normed_mix, axis=0)
    d_tokens = (
        (d_resid + norm_back(d_h_mix, normed_mix, scale_mix, gain_mix))
        .astype(jnp.bfloat16)
        .reshape(seq_count, tok_rows, model_width)
    )
    summed = (
        lax.psum_scatter(g_w_in, "seq", scatter_dimension=1, tiled=True),
        lax.psum_scatter(g_w_out, "seq", scatter_dimension=1, tiled=True),
        lax.psum_scatter(g_kernel, "seq", scatter_dimension=2, tiled=True),
        lax.psum_scatter(g_gain_mix, "seq", scatter_dimension=0, tiled=True),
        lax.psum_scatter(g_w_gate, "seq", scatter_dimension=0, tiled=True),
        lax.psum_scatter(g_w_up, "seq", scatter_dimension=0, tiled=True),
        lax.psum_scatter(g_w_down, "seq", scatter_dimension=1, tiled=True),
        lax.psum_scatter(g_gain_ffn, "seq", scatter_dimension=0, tiled=True),
    )
    sum_in, sum_out, sum_kernel, sum_gain_mix, sum_gate, sum_up, sum_down, sum_gain_ffn = summed
    return (
        block_out,
        d_tokens,
        sum_gain_mix,
        sum_in,
        sum_kernel,
        sum_out,
        sum_gain_ffn,
        sum_gate,
        sum_up,
        sum_down,
    )


def solution(mesh):
    body = fused_body if mesh.shape["seq"] == 4 * NZ else general_body
    placed = (
        P(None, "seq", None),
        P(),
        P(None, None, "chan"),
        P(None, "chan"),
        P("chan", None),
        P(),
        P(None, "chan"),
        P(None, "chan"),
        P("chan", None),
        P(None, "seq", None),
    )
    return jax.shard_map(
        body,
        mesh=mesh,
        in_specs=placed,
        out_specs=(
            P(None, "seq", None),
            P(None, "seq", None),
            P("seq"),
            P(None, "seq", "chan"),
            P(None, "chan", "seq"),
            P("chan", "seq"),
            P("seq"),
            P("seq", "chan"),
            P("seq", "chan"),
            P("chan", "seq"),
        ),
        check_vma=False,
    )
```

```python
import functools

import jax
import jax.numpy as jnp
from jax import lax
from jax.experimental import pallas as pl
from jax.experimental.pallas import tpu as pltpu
from jax.sharding import PartitionSpec as P

epsilon = 1e-05
BF = jnp.bfloat16
F32 = jnp.float32
MESH = pl.DeviceIdType.MESH
LANE = 128
NZ = 4
ROWS_CHUNK = 128
SMALL = 256
ZF_COLS = 1280


def nn(a, b):
    return jnp.dot(a, b, preferred_element_type=F32)


def tn(a, b):
    return lax.dot_general(a, b, (((0,), (0,)), ((), ())), preferred_element_type=F32)


def nt(a, b):
    return lax.dot_general(a, b, (((1,), (1,)), ((), ())), preferred_element_type=F32)


def inv_rms(v):
    return lax.rsqrt(jnp.mean(v * v, axis=-1, keepdims=True) + epsilon)


class Take:
    def __init__(self, limit):
        self.used, self.limit = 0, limit

    def __call__(self, count=1):
        base = self.used
        self.used += count
        assert self.used <= self.limit
        return base


N_SEND, N_RECV, N_LOCAL = 128, 192, 64

SCHEDULE = {
    "dhA": (("end", (2, 0)), ("mid", (0, 0)), ("mid", (0, 2)),),
    "dhD": (("end", (1, 0)),),
    "dnA": (("mid", "pair"),),
    "nb0": (("end", (1, 2)),),
    "nb1": (("mid", (2, 0)),),
    "nb2": (("end", (3, 0)),),
    "nb3": (("end", (2, 1)),),
    "cb": (("end", (3, 1)),),
    "d1a": (("end", (2, 2)), ("mid", (1, 0)), ("mid", (0, 1)), ("mid", (3, 0)),),
    "tail": (("mid", (1, 1)),),
    "d1b": (("mid", (2, 2)),),
    "gc1": (("end", "pair"),),
    "gc3": (("end", (1, 3)), ("end", (1, 1)), ("end", (4, 0)), ("end", (4, 1)),),
    "blk0": (("mid", (3, 2)),),
    "blk1": (("mid", (2, 3)), ("mid", (1, 2)),),
    "blk3": (("end", (3, 2)), ("mid", (2, 1)),),
    "dt0": (("mid", (4, 0)), ("mid", (1, 3)), ("mid", (3, 1)), ("mid", (4, 1)), ("mid", (4, 2)),),
    "dt1": (("end", (2, 3)), ("end", (4, 2)), ("end", "pair sum"),),
    "dt2": (("end", (3, 3)),),
    "sm": (("end", (4, 3)), ("mid", "pair sum"), ("mid", (3, 3)), ("mid", (4, 3)),),
}


def step_kernel(
    dims,
    tokens, gain_mix_hbm, w_in, taps_hbm, w_out, gain_ffn_hbm, w_gate, w_up, w_down, cot,
    block_out, d_tokens, g_ffn, g_conv, small_out,
    gb0, gb1, gb2, gb3, gb4, yb0, yb1, yb2, yb3, yb4, zb0, zb1, zb2, zb3, zb4,
    cr_dh, cr_dn,
    gain_mix, taps, gain_ffn, tok_v, wg_v, wu_v, wd_v, dy_v, h2_v, h1_v, hid, dg, du, pb, pc, px, bx, gated, resid, gall,
    ring, xr_dh, xr_dn, xr_d1, rb, ld, outs, halo_s, halo_r, dhalo_s, dhalo_r, tail, pb_tail, px_tail,
    sm, sm_o, sm_t, sm_r, ss, rs, ls,
):
    R, T, D, CL, FL, FW = dims
    S = R // T
    CH = CL // 2
    GR = D // NZ
    SR = GR // 2
    DR = SR // 2
    NCH = R // ROWS_CHUNK
    take_s, take_r, take_l = Take(N_SEND), Take(N_RECV), Take(N_LOCAL)

    s = lax.axis_index("seq")
    x = lax.axis_index("chan")
    n_seq = 4 * NZ
    z, y, c = s // 4, (s // 2) % 2, s % 2

    def did(z_, y_, c_):
        return ((z_ * 2 + y_) * 2 + c_, x)

    core_dev = did(z, y, 1 - c)
    y_dev = did(z, 1 - y, c)
    x_dev = (s, 1 - x)
    mid = jnp.logical_and(z > 0, z < NZ - 1)
    end = jnp.logical_not(mid)

    def remote(src, dst, si, ri, dev):
        return pltpu.make_async_remote_copy(
            src_ref=src, dst_ref=dst, send_sem=ss.at[si], recv_sem=rs.at[ri],
            device_id=dev, device_id_type=MESH,
        )

    def wait_recv(dst, ri):
        remote(dst, dst, 0, ri, core_dev).wait_recv()

    def wait_send(src, si):
        remote(src, src, si, 0, core_dev).wait_send()

    def local(src, dst, li):
        return pltpu.make_async_copy(src, dst, ls.at[li])

    l_tok, l_win, l_wout, l_dy, l_small = take_l(), take_l(3), take_l(), take_l(), take_l(3)
    ld_tok = local(tokens, tok_v, l_tok)
    ld_tok.start()
    win_views = [wg_v.at[:, pl.ds(0, CL)], wg_v.at[:, pl.ds(CL, CL)], wu_v.at[:, pl.ds(0, CL)]]
    wout_view = wd_v.at[pl.ds(pl.multiple_of(x * CL, CL), CL), :]

    def load_w_in():
        return [local(w_in.at[m], win_views[m], l_win + m) for m in range(3)]

    for cp in load_w_in():
        cp.start()
    ld_small = [
        local(src, dst, l_small + i)
        for i, (src, dst) in enumerate(
            ((gain_mix_hbm, gain_mix), (taps_hbm, taps), (gain_ffn_hbm, gain_ffn))
        )
    ]
    for cp in ld_small:
        cp.start()
    ld_wout = local(w_out, wout_view, l_wout)
    ld_wout.start()
    ld_dy = local(cot, dy_v.at[0], l_dy)

    bar = pltpu.get_barrier_semaphore()

    def greet(dev):
        pl.semaphore_signal(bar, inc=1, device_id=dev, device_id_type=MESH)

    greet(core_dev)
    greet(x_dev)
    others = [(k, did((z + k // 2) % NZ, (y + k % 2) % 2, c)) for k in range(1, 2 * NZ)]
    for _, dev in others:
        greet(dev)
    has_prev = s > 0
    has_next = s < n_seq - 1
    prev_dev = ((s + n_seq - 1) % n_seq, x)
    next_dev = ((s + 1) % n_seq, x)
    greet(prev_dev)
    greet(next_dev)
    pl.semaphore_wait(bar, 3 + 2 * NZ)

    SUBS = 2
    ER = CL // 8
    PR = ER // SUBS
    zi = z % 2
    z_dev = did(z + 1 - 2 * zi, y, c)
    mine_e = zi * 4 + y * 2 + c
    pair_e = zi * 4 + (1 - y) * 2 + c
    line_e = (1 - zi) * 4 + y * 2 + c
    far_e = (1 - zi) * 4 + (1 - y) * 2 + c
    w_sems = {}

    def w_rows(half, eighth, sub):
        return wd_v.at[pl.ds(pl.multiple_of(half * CL + eighth * ER + sub * PR, PR), PR), :]

    def w_copy(name, eighth, sub, dev):
        if (name, sub) not in w_sems:
            w_sems[name, sub] = take_s(), take_r()
        ref = w_rows(1 - x, eighth, sub)
        return remote(ref, ref, *w_sems[name, sub], dev)

    def w_came(name, eighth, sub):
        wait_recv(w_rows(1 - x, eighth, sub), w_sems[name, sub][1])

    def w_over_x(sub):
        if ("x", sub) not in w_sems:
            w_sems["x", sub] = take_s(), take_r()
        src = w_out.at[pl.ds(pl.multiple_of(mine_e * ER + sub * PR, PR), PR), :]
        return remote(src, w_rows(x, mine_e, sub), *w_sems["x", sub], x_dev)

    w_sent = []

    def w_pass(name, eighth, sub, targets):
        w_came(name, eighth, sub)
        for to, dev in targets:
            w_copy(to, eighth, sub, dev).start()
            w_sent.append((to, eighth, sub, dev))

    def w_mine(sub):
        w_pass("x", mine_e, sub, (("z", z_dev), ("y", y_dev), ("core", core_dev)))

    def w_pair(sub):
        to = (("zy", z_dev),) if sub == 0 else ()
        w_pass("y", pair_e, sub, to + (("core pair", core_dev),))

    def w_line(sub):
        to = (("zy", y_dev),) if sub == 1 else ()
        w_pass("z", line_e, sub, to + (("core line", core_dev),))

    def w_far(sub):
        w_pass("zy", far_e, sub, (("core far", core_dev),))

    for sub in range(SUBS):
        w_over_x(sub).start()

    l_w = take_l(3)
    win_start = pl.multiple_of(c * (FL - FW), LANE)
    ld_wg = local(w_gate.at[:, pl.ds(win_start, FW)], wg_v, l_w)
    ld_wu = local(w_up.at[:, pl.ds(win_start, FW)], wu_v, l_w + 1)
    ld_wd = local(w_down.at[pl.ds(win_start, FW), :], wd_v, l_w + 2)

    sm[...] = jnp.zeros_like(sm)
    for cp in ld_small:
        cp.wait()
    gain_mix_row = gain_mix[...].reshape(1, D)
    gain_ffn_row = gain_ffn[...].reshape(1, D)
    k_taps = [taps[t : t + 1, :] for t in range(3)]

    ld_tok.wait()

    CPS = T // ROWS_CHUNK
    NC = CL // 256
    s_h1, r_h1 = take_s(S), take_r(S)
    s_ha, r_ha = take_s(S), take_r(S)
    s_mx, r_mx = take_s(NCH), take_r(NCH)
    row_iota = lax.broadcasted_iota(jnp.int32, (T, 256), 0)
    top_iota = row_iota[0:16]

    def conv_terms(now, h, iota):
        h14 = jnp.broadcast_to(h[14:15], now.shape)
        h15 = jnp.broadcast_to(h[15:16], now.shape)
        one = jnp.where(iota == 0, h15, pltpu.roll(now, 1, 0))
        two = jnp.where(iota == 0, h14, jnp.where(iota == 1, h15, pltpu.roll(now, 2, 0)))
        return now, one, two

    def tap_cols(cols):
        return [taps[t : t + 1, cols] for t in range(3)]

    def convolve(terms, cols):
        now, one, two = terms
        k0, k1, k2 = tap_cols(cols)
        return k0 * two + k1 * one + k2 * now

    def h1_send(q):
        rows = pl.ds(q * T, T)
        return remote(h1_v.at[0, rows], h1_v.at[1, rows], s_h1 + q, r_h1 + q, core_dev)

    def halo_send(q):
        return remote(halo_s.at[q], halo_r.at[q], s_ha + q, r_ha + q, next_dev)

    own_cols = pl.ds(pl.multiple_of(x * CL, CL), CL)
    other_cols = pl.ds(pl.multiple_of((1 - x) * CL, CL), CL)

    def gated_send(k):
        ref = gall.at[k, :, own_cols]
        return remote(ref, ref, s_mx + k, r_mx + k, x_dev)

    def mixer_out(k):
        gall[k, :, own_cols] = gated[k * ROWS_CHUNK : (k + 1) * ROWS_CHUNK, :]
        gated_send(k).start()

    for q in range(S):
        rows = pl.ds(q * T, T)

        def norm_rows(k, _, q=q):
            chunk = pl.ds(pl.multiple_of(q * T + k * ROWS_CHUNK, ROWS_CHUNK), ROWS_CHUNK)
            xv = tok_v[chunk, :].astype(F32)
            h1_v[0, chunk, :] = (xv * inv_rms(xv) * gain_mix_row).astype(BF)
            return 0

        lax.fori_loop(0, CPS, norm_rows, 0)
        if q == 0:
            for cp in load_w_in():
                cp.wait()

        def in_proj(j, _, q=q, rows=rows):
            cols = pl.ds(pl.multiple_of(j * 256, 256), 256)
            cols1 = pl.ds(pl.multiple_of(CL + j * 256, 256), 256)
            h = h1_v[0, rows, :]
            b = nn(h, wg_v[:, cols])
            pb[rows, cols] = b.astype(BF)
            xx = nn(h, wu_v[:, cols])
            px[rows, cols] = xx.astype(BF)
            inner = (b * xx).astype(BF)
            bx[rows, cols] = inner
            halo_s[q, :, cols] = inner[T - 16 : T]
            pcv = nn(h, wg_v[:, cols1])
            pc[rows, cols] = pcv.astype(BF)
            now = inner.astype(F32)
            cv = convolve(conv_terms(now, jnp.zeros_like(now[0:16]), row_iota), cols)
            gated[rows, cols] = (pcv * cv).astype(BF)
            return 0

        lax.fori_loop(0, NC, in_proj, 0)
        if q == S - 1:
            ld_wg.start()
            ld_wu.start()

        @pl.when(has_next)
        def _(q=q):
            halo_send(q).start()

        for k in range(CPS - 1, 0, -1):
            mixer_out(q * CPS + k)
        if q > 0:
            w_mine(1)

        @pl.when(has_prev)
        def _(q=q):
            wait_recv(halo_r.at[q], r_ha + q)

        @pl.when(jnp.logical_not(has_prev))
        def _(q=q):
            halo_r[q] = jnp.zeros_like(halo_r[q])

        def conv_top(j, _, q=q):
            cols = pl.ds(pl.multiple_of(j * 256, 256), 256)
            top = pl.ds(q * T, 16)
            now = bx[top, cols].astype(F32)
            cv = convolve(conv_terms(now, halo_r[q, :, cols].astype(F32), top_iota), cols)
            gated[top, cols] = (pc[top, cols].astype(F32) * cv).astype(BF)
            return 0

        lax.fori_loop(0, NC, conv_top, 0)
        mixer_out(q * CPS)
        if q == 0:
            w_mine(0)
        h1_send(q).start()
        if q == 0:
            ld_dy.start()
            s_dy, r_dy = take_s(), take_r()
            send_dy = remote(cot, dy_v.at[1], s_dy, r_dy, core_dev)
            send_dy.start()
    w_line(0)
    w_pair(0)
    w_line(1)
    w_pair(1)

    s_h2, r_h2 = take_s(NCH), take_r(NCH)
    ld_wg.wait()
    ld_wu.wait()
    NF, NA = FW // 256, ZF_COLS // 256
    overlap = 2 * FW - FL
    col_iota = lax.broadcasted_iota(jnp.int32, (2 * ROWS_CHUNK, 256), 1)

    def sent(n):
        return (n // CPS) * CPS + (CPS - 1 - n % CPS)

    def ffn_tile(h, cols, keep):
        g = nn(h, wg_v[:, cols])
        u = nn(h, wu_v[:, cols])
        sg = jax.nn.sigmoid(g)
        si = g * sg
        slope = u * sg * (1.0 + g * (1.0 - sg))
        if keep is not None:
            si, slope = jnp.where(keep, si, 0.0), jnp.where(keep, slope, 0.0)
        return (si * u).astype(BF), slope.astype(BF), si.astype(BF)

    def residual_chunk(k):
        rows = pl.ds(pl.multiple_of(k * ROWS_CHUNK, ROWS_CHUNK), ROWS_CHUNK)
        wait_recv(gall.at[k, :, other_cols], r_mx + k)

        def out_tile(j, _):
            cols = pl.ds(pl.multiple_of(j * 512, 512), 512)
            resid[rows, cols] = tok_v[rows, cols].astype(F32) + nn(gall[k], wd_v[0 : 2 * CL, cols])
            return 0

        lax.fori_loop(0, D // 512, out_tile, 0, unroll=True)
        res = resid[rows, :]
        h2_v[0, rows, :] = (res * inv_rms(res) * gain_ffn_row).astype(BF)
        remote(h2_v.at[0, rows], h2_v.at[1, rows], s_h2 + k, r_h2 + k, core_dev).start()

    def forward_chunk(k):
        rows = pl.ds(pl.multiple_of(k * ROWS_CHUNK, ROWS_CHUNK), ROWS_CHUNK)
        wait_recv(h2_v.at[1, rows], r_h2 + k)

        def tile(j, _):
            cols = pl.ds(pl.multiple_of(j * 256, 256), 256)
            h = h2_v[:, rows, :].reshape(2 * ROWS_CHUNK, D)
            keep = col_iota + j * 256 >= c * overlap
            for ref, v in zip((hid, dg, du), ffn_tile(h, cols, keep)):
                ref[:, rows, cols] = v.reshape(2, ROWS_CHUNK, 256)
            return 0

        lax.fori_loop(0, NA, tile, 0, unroll=True)

    def forward_rest(slot):
        for j in range(NA, NF):
            cols = slice(j * 256, (j + 1) * 256)
            for ref, v in zip((hid, dg, du), ffn_tile(h2_v[slot], cols, None)):
                ref[slot, :, cols] = v

    for sub in range(SUBS):
        w_far(sub)
    ld_wout.wait()
    for sub in range(SUBS):
        for name, eighth in (("core", mine_e), ("core pair", pair_e), ("core line", line_e), ("core far", far_e)):
            w_came(name, eighth + 1 - 2 * c, sub)
    residual_chunk(sent(0))

    def chunk_loop(n, _):
        @pl.when(n + 1 < NCH)
        def _():
            residual_chunk(sent(n + 1))

        forward_chunk(sent(n))
        return 0

    lax.fori_loop(0, NCH, chunk_loop, 0)
    for sub in range(SUBS):
        w_over_x(sub).wait_send()
    for item in w_sent:
        w_copy(*item).wait_send()
    ld_wd.start()
    ld_dy.wait()
    send_dy.wait()
    for k in range(NCH):
        gated_send(k).wait_send()
        wait_send(h2_v.at[0, pl.ds(k * ROWS_CHUNK, ROWS_CHUNK)], s_h2 + k)

    gbs = [gb0, gb1, gb2, gb3, gb4]
    ybs = [yb0, yb1, yb2, yb3, yb4]
    zbs = [zb0, zb1, zb2, zb3, zb4]
    widths = [ZF_COLS, FW - ZF_COLS, FW, FW, 2 * CL]
    s_y = [None] + [take_s(NZ) for _ in range(4)]
    r_y = [None] + [take_r(NZ) for _ in range(4)]
    s_z = [take_s(2 * NZ)] + [take_s(NZ) for _ in range(4)]
    r_z = [take_r(4 * NZ)] + [take_r(2 * NZ) for _ in range(4)]

    def order(e):
        if e == NZ - 1:
            return z
        per_z = {0: (3, 2, 1), 1: (3, 0, 2), 2: (0, 3, 1), 3: (0, 1, 2)}
        v = per_z[3][e]
        for zz in range(3):
            v = jnp.where(z == zz, per_z[zz][e], v)
        return v

    def order_dyn(u):
        v = order(NZ - 1)
        for e in range(NZ - 1):
            v = jnp.where(u == e, order(e), v)
        return v

    def per_core(j, act):
        if j in (1, 4):
            act(lambda ref: ref)
            return

        @pl.when(c == 0)
        def _():
            act(lambda ref: ref)

        @pl.when(c == 1)
        def _():
            act(lambda ref: ref.at[:, pl.ds(overlap, widths[j] - overlap)])

    def z_send(j, src, e, zp, h=None):
        to_right = zp > z
        d = jnp.where(to_right, 0, 1)
        dev = did(jnp.clip(jnp.where(to_right, z + 1, z - 1), 0, NZ - 1), y, c)
        if h is None:
            dst, si, ri = zbs[j].at[d, zp], s_z[j] + e, r_z[j] + d * NZ + zp
        else:
            dst, si, ri = zbs[j].at[d, zp, h], s_z[j] + 2 * e + h, r_z[j] + (d * NZ + zp) * 2 + h
        per_core(j, lambda cut: remote(cut(src), cut(dst), si, ri, dev).start())

    l_g = take_l(12)

    def y_send(j, u):
        zp = order_dyn(u) if not isinstance(u, int) else order(u)
        src, dst = gbs[j].at[zp, 1 - y], ybs[j].at[zp]
        per_core(j, lambda cut: remote(cut(src), cut(dst), s_y[j] + u, r_y[j] + u, y_dev).start())

    def g_block(lhs_ref, rhs_ref, zp, pair, parts=(0, 1)):
        lhs = lhs_ref[:, :, pl.ds(pl.multiple_of(zp * GR, GR), GR)].reshape(2 * R, GR)
        cut = ZF_COLS
        for n in parts:
            cols = slice(0, cut) if n == 0 else slice(cut, FW)
            v = tn(lhs, rhs_ref[:, :, cols].reshape(2 * R, cols.stop - cols.start)).astype(BF)
            outs[2 * pair, :, cols] = v[:SR]
            outs[2 * pair + 1, :, cols] = v[SR:]

    def line_copies(u):
        zp = order(u)
        return [
            local(outs.at[2 * (u % 2) + h, :, pl.ds(0, ZF_COLS)], gb0.at[zp, h], l_g + 2 * (u % 2) + h)
            for h in range(2)
        ]

    def pair_copies(u):
        zp = order(u)
        return [
            local(
                outs.at[2 * (u % 2) + h, :, pl.ds(ZF_COLS, FW - ZF_COLS)],
                gb1.at[zp, h], l_g + 4 + 2 * (u % 2) + h,
            )
            for h in range(2)
        ]

    def start(copies):
        for cp in copies:
            cp.start()

    def wait(copies):
        for cp in copies:
            cp.wait()

    def line_sends(u):
        wait(line_copies(u))
        if u < NZ - 1:

            @pl.when(end)
            def _():
                for h in range(2):
                    z_send(0, gb0.at[order(u), h], u, order(u), h)

    def pair_sends(u):
        wait(pair_copies(u))
        y_send(1, u)

    for u in range(NZ):
        g_block(dy_v, hid, order(u), u % 2, (0,))
        start(line_copies(u))
        if u == 0:
            forward_rest(0)
            line_sends(0)
            forward_rest(1)
        else:
            pair_sends(u - 1)
        g_block(dy_v, hid, order(u), u % 2, (1,))
        start(pair_copies(u))
        if u > 0:
            line_sends(u)
    pair_sends(NZ - 1)

    ld_wd.wait()

    def hid_back(slot, _):
        for j in range(NF):
            cols = slice(j * 256, (j + 1) * 256)
            dh = nt(dy_v[slot], wd_v[cols, :])
            dg[slot, :, cols] = (dh * dg[slot, :, cols].astype(F32)).astype(BF)
            du[slot, :, cols] = (dh * du[slot, :, cols].astype(F32)).astype(BF)
        return 0

    lax.fori_loop(0, 2, hid_back, 0)

    def plain_copies(gb, zp, pair):
        return [local(outs.at[2 * pair + h], gb.at[zp, h], l_g + 2 * pair + h) for h in range(2)]

    def gate_up(u, _):
        zp = order_dyn(u)

        def up_sends(u):
            for cp in plain_copies(gb3, order_dyn(u), 1):
                cp.wait()

            @pl.when(u < 2)
            def _():
                y_send(3, u)

        g_block(h2_v, dg, zp, 0, (0,))

        @pl.when(u > 0)
        def _():
            up_sends(u - 1)

        g_block(h2_v, dg, zp, 0, (1,))
        for cp in plain_copies(gb2, zp, 0):
            cp.start()
        g_block(h2_v, du, zp, 1, (0,))
        for cp in plain_copies(gb2, zp, 0):
            cp.wait()

        @pl.when(u < 3)
        def _():
            y_send(2, u)

        g_block(h2_v, du, zp, 1, (1,))
        for cp in plain_copies(gb3, zp, 1):
            cp.start()
        return 0

    lax.fori_loop(0, NZ, gate_up, 0)
    for cp in plain_copies(gb3, order(NZ - 1), 1):
        cp.wait()

    l_e = take_l(4)
    is_role = {"end": end, "mid": mid}
    slot_last = {role: [None] * outs.shape[0] for role in is_role}
    slot_next = {role: 0 for role in is_role}

    def claim_slot(role):
        o = slot_next[role]
        slot_next[role] = (o + 1) % outs.shape[0]
        if slot_last[role][o] is not None:
            slot_last[role][o]()
            slot_last[role][o] = None
        return o

    ADD_ROWS = 32

    def add_into(dst, srcs):
        def rows_add(k, _):
            rows = pl.ds(pl.multiple_of(k * ADD_ROWS, ADD_ROWS), ADD_ROWS)
            acc = srcs[0][rows, :].astype(F32)
            for src in srcs[1:]:
                acc = acc + src[rows, :].astype(F32)
            dst[rows, :] = acc.astype(BF)
            return 0

        lax.fori_loop(0, SR // ADD_ROWS, rows_add, 0)

    def fetch(j, srcs):
        w = widths[j]
        views, copies = [], []
        for i, (src, ri) in enumerate(srcs):
            if ri is not None:
                per_core(j, lambda cut: wait_recv(cut(src), ri))
            views.append(ld.at[i, :, pl.ds(0, w)])
            copies.append(local(src, views[-1], l_e + i))
            copies[-1].start()
        for cp in copies:
            cp.wait()
        return views

    def from_line(j, d, zp, h=None):
        if h is None:
            return zbs[j].at[d, zp], r_z[j] + d * NZ + zp
        return zbs[j].at[d, zp, h], r_z[j] + (d * NZ + zp) * 2 + h

    def line_event(role, j, e):
        @pl.when(is_role[role])
        def _():
            zp = order(e)
            w = widths[j]
            d = jnp.where(zp > z, 0, 1)
            for h in (0, 1) if j == 0 else (None,):
                o = claim_slot(role)
                dst = outs.at[o, :, pl.ds(0, w)]
                if h is None:
                    srcs = [(gbs[j].at[zp, y], None), (ybs[j].at[zp], r_y[j] + e)]
                    si = s_z[j] + e
                else:
                    srcs = [(gbs[j].at[zp, h], None)]
                    si = s_z[j] + 2 * e + h
                if role == "mid":
                    srcs.append(from_line(j, d, zp, h))
                add_into(dst, fetch(j, srcs))
                z_send(j, dst, e, zp, h)
                slot_last[role][o] = functools.partial(sent_slot, j, o, si)

    def sent_slot(j, o, si):
        per_core(j, lambda cut: wait_send(cut(outs.at[o, :, pl.ds(0, widths[j])]), si))

    def own_shard(role, j, h=None):
        if h is None:
            srcs = [(gbs[j].at[z, y], None), (ybs[j].at[z], r_y[j] + NZ - 1)]
        else:
            srcs = [(gbs[j].at[z, h], None)]
        if role == "mid":
            near = jnp.where(z < NZ // 2, 0, 1)
            return srcs + [from_line(j, 1 - near, z, h), from_line(j, near, z, h)]
        return srcs + [from_line(j, jnp.where(z == 0, 1, 0), z, h)]

    def swap_pieces(j):
        if j == 4:
            return [(None, 0, 4 * CH, g_conv.at[c], 0)]
        mat = g_ffn.at[{0: 0, 1: 0, 2: 1, 3: 2}[j]]
        w = widths[j]
        if j == 1:
            return [(None, 0, w, mat, c * (FL - FW) + ZF_COLS)]
        return [(0, 0, w, mat, 0), (1, overlap, w - overlap, mat, FL - FW + overlap)]

    swap_sems = [[(take_s(), take_r(), take_l()) for _ in swap_pieces(j)] for j in range(5)]

    def swap(j, o):
        items = []
        for (core, c0, w, mat, to), (si, ri, li) in zip(swap_pieces(j), swap_sems[j]):
            to = to if isinstance(to, int) else pl.multiple_of(to, LANE)
            target = mat.at[:, pl.ds(to, w)]
            mine = outs.at[o, pl.ds(pl.multiple_of(c * DR, DR), DR), pl.ds(c0, w)]
            other = outs.at[o, pl.ds(pl.multiple_of((1 - c) * DR, DR), DR), pl.ds(c0, w)]
            items.append((core, local(mine, target, li), remote(other, target, si, ri, core_dev), target))
        return items

    def swap_start(j, o):
        for core, keep, give, _ in swap(j, o):
            if core is None:
                keep.start()
                give.start()
            else:

                @pl.when(c == core)
                def _():
                    keep.start()
                    give.start()

    def swap_finish(j, o):
        for (core, keep, give, target), (_, ri, _) in zip(swap(j, o), swap_sems[j]):
            if core is None:
                keep.wait()
                give.wait_send()
                wait_recv(target, ri)
            else:

                @pl.when(c == core)
                def _():
                    keep.wait()
                    give.wait_send()

                @pl.when(c != core)
                def _():
                    wait_recv(target, ri)

    def final_event(role, j):
        @pl.when(is_role[role])
        def _():
            o = claim_slot(role)
            w = widths[j]
            add_into(outs.at[o, :, pl.ds(0, w)], fetch(j, own_shard(role, j)))
            swap_start(j, o)
            slot_last[role][o] = functools.partial(swap_finish, j, o)

    s_f0, r_f0 = take_s(), take_r()
    w0 = widths[0]

    def final0_send(role):
        @pl.when(is_role[role])
        def _():
            o = claim_slot(role)
            dst = outs.at[o, :, pl.ds(0, w0)]
            add_into(dst, fetch(0, own_shard(role, 0, 1 - y)))
            cp = local(dst, gb0.at[z, 1 - y], l_e)
            cp.start()
            cp.wait()
            src = gb0.at[z, 1 - y]
            per_core(0, lambda cut: remote(cut(src), cut(yb0), s_f0, r_f0, y_dev).start())

    def final0_finish(role):
        @pl.when(is_role[role])
        def _():
            o = claim_slot(role)
            dst = outs.at[o, :, pl.ds(0, w0)]
            add_into(dst, fetch(0, own_shard(role, 0, y)))
            add_into(dst, [dst] + fetch(0, [(yb0, r_f0)]))
            swap_start(0, o)
            slot_last[role][o] = functools.partial(swap_finish, 0, o)

    def hook(name):
        for role, event in SCHEDULE.get(name, ()):
            if event == "pair":
                final0_send(role)
            elif event == "pair sum":
                final0_finish(role)
            elif event[1] == NZ - 1:
                final_event(role, event[0])
            else:
                line_event(role, *event)

    def chunks(name, count, body):
        first = 0
        for k in range(count):
            if SCHEDULE.get(name + str(k)) or k == count - 1:
                lax.fori_loop(first, k + 1, body, 0)
                first = k + 1
                hook(name + str(k))

    HALF = 2 * ROWS_CHUNK

    def split_sum(name, product, cr, xr, base_d):
        s_c, r_c = take_s(2), take_r(2)
        s_x, r_x = take_s(NCH), take_r(NCH)
        l_c = take_l()

        def give(k, _):
            def tile(n, _):
                cols = pl.ds(pl.multiple_of(n * 512, 512), 512)
                v = product(1, k * HALF, n).astype(BF)
                gall[pl.ds(2 * k, 2), :, cols] = v.reshape(2, ROWS_CHUNK, 512)
                return 0

            lax.fori_loop(0, D // 512, tile, 0)
            remote(
                gall.at[pl.ds(2 * k, 2)], cr.at[pl.ds(2 * k, 2)], s_c + k, r_c + k, core_dev
            ).start()
            return 0

        lax.fori_loop(0, 2, give, 0)
        hook(name + "A")

        def keep(k, _):
            src = cr.at[pl.ds(2 * k, 2)]
            wait_recv(src, r_c + k)
            cp = local(src, rb, l_c)
            cp.start()
            cp.wait()

            def tile(n, _):
                cols = pl.ds(pl.multiple_of(n * 512, 512), 512)
                v = product(0, k * HALF, n) + rb[:, :, cols].reshape(HALF, 512).astype(F32)
                ring[pl.ds(base_d + 2 * k, 2), :, cols] = v.astype(BF).reshape(2, ROWS_CHUNK, 512)
                return 0

            lax.fori_loop(0, D // 512, tile, 0)
            for i in range(2):
                remote(
                    ring.at[base_d + 2 * k + i], xr.at[2 * k + i], s_x + 2 * k + i, r_x + 2 * k + i, x_dev
                ).start()
            return 0

        lax.fori_loop(0, 2, keep, 0)
        for k in range(2):
            wait_send(gall.at[pl.ds(2 * k, 2)], s_c + k)
        hook(name + "D")
        return s_x, r_x

    def rows_at(ref, slot, r0):
        return ref[slot, pl.ds(pl.multiple_of(r0, HALF), HALF), :]

    def dh_product(slot, r0, n):
        cols = pl.ds(pl.multiple_of(n * 512, 512), 512)
        return nt(rows_at(dg, slot, r0), wg_v[cols, :]) + nt(rows_at(du, slot, r0), wu_v[cols, :])

    def dn_product(slot, r0, n):
        cols = pl.ds(pl.multiple_of(n * 512, 512), 512)
        return nn(rows_at(hid, slot, r0), wd_v[:, cols])

    s_xdh, r_xdh = split_sum("dh", dh_product, cr_dh, xr_dh, 0)
    s_xdn, r_xdn = split_sum("dn", dn_product, cr_dn, xr_dn, 4)
    for cp in load_w_in():
        cp.start()
    ld_wout = local(w_out, wd_v.at[pl.ds(0, CL), :], l_wout)
    ld_wout.start()

    s_do, r_do = take_s(NCH), take_r(NCH)

    def ffn_norm_back(k, _):
        rows = pl.ds(pl.multiple_of(k * ROWS_CHUNK, ROWS_CHUNK), ROWS_CHUNK)
        wait_recv(xr_dh.at[k], r_xdh + k)
        d_h = ring[k].astype(F32) + xr_dh[k].astype(F32)
        res = resid[rows, :]
        s2 = inv_rms(res)
        n2 = res * s2
        sm[0, 1:2, :] += jnp.sum(d_h * n2, axis=0, keepdims=True)
        e2 = d_h * gain_ffn_row
        d_res = dy_v[0, rows, :].astype(F32) + s2 * (
            e2 - n2 * jnp.mean(e2 * n2, axis=-1, keepdims=True)
        )
        h2_v[0, rows, :] = d_res.astype(BF)
        remote(h2_v.at[0, rows], h2_v.at[1, rows], s_do + k, r_do + k, core_dev).start()
        return 0

    chunks("nb", NCH, ffn_norm_back)
    for k in range(NCH):
        wait_send(ring.at[k], s_xdh + k)

    for cp in load_w_in():
        cp.wait()
    ld_wout.wait()
    for q in range(S):

        def conv_back(j, _, q=q):
            cols = pl.ds(pl.multiple_of(j * 256, 256), 256)
            rows = pl.ds(q * T, T)
            now, one, two = conv_terms(
                bx[rows, cols].astype(F32), halo_r[q, :, cols].astype(F32), row_iota
            )
            k0, k1, k2 = tap_cols(cols)
            cv = k0 * two + k1 * one + k2 * now
            d_g = nt(h2_v[0, q * T : q * T + T, :], wd_v[cols, :])
            d_cv = d_g * pc[rows, cols].astype(F32)
            sm[0, 2:3, cols] += jnp.sum(d_cv * two, axis=0, keepdims=True)
            sm[0, 3:4, cols] += jnp.sum(d_cv * one, axis=0, keepdims=True)
            sm[0, 4:5, cols] += jnp.sum(d_cv * now, axis=0, keepdims=True)
            after1 = jnp.where(row_iota < T - 1, pltpu.roll(d_cv, T - 1, 0), 0.0)
            after2 = jnp.where(row_iota < T - 2, pltpu.roll(d_cv, T - 2, 0), 0.0)
            d_bx = k2 * d_cv + k1 * after1 + k0 * after2
            dhalo_s[q, :, cols] = d_cv[0:8]
            tail[q, :, cols] = d_bx[T - 16 : T]
            old_b = pb[rows, cols]
            old_x = px[rows, cols]
            pb_tail[q, :, cols] = old_b[T - 16 : T]
            px_tail[q, :, cols] = old_x[T - 16 : T]
            low = d_bx.astype(BF).astype(F32)
            pb[rows, cols] = (low * old_x.astype(F32)).astype(BF)
            px[rows, cols] = (low * old_b.astype(F32)).astype(BF)
            pc[rows, cols] = (d_g * cv).astype(BF)
            return 0

        lax.fori_loop(0, NC, conv_back, 0)

    s_dha, r_dha = take_s(), take_r()
    send_dhalo = remote(dhalo_s, dhalo_r, s_dha, r_dha, prev_dev)

    @pl.when(has_prev)
    def _():
        send_dhalo.start()

    y_send(3, 2)
    y_send(2, 3)

    hook("cb")

    s_x1, r_x1 = take_s(NCH), take_r(NCH)

    def d1_part(name, ids):
        def tile(n, _):
            cols = pl.ds(pl.multiple_of(n * 512, 512), 512)

            def rows_of(ref):
                return jnp.concatenate(
                    [ref[k * ROWS_CHUNK : (k + 1) * ROWS_CHUNK, :] for k in ids], axis=0
                )

            v = (
                nt(rows_of(pb), wg_v[cols, 0:CL])
                + nt(rows_of(pc), wg_v[cols, CL : 2 * CL])
                + nt(rows_of(px), wu_v[cols, 0:CL])
            ).astype(BF)
            for i, k in enumerate(ids):
                ring[k, :, cols] = v[i * ROWS_CHUNK : (i + 1) * ROWS_CHUNK]
            return 0

        lax.fori_loop(0, D // 512, tile, 0)
        for k in ids:
            remote(ring.at[k], xr_d1.at[k], s_x1 + k, r_x1 + k, x_dev).start()
        hook(name)

    d1_part("d1a", [q * CPS + k for q in range(S) for k in range(CPS - 1)])

    @pl.when(has_next)
    def _():
        wait_recv(dhalo_r, r_dha)

    @pl.when(jnp.logical_not(has_next))
    def _():
        dhalo_r[...] = jnp.zeros_like(dhalo_r)

    tail_iota = lax.broadcasted_iota(jnp.int32, (16, CL), 0)
    for q in range(S):
        first = jnp.broadcast_to(dhalo_r[q, 0:1, :], (16, CL))
        second = jnp.broadcast_to(dhalo_r[q, 1:2, :], (16, CL))
        fix = jnp.where(
            tail_iota == 14,
            k_taps[0] * first,
            jnp.where(tail_iota == 15, k_taps[1] * first + k_taps[0] * second, 0.0),
        )
        low = (tail[q] + fix).astype(BF).astype(F32)
        rows = pl.ds(q * T + T - 16, 16)
        pb[rows, :] = (low * px_tail[q].astype(F32)).astype(BF)
        px[rows, :] = (low * pb_tail[q].astype(F32)).astype(BF)

    s_dp, r_dp = take_s(4), take_r(4)
    theirs = pl.ds(pl.multiple_of((1 - c) * CH, LANE), CH)
    ours = pl.ds(pl.multiple_of(c * CH, LANE), CH)
    dp_sends = [
        remote(ref.at[:, theirs], dy_v.at[1, :, pl.ds(m * CH, CH)], s_dp + m, r_dp + m, core_dev)
        for m, ref in enumerate((pb, pc, px, gated))
    ]
    for cp in dp_sends:
        cp.start()
    hook("tail")

    d1_part("d1b", [q * CPS + k for q in range(S) for k in range(1, CPS)])

    for q in range(S):
        wait_recv(h1_v.at[1, pl.ds(q * T, T)], r_h1 + q)
    for k in range(NCH):
        rows = pl.ds(k * ROWS_CHUNK, ROWS_CHUNK)
        wait_recv(h2_v.at[1, rows], r_do + k)
    for m in range(4):
        wait_recv(dy_v.at[1, :, pl.ds(m * CH, CH)], r_dp + m)
    W4 = widths[4]
    g4 = [dg.at[i, pl.ds(k * SR, SR), pl.ds(0, W4)] for i in range(2) for k in range(2)]

    def g_mixer(u, _):
        zp = order_dyn(u)
        zc = pl.ds(pl.multiple_of(zp * GR, GR), GR)
        for m, (mine, lhs) in enumerate(((pb, h1_v), (pc, h1_v), (px, h1_v), (gated, h2_v))):
            v = tn(lhs[0, :, zc], mine[:, ours]) + tn(
                lhs[1, :, zc], dy_v[1, :, m * CH : (m + 1) * CH]
            )
            v = v.astype(BF)
            g4[0][:, m * CH : (m + 1) * CH] = v[:SR]
            g4[1][:, m * CH : (m + 1) * CH] = v[SR:]
        cps = [local(g4[h], gb4.at[zp, h], l_g + h) for h in range(2)]
        for cp in cps:
            cp.start()
        for cp in cps:
            cp.wait()

        @pl.when(u < NZ - 1)
        def _():
            y_send(4, u)

        return 0

    chunks("gc", NZ, g_mixer)
    for j in (3, 4):
        y_send(j, NZ - 1)

    l_o = take_l(2)

    def put_rows(v, out, rows, n):
        slot = n % 2
        cp = local(rb.at[slot], out.at[rows, :], l_o + slot)

        @pl.when(n >= 2)
        def _():
            cp.wait()

        rb[slot] = v
        cp.start()

    def put_done(out):
        for slot in range(2):
            local(rb.at[slot], out.at[pl.ds(0, ROWS_CHUNK), :], l_o + slot).wait()

    def block_chunk(k, _):
        rows = pl.ds(pl.multiple_of(k * ROWS_CHUNK, ROWS_CHUNK), ROWS_CHUNK)
        wait_recv(xr_dn.at[k], r_xdn + k)
        total = ring[4 + k].astype(F32) + xr_dn[k].astype(F32)
        put_rows((resid[rows, :] + total).astype(BF), block_out, rows, k)
        return 0

    chunks("blk", NCH, block_chunk)
    put_done(block_out)

    def mix_norm_back(n, _):
        k = (n % S) * CPS + n // S
        rows = pl.ds(pl.multiple_of(k * ROWS_CHUNK, ROWS_CHUNK), ROWS_CHUNK)
        wait_recv(xr_d1.at[k], r_x1 + k)
        d_h = ring[k].astype(F32) + xr_d1[k].astype(F32)
        xv = tok_v[rows, :].astype(F32)
        s1 = inv_rms(xv)
        n1 = xv * s1
        sm[0, 0:1, :] += jnp.sum(d_h * n1, axis=0, keepdims=True)
        e1 = d_h * gain_mix_row
        out = h2_v[0, rows, :].astype(F32) + s1 * (
            e1 - n1 * jnp.mean(e1 * n1, axis=-1, keepdims=True)
        )
        put_rows(out.astype(BF), d_tokens, rows, n)
        return 0

    chunks("dt", NCH, mix_norm_back)
    put_done(d_tokens)

    s_sm, r_sm = take_s(2 * NZ), take_r(2 * NZ)
    a = remote(sm.at[0], sm_o, s_sm, r_sm, core_dev)
    a.start()
    a.wait()
    chip_sum = sm[0] + sm_o[...]
    gain_w, tap_w = 2 * D // n_seq, 2 * CL // n_seq
    is_gain = lax.broadcasted_iota(jnp.int32, sm_t.shape[1:], 0) < 2
    for q in range(2 * NZ):
        gains = pltpu.roll(chip_sum, (D - q * gain_w) % D, 1)[:, 0:SMALL]
        tap_sums = pltpu.roll(chip_sum, (D - q * tap_w) % D, 1)[:, 0:SMALL]
        sm_t[q] = jnp.where(is_gain, gains, tap_sums)
    for k, dev in others:
        remote(sm_t.at[dev[0] // 2], sm_r.at[k], s_sm + k, r_sm + k, dev).start()
    @pl.when(end)
    def _():
        for e in range(NZ - 1):
            for h in range(2):
                per_core(0, lambda cut: wait_send(cut(gb0.at[0, h]), s_z[0] + 2 * e + h))

    for j in range(1, 5):
        for u in range(NZ - 1):
            per_core(j, lambda cut: wait_send(cut(ybs[j].at[0]), s_y[j] + u))
    for q in range(S):
        h1_send(q).wait_send()
    for k in range(NCH):
        wait_send(h2_v.at[0, pl.ds(k * ROWS_CHUNK, ROWS_CHUNK)], s_do + k)
        wait_send(ring.at[k], s_x1 + k)
        wait_send(ring.at[4 + k], s_xdn + k)
    for cp in dp_sends:
        cp.wait_send()

    @pl.when(has_next)
    def _():
        for q in range(S):
            halo_send(q).wait_send()

    @pl.when(has_prev)
    def _():
        send_dhalo.wait_send()

    hook("sm")

    total = sm_t[s // 2]
    for k, _ in others:
        wait_recv(sm_r.at[k], r_sm + k)
        total = total + sm_r[k]
    for k, _ in others:
        wait_send(sm_t.at[0], s_sm + k)
    sm_r[0] = total
    out_small = local(sm_r.at[0], small_out, l_small)
    out_small.start()
    out_small.wait()

    for role, cond in is_role.items():

        @pl.when(cond)
        def _(role=role):
            for finish in slot_last[role]:
                if finish is not None:
                    finish()

    for j in range(1, 5):
        per_core(j, lambda cut: wait_send(cut(ybs[j].at[0]), s_y[j] + NZ - 1))
    per_core(0, lambda cut: wait_send(cut(yb0), s_f0))


def fused_body(tokens, gain_mix, w_in, kernel, w_out, gain_ffn, w_gate, w_up, w_down, cotangent):
    S, T, D = tokens.shape
    CL = w_out.shape[0]
    FL = w_gate.shape[1]
    R = S * T
    n_seq = lax.axis_size("seq")
    tiles = FL // LANE
    FW = -(-tiles // 2) * LANE
    GR = D // NZ
    SR = GR // 2
    DR = SR // 2
    widths = [ZF_COLS, FW - ZF_COLS, FW, FW, 2 * CL]
    NCH = R // ROWS_CHUNK

    def sds(shape, dtype=BF):
        return jax.ShapeDtypeStruct(shape, dtype)

    outs = [sds((R, D)), sds((R, D)), sds((3, DR, FL)), sds((2, DR, 2 * CL)), sds((8, SMALL), F32)]
    outs += [sds((NZ, 2, SR, w)) for w in widths]
    outs += [sds((SR, widths[0]))] + [sds((NZ, SR, w)) for w in widths[1:]]
    outs += [sds((2, NZ, 2, SR, widths[0]))] + [sds((2, NZ, SR, w)) for w in widths[1:]]
    outs += [sds((NCH, ROWS_CHUNK, D))] * 2
    any_spec = pl.BlockSpec(memory_space=pl.ANY)
    V = pltpu.VMEM
    scratch = [
        V((D,), F32),
        V((3, CL), F32),
        V((D,), F32),
        V((R, D), BF),
        V((D, FW), BF),
        V((D, FW), BF),
        V((FW, D), BF),
        V((2, R, D), BF),
        V((2, R, D), BF),
        V((2, R, D), BF),
        V((2, R, FW), BF),
        V((2, R, FW), BF),
        V((2, R, FW), BF),
        V((R, CL), BF),
        V((R, CL), BF),
        V((R, CL), BF),
        V((R, CL), BF),
        V((R, CL), BF),
        V((R, D), F32),
        V((NCH, ROWS_CHUNK, D), BF),
        V((8, ROWS_CHUNK, D), BF),
        V((NCH, ROWS_CHUNK, D), BF),
        V((NCH, ROWS_CHUNK, D), BF),
        V((NCH, ROWS_CHUNK, D), BF),
        V((2, ROWS_CHUNK, D), BF),
        V((4, SR, FW), BF),
        V((4, SR, FW), BF),
        V((S, 16, CL), BF),
        V((S, 16, CL), BF),
        V((S, 8, CL), F32),
        V((S, 8, CL), F32),
        V((S, 16, CL), F32),
        V((S, 16, CL), BF),
        V((S, 16, CL), BF),
        V((1, 8, D), F32),
        V((8, D), F32),
        V((2 * NZ, 8, SMALL), F32),
        V((2 * NZ, 8, SMALL), F32),
        pltpu.SemaphoreType.DMA((N_SEND,)),
        pltpu.SemaphoreType.DMA((N_RECV,)),
        pltpu.SemaphoreType.DMA((N_LOCAL,)),
    ]
    flops = 2 * R * D * (4 * CL + 3 * FL) * 3
    res = pl.pallas_call(
        functools.partial(step_kernel, (R, T, D, CL, FL, FW)),
        out_shape=outs,
        in_specs=[any_spec] * 10,
        out_specs=[any_spec] * len(outs),
        scratch_shapes=scratch,
        compiler_params=pltpu.CompilerParams(
            collective_id=0, has_side_effects=True, vmem_limit_bytes=63 << 20
        ),
        cost_estimate=pl.CostEstimate(flops=flops, bytes_accessed=200 << 20, transcendentals=0),
        name="block_step",
    )(
        tokens.reshape(R, D), gain_mix, w_in, kernel, w_out,
        gain_ffn, w_gate, w_up, w_down, cotangent.reshape(R, D),
    )
    block_out, d_tokens, g_mix, g_in, g_taps, g_out, g_gain, g_gate, g_up, g_down = finish(
        n_seq, *res[:5]
    )
    return (
        block_out.reshape(S, T, D),
        d_tokens.reshape(S, T, D),
        g_mix, g_in, g_taps, g_out.T, g_gain, g_gate, g_up, g_down.T,
    )


def finish_kernel(
    n_seq, block_in, d_in, ffn_in, conv_in, small_in,
    block_out, d_out, g_mix, g_in, g_taps, g_out, g_gain, g_gate, g_up, g_down,
    block_v, d_v, ffn, conv, small, gate_v, up_v, down_v, in_v, out_v, mix_v, taps_v, gain_v, sem,
):
    D = d_in.shape[1]
    CL = conv_in.shape[2] // 2
    s = lax.axis_index("seq")
    count = [0]

    def copy(src, dst):
        count[0] += 1
        cp = pltpu.make_async_copy(src, dst, sem.at[count[0] - 1])
        cp.start()
        return cp

    loads = [copy(ffn_in.at[0], ffn.at[0]), copy(conv_in, conv), copy(small_in, small)]
    loads += [copy(ffn_in.at[m], ffn.at[m]) for m in (1, 2)]
    passing = [copy(block_in, block_v), copy(d_in, d_v)]
    stores = []
    loads[0].wait()
    down_v[...] = ffn[0].astype(F32)
    stores.append(copy(down_v, g_down))
    loads[1].wait()
    half = CL // 2
    for core in range(2):
        for m in range(3):
            in_v[m, :, core * half : (core + 1) * half] = conv[core, :, m * half : (m + 1) * half].astype(F32)
    stores.append(copy(in_v, g_in))
    for core in range(2):
        out_v[:, core * half : (core + 1) * half] = conv[core, :, 3 * half : 4 * half].astype(F32)
    stores.append(copy(out_v, g_out))
    passing[0].wait()
    stores.append(copy(block_v, block_out))
    passing[1].wait()
    stores.append(copy(d_v, d_out))
    loads[3].wait()
    gate_v[...] = ffn[1].astype(F32)
    stores.append(copy(gate_v, g_gate))
    loads[4].wait()
    up_v[...] = ffn[2].astype(F32)
    stores.append(copy(up_v, g_up))
    loads[2].wait()
    per_d, per_c = D // n_seq, CL // n_seq
    mine = pltpu.roll(small[...], SMALL - (s % 2) * per_d, 1)
    mix_v[...] = mine[0, 0:per_d]
    gain_v[...] = mine[1, 0:per_d]
    mine = pltpu.roll(small[...], SMALL - (s % 2) * per_c, 1)
    for t in range(3):
        taps_v[t] = mine[2 + t : 3 + t, 0:per_c]
    stores += [copy(mix_v, g_mix), copy(gain_v, g_gain), copy(taps_v, g_taps)]
    for cp in stores:
        cp.wait()


def finish(n_seq, block_out, d_tokens, g_ffn, g_conv, small):
    R, D = block_out.shape
    _, DR, FL = g_ffn.shape
    CL = g_conv.shape[2] // 2
    any_spec = pl.BlockSpec(memory_space=pl.ANY)
    V = pltpu.VMEM
    tails = [
        (DR, FL), (DR, FL), (DR, FL), (3, DR, CL), (DR, CL),
        (D // n_seq,), (3, 1, CL // n_seq), (D // n_seq,),
    ]
    gate, up, down, inp, out, mix, taps, gain = [jax.ShapeDtypeStruct(t, F32) for t in tails]
    low = jax.ShapeDtypeStruct((R, D), BF)
    return pl.pallas_call(
        functools.partial(finish_kernel, n_seq),
        out_shape=[low, low, mix, inp, taps, out, gain, gate, up, down],
        in_specs=[any_spec] * 5,
        out_specs=[any_spec] * 10,
        scratch_shapes=[V((R, D), BF), V((R, D), BF), V(g_ffn.shape, BF), V(g_conv.shape, BF), V(small.shape, F32)]
        + [V(t, F32) for t in tails]
        + [pltpu.SemaphoreType.DMA((20,))],
        compiler_params=pltpu.CompilerParams(vmem_limit_bytes=63 << 20),
        name="finish",
    )(block_out, d_tokens, g_ffn, g_conv, small)


def from_behind(value, axis, by):
    count = lax.axis_size(axis)
    pairs = [(i, i + by) for i in range(count) if 0 <= i + by < count]
    return lax.ppermute(value, axis, pairs)


def rms_scale(vector):
    return lax.rsqrt(jnp.mean(vector * vector, axis=-1, keepdims=True) + epsilon)


def norm_back(d_normout, normed, inv_scale, gain_vec):
    d_normed = d_normout * gain_vec
    return inv_scale * (d_normed - normed * jnp.mean(d_normed * normed, axis=-1, keepdims=True))


def matmul(lhs_mat, rhs_mat):
    return jnp.dot(lhs_mat, rhs_mat, preferred_element_type=jnp.float32)


def left_trans(lhs_mat, rhs_mat):
    return lax.dot_general(
        lhs_mat, rhs_mat, (((0,), (0,)), ((), ())), preferred_element_type=jnp.float32
    )


def right_trans(lhs_mat, rhs_mat):
    return lax.dot_general(
        lhs_mat, rhs_mat, (((1,), (1,)), ((), ())), preferred_element_type=jnp.float32
    )


def general_body(tokens, gain_mix, w_in, kernel, w_out, gain_ffn, w_gate, w_up, w_down, cotangent):
    seq_count, tok_rows, model_width = tokens.shape
    row_count = seq_count * tok_rows
    tokens_f = tokens.astype(jnp.float32).reshape(row_count, model_width)
    scale_mix = rms_scale(tokens_f)
    normed_mix = tokens_f * scale_mix
    h_mix = (normed_mix * gain_mix).astype(jnp.bfloat16)
    proj_b = matmul(h_mix, w_in[0])
    proj_c = matmul(h_mix, w_in[1])
    proj_x = matmul(h_mix, w_in[2])
    conv_in = (proj_b * proj_x).astype(jnp.bfloat16).reshape(seq_count, tok_rows, -1)
    before = from_behind(conv_in[:, tok_rows - 2 :, :], "seq", 1)
    extended = jnp.concatenate([before, conv_in], axis=1).astype(jnp.float32)
    conv_out = (
        kernel[0] * extended[:, :-2] + kernel[1] * extended[:, 1:-1] + kernel[2] * extended[:, 2:]
    )
    conv_flat = conv_out.reshape(row_count, -1)
    gated = (proj_c * conv_flat).astype(jnp.bfloat16)
    mixed_sum = lax.psum(matmul(gated, w_out).astype(jnp.bfloat16), "chan").astype(jnp.float32)
    residual = tokens_f + mixed_sum
    scale_ffn = rms_scale(residual)
    normed_ffn = residual * scale_ffn
    h_ffn = (normed_ffn * gain_ffn).astype(jnp.bfloat16)
    gate_pre = matmul(h_ffn, w_gate)
    up_value = matmul(h_ffn, w_up)
    sigmoid_gate = jax.nn.sigmoid(gate_pre)
    silu_gate = gate_pre * sigmoid_gate
    hidden = (silu_gate * up_value).astype(jnp.bfloat16)
    ffn_total = lax.psum(matmul(hidden, w_down).astype(jnp.bfloat16), "chan").astype(jnp.float32)
    block_out = (
        (residual + ffn_total).astype(jnp.bfloat16).reshape(seq_count, tok_rows, model_width)
    )
    grad_out = cotangent.reshape(row_count, model_width)
    g_w_down = left_trans(hidden, grad_out)
    d_hidden = right_trans(grad_out, w_down)
    d_gate = (d_hidden * up_value * sigmoid_gate * (1.0 + gate_pre * (1.0 - sigmoid_gate))).astype(
        jnp.bfloat16
    )
    d_up = (d_hidden * silu_gate).astype(jnp.bfloat16)
    g_w_gate = left_trans(h_ffn, d_gate)
    g_w_up = left_trans(h_ffn, d_up)
    d_h_ffn = lax.psum(
        (right_trans(d_gate, w_gate) + right_trans(d_up, w_up)).astype(jnp.bfloat16), "chan"
    ).astype(jnp.float32)
    g_gain_ffn = jnp.sum(d_h_ffn * normed_ffn, axis=0)
    d_resid = grad_out.astype(jnp.float32) + norm_back(d_h_ffn, normed_ffn, scale_ffn, gain_ffn)
    d_mixed = d_resid.astype(jnp.bfloat16)
    g_w_out = left_trans(gated, d_mixed)
    d_gated = right_trans(d_mixed, w_out)
    d_proj_c = (d_gated * conv_flat).astype(jnp.bfloat16)
    d_conv = (d_gated * proj_c).reshape(seq_count, tok_rows, -1)
    after_rows = from_behind(d_conv[:, :2, :], "seq", -1)
    ext_back = jnp.concatenate([d_conv, after_rows], axis=1)
    d_conv_in = (
        kernel[2] * ext_back[:, :-2] + kernel[1] * ext_back[:, 1:-1] + kernel[0] * ext_back[:, 2:]
    )
    g_kernel = jnp.stack(
        [
            jnp.sum(d_conv * extended[:, :-2], axis=(0, 1)),
            jnp.sum(d_conv * extended[:, 1:-1], axis=(0, 1)),
            jnp.sum(d_conv * extended[:, 2:], axis=(0, 1)),
        ]
    ).reshape(3, 1, -1)
    d_conv_low = d_conv_in.reshape(row_count, -1).astype(jnp.bfloat16)
    d_proj_b = (d_conv_low * proj_x).astype(jnp.bfloat16)
    d_proj_x = (d_conv_low * proj_b).astype(jnp.bfloat16)
    g_w_in = jnp.stack(
        [left_trans(h_mix, d_proj_b), left_trans(h_mix, d_proj_c), left_trans(h_mix, d_proj_x)]
    )
    d_h_mix = lax.psum(
        (
            right_trans(d_proj_b, w_in[0])
            + right_trans(d_proj_c, w_in[1])
            + right_trans(d_proj_x, w_in[2])
        ).astype(jnp.bfloat16),
        "chan",
    ).astype(jnp.float32)
    g_gain_mix = jnp.sum(d_h_mix * normed_mix, axis=0)
    d_tokens = (
        (d_resid + norm_back(d_h_mix, normed_mix, scale_mix, gain_mix))
        .astype(jnp.bfloat16)
        .reshape(seq_count, tok_rows, model_width)
    )
    summed = (
        lax.psum_scatter(g_w_in, "seq", scatter_dimension=1, tiled=True),
        lax.psum_scatter(g_w_out, "seq", scatter_dimension=1, tiled=True),
        lax.psum_scatter(g_kernel, "seq", scatter_dimension=2, tiled=True),
        lax.psum_scatter(g_gain_mix, "seq", scatter_dimension=0, tiled=True),
        lax.psum_scatter(g_w_gate, "seq", scatter_dimension=0, tiled=True),
        lax.psum_scatter(g_w_up, "seq", scatter_dimension=0, tiled=True),
        lax.psum_scatter(g_w_down, "seq", scatter_dimension=1, tiled=True),
        lax.psum_scatter(g_gain_ffn, "seq", scatter_dimension=0, tiled=True),
    )
    sum_in, sum_out, sum_kernel, sum_gain_mix, sum_gate, sum_up, sum_down, sum_gain_ffn = summed
    return (
        block_out,
        d_tokens,
        sum_gain_mix,
        sum_in,
        sum_kernel,
        sum_out,
        sum_gain_ffn,
        sum_gate,
        sum_up,
        sum_down,
    )


def solution(mesh):
    body = fused_body if mesh.shape["seq"] == 4 * NZ else general_body
    placed = (
        P(None, "seq", None),
        P(),
        P(None, None, "chan"),
        P(None, "chan"),
        P("chan", None),
        P(),
        P(None, "chan"),
        P(None, "chan"),
        P("chan", None),
        P(None, "seq", None),
    )
    return jax.shard_map(
        body,
        mesh=mesh,
        in_specs=placed,
        out_specs=(
            P(None, "seq", None),
            P(None, "seq", None),
            P("seq"),
            P(None, "seq", "chan"),
            P(None, "chan", "seq"),
            P("chan", "seq"),
            P("seq"),
            P("seq", "chan"),
            P("seq", "chan"),
            P("chan", "seq"),
        ),
        check_vma=False,
    )
```
